32 devices in a mesh: dp: 32 (over z, y, x, core).
Axes of the slice: x: 2, y: 2, z: 4, core: 2. Of those that a mesh axis runs over, the one named last changes fastest.
Arguments:
- block_in: bfloat16 [4096, 2048], P('dp'), may hold values from -6 to 6
- out_grad: bfloat16 [4096, 2048], P('dp'), may hold values from -6 to 6
- norm1_gain: float32 [2048], P('dp'), may hold values from 0.5 to 1.5
- conv_weight: float32 [6144, 4], P('dp'), may hold values from -3 to 3
- head_gain: float32 [2048], P('dp'), may hold values from 0.5 to 1.5
- qkv_weight: float32 [2048, 6144], P('dp'), may hold values from -0.125 to 0.125
- beta_weight: float32 [2048, 16], P('dp'), may hold values from -0.125 to 0.125
- gate_weight: float32 [2048, 2048], P('dp'), may hold values from -0.125 to 0.125
- out_weight: float32 [2048, 2048], P('dp'), may hold values from -0.125 to 0.125
- norm2_gain: float32 [2048], P('dp'), may hold values from 0.5 to 1.5
- updown_weight: float32 [2048, 11264], P('dp'), may hold values from -0.125 to 0.125
- down_weight: float32 [5632, 2048], P('dp'), may hold values from -0.078125 to 0.078125
- seq_blocks: int32 [32, 2], P('dp'), may hold values from 0 to 2, as said below
- lead_blocks: int32 [32], P('dp'), may hold values from 0 to 1, as said below
Outputs:
- block_out: bfloat16 [4096, 2048], P('dp')
- input_grad: bfloat16 [4096, 2048], P('dp')
- norm1_gain_grad: float32 [2048], P('dp')
- conv_weight_grad: float32 [6144, 4], P('dp')
- head_gain_grad: float32 [2048], P('dp')
- qkv_weight_grad: float32 [2048, 6144], P('dp')
- beta_weight_grad: float32 [2048, 16], P('dp')
- gate_weight_grad: float32 [2048, 2048], P('dp')
- out_weight_grad: float32 [2048, 2048], P('dp')
- norm2_gain_grad: float32 [2048], P('dp')
- updown_weight_grad: float32 [2048, 11264], P('dp')
- down_weight_grad: float32 [5632, 2048], P('dp')
The draws below stay inside these ranges and needn't reach their ends.
Inputs may be any that keep to these rules, and one draw needn't show every extreme that they name: `seq_blocks`: row r gives device r's two sequence lengths in blocks of 64 rows; the first is at least 1, the second may be 0, both together at most 2; some device holds one sequence of 2 blocks. `lead_blocks`: padding blocks before device r's sequences; together with both lengths at most 2; the blocks after the sequences are padding.
All inputs are finite; a program needn't handle non-finite values.
Results may differ from the reference program's by a relative error of at most 0.012.
The reference program's roundings to bfloat16 on the way count: a program that leaves them out, or rounds other values in their place, can miss the bound.
Values may be sent and summed in bfloat16 or wider, within the bound.
No kernel may reach another device: no remote copies, remote signals or barrier semaphores. Data moves between devices by JAX's collectives and lax.ppermute only.
A program may use at most 448 MiB of HBM per device.

```python
import jax
import jax.numpy as jnp
from jax import lax

D = 2048
HEADS = 16
HEAD_DIM = 128
FF = 5632
KERNEL = 4
BLOCK_ROWS = 64
TOK_DEV = 128
TOKENS = 4096
BLOCKS_DEV = 2
N_DP = 32


def layout_draw(key):
    keys = jax.random.split(key, 5)
    first_len = jax.random.randint(keys[0], (N_DP,), 1, BLOCKS_DEV + 1)
    second_len = jax.random.randint(keys[1], (N_DP,), 0, BLOCKS_DEV + 1)
    second_len = jnp.minimum(second_len, BLOCKS_DEV - first_len)
    spare = BLOCKS_DEV - first_len - second_len
    lead_count = jax.random.randint(keys[2], (N_DP,), 0, BLOCKS_DEV) % (spare + 1)
    full_device = jax.random.randint(keys[3], (), 0, N_DP)
    short_device = (full_device + 1 + jax.random.randint(keys[4], (), 0, N_DP - 1)) % N_DP
    position = jnp.arange(N_DP)
    first_len = jnp.where(position == full_device, BLOCKS_DEV, first_len)
    second_len = jnp.where(position == full_device, 0, second_len)
    lead_count = jnp.where(position == full_device, 0, lead_count)
    first_len = jnp.where(position == short_device, 1, first_len)
    second_len = jnp.where(position == short_device, 0, second_len)
    lead_count = jnp.where(position == short_device, BLOCKS_DEV - 1, lead_count)
    return (first_len.astype(jnp.int32), second_len.astype(jnp.int32), lead_count.astype(jnp.int32))


def draw_seq_blocks(key, part):
    first_len, second_len, lead_count = layout_draw(key)
    return jnp.stack([first_len, second_len], 1).astype(jnp.int32)


def draw_lead_blocks(key, part):
    first_len, second_len, lead_count = layout_draw(key)
    return lead_count.astype(jnp.int32)


def strengthened(values, own_key, source, target, blocks, factor):
    owner, partner = [(jnp.arange(values.shape[dim]) // (values.shape[dim] // blocks)).reshape([-1 if axis == dim else 1 for axis in range(values.ndim)]) for dim in (source, target)]
    chosen = jax.random.permutation(own_key, blocks)[partner]
    strong = (owner == chosen) | (owner == (partner + blocks // 2) % blocks)
    return jnp.where(strong, factor * values, values)


def steps_of(rng, shape, cuts, smallest, largest):
    level, own = 1.0, jax.random.fold_in(rng, 6)
    for dim, parts in cuts:
        heights = jnp.exp(jax.random.uniform(jax.random.fold_in(own, dim), (parts,), jnp.float32, smallest / len(cuts), largest / len(cuts)))
        level = level * jnp.repeat(heights, shape[dim] // parts).reshape([-1 if axis == dim else 1 for axis in range(len(shape))])
    return level


def centred(key, dims, deviation, most, cuts=(), kind=jnp.bfloat16):
    array = jax.random.normal(key, dims, jnp.float32) * deviation
    if len(cuts) > 0:
        array = steps_of(key, dims, cuts, -0.22, 0.18) * array
    return jnp.clip(array, min=-most, max=most).astype(kind)


def heavy_noise(key, extent, width, limit, shards, heavy, held_as=jnp.bfloat16):
    array = width * jax.random.normal(key, extent, jnp.float32)
    if shards:
        array = array * steps_of(key, extent, shards, -0.22, 0.18)
    return jnp.clip(strengthened(array, jax.random.fold_in(key, 3), *heavy), -limit, limit).astype(held_as)


def setup_inputs(seed: int = 0) -> dict:
    arg_keys = jax.random.split(jax.random.key(seed), 15)
    return {
        "block_in": heavy_noise(arg_keys[0], (TOKENS, D), 1.0, 6.0, ((0, 32),), (0, 1, 32, 2.75)),
        "out_grad": centred(arg_keys[1], (TOKENS, D), 1.0, 6.0, ((0, 32),)),
        "norm1_gain": jnp.clip(1.0 + 0.1 * jax.random.normal(arg_keys[2], (D,), jnp.float32), 0.5, 1.5),
        "conv_weight": centred(arg_keys[3], (3 * D, KERNEL), 0.5, 3.0, ((0, 32),), jnp.float32),
        "head_gain": jnp.clip(1.0 + 0.1 * jax.random.normal(arg_keys[4], (D,), jnp.float32), 0.5, 1.5),
        "qkv_weight": centred(arg_keys[5], (D, 3 * D), D ** -0.5, 0.125, ((0, 32),), jnp.float32),
        "beta_weight": centred(arg_keys[6], (D, HEADS), D ** -0.5, 0.125, ((0, 32),), jnp.float32),
        "gate_weight": centred(arg_keys[7], (D, D), D ** -0.5, 0.125, ((0, 32),), jnp.float32),
        "out_weight": centred(arg_keys[8], (D, D), D ** -0.5, 0.125, ((0, 32),), jnp.float32),
        "norm2_gain": jnp.clip(1.0 + 0.1 * jax.random.normal(arg_keys[9], (D,), jnp.float32), 0.5, 1.5),
        "updown_weight": centred(arg_keys[10], (D, 2 * FF), D ** -0.5, 0.125, ((0, 32),), jnp.float32),
        "down_weight": centred(arg_keys[11], (FF, D), FF ** -0.5, 0.078125, ((0, 32),), jnp.float32),
        "seq_blocks": draw_seq_blocks(jax.random.fold_in(arg_keys[14], 71), 0),
        "lead_blocks": draw_lead_blocks(jax.random.fold_in(arg_keys[14], 71), 0),
    }


@jax.custom_vjp
def low(v):
    return lax.optimization_barrier(v.astype(jnp.bfloat16)).astype(jnp.float32)

@jax.custom_vjp
def low_back(v):
    return v

def low_keep(v):
    return (low(v), None)

def low_pass(kept, grad):
    return (grad,)

def back_keep(v):
    return (v, None)

def back_low(kept, grad):
    return (low(grad),)
low.defvjp(low_keep, low_pass)
low_back.defvjp(back_keep, back_low)
HIGHEST = lax.Precision.HIGHEST

def exact_product(left, right):
    return jnp.dot(left.astype(jnp.float32), right.astype(jnp.float32), precision=HIGHEST, preferred_element_type=jnp.float32)

def rms_scale(values, gain_vector):
    return values * lax.rsqrt(lax.optimization_barrier(jnp.mean(values * values, -1, keepdims=True)) + 1e-06) * gain_vector

def block_layout(first_len, second_len, lead_count):
    position = jnp.arange(BLOCKS_DEV, dtype=jnp.int32)
    in_first = (position >= lead_count) & (position < lead_count + first_len)
    in_second = (position >= lead_count + first_len) & (position < lead_count + first_len + second_len)
    doc_block = jnp.where(in_first, 1, jnp.where(in_second, 2, 0)).astype(jnp.int32)
    starts = (position == lead_count) | (position == lead_count + first_len) & (second_len > 0)
    persist = jnp.where(starts, 0.0, 1.0).astype(jnp.float32)
    doc_rows = jnp.repeat(doc_block, BLOCK_ROWS)
    live = (doc_rows > 0).astype(jnp.float32)
    return (doc_rows, persist, live)

def causal_conv(pre_values, taps, doc_rows):
    summed = pre_values * taps[:, 0]
    for offset in range(1, KERNEL):
        shifted = jnp.concatenate([jnp.zeros((offset, pre_values.shape[1]), jnp.float32), pre_values[:-offset]], 0)
        earlier = jnp.concatenate([jnp.full((offset,), -1, jnp.int32), doc_rows[:-offset]], 0)
        matching = (earlier == doc_rows).astype(jnp.float32)[:, None]
        summed = summed + taps[:, offset] * shifted * matching
    return summed

def unit_norm(values):
    return values * lax.rsqrt(lax.optimization_barrier(jnp.sum(values * values, -1, keepdims=True)) + 1e-06)

def delta_rule(query_heads, key_heads, value_heads, strengths, persist):

    def blocks(values):
        return values.reshape(BLOCKS_DEV, BLOCK_ROWS, HEADS, HEAD_DIM).transpose(0, 2, 1, 3)
    query_block = blocks(query_heads)
    key_block = blocks(key_heads)
    value_block = blocks(value_heads)
    strength_block = strengths.reshape(BLOCKS_DEV, BLOCK_ROWS, HEADS).transpose(0, 2, 1)[..., None]
    key_scaled = key_block * strength_block
    lower_part = jnp.tril(jnp.einsum('nhid,nhjd->nhij', key_scaled, key_block, precision=HIGHEST), -1)
    system = lower_part + jnp.eye(BLOCK_ROWS, dtype=jnp.float32)
    w_block = jax.scipy.linalg.solve_triangular(system, key_scaled, lower=True, unit_diagonal=True)
    u_block = jax.scipy.linalg.solve_triangular(system, value_block * strength_block, lower=True, unit_diagonal=True)
    scores = jnp.tril(jnp.einsum('nhid,nhjd->nhij', query_block, key_block, precision=HIGHEST))

    def advance(memory, inputs):
        w_part, u_part, query_part, key_part, score_part, factor = inputs
        memory = memory * factor
        corrected = u_part - jnp.einsum('hid,hed->hie', w_part, memory, precision=HIGHEST)
        emitted = jnp.einsum('hid,hed->hie', query_part, memory, precision=HIGHEST)
        emitted = emitted + jnp.einsum('hij,hje->hie', score_part, corrected, precision=HIGHEST)
        memory = memory + jnp.einsum('hie,hid->hed', corrected, key_part, precision=HIGHEST)
        return (memory, emitted)
    initial = jnp.zeros((HEADS, HEAD_DIM, HEAD_DIM), jnp.float32)
    closing, emitted = lax.scan(jax.checkpoint(advance), initial, (w_block, u_block, query_block, key_block, scores, persist))
    return emitted.transpose(0, 2, 1, 3).reshape(BLOCKS_DEV * BLOCK_ROWS, HEADS * HEAD_DIM)

def mixer(qkv_pre, beta_pre, gate_pre, taps, head_vector, doc_rows, persist, live):
    convolved = jax.nn.silu(causal_conv(qkv_pre, taps, doc_rows))
    query_heads = unit_norm(convolved[:, :D].reshape(-1, HEADS, HEAD_DIM)) * HEAD_DIM ** (-0.5)
    key_heads = unit_norm(convolved[:, D:2 * D].reshape(-1, HEADS, HEAD_DIM))
    value_heads = convolved[:, 2 * D:].reshape(-1, HEADS, HEAD_DIM)
    strengths = jax.nn.sigmoid(beta_pre) * live[:, None]
    head_out = delta_rule(query_heads, key_heads, value_heads, strengths, persist).reshape(-1, HEADS, HEAD_DIM)
    scaled = head_out * lax.rsqrt(lax.optimization_barrier(jnp.mean(head_out * head_out, -1, keepdims=True)) + 1e-05)
    return scaled.reshape(-1, D) * head_vector * jax.nn.silu(gate_pre) * live[:, None]

def forward(inputs, weights, doc_rows, persist, live):
    gain_one, conv_full, head_full, w_qkv, w_beta, w_gate, w_out, gain_two, w_updown, w_down = [low(weight) for weight in weights]
    count = inputs.shape[0]
    flat = inputs.reshape(count * TOK_DEV, D)
    normed = low(rms_scale(flat, gain_one))
    qkv_pre = low_back(exact_product(normed, w_qkv))
    beta_pre = low_back(exact_product(normed, w_beta))
    gate_pre = low_back(exact_product(normed, w_gate))
    mixed = jax.vmap(mixer, in_axes=(0, 0, 0, None, None, 0, 0, 0))(qkv_pre.reshape(count, TOK_DEV, 3 * D), beta_pre.reshape(count, TOK_DEV, HEADS), gate_pre.reshape(count, TOK_DEV, D), conv_full, head_full, doc_rows, persist, live)
    mixed = low(mixed.reshape(count * TOK_DEV, D))
    hidden = flat + low_back(exact_product(mixed, w_out))
    normed_two = low(rms_scale(hidden, gain_two))
    updown = low_back(exact_product(normed_two, w_updown))
    active = low(jax.nn.silu(updown[:, :FF]) * updown[:, FF:])
    result = hidden + low_back(exact_product(active, w_down))
    return result.reshape(count, TOK_DEV, D)

def reference(block_in, out_grad, norm1_gain, conv_weight, head_gain, qkv_weight, beta_weight, gate_weight, out_weight, norm2_gain, updown_weight, down_weight, seq_blocks, lead_blocks):
    group = min(N_DP, max(1, 4096 // TOK_DEV))
    steps_count = N_DP // group
    doc_rows, persist, live = jax.vmap(block_layout)(seq_blocks[:, 0], seq_blocks[:, 1], lead_blocks)
    weights = (norm1_gain, conv_weight, head_gain, qkv_weight, beta_weight, gate_weight, out_weight, norm2_gain, updown_weight, down_weight)

    def regroup(values):
        return values.reshape((steps_count, group) + values.shape[1:])
    inputs = block_in.astype(jnp.float32).reshape(steps_count, group, TOK_DEV, D)
    cotangent = out_grad.astype(jnp.float32).reshape(steps_count, group, TOK_DEV, D)

    def advance(totals, pieces):
        piece_in, piece_cot, piece_docs, piece_persist, piece_live = pieces

        def closure(values, *params):
            return forward(values, params, piece_docs, piece_persist, piece_live)
        result, pullback = jax.vjp(closure, piece_in, *weights)
        grads = pullback(piece_cot)
        totals = tuple((left + right for left, right in zip(totals, grads[1:])))
        return (totals, (result, grads[0]))
    zeros = tuple((jnp.zeros_like(weight) for weight in weights))
    totals, (outputs, input_grads) = lax.scan(advance, zeros, (inputs, cotangent, regroup(doc_rows), regroup(persist), regroup(live)))
    outputs = outputs.reshape(TOKENS, D).astype(jnp.bfloat16)
    input_grads = input_grads.reshape(TOKENS, D).astype(jnp.bfloat16)
    return (outputs, input_grads, totals[0], totals[1], totals[2], totals[3], totals[4], totals[5], totals[6], totals[7], totals[8], totals[9])
```

```python
import jax
import jax.numpy as jnp
from jax import lax
from jax.sharding import PartitionSpec as P

D = 2048
HEADS = 16
HEAD_DIM = 128
FF = 5632
KERNEL = 4
BLOCK_ROWS = 64
BLOCKS_DEV = 2


HIGHEST = lax.Precision.HIGHEST
MODEL = 32


def rms_scale(values, gain_vector):
    return values * lax.rsqrt(jnp.mean(values * values, -1, keepdims=True) + 1e-06) * gain_vector


def block_layout(first_len, second_len, lead_count):
    position = jnp.arange(BLOCKS_DEV, dtype=jnp.int32)
    in_first = (position >= lead_count) & (position < lead_count + first_len)
    in_second = (position >= lead_count + first_len) & (
        position < lead_count + first_len + second_len
    )
    doc_block = jnp.where(in_first, 1, jnp.where(in_second, 2, 0)).astype(jnp.int32)
    starts = (position == lead_count) | (position == lead_count + first_len) & (second_len > 0)
    persist = jnp.where(starts, 0.0, 1.0).astype(jnp.float32)
    doc_rows = jnp.repeat(doc_block, BLOCK_ROWS)
    live = (doc_rows > 0).astype(jnp.float32)
    return (doc_rows, persist, live)


def causal_conv(pre_values, taps, doc_rows):
    summed = pre_values * taps[:, 0]
    for offset in range(1, KERNEL):
        shifted = jnp.concatenate(
            [jnp.zeros((offset, pre_values.shape[1]), jnp.float32), pre_values[:-offset]], 0
        )
        earlier = jnp.concatenate([jnp.full((offset,), -1, jnp.int32), doc_rows[:-offset]], 0)
        matching = (earlier == doc_rows).astype(jnp.float32)[:, None]
        summed = summed + taps[:, offset] * shifted * matching
    return summed


def unit_norm(values):
    return values * lax.rsqrt(jnp.sum(values * values, -1, keepdims=True) + 1e-06)


def delta_rule(query_heads, key_heads, value_heads, strengths, persist):

    def blocks(values):
        return values.reshape(BLOCKS_DEV, BLOCK_ROWS, HEADS, HEAD_DIM).transpose(0, 2, 1, 3)

    query_block = blocks(query_heads)
    key_block = blocks(key_heads)
    value_block = blocks(value_heads)
    strength_block = strengths.reshape(BLOCKS_DEV, BLOCK_ROWS, HEADS).transpose(0, 2, 1)[..., None]
    key_scaled = key_block * strength_block
    lower_part = jnp.tril(
        jnp.einsum("nhid,nhjd->nhij", key_scaled, key_block, precision=HIGHEST), -1
    )
    system = lower_part + jnp.eye(BLOCK_ROWS, dtype=jnp.float32)
    w_block = jax.scipy.linalg.solve_triangular(system, key_scaled, lower=True, unit_diagonal=True)
    u_block = jax.scipy.linalg.solve_triangular(
        system, value_block * strength_block, lower=True, unit_diagonal=True
    )
    scores = jnp.tril(jnp.einsum("nhid,nhjd->nhij", query_block, key_block, precision=HIGHEST))

    def advance(memory, inputs):
        w_part, u_part, query_part, key_part, score_part, factor = inputs
        memory = memory * factor
        corrected = u_part - jnp.einsum("hid,hed->hie", w_part, memory, precision=HIGHEST)
        emitted = jnp.einsum("hid,hed->hie", query_part, memory, precision=HIGHEST)
        emitted = emitted + jnp.einsum("hij,hje->hie", score_part, corrected, precision=HIGHEST)
        memory = memory + jnp.einsum("hie,hid->hed", corrected, key_part, precision=HIGHEST)
        return (memory, emitted)

    initial = jnp.zeros((HEADS, HEAD_DIM, HEAD_DIM), jnp.float32)
    closing, emitted = lax.scan(
        jax.checkpoint(advance),
        initial,
        (w_block, u_block, query_block, key_block, scores, persist),
    )
    return emitted.transpose(0, 2, 1, 3).reshape(BLOCKS_DEV * BLOCK_ROWS, HEADS * HEAD_DIM)


def mixer(qkv_pre, beta_pre, gate_pre, taps, head_vector, doc_rows, persist, live):
    convolved = jax.nn.silu(causal_conv(qkv_pre, taps, doc_rows))
    query_heads = unit_norm(convolved[:, :D].reshape(-1, HEADS, HEAD_DIM)) * HEAD_DIM ** (-0.5)
    key_heads = unit_norm(convolved[:, D : 2 * D].reshape(-1, HEADS, HEAD_DIM))
    value_heads = convolved[:, 2 * D :].reshape(-1, HEADS, HEAD_DIM)
    strengths = jax.nn.sigmoid(beta_pre) * live[:, None]
    head_out = delta_rule(query_heads, key_heads, value_heads, strengths, persist).reshape(
        -1, HEADS, HEAD_DIM
    )
    scaled = head_out * lax.rsqrt(jnp.mean(head_out * head_out, -1, keepdims=True) + 1e-05)
    return scaled.reshape(-1, D) * head_vector * jax.nn.silu(gate_pre) * live[:, None]


def plain_product(left, right):
    return jnp.dot(left, right, preferred_element_type=jnp.float32)


def rows_product(left, right):
    return lax.dot_general(
        left, right, (((0,), (0,)), ((), ())), preferred_element_type=jnp.float32
    )


def transposed_product(left, right):
    return lax.dot_general(
        left, right, (((1,), (1,)), ((), ())), preferred_element_type=jnp.float32
    )


def count_devices(axis="dp"):
    return lax.axis_size(axis)


def group_lists(devices):
    parts = min(MODEL, devices)
    copies = devices // parts
    model_groups = [[m * copies + t for m in range(parts)] for t in range(copies)]
    copy_groups = [[m * copies + t for t in range(copies)] for m in range(parts)]
    return parts, copies, model_groups, copy_groups


def body(
    block_in,
    out_grad,
    norm1_gain,
    conv_weight,
    head_gain,
    qkv_weight,
    beta_weight,
    gate_weight,
    out_weight,
    norm2_gain,
    updown_weight,
    down_weight,
    seq_blocks,
    lead_blocks,
):
    devices = count_devices()
    parts, copies, model_groups, copy_groups = group_lists(devices)
    if copies == 1:
        model_groups = None
    rows_own = updown_weight.shape[0]
    units = FF // parts
    doc_rows, persist, live = block_layout(seq_blocks[0, 0], seq_blocks[0, 1], lead_blocks[0])
    bf = jnp.bfloat16
    f32 = jnp.float32

    def gather(values, groups=None):
        return lax.all_gather(values, "dp", axis=0, tiled=True, axis_index_groups=groups)

    def scatter(values, groups=None):
        return lax.psum_scatter(
            values, "dp", scatter_dimension=0, tiled=True, axis_index_groups=groups
        )

    def exchange(values):
        return lax.all_to_all(
            values, "dp", split_axis=0, concat_axis=0, axis_index_groups=model_groups, tiled=True
        )

    small = jnp.concatenate(
        [
            beta_weight,
            conv_weight.reshape(rows_own, -1),
            norm1_gain[:, None],
            head_gain[:, None],
            norm2_gain[:, None],
        ],
        1,
    ).astype(bf)
    taps_width = KERNEL * 3
    small_width = 128
    small = jnp.pad(small, ((0, 0), (0, small_width - small.shape[1])))
    first_weights = gather(jnp.concatenate([qkv_weight.astype(bf), small], 1))
    w_qkv = first_weights[:, : 3 * D]
    small_full = first_weights[:, 3 * D :]
    w_beta = small_full[:, :HEADS]
    conv_full = small_full[:, HEADS : HEADS + taps_width].reshape(3 * D, KERNEL)
    gain_one = small_full[:, HEADS + taps_width]
    head_full = small_full[:, HEADS + taps_width + 1]
    gain_two = small_full[:, HEADS + taps_width + 2]
    second_weights = gather(
        jnp.concatenate([gate_weight.astype(bf), out_weight.astype(bf)], 1)
    )
    w_gate = second_weights[:, :D]
    w_out = second_weights[:, D:]

    pieces = updown_weight.astype(bf).reshape(rows_own, 2, parts, units).transpose(2, 0, 1, 3)
    pieces = exchange(pieces.reshape(parts, rows_own, 2 * units))
    w_down = down_weight.astype(bf)
    if copies > 1:
        pieces = lax.all_gather(pieces, "dp", axis=1, axis_index_groups=copy_groups)
        w_down = gather(w_down, copy_groups)
    w_updown = pieces.reshape(D, 2 * units)
    cotangent = gather(out_grad, model_groups)

    inputs = block_in.astype(f32)
    normed_full, norm_one_back = jax.vjp(rms_scale, inputs, gain_one.astype(f32))
    normed = normed_full.astype(bf)
    qkv_pre = plain_product(normed, w_qkv)
    beta_pre = plain_product(normed, w_beta)
    gate_pre = plain_product(normed, w_gate)

    def local_mixer(qkv_values, beta_values, gate_values, taps, head_vector):
        return mixer(
            qkv_values, beta_values, gate_values, taps, head_vector, doc_rows, persist, live
        )

    mixed_full, mixer_back = jax.vjp(
        local_mixer,
        qkv_pre,
        beta_pre,
        gate_pre,
        conv_full.astype(f32),
        head_full.astype(f32),
    )
    mixed = mixed_full.astype(bf)
    hidden = inputs + plain_product(mixed, w_out)
    normed_two_full, norm_two_back = jax.vjp(rms_scale, hidden, gain_two.astype(f32))
    normed_two = gather(normed_two_full.astype(bf), model_groups)

    def swiglu_units(updown):
        return jax.nn.silu(updown[:, :units]) * updown[:, units:]

    updown = plain_product(normed_two, w_updown)
    active_full, swiglu_back = jax.vjp(swiglu_units, updown)
    active = active_full.astype(bf)
    d_active = transposed_product(cotangent, w_down)
    d_updown = swiglu_back(d_active)[0].astype(bf)
    d_normed_two = scatter(
        transposed_product(d_updown, w_updown).astype(bf), model_groups
    ).astype(f32)
    block_out = scatter(plain_product(active, w_down).astype(bf), model_groups)
    block_out = (hidden + block_out.astype(f32)).astype(bf)
    down_shard = rows_product(active, cotangent)
    updown_grad = rows_product(normed_two, d_updown)
    if copies > 1:
        down_shard = scatter(down_shard, copy_groups)
        updown_grad = updown_grad.reshape(parts, copies, rows_own, 2 * units)
        updown_grad = lax.psum_scatter(
            updown_grad, "dp", scatter_dimension=1, axis_index_groups=copy_groups
        )
    updown_grad = exchange(updown_grad.reshape(parts, rows_own, 2 * units).astype(bf))
    updown_shard = updown_grad.reshape(parts, rows_own, 2, units).transpose(1, 2, 0, 3)
    updown_shard = updown_shard.reshape(rows_own, 2 * FF).astype(f32)

    d_hidden_part, gain_two_grad = norm_two_back(d_normed_two)
    d_hidden = out_grad.astype(f32) + d_hidden_part
    d_mixed = d_hidden.astype(bf)
    out_shard = scatter(rows_product(mixed, d_mixed).astype(bf)).astype(f32)
    d_mixer = transposed_product(d_mixed, w_out)
    d_qkv_full, d_beta_full, d_gate_full, conv_grad, head_grad = mixer_back(d_mixer)
    d_qkv = d_qkv_full.astype(bf)
    d_beta = d_beta_full.astype(bf)
    d_gate = d_gate_full.astype(bf)
    qkv_grad = rows_product(normed, d_qkv)
    beta_grad = rows_product(normed, d_beta)
    gate_grad = rows_product(normed, d_gate)
    d_normed = (
        transposed_product(d_qkv, w_qkv)
        + transposed_product(d_beta, w_beta)
        + transposed_product(d_gate, w_gate)
    )
    d_inputs, gain_one_grad = norm_one_back(d_normed)
    input_grad = (d_hidden + d_inputs).astype(bf)
    small_grad = jnp.concatenate(
        [
            beta_grad,
            conv_grad.reshape(D, -1),
            gain_one_grad[:, None],
            head_grad[:, None],
            gain_two_grad[:, None],
        ],
        1,
    )
    small_grad = jnp.pad(small_grad, ((0, 0), (0, small_width - small_grad.shape[1])))
    gate_shard = scatter(gate_grad.astype(bf)).astype(f32)
    last_shard = scatter(
        jnp.concatenate([qkv_grad.astype(bf), small_grad.astype(bf)], 1)
    ).astype(f32)
    qkv_shard = last_shard[:, : 3 * D]
    small_shard = last_shard[:, 3 * D :]
    return (
        block_out,
        input_grad,
        small_shard[:, HEADS + taps_width],
        small_shard[:, HEADS : HEADS + taps_width].reshape(-1, KERNEL),
        small_shard[:, HEADS + taps_width + 1],
        qkv_shard,
        small_shard[:, :HEADS],
        gate_shard,
        out_shard,
        small_shard[:, HEADS + taps_width + 2],
        updown_shard,
        down_shard,
    )


def solution(mesh):
    placed = (
        P("dp", None),
        P("dp", None),
        P("dp"),
        P("dp", None),
        P("dp"),
        P("dp", None),
        P("dp", None),
        P("dp", None),
        P("dp", None),
        P("dp"),
        P("dp", None),
        P("dp", None),
        P("dp", None),
        P("dp"),
    )
    return jax.shard_map(
        body,
        mesh=mesh,
        in_specs=placed,
        out_specs=(
            P("dp", None),
            P("dp", None),
            P("dp"),
            P("dp", None),
            P("dp"),
            P("dp", None),
            P("dp", None),
            P("dp", None),
            P("dp", None),
            P("dp"),
            P("dp", None),
            P("dp", None),
        ),
        check_vma=False,
    )
```

```python
import jax
import jax.numpy as jnp
from jax import lax
from jax.sharding import PartitionSpec as P

D = 2048
HEADS = 16
HEAD_DIM = 128
FF = 5632
KERNEL = 4
BLOCK_ROWS = 64
BLOCKS_DEV = 2


HIGHEST = lax.Precision.HIGHEST
MODEL = 16


def rms_scale(values, gain_vector):
    return values * lax.rsqrt(jnp.mean(values * values, -1, keepdims=True) + 1e-06) * gain_vector


def block_layout(first_len, second_len, lead_count):
    position = jnp.arange(BLOCKS_DEV, dtype=jnp.int32)
    in_first = (position >= lead_count) & (position < lead_count + first_len)
    in_second = (position >= lead_count + first_len) & (
        position < lead_count + first_len + second_len
    )
    doc_block = jnp.where(in_first, 1, jnp.where(in_second, 2, 0)).astype(jnp.int32)
    starts = (position == lead_count) | (position == lead_count + first_len) & (second_len > 0)
    persist = jnp.where(starts, 0.0, 1.0).astype(jnp.float32)
    doc_rows = jnp.repeat(doc_block, BLOCK_ROWS)
    live = (doc_rows > 0).astype(jnp.float32)
    return (doc_rows, persist, live)


def causal_conv(pre_values, taps, doc_rows):
    summed = pre_values * taps[:, 0]
    for offset in range(1, KERNEL):
        shifted = jnp.concatenate(
            [jnp.zeros((offset, pre_values.shape[1]), jnp.float32), pre_values[:-offset]], 0
        )
        earlier = jnp.concatenate([jnp.full((offset,), -1, jnp.int32), doc_rows[:-offset]], 0)
        matching = (earlier == doc_rows).astype(jnp.float32)[:, None]
        summed = summed + taps[:, offset] * shifted * matching
    return summed


def unit_norm(values):
    return values * lax.rsqrt(jnp.sum(values * values, -1, keepdims=True) + 1e-06)


def delta_rule(query_heads, key_heads, value_heads, strengths, persist):

    def blocks(values):
        return values.reshape(BLOCKS_DEV, BLOCK_ROWS, HEADS, HEAD_DIM).transpose(0, 2, 1, 3)

    query_block = blocks(query_heads)
    key_block = blocks(key_heads)
    value_block = blocks(value_heads)
    strength_block = strengths.reshape(BLOCKS_DEV, BLOCK_ROWS, HEADS).transpose(0, 2, 1)[..., None]
    key_scaled = key_block * strength_block
    lower_part = jnp.tril(
        jnp.einsum("nhid,nhjd->nhij", key_scaled, key_block, precision=HIGHEST), -1
    )
    system = lower_part + jnp.eye(BLOCK_ROWS, dtype=jnp.float32)
    w_block = jax.scipy.linalg.solve_triangular(system, key_scaled, lower=True, unit_diagonal=True)
    u_block = jax.scipy.linalg.solve_triangular(
        system, value_block * strength_block, lower=True, unit_diagonal=True
    )
    scores = jnp.tril(jnp.einsum("nhid,nhjd->nhij", query_block, key_block, precision=HIGHEST))

    def advance(memory, inputs):
        w_part, u_part, query_part, key_part, score_part, factor = inputs
        memory = memory * factor
        corrected = u_part - jnp.einsum("hid,hed->hie", w_part, memory, precision=HIGHEST)
        emitted = jnp.einsum("hid,hed->hie", query_part, memory, precision=HIGHEST)
        emitted = emitted + jnp.einsum("hij,hje->hie", score_part, corrected, precision=HIGHEST)
        memory = memory + jnp.einsum("hie,hid->hed", corrected, key_part, precision=HIGHEST)
        return (memory, emitted)

    initial = jnp.zeros((HEADS, HEAD_DIM, HEAD_DIM), jnp.float32)
    closing, emitted = lax.scan(
        jax.checkpoint(advance),
        initial,
        (w_block, u_block, query_block, key_block, scores, persist),
    )
    return emitted.transpose(0, 2, 1, 3).reshape(BLOCKS_DEV * BLOCK_ROWS, HEADS * HEAD_DIM)


def mixer(qkv_pre, beta_pre, gate_pre, taps, head_vector, doc_rows, persist, live):
    convolved = jax.nn.silu(causal_conv(qkv_pre, taps, doc_rows))
    query_heads = unit_norm(convolved[:, :D].reshape(-1, HEADS, HEAD_DIM)) * HEAD_DIM ** (-0.5)
    key_heads = unit_norm(convolved[:, D : 2 * D].reshape(-1, HEADS, HEAD_DIM))
    value_heads = convolved[:, 2 * D :].reshape(-1, HEADS, HEAD_DIM)
    strengths = jax.nn.sigmoid(beta_pre) * live[:, None]
    head_out = delta_rule(query_heads, key_heads, value_heads, strengths, persist).reshape(
        -1, HEADS, HEAD_DIM
    )
    scaled = head_out * lax.rsqrt(jnp.mean(head_out * head_out, -1, keepdims=True) + 1e-05)
    return scaled.reshape(-1, D) * head_vector * jax.nn.silu(gate_pre) * live[:, None]


def plain_product(left, right):
    return jnp.dot(left, right, preferred_element_type=jnp.float32)


def rows_product(left, right):
    return lax.dot_general(
        left, right, (((0,), (0,)), ((), ())), preferred_element_type=jnp.float32
    )


def transposed_product(left, right):
    return lax.dot_general(
        left, right, (((1,), (1,)), ((), ())), preferred_element_type=jnp.float32
    )


def count_devices(axis="dp"):
    return lax.axis_size(axis)


def group_lists(devices):
    parts = min(MODEL, devices)
    copies = devices // parts
    model_groups = [[m * copies + t for m in range(parts)] for t in range(copies)]
    copy_groups = [[m * copies + t for t in range(copies)] for m in range(parts)]
    return parts, copies, model_groups, copy_groups


def body(
    block_in,
    out_grad,
    norm1_gain,
    conv_weight,
    head_gain,
    qkv_weight,
    beta_weight,
    gate_weight,
    out_weight,
    norm2_gain,
    updown_weight,
    down_weight,
    seq_blocks,
    lead_blocks,
):
    devices = count_devices()
    parts, copies, model_groups, copy_groups = group_lists(devices)
    if copies == 1:
        model_groups = None
    rows_own = updown_weight.shape[0]
    units = FF // parts
    doc_rows, persist, live = block_layout(seq_blocks[0, 0], seq_blocks[0, 1], lead_blocks[0])
    bf = jnp.bfloat16
    f32 = jnp.float32

    def gather(values, groups=None):
        return lax.all_gather(values, "dp", axis=0, tiled=True, axis_index_groups=groups)

    def scatter(values, groups=None):
        return lax.psum_scatter(
            values, "dp", scatter_dimension=0, tiled=True, axis_index_groups=groups
        )

    def exchange(values):
        return lax.all_to_all(
            values, "dp", split_axis=0, concat_axis=0, axis_index_groups=model_groups, tiled=True
        )

    copy_rank = lax.axis_index("dp") % copies
    partners = [(i, i + 1 - 2 * (i % 2)) for i in range(devices)]

    def gather_copies(values):
        if copies != 2:
            return lax.all_gather(values, "dp", axis=0, axis_index_groups=copy_groups)
        other = lax.ppermute(values, "dp", partners)
        first = copy_rank == 0
        return jnp.stack([jnp.where(first, values, other), jnp.where(first, other, values)])

    def scatter_copies(values):
        values = jnp.moveaxis(values, 1, 0)
        if copies != 2:
            return lax.psum_scatter(
                values.astype(bf), "dp", scatter_dimension=0, axis_index_groups=copy_groups
            ).astype(f32)
        other = lax.dynamic_index_in_dim(values, 1 - copy_rank, 0, keepdims=False).astype(bf)
        own = lax.dynamic_index_in_dim(values, copy_rank, 0, keepdims=False)
        return own + lax.ppermute(other, "dp", partners).astype(f32)

    small = jnp.concatenate(
        [
            beta_weight,
            conv_weight.reshape(rows_own, -1),
            norm1_gain[:, None],
            head_gain[:, None],
            norm2_gain[:, None],
        ],
        1,
    ).astype(bf)
    taps_width = KERNEL * 3
    small_width = 128
    small = jnp.pad(small, ((0, 0), (0, small_width - small.shape[1])))
    first_weights = gather(jnp.concatenate([qkv_weight.astype(bf), small], 1))
    w_qkv = first_weights[:, : 3 * D]
    small_full = first_weights[:, 3 * D :]
    w_beta = small_full[:, :HEADS]
    conv_full = small_full[:, HEADS : HEADS + taps_width].reshape(3 * D, KERNEL)
    gain_one = small_full[:, HEADS + taps_width]
    head_full = small_full[:, HEADS + taps_width + 1]
    gain_two = small_full[:, HEADS + taps_width + 2]
    second_weights = gather(
        jnp.concatenate([gate_weight.astype(bf), out_weight.astype(bf)], 1)
    )
    w_gate = second_weights[:, :D]
    w_out = second_weights[:, D:]

    pieces = updown_weight.astype(bf).reshape(rows_own, 2, parts, units).transpose(2, 0, 1, 3)
    pieces = exchange(pieces.reshape(parts, rows_own, 2 * units))
    w_down = down_weight.astype(bf)
    if copies > 1:
        pieces = gather_copies(pieces).transpose(1, 0, 2, 3)
        w_down = gather_copies(w_down).reshape(units, D)
    w_updown = pieces.reshape(D, 2 * units)
    cotangent = gather(out_grad, model_groups)

    inputs = block_in.astype(f32)
    normed_full, norm_one_back = jax.vjp(rms_scale, inputs, gain_one.astype(f32))
    normed = normed_full.astype(bf)
    qkv_pre = plain_product(normed, w_qkv)
    beta_pre = plain_product(normed, w_beta)
    gate_pre = plain_product(normed, w_gate)

    def local_mixer(qkv_values, beta_values, gate_values, taps, head_vector):
        return mixer(
            qkv_values, beta_values, gate_values, taps, head_vector, doc_rows, persist, live
        )

    mixed_full, mixer_back = jax.vjp(
        local_mixer,
        qkv_pre,
        beta_pre,
        gate_pre,
        conv_full.astype(f32),
        head_full.astype(f32),
    )
    mixed = mixed_full.astype(bf)
    hidden = inputs + plain_product(mixed, w_out)
    normed_two_full, norm_two_back = jax.vjp(rms_scale, hidden, gain_two.astype(f32))
    normed_two = gather(normed_two_full.astype(bf), model_groups)

    def swiglu_units(updown):
        return jax.nn.silu(updown[:, :units]) * updown[:, units:]

    updown = plain_product(normed_two, w_updown)
    active_full, swiglu_back = jax.vjp(swiglu_units, updown)
    active = active_full.astype(bf)
    d_active = transposed_product(cotangent, w_down)
    d_updown = swiglu_back(d_active)[0].astype(bf)
    d_normed_two = scatter(
        transposed_product(d_updown, w_updown).astype(bf), model_groups
    ).astype(f32)
    block_out = scatter(plain_product(active, w_down).astype(bf), model_groups)
    block_out = (hidden + block_out.astype(f32)).astype(bf)
    down_shard = rows_product(active, cotangent)
    updown_grad = rows_product(normed_two, d_updown)
    if copies > 1:
        down_shard = scatter_copies(down_shard.reshape(1, copies, -1, D))[0]
        updown_grad = scatter_copies(updown_grad.reshape(parts, copies, rows_own, 2 * units))
    updown_grad = exchange(updown_grad.reshape(parts, rows_own, 2 * units).astype(bf))
    updown_shard = updown_grad.reshape(parts, rows_own, 2, units).transpose(1, 2, 0, 3)
    updown_shard = updown_shard.reshape(rows_own, 2 * FF).astype(f32)

    d_hidden_part, gain_two_grad = norm_two_back(d_normed_two)
    d_hidden = out_grad.astype(f32) + d_hidden_part
    d_mixed = d_hidden.astype(bf)
    out_shard = scatter(rows_product(mixed, d_mixed).astype(bf)).astype(f32)
    d_mixer = transposed_product(d_mixed, w_out)
    d_qkv_full, d_beta_full, d_gate_full, conv_grad, head_grad = mixer_back(d_mixer)
    d_qkv = d_qkv_full.astype(bf)
    d_beta = d_beta_full.astype(bf)
    d_gate = d_gate_full.astype(bf)
    qkv_grad = rows_product(normed, d_qkv)
    beta_grad = rows_product(normed, d_beta)
    gate_grad = rows_product(normed, d_gate)
    d_normed = (
        transposed_product(d_qkv, w_qkv)
        + transposed_product(d_beta, w_beta)
        + transposed_product(d_gate, w_gate)
    )
    d_inputs, gain_one_grad = norm_one_back(d_normed)
    input_grad = (d_hidden + d_inputs).astype(bf)
    small_grad = jnp.concatenate(
        [
            beta_grad,
            conv_grad.reshape(D, -1),
            gain_one_grad[:, None],
            head_grad[:, None],
            gain_two_grad[:, None],
        ],
        1,
    )
    small_grad = jnp.pad(small_grad, ((0, 0), (0, small_width - small_grad.shape[1])))
    gate_shard = scatter(gate_grad.astype(bf)).astype(f32)
    last_shard = scatter(
        jnp.concatenate([qkv_grad.astype(bf), small_grad.astype(bf)], 1)
    ).astype(f32)
    qkv_shard = last_shard[:, : 3 * D]
    small_shard = last_shard[:, 3 * D :]
    return (
        block_out,
        input_grad,
        small_shard[:, HEADS + taps_width],
        small_shard[:, HEADS : HEADS + taps_width].reshape(-1, KERNEL),
        small_shard[:, HEADS + taps_width + 1],
        qkv_shard,
        small_shard[:, :HEADS],
        gate_shard,
        out_shard,
        small_shard[:, HEADS + taps_width + 2],
        updown_shard,
        down_shard,
    )


def solution(mesh):
    placed = (
        P("dp", None),
        P("dp", None),
        P("dp"),
        P("dp", None),
        P("dp"),
        P("dp", None),
        P("dp", None),
        P("dp", None),
        P("dp", None),
        P("dp"),
        P("dp", None),
        P("dp", None),
        P("dp", None),
        P("dp"),
    )
    return jax.shard_map(
        body,
        mesh=mesh,
        in_specs=placed,
        out_specs=(
            P("dp", None),
            P("dp", None),
            P("dp"),
            P("dp", None),
            P("dp"),
            P("dp", None),
            P("dp", None),
            P("dp", None),
            P("dp", None),
            P("dp"),
            P("dp", None),
            P("dp", None),
        ),
        check_vma=False,
    )
```

```python
import jax
import jax.numpy as jnp
from jax import lax
from jax.sharding import PartitionSpec as P

D = 2048
HEADS = 16
HEAD_DIM = 128
FF = 5632
KERNEL = 4
BLOCK_ROWS = 64
BLOCKS_DEV = 2


HIGHEST = lax.Precision.HIGHEST
MODEL = 4


def rms_scale(values, gain_vector):
    return values * lax.rsqrt(jnp.mean(values * values, -1, keepdims=True) + 1e-06) * gain_vector


def block_layout(first_len, second_len, lead_count):
    position = jnp.arange(BLOCKS_DEV, dtype=jnp.int32)
    in_first = (position >= lead_count) & (position < lead_count + first_len)
    in_second = (position >= lead_count + first_len) & (
        position < lead_count + first_len + second_len
    )
    doc_block = jnp.where(in_first, 1, jnp.where(in_second, 2, 0)).astype(jnp.int32)
    starts = (position == lead_count) | (position == lead_count + first_len) & (second_len > 0)
    persist = jnp.where(starts, 0.0, 1.0).astype(jnp.float32)
    doc_rows = jnp.repeat(doc_block, BLOCK_ROWS)
    live = (doc_rows > 0).astype(jnp.float32)
    return (doc_rows, persist, live)


def causal_conv(pre_values, taps, doc_rows):
    summed = pre_values * taps[:, 0]
    for offset in range(1, KERNEL):
        shifted = jnp.concatenate(
            [jnp.zeros((offset, pre_values.shape[1]), jnp.float32), pre_values[:-offset]], 0
        )
        earlier = jnp.concatenate([jnp.full((offset,), -1, jnp.int32), doc_rows[:-offset]], 0)
        matching = (earlier == doc_rows).astype(jnp.float32)[:, None]
        summed = summed + taps[:, offset] * shifted * matching
    return summed


def unit_norm(values):
    return values * lax.rsqrt(jnp.sum(values * values, -1, keepdims=True) + 1e-06)


def delta_rule(query_heads, key_heads, value_heads, strengths, persist):

    def blocks(values):
        return values.reshape(BLOCKS_DEV, BLOCK_ROWS, HEADS, HEAD_DIM).transpose(0, 2, 1, 3)

    query_block = blocks(query_heads)
    key_block = blocks(key_heads)
    value_block = blocks(value_heads)
    strength_block = strengths.reshape(BLOCKS_DEV, BLOCK_ROWS, HEADS).transpose(0, 2, 1)[..., None]
    key_scaled = key_block * strength_block
    lower_part = jnp.tril(
        jnp.einsum("nhid,nhjd->nhij", key_scaled, key_block, precision=HIGHEST), -1
    )
    system = lower_part + jnp.eye(BLOCK_ROWS, dtype=jnp.float32)
    w_block = jax.scipy.linalg.solve_triangular(system, key_scaled, lower=True, unit_diagonal=True)
    u_block = jax.scipy.linalg.solve_triangular(
        system, value_block * strength_block, lower=True, unit_diagonal=True
    )
    scores = jnp.tril(jnp.einsum("nhid,nhjd->nhij", query_block, key_block, precision=HIGHEST))

    def advance(memory, inputs):
        w_part, u_part, query_part, key_part, score_part, factor = inputs
        memory = memory * factor
        corrected = u_part - jnp.einsum("hid,hed->hie", w_part, memory, precision=HIGHEST)
        emitted = jnp.einsum("hid,hed->hie", query_part, memory, precision=HIGHEST)
        emitted = emitted + jnp.einsum("hij,hje->hie", score_part, corrected, precision=HIGHEST)
        memory = memory + jnp.einsum("hie,hid->hed", corrected, key_part, precision=HIGHEST)
        return (memory, emitted)

    initial = jnp.zeros((HEADS, HEAD_DIM, HEAD_DIM), jnp.float32)
    closing, emitted = lax.scan(
        jax.checkpoint(advance),
        initial,
        (w_block, u_block, query_block, key_block, scores, persist),
    )
    return emitted.transpose(0, 2, 1, 3).reshape(BLOCKS_DEV * BLOCK_ROWS, HEADS * HEAD_DIM)


def mixer(qkv_pre, beta_pre, gate_pre, taps, head_vector, doc_rows, persist, live):
    convolved = jax.nn.silu(causal_conv(qkv_pre, taps, doc_rows))
    query_heads = unit_norm(convolved[:, :D].reshape(-1, HEADS, HEAD_DIM)) * HEAD_DIM ** (-0.5)
    key_heads = unit_norm(convolved[:, D : 2 * D].reshape(-1, HEADS, HEAD_DIM))
    value_heads = convolved[:, 2 * D :].reshape(-1, HEADS, HEAD_DIM)
    strengths = jax.nn.sigmoid(beta_pre) * live[:, None]
    head_out = delta_rule(query_heads, key_heads, value_heads, strengths, persist).reshape(
        -1, HEADS, HEAD_DIM
    )
    scaled = head_out * lax.rsqrt(jnp.mean(head_out * head_out, -1, keepdims=True) + 1e-05)
    return scaled.reshape(-1, D) * head_vector * jax.nn.silu(gate_pre) * live[:, None]


def plain_product(left, right):
    return jnp.dot(left, right, preferred_element_type=jnp.float32)


def rows_product(left, right):
    return lax.dot_general(
        left, right, (((0,), (0,)), ((), ())), preferred_element_type=jnp.float32
    )


def transposed_product(left, right):
    return lax.dot_general(
        left, right, (((1,), (1,)), ((), ())), preferred_element_type=jnp.float32
    )


def count_devices(axis="dp"):
    return lax.axis_size(axis)


def group_lists(devices):
    parts = min(MODEL, devices)
    copies = devices // parts
    model_groups = [[m * copies + t for m in range(parts)] for t in range(copies)]
    copy_groups = [[m * copies + t for t in range(copies)] for m in range(parts)]
    return parts, copies, model_groups, copy_groups


def body(
    block_in,
    out_grad,
    norm1_gain,
    conv_weight,
    head_gain,
    qkv_weight,
    beta_weight,
    gate_weight,
    out_weight,
    norm2_gain,
    updown_weight,
    down_weight,
    seq_blocks,
    lead_blocks,
):
    devices = count_devices()
    parts, copies, model_groups, copy_groups = group_lists(devices)
    if copies == 1:
        model_groups = None
    rows_own = updown_weight.shape[0]
    units = FF // parts
    doc_rows, persist, live = block_layout(seq_blocks[0, 0], seq_blocks[0, 1], lead_blocks[0])
    bf = jnp.bfloat16
    f32 = jnp.float32

    def gather(values, groups=None):
        return lax.all_gather(values, "dp", axis=0, tiled=True, axis_index_groups=groups)

    def scatter(values, groups=None):
        return lax.psum_scatter(
            values, "dp", scatter_dimension=0, tiled=True, axis_index_groups=groups
        )

    def exchange(values):
        return lax.all_to_all(
            values, "dp", split_axis=0, concat_axis=0, axis_index_groups=model_groups, tiled=True
        )

    def shift(values, step):
        pairs = [
            (m * copies + t, (m + step) % parts * copies + t)
            for m in range(parts)
            for t in range(copies)
        ]
        return lax.ppermute(values, "dp", pairs)

    def gather_rows(values):
        return jnp.concatenate([values] + [shift(values, step) for step in range(1, parts)], 0)

    def scatter_rows(terms):
        terms = terms.reshape(parts, -1, terms.shape[1])
        total = terms[0]
        for step in range(1, parts):
            total = total + shift(terms[step].astype(bf), -step).astype(f32)
        return total

    def gather_copies(values):
        return lax.all_gather(values, "dp", axis=0, axis_index_groups=copy_groups)

    def scatter_copies(values):
        return lax.psum_scatter(
            values.astype(bf),
            "dp",
            scatter_dimension=0,
            axis_index_groups=copy_groups,
            tiled=True,
        ).astype(f32)

    def to_wire(values):
        return values.reshape(-1, parts, copies, rows_own).swapaxes(1, 2).reshape(-1, D)

    def from_wire(values):
        return values.reshape(-1, copies, parts, rows_own).swapaxes(1, 2).reshape(-1, D)

    small = jnp.concatenate(
        [
            beta_weight,
            conv_weight.reshape(rows_own, -1),
            norm1_gain[:, None],
            head_gain[:, None],
            norm2_gain[:, None],
        ],
        1,
    ).astype(bf)
    taps_width = KERNEL * 3
    small_width = 128
    small = jnp.pad(small, ((0, 0), (0, small_width - small.shape[1])))
    first_weights = gather(jnp.concatenate([qkv_weight.astype(bf), small], 1))
    w_qkv = first_weights[:, : 3 * D]
    small_full = first_weights[:, 3 * D :]
    w_beta = small_full[:, :HEADS]
    conv_full = small_full[:, HEADS : HEADS + taps_width].reshape(3 * D, KERNEL)
    gain_one = small_full[:, HEADS + taps_width]
    head_full = small_full[:, HEADS + taps_width + 1]
    gain_two = small_full[:, HEADS + taps_width + 2]
    second_weights = gather(
        jnp.concatenate([gate_weight.astype(bf), out_weight.astype(bf)], 1)
    )
    w_gate = second_weights[:, :D]
    w_out = second_weights[:, D:]

    pieces = updown_weight.astype(bf).reshape(rows_own, 2, parts, units).transpose(2, 0, 1, 3)
    pieces = exchange(pieces.reshape(parts, rows_own, 2 * units))
    w_down = down_weight.astype(bf)
    if copies > 1:
        pieces = gather_copies(pieces)
        w_down = gather_copies(w_down).reshape(units, D)
    w_updown = pieces.reshape(D, 2 * units)
    cotangent = gather_rows(out_grad)

    inputs = block_in.astype(f32)
    normed_full, norm_one_back = jax.vjp(rms_scale, inputs, gain_one.astype(f32))
    normed = normed_full.astype(bf)
    qkv_pre = plain_product(normed, w_qkv)
    beta_pre = plain_product(normed, w_beta)
    gate_pre = plain_product(normed, w_gate)

    def local_mixer(qkv_values, beta_values, gate_values, taps, head_vector):
        return mixer(
            qkv_values, beta_values, gate_values, taps, head_vector, doc_rows, persist, live
        )

    mixed_full, mixer_back = jax.vjp(
        local_mixer,
        qkv_pre,
        beta_pre,
        gate_pre,
        conv_full.astype(f32),
        head_full.astype(f32),
    )
    mixed = mixed_full.astype(bf)
    hidden = inputs + plain_product(mixed, w_out)
    normed_two_full, norm_two_back = jax.vjp(rms_scale, hidden, gain_two.astype(f32))
    normed_two = gather_rows(to_wire(normed_two_full.astype(bf)))

    def swiglu_units(updown):
        return jax.nn.silu(updown[:, :units]) * updown[:, units:]

    updown = plain_product(normed_two, w_updown)
    active_full, swiglu_back = jax.vjp(swiglu_units, updown)
    active = active_full.astype(bf)
    d_active = transposed_product(cotangent, w_down)
    d_updown = swiglu_back(d_active)[0].astype(bf)
    d_normed_two = from_wire(scatter_rows(transposed_product(d_updown, w_updown)))
    block_out = (hidden + scatter_rows(plain_product(active, w_down))).astype(bf)
    down_shard = rows_product(active, cotangent)
    updown_grad = rows_product(normed_two, d_updown)
    if copies > 1:
        down_shard = scatter_copies(down_shard)
        updown_grad = scatter_copies(updown_grad)
    updown_grad = exchange(updown_grad.reshape(parts, rows_own, 2 * units).astype(bf))
    updown_shard = updown_grad.reshape(parts, rows_own, 2, units).transpose(1, 2, 0, 3)
    updown_shard = updown_shard.reshape(rows_own, 2 * FF).astype(f32)

    d_hidden_part, gain_two_grad = norm_two_back(d_normed_two)
    d_hidden = out_grad.astype(f32) + d_hidden_part
    d_mixed = d_hidden.astype(bf)
    out_shard = scatter(rows_product(mixed, d_mixed).astype(bf)).astype(f32)
    d_mixer = transposed_product(d_mixed, w_out)
    d_qkv_full, d_beta_full, d_gate_full, conv_grad, head_grad = mixer_back(d_mixer)
    d_qkv = d_qkv_full.astype(bf)
    d_beta = d_beta_full.astype(bf)
    d_gate = d_gate_full.astype(bf)
    qkv_grad = rows_product(normed, d_qkv)
    beta_grad = rows_product(normed, d_beta)
    gate_grad = rows_product(normed, d_gate)
    d_normed = (
        transposed_product(d_qkv, w_qkv)
        + transposed_product(d_beta, w_beta)
        + transposed_product(d_gate, w_gate)
    )
    d_inputs, gain_one_grad = norm_one_back(d_normed)
    input_grad = (d_hidden + d_inputs).astype(bf)
    small_grad = jnp.concatenate(
        [
            beta_grad,
            conv_grad.reshape(D, -1),
            gain_one_grad[:, None],
            head_grad[:, None],
            gain_two_grad[:, None],
        ],
        1,
    )
    small_grad = jnp.pad(small_grad, ((0, 0), (0, small_width - small_grad.shape[1])))
    gate_shard = scatter(gate_grad.astype(bf)).astype(f32)
    last_shard = scatter(
        jnp.concatenate([qkv_grad.astype(bf), small_grad.astype(bf)], 1)
    ).astype(f32)
    qkv_shard = last_shard[:, : 3 * D]
    small_shard = last_shard[:, 3 * D :]
    return (
        block_out,
        input_grad,
        small_shard[:, HEADS + taps_width],
        small_shard[:, HEADS : HEADS + taps_width].reshape(-1, KERNEL),
        small_shard[:, HEADS + taps_width + 1],
        qkv_shard,
        small_shard[:, :HEADS],
        gate_shard,
        out_shard,
        small_shard[:, HEADS + taps_width + 2],
        updown_shard,
        down_shard,
    )


def solution(mesh):
    placed = (
        P("dp", None),
        P("dp", None),
        P("dp"),
        P("dp", None),
        P("dp"),
        P("dp", None),
        P("dp", None),
        P("dp", None),
        P("dp", None),
        P("dp"),
        P("dp", None),
        P("dp", None),
        P("dp", None),
        P("dp"),
    )
    return jax.shard_map(
        body,
        mesh=mesh,
        in_specs=placed,
        out_specs=(
            P("dp", None),
            P("dp", None),
            P("dp"),
            P("dp", None),
            P("dp"),
            P("dp", None),
            P("dp", None),
            P("dp", None),
            P("dp", None),
            P("dp"),
            P("dp", None),
            P("dp", None),
        ),
        check_vma=False,
    )
```

```python
import jax
import jax.numpy as jnp
from jax import lax
from jax.experimental import pallas as pl
from jax.experimental.pallas import tpu as pltpu
from jax.sharding import PartitionSpec as P

D = 2048
HEADS = 16
HEAD_DIM = 128
FF = 5632
KERNEL = 4
BLOCK_ROWS = 64
BLOCKS_DEV = 2
GROUP_ROWS = BLOCK_ROWS * BLOCKS_DEV
SMALL = 128
MODEL = 4

f32 = jnp.float32
bf = jnp.bfloat16


def block_layout(first_len, second_len, lead_count):
    position = jnp.arange(BLOCKS_DEV, dtype=jnp.int32)
    in_first = (position >= lead_count) & (position < lead_count + first_len)
    in_second = (position >= lead_count + first_len) & (
        position < lead_count + first_len + second_len
    )
    doc_block = jnp.where(in_first, 1, jnp.where(in_second, 2, 0)).astype(jnp.int32)
    starts = (position == lead_count) | (position == lead_count + first_len) & (second_len > 0)
    persist = jnp.where(starts, 0.0, 1.0).astype(f32)
    live = (doc_block > 0).astype(f32)
    same = (doc_block[0] == doc_block[1]).astype(f32)
    return jnp.stack([live[0], live[1], same, persist[1]])


def rms_scale(values, gain_vector):
    return values * lax.rsqrt(jnp.mean(values * values, -1, keepdims=True) + 1e-06) * gain_vector


def plain_product(left, right):
    return jnp.dot(left, right, preferred_element_type=f32)


def rows_product(left, right):
    return lax.dot_general(left, right, (((0,), (0,)), ((), ())), preferred_element_type=f32)


def transposed_product(left, right):
    return lax.dot_general(left, right, (((1,), (1,)), ((), ())), preferred_element_type=f32)


def halves(values):
    high = values.astype(bf)
    return high, (values - high.astype(f32)).astype(bf)


def exact(left, right, left_dim, right_dim):
    left_high, left_low = left if isinstance(left, tuple) else halves(left)
    right_high, right_low = right if isinstance(right, tuple) else halves(right)
    return lax.dot_general(
        jnp.concatenate([left_high, left_high, left_low], left_dim),
        jnp.concatenate([right_high, right_low, right_high], right_dim),
        (((left_dim,), (right_dim,)), ((), ())),
        preferred_element_type=f32,
    )


def stacked(first, second):
    return tuple(jnp.concatenate([a, b], 0) for a, b in zip(first, second))


class Tile:
    def __init__(self, layout_ref, group):
        live_first, live_second, same, persist = (layout_ref[group, i] for i in range(4))
        shape = (GROUP_ROWS, HEAD_DIM)
        row = lax.broadcasted_iota(jnp.int32, shape, 0)
        col = lax.broadcasted_iota(jnp.int32, shape, 1)
        late = row >= BLOCK_ROWS
        self.row, self.col = row, col
        self.live = jnp.where(late, live_second, live_first)
        self.taps = [None] + [
            jnp.where(
                row < offset,
                0.0,
                jnp.where(late & (row < BLOCK_ROWS + offset), same, 1.0),
            )
            for offset in range(1, KERNEL)
        ]
        cross = jnp.where(late & (col < BLOCK_ROWS), persist, 1.0)
        self.lower = jnp.where(row > col, cross, 0.0)
        self.lower_full = jnp.where(row >= col, cross, 0.0)

    def earlier(self, values, offset):
        return pltpu.roll(values, offset, 0) * self.taps[offset]

    def later(self, values, offset):
        return pltpu.roll(values * self.taps[offset], GROUP_ROWS - offset, 0)


def convolve(tile, values, taps):
    total = values * taps[0]
    for offset in range(1, KERNEL):
        total = total + tile.earlier(values, offset) * taps[offset]
    return total


def unit_scale(values):
    return lax.rsqrt(jnp.sum(values * values, -1, keepdims=True) + 1e-06)


def head_columns(part_width, section, head):
    return pl.ds(section * part_width + head * HEAD_DIM, HEAD_DIM)


def unit_inverses(tile, lowers):
    eye = jnp.where(tile.row == tile.col, 1.0, 0.0)
    inverses = None
    size = 1
    while size < GROUP_ROWS:
        pair = tile.row // (2 * size) == tile.col // (2 * size)
        split = pair & (tile.row // size != tile.col // size)
        parts = [jnp.where(split, lower, 0.0) for lower in lowers]
        if inverses is None:
            inverses = [eye - part for part in parts]
        else:
            kept = [halves(inverse) for inverse in inverses]
            inner = [exact(part, known, 1, 0) for part, known in zip(parts, kept)]
            outer = [exact(known, value, 1, 0) for known, value in zip(kept, inner)]
            inverses = [inverse - value for inverse, value in zip(inverses, outer)]
        size *= 2
    return inverses


def mixer_forward_kernel(
    layout_ref, pre_ref, param_ref, mixed_ref, inverse_ref, score_ref, solved_ref, out_ref
):
    width = mixed_ref.shape[1]
    heads = range(width // HEAD_DIM)
    tile = Tile(layout_ref, pl.program_id(0))
    queries, keys, values, strengths = [], [], [], []
    for head in heads:
        parts = []
        for section in range(3):
            columns = head_columns(width, section, head)
            taps = [param_ref[offset : offset + 1, columns] for offset in range(KERNEL)]
            convolved = convolve(tile, pre_ref[:, columns], taps)
            parts.append(convolved * jax.nn.sigmoid(convolved))
        queries.append(parts[0] * (unit_scale(parts[0]) * HEAD_DIM**-0.5))
        keys.append(parts[1] * unit_scale(parts[1]))
        values.append(parts[2])
        start = 4 * width + head
        strengths.append(jax.nn.sigmoid(pre_ref[:, start : start + 1]) * tile.live)
    lowers, scores = [], []
    for head in heads:
        key_halves = halves(keys[head])
        both = exact(stacked(key_halves, halves(queries[head])), key_halves, 1, 1)
        lowers.append(both[:GROUP_ROWS] * strengths[head] * tile.lower)
        scores.append(both[GROUP_ROWS:] * tile.lower_full)
    inverses = unit_inverses(tile, lowers)
    solved = [exact(inverses[head], values[head] * strengths[head], 1, 0) for head in heads]
    outs = [exact(scores[head], solved[head], 1, 0) for head in heads]
    for head in heads:
        out = outs[head]
        scaled = out * lax.rsqrt(jnp.mean(out * out, -1, keepdims=True) + 1e-05)
        gate = pre_ref[:, head_columns(width, 3, head)]
        gain = param_ref[KERNEL : KERNEL + 1, head_columns(width, 0, head)]
        mixed = scaled * gain * (gate * jax.nn.sigmoid(gate)) * tile.live
        mixed_ref[:, head_columns(width, 0, head)] = mixed.astype(bf)
        inverse_ref[head] = inverses[head]
        score_ref[head] = scores[head]
        solved_ref[head] = solved[head]
        out_ref[head] = out


def mixer_backward_kernel(
    layout_ref,
    pre_ref,
    param_ref,
    grad_ref,
    inverse_ref,
    score_ref,
    solved_ref,
    out_ref,
    d_pre_ref,
    d_param_ref,
):
    width = grad_ref.shape[1]
    heads = range(width // HEAD_DIM)
    tile = Tile(layout_ref, pl.program_id(0))

    @pl.when(pl.program_id(0) == 0)
    def _():
        d_param_ref[...] = jnp.zeros_like(d_param_ref)

    def along(values):
        return jnp.sum(values, -1, keepdims=True)

    d_outs = []
    for head in heads:
        columns = head_columns(width, 0, head)
        d_mixed = grad_ref[:, columns] * tile.live
        out = out_ref[head]
        scale = lax.rsqrt(jnp.mean(out * out, -1, keepdims=True) + 1e-05)
        scaled = out * scale
        gate = pre_ref[:, head_columns(width, 3, head)]
        gate_open = jax.nn.sigmoid(gate)
        gain = param_ref[KERNEL : KERNEL + 1, columns]
        gated = d_mixed * (gate * gate_open)
        d_param_ref[KERNEL : KERNEL + 1, columns] += jnp.sum(gated * scaled, 0, keepdims=True)
        d_gate = d_mixed * scaled * gain * (gate_open * (1.0 + gate * (1.0 - gate_open)))
        d_pre_ref[:, head_columns(width, 3, head)] = d_gate.astype(bf)
        d_scaled = gated * gain
        mean = jnp.mean(d_scaled * out, -1, keepdims=True)
        d_outs.append(scale * d_scaled - out * (scale * scale * scale * mean))
    d_out_halves = [halves(value) for value in d_outs]
    solved_halves = [halves(solved_ref[head]) for head in heads]
    d_solved = [exact(score_ref[head], d_out_halves[head], 0, 0) for head in heads]
    d_scores = [
        exact(d_out_halves[head], solved_halves[head], 1, 1) * tile.lower_full for head in heads
    ]
    d_inner = [exact(inverse_ref[head], d_solved[head], 0, 0) for head in heads]
    d_lowers = [exact(d_inner[head], solved_halves[head], 1, 1) * -tile.lower for head in heads]
    d_beta = jnp.zeros((GROUP_ROWS, SMALL), f32)
    for head in heads:
        pres, convolved, opened, active = [], [], [], []
        for section in range(3):
            columns = head_columns(width, section, head)
            taps = [param_ref[offset : offset + 1, columns] for offset in range(KERNEL)]
            pres.append(pre_ref[:, columns])
            convolved.append(convolve(tile, pres[section], taps))
            opened.append(jax.nn.sigmoid(convolved[section]))
            active.append(convolved[section] * opened[section])
        query_scale = unit_scale(active[0])
        key_scale = unit_scale(active[1])
        query_unit = active[0] * query_scale
        key = active[1] * key_scale
        start = 4 * width + head
        opening = jax.nn.sigmoid(pre_ref[:, start : start + 1])
        strength = opening * tile.live
        d_both = stacked(halves(d_lowers[head]), halves(d_scores[head]))
        by_key = exact(d_both, key, 1, 0)
        d_query = by_key[GROUP_ROWS:] * HEAD_DIM**-0.5
        from_lower = by_key[:GROUP_ROWS]
        weighted = stacked(halves(key * strength), halves(query_unit * HEAD_DIM**-0.5))
        d_key = strength * from_lower + exact(d_both, weighted, 0, 0)
        d_strength = along(d_inner[head] * active[2] + from_lower * key)
        d_value = d_inner[head] * strength
        d_opening = d_strength * (opening * (1.0 - opening)) * tile.live
        d_beta = d_beta + jnp.where(tile.col == head, d_opening, 0.0)
        d_active = [
            (d_query - query_unit * along(query_unit * d_query)) * query_scale,
            (d_key - key * along(key * d_key)) * key_scale,
            d_value,
        ]
        for section in range(3):
            columns = head_columns(width, section, head)
            taps = [param_ref[offset : offset + 1, columns] for offset in range(KERNEL)]
            slope = opened[section] * (1.0 + convolved[section] * (1.0 - opened[section]))
            d_convolved = d_active[section] * slope
            d_pre = d_convolved * taps[0]
            sums = [jnp.sum(d_convolved * pres[section], 0, keepdims=True)]
            for offset in range(1, KERNEL):
                d_pre = d_pre + tile.later(d_convolved, offset) * taps[offset]
                sums.append(
                    jnp.sum(d_convolved * tile.earlier(pres[section], offset), 0, keepdims=True)
                )
            d_param_ref[0:KERNEL, columns] += jnp.concatenate(sums, 0)
            d_pre_ref[:, columns] = d_pre.astype(bf)
    d_pre_ref[:, 4 * width :] = d_beta.astype(bf)


def mixer_specs(width):
    wide = 4 * width + SMALL
    heads = width // HEAD_DIM
    layout = pl.BlockSpec(memory_space=pltpu.SMEM)
    pre = pl.BlockSpec((GROUP_ROWS, wide), lambda group: (group, 0))
    param = pl.BlockSpec((2 * KERNEL, 3 * width), lambda group: (0, 0))
    narrow = pl.BlockSpec((GROUP_ROWS, width), lambda group: (group, 0))
    square = pl.BlockSpec((heads, GROUP_ROWS, HEAD_DIM), lambda group: (group, 0, 0))
    return layout, pre, param, narrow, square


def mixer_call(kernel, groups, width, in_specs, out_specs, out_shape):
    return pl.pallas_call(
        kernel,
        grid=(groups,),
        in_specs=in_specs,
        out_specs=out_specs,
        out_shape=out_shape,
        compiler_params=pltpu.CompilerParams(
            dimension_semantics=("arbitrary",), vmem_limit_bytes=48 * 2**20
        ),
        cost_estimate=pl.CostEstimate(
            flops=groups * width * 2**26, bytes_accessed=2**23, transcendentals=2**21
        ),
    )


def mixer_forward(layout, pre, params, width):
    groups = layout.shape[0]
    layout_spec, pre_spec, param_spec, narrow, square = mixer_specs(width)
    squares = jax.ShapeDtypeStruct((groups * width // HEAD_DIM, GROUP_ROWS, HEAD_DIM), f32)
    return mixer_call(
        mixer_forward_kernel,
        groups,
        width,
        [layout_spec, pre_spec, param_spec],
        [narrow] + [square] * 4,
        [jax.ShapeDtypeStruct((groups * GROUP_ROWS, width), bf)] + [squares] * 4,
    )(layout, pre, params)


def mixer_backward(layout, pre, params, d_mixer, kept, width):
    groups = layout.shape[0]
    layout_spec, pre_spec, param_spec, narrow, square = mixer_specs(width)
    return mixer_call(
        mixer_backward_kernel,
        groups,
        width,
        [layout_spec, pre_spec, param_spec, narrow] + [square] * 4,
        [pre_spec, param_spec],
        [
            jax.ShapeDtypeStruct(pre.shape, bf),
            jax.ShapeDtypeStruct(params.shape, f32),
        ],
    )(layout, pre, params, d_mixer, *kept)


def body(
    block_in,
    out_grad,
    norm1_gain,
    conv_weight,
    head_gain,
    qkv_weight,
    beta_weight,
    gate_weight,
    out_weight,
    norm2_gain,
    updown_weight,
    down_weight,
    seq_blocks,
    lead_blocks,
):
    devices = lax.axis_size("dp")
    parts = MODEL
    copies = devices // parts
    part = lax.axis_index("dp") // copies
    copy = lax.axis_index("dp") % copies
    rows_own = qkv_weight.shape[0]
    width = D // parts
    units = FF // parts
    heads_part = HEADS // parts
    wide = 4 * width + SMALL
    model_groups = [[m * copies + t for m in range(parts)] for t in range(copies)]
    copy_groups = [[m * copies + t for t in range(copies)] for m in range(parts)]

    def exchange(values):
        return lax.all_to_all(
            values, "dp", split_axis=0, concat_axis=0, axis_index_groups=model_groups, tiled=True
        )

    def shift(values, step):
        pairs = [
            (m * copies + t, (m + step) % parts * copies + t)
            for m in range(parts)
            for t in range(copies)
        ]
        return lax.ppermute(values, "dp", pairs)

    def gather_rows(values):
        return jnp.concatenate([values] + [shift(values, step) for step in range(1, parts)], 0)

    def scatter_rows(terms):
        terms = terms.reshape(parts, -1, terms.shape[1])
        total = terms[0]
        for step in range(1, parts):
            total = total + shift(terms[step].astype(bf), -step).astype(f32)
        return total

    def gather_copies(values):
        return lax.all_gather(values, "dp", axis=0, axis_index_groups=copy_groups, tiled=True)

    def scatter_copies(values):
        return lax.psum_scatter(
            values.astype(bf),
            "dp",
            scatter_dimension=0,
            axis_index_groups=copy_groups,
            tiled=True,
        )

    def to_wire(values):
        return values.reshape(-1, parts, copies, rows_own).swapaxes(1, 2).reshape(-1, D)

    def from_wire(values):
        return values.reshape(-1, copies, parts, rows_own).swapaxes(1, 2).reshape(-1, D)

    lanes = -(-3 * rows_own // 128) * 128
    numbers = jnp.concatenate([seq_blocks[0], lead_blocks]).astype(f32)
    small = [conv_weight.T, norm1_gain[None], head_gain[None], norm2_gain[None], numbers[None]]
    small = [jnp.pad(rows, ((0, 0), (0, lanes - rows.shape[1]))) for rows in small]
    small = jnp.pad(jnp.concatenate(small, 0).astype(bf), ((0, 2 * KERNEL), (0, 0)))
    small = lax.all_gather(small, "dp", axis=0, tiled=True).reshape(devices, 4 * KERNEL, lanes)
    taps = small[:, :KERNEL, : 3 * rows_own].swapaxes(0, 1).reshape(KERNEL, 3, parts, width)
    taps = lax.dynamic_index_in_dim(taps, part, 2, keepdims=False).reshape(KERNEL, 3 * width)
    gain_one, head_full, gain_two = (
        small[:, KERNEL + i, :rows_own].reshape(1, D).astype(f32) for i in range(3)
    )
    head_part = lax.dynamic_slice_in_dim(head_full, part * width, width, 1)
    params = jnp.concatenate([taps.astype(f32), jnp.pad(head_part, ((0, 0), (0, 2 * width)))], 0)
    params = jnp.pad(params, ((0, KERNEL - 1), (0, 0)))
    layouts = []
    for step in range(parts):
        owner = (part - step) % parts * copies + copy
        numbers = lax.dynamic_index_in_dim(small, owner, 0, keepdims=False)[KERNEL + 3]
        layouts.append(block_layout(*(numbers[i].astype(jnp.int32) for i in range(3))))
    layouts = jnp.stack(layouts)

    pieces = jnp.concatenate([qkv_weight, gate_weight], 1).astype(bf)
    pieces = pieces.reshape(rows_own, 4, parts, width).transpose(2, 0, 1, 3)
    strength_pieces = beta_weight.astype(bf).reshape(rows_own, parts, heads_part).swapaxes(0, 1)
    strength_pieces = jnp.pad(strength_pieces, ((0, 0), (0, 0), (0, SMALL - heads_part)))
    pieces = jnp.concatenate([pieces.reshape(parts, rows_own, 4 * width), strength_pieces], 2)
    w_mixer = gather_copies(exchange(pieces).reshape(parts * rows_own, wide))
    w_out = gather_copies(out_weight.astype(bf))

    pieces = updown_weight.astype(bf).reshape(rows_own, 2, parts, units).transpose(2, 0, 1, 3)
    pieces = exchange(pieces.reshape(parts, rows_own, 2 * units))
    w_updown = gather_copies(pieces.reshape(parts * rows_own, 2 * units))
    w_down = gather_copies(down_weight.astype(bf))

    inputs = block_in.astype(f32)
    input_rows = to_wire(gather_rows(block_in)).astype(f32)
    input_scale = lax.rsqrt(jnp.mean(input_rows * input_rows, -1, keepdims=True) + 1e-06)
    normed = (input_rows * input_scale * to_wire(gain_one)).astype(bf)
    cotangent = gather_rows(out_grad)

    pre = plain_product(normed, w_mixer)
    mixed, *kept = mixer_forward(layouts, pre, params, width)
    hidden = inputs + scatter_rows(plain_product(mixed, w_out))
    normed_two, norm_two_back = jax.vjp(rms_scale, hidden, gain_two)
    normed_two = gather_rows(to_wire(normed_two.astype(bf)))

    def swiglu_units(updown):
        return jax.nn.silu(updown[:, :units]) * updown[:, units:]

    updown = plain_product(normed_two, w_updown)
    active, swiglu_back = jax.vjp(swiglu_units, updown)
    active = active.astype(bf)
    d_active = transposed_product(cotangent, w_down)
    d_updown = swiglu_back(d_active)[0].astype(bf)
    d_normed_two = from_wire(scatter_rows(transposed_product(d_updown, w_updown)))
    block_out = (hidden + scatter_rows(plain_product(active, w_down))).astype(bf)
    down_shard = scatter_copies(rows_product(active, cotangent)).astype(f32)
    updown_grad = scatter_copies(rows_product(normed_two, d_updown))
    updown_grad = exchange(updown_grad.reshape(parts, rows_own, 2 * units))
    updown_shard = updown_grad.reshape(parts, rows_own, 2, units).transpose(1, 2, 0, 3)
    updown_shard = updown_shard.reshape(rows_own, 2 * FF).astype(f32)

    d_hidden_part, gain_two_grad = norm_two_back(d_normed_two)
    d_hidden = out_grad.astype(f32) + d_hidden_part
    d_mixed = gather_rows(d_hidden.astype(bf))
    d_mixer = transposed_product(d_mixed, w_out)
    d_pre, d_params = mixer_backward(layouts, pre, params, d_mixer, kept, width)
    out_shard = scatter_copies(rows_product(mixed, d_mixed)).astype(f32)

    d_normed_terms = transposed_product(d_pre, w_mixer)
    gain_one_grad = jnp.sum(d_normed_terms * (input_rows * input_scale), 0)
    d_normed = from_wire(scatter_rows(d_normed_terms))
    _, norm_one_back = jax.vjp(lambda values: rms_scale(values, gain_one), inputs)
    input_grad = (d_hidden + norm_one_back(d_normed)[0]).astype(bf)

    taps_grad = d_params[:KERNEL].reshape(KERNEL, 3, 1, width)
    taps_grad = lax.dynamic_update_slice_in_dim(
        jnp.zeros((KERNEL, 3, parts, width), f32), taps_grad, part, 2
    )
    taps_grad = taps_grad.reshape(KERNEL, 3 * D).T.reshape(D, 3 * KERNEL)
    head_grad = lax.dynamic_update_slice_in_dim(
        jnp.zeros((D,), f32), d_params[KERNEL, :width], part * width, 0
    )
    columns = jnp.concatenate([taps_grad, head_grad[:, None], gain_two_grad.reshape(D, 1)], 1)
    columns = columns.reshape(parts, copies, rows_own, -1).swapaxes(0, 1).reshape(D, -1)
    columns = jnp.concatenate([columns, gain_one_grad[:, None]], 1)
    first = 4 * width + heads_part
    columns = jnp.pad(columns, ((0, 0), (first, wide - first - columns.shape[1])))
    mixer_grad = scatter_copies(rows_product(normed, d_pre) + columns)
    mixer_grad = exchange(mixer_grad.reshape(parts, rows_own, wide))
    main = mixer_grad[:, :, : 4 * width].reshape(parts, rows_own, 4, width).transpose(1, 2, 0, 3)
    main = main.reshape(rows_own, 4 * D).astype(f32)
    beta_shard = mixer_grad[:, :, 4 * width : first].swapaxes(0, 1).reshape(rows_own, HEADS)
    sums = jnp.sum(mixer_grad[:, :, first:].astype(f32), 0)
    taps_width = 3 * KERNEL
    return (
        block_out,
        input_grad,
        sums[:, taps_width + 2],
        sums[:, :taps_width].reshape(-1, KERNEL),
        sums[:, taps_width],
        main[:, : 3 * D],
        beta_shard.astype(f32),
        main[:, 3 * D :],
        out_shard,
        sums[:, taps_width + 1],
        updown_shard,
        down_shard,
    )


def solution(mesh):
    placed = (
        P("dp", None),
        P("dp", None),
        P("dp"),
        P("dp", None),
        P("dp"),
        P("dp", None),
        P("dp", None),
        P("dp", None),
        P("dp", None),
        P("dp"),
        P("dp", None),
        P("dp", None),
        P("dp", None),
        P("dp"),
    )
    return jax.shard_map(
        body,
        mesh=mesh,
        in_specs=placed,
        out_specs=(
            P("dp", None),
            P("dp", None),
            P("dp"),
            P("dp", None),
            P("dp"),
            P("dp", None),
            P("dp", None),
            P("dp", None),
            P("dp", None),
            P("dp"),
            P("dp", None),
            P("dp", None),
        ),
        check_vma=False,
    )
```

```python
import jax
import jax.numpy as jnp
from jax import lax
from jax.experimental import pallas as pl
from jax.experimental.pallas import tpu as pltpu
from jax.sharding import PartitionSpec as P

D = 2048
HEADS = 16
HEAD_DIM = 128
FF = 5632
KERNEL = 4
BLOCK_ROWS = 64
BLOCKS_DEV = 2
GROUP_ROWS = BLOCK_ROWS * BLOCKS_DEV
SMALL = 128
MODEL = 4

f32 = jnp.float32
bf = jnp.bfloat16


def block_layouts(first, second, lead):
    def doc(block):
        in_first = (block >= lead) & (block < lead + first)
        in_second = (block >= lead + first) & (block < lead + first + second)
        return jnp.where(in_first, 1, jnp.where(in_second, 2, 0))

    starts = (lead == 1) | (lead + first == 1) & (second > 0)
    columns = [doc(0) > 0, doc(1) > 0, doc(0) == doc(1), ~starts]
    return jnp.stack(columns, 1).astype(f32)


def plain_product(left, right):
    return jnp.dot(left, right, preferred_element_type=f32)


def rows_product(left, right):
    return lax.dot_general(left, right, (((0,), (0,)), ((), ())), preferred_element_type=f32)


def transposed_product(left, right):
    return lax.dot_general(left, right, (((1,), (1,)), ((), ())), preferred_element_type=f32)


def halves(values):
    high = values.astype(bf)
    return high, (values - high.astype(f32)).astype(bf)


def exact(left, right, left_dim, right_dim):
    left_high, left_low = left if isinstance(left, tuple) else halves(left)
    right_high, right_low = right if isinstance(right, tuple) else halves(right)
    return lax.dot_general(
        jnp.concatenate([left_high, left_high, left_low], left_dim),
        jnp.concatenate([right_high, right_low, right_high], right_dim),
        (((left_dim,), (right_dim,)), ((), ())),
        preferred_element_type=f32,
    )


def stacked(first, second):
    return tuple(jnp.concatenate([a, b], 0) for a, b in zip(first, second))


class Tile:
    def __init__(self, layout_ref, group):
        live_first, live_second, same, persist = (layout_ref[group, i] for i in range(4))
        shape = (GROUP_ROWS, HEAD_DIM)
        row = lax.broadcasted_iota(jnp.int32, shape, 0)
        col = lax.broadcasted_iota(jnp.int32, shape, 1)
        late = row >= BLOCK_ROWS
        self.row, self.col = row, col
        self.live = jnp.where(late, live_second, live_first)
        self.taps = [None] + [
            jnp.where(
                row < offset,
                0.0,
                jnp.where(late & (row < BLOCK_ROWS + offset), same, 1.0),
            )
            for offset in range(1, KERNEL)
        ]
        cross = jnp.where(late & (col < BLOCK_ROWS), persist, 1.0)
        self.lower = jnp.where(row > col, cross, 0.0)
        self.lower_full = jnp.where(row >= col, cross, 0.0)

    def earlier(self, values, offset):
        return pltpu.roll(values, offset, 0) * self.taps[offset]

    def later(self, values, offset):
        return pltpu.roll(values * self.taps[offset], GROUP_ROWS - offset, 0)


def convolve(tile, values, taps):
    total = values * taps[0]
    for offset in range(1, KERNEL):
        total = total + tile.earlier(values, offset) * taps[offset]
    return total


def unit_scale(values):
    return lax.rsqrt(jnp.sum(values * values, -1, keepdims=True) + 1e-06)


def head_columns(part_width, section, head):
    return pl.ds(section * part_width + head * HEAD_DIM, HEAD_DIM)


def unit_inverses(tile, lowers):
    eye = jnp.where(tile.row == tile.col, 1.0, 0.0)
    inverses = None
    size = 1
    while size < GROUP_ROWS:
        pair = tile.row // (2 * size) == tile.col // (2 * size)
        split = pair & (tile.row // size != tile.col // size)
        parts = [jnp.where(split, lower, 0.0) for lower in lowers]
        if inverses is None:
            inverses = [eye - part for part in parts]
        else:
            kept = [halves(inverse) for inverse in inverses]
            inner = [exact(part, known, 1, 0) for part, known in zip(parts, kept)]
            outer = [exact(known, value, 1, 0) for known, value in zip(kept, inner)]
            inverses = [inverse - value for inverse, value in zip(inverses, outer)]
        size *= 2
    return inverses


def mixer_forward_kernel(
    layout_ref, pre_ref, param_ref, mixed_ref, inverse_ref, score_ref, solved_ref, out_ref
):
    width = mixed_ref.shape[1]
    heads = range(width // HEAD_DIM)
    tile = Tile(layout_ref, pl.program_id(0))
    queries, keys, values, strengths = [], [], [], []
    for head in heads:
        parts = []
        for section in range(3):
            columns = head_columns(width, section, head)
            taps = [param_ref[offset : offset + 1, columns] for offset in range(KERNEL)]
            convolved = convolve(tile, pre_ref[:, columns], taps)
            parts.append(convolved * jax.nn.sigmoid(convolved))
        queries.append(parts[0] * (unit_scale(parts[0]) * HEAD_DIM**-0.5))
        keys.append(parts[1] * unit_scale(parts[1]))
        values.append(parts[2])
        start = 4 * width + head
        strengths.append(jax.nn.sigmoid(pre_ref[:, start : start + 1]) * tile.live)
    lowers, scores = [], []
    for head in heads:
        key_halves = halves(keys[head])
        both = exact(stacked(key_halves, halves(queries[head])), key_halves, 1, 1)
        lowers.append(both[:GROUP_ROWS] * strengths[head] * tile.lower)
        scores.append(both[GROUP_ROWS:] * tile.lower_full)
    inverses = unit_inverses(tile, lowers)
    solved = [exact(inverses[head], values[head] * strengths[head], 1, 0) for head in heads]
    outs = [exact(scores[head], solved[head], 1, 0) for head in heads]
    for head in heads:
        out = outs[head]
        scaled = out * lax.rsqrt(jnp.mean(out * out, -1, keepdims=True) + 1e-05)
        gate = pre_ref[:, head_columns(width, 3, head)]
        gain = param_ref[KERNEL : KERNEL + 1, head_columns(width, 0, head)]
        mixed = scaled * gain * (gate * jax.nn.sigmoid(gate)) * tile.live
        mixed_ref[:, head_columns(width, 0, head)] = mixed.astype(bf)
        inverse_ref[head] = inverses[head]
        score_ref[head] = scores[head]
        solved_ref[head] = solved[head]
        out_ref[head] = out


def mixer_backward_kernel(
    layout_ref,
    pre_ref,
    param_ref,
    grad_ref,
    inverse_ref,
    score_ref,
    solved_ref,
    out_ref,
    d_pre_ref,
    d_param_ref,
):
    width = grad_ref.shape[1]
    heads = range(width // HEAD_DIM)
    tile = Tile(layout_ref, pl.program_id(0))

    @pl.when(pl.program_id(0) == 0)
    def _():
        d_param_ref[...] = jnp.zeros_like(d_param_ref)

    def along(values):
        return jnp.sum(values, -1, keepdims=True)

    d_outs = []
    for head in heads:
        columns = head_columns(width, 0, head)
        d_mixed = grad_ref[:, columns] * tile.live
        out = out_ref[head]
        scale = lax.rsqrt(jnp.mean(out * out, -1, keepdims=True) + 1e-05)
        scaled = out * scale
        gate = pre_ref[:, head_columns(width, 3, head)]
        gate_open = jax.nn.sigmoid(gate)
        gain = param_ref[KERNEL : KERNEL + 1, columns]
        gated = d_mixed * (gate * gate_open)
        d_param_ref[KERNEL : KERNEL + 1, columns] += jnp.sum(gated * scaled, 0, keepdims=True)
        d_gate = d_mixed * scaled * gain * (gate_open * (1.0 + gate * (1.0 - gate_open)))
        d_pre_ref[:, head_columns(width, 3, head)] = d_gate.astype(bf)
        d_scaled = gated * gain
        mean = jnp.mean(d_scaled * out, -1, keepdims=True)
        d_outs.append(scale * d_scaled - out * (scale * scale * scale * mean))
    d_out_halves = [halves(value) for value in d_outs]
    solved_halves = [halves(solved_ref[head]) for head in heads]
    d_solved = [exact(score_ref[head], d_out_halves[head], 0, 0) for head in heads]
    d_scores = [
        exact(d_out_halves[head], solved_halves[head], 1, 1) * tile.lower_full for head in heads
    ]
    d_inner = [exact(inverse_ref[head], d_solved[head], 0, 0) for head in heads]
    d_lowers = [exact(d_inner[head], solved_halves[head], 1, 1) * -tile.lower for head in heads]
    d_beta = jnp.zeros((GROUP_ROWS, SMALL), f32)
    for head in heads:
        pres, convolved, opened, active = [], [], [], []
        for section in range(3):
            columns = head_columns(width, section, head)
            taps = [param_ref[offset : offset + 1, columns] for offset in range(KERNEL)]
            pres.append(pre_ref[:, columns])
            convolved.append(convolve(tile, pres[section], taps))
            opened.append(jax.nn.sigmoid(convolved[section]))
            active.append(convolved[section] * opened[section])
        query_scale = unit_scale(active[0])
        key_scale = unit_scale(active[1])
        query_unit = active[0] * query_scale
        key = active[1] * key_scale
        start = 4 * width + head
        opening = jax.nn.sigmoid(pre_ref[:, start : start + 1])
        strength = opening * tile.live
        d_both = stacked(halves(d_lowers[head]), halves(d_scores[head]))
        by_key = exact(d_both, key, 1, 0)
        d_query = by_key[GROUP_ROWS:] * HEAD_DIM**-0.5
        from_lower = by_key[:GROUP_ROWS]
        weighted = stacked(halves(key * strength), halves(query_unit * HEAD_DIM**-0.5))
        d_key = strength * from_lower + exact(d_both, weighted, 0, 0)
        d_strength = along(d_inner[head] * active[2] + from_lower * key)
        d_value = d_inner[head] * strength
        d_opening = d_strength * (opening * (1.0 - opening)) * tile.live
        d_beta = d_beta + jnp.where(tile.col == head, d_opening, 0.0)
        d_active = [
            (d_query - query_unit * along(query_unit * d_query)) * query_scale,
            (d_key - key * along(key * d_key)) * key_scale,
            d_value,
        ]
        for section in range(3):
            columns = head_columns(width, section, head)
            taps = [param_ref[offset : offset + 1, columns] for offset in range(KERNEL)]
            slope = opened[section] * (1.0 + convolved[section] * (1.0 - opened[section]))
            d_convolved = d_active[section] * slope
            d_pre = d_convolved * taps[0]
            sums = [jnp.sum(d_convolved * pres[section], 0, keepdims=True)]
            for offset in range(1, KERNEL):
                d_pre = d_pre + tile.later(d_convolved, offset) * taps[offset]
                sums.append(
                    jnp.sum(d_convolved * tile.earlier(pres[section], offset), 0, keepdims=True)
                )
            d_param_ref[0:KERNEL, columns] += jnp.concatenate(sums, 0)
            d_pre_ref[:, columns] = d_pre.astype(bf)
    d_pre_ref[:, 4 * width :] = d_beta.astype(bf)


def mixer_specs(width):
    wide = 4 * width + SMALL
    heads = width // HEAD_DIM
    layout = pl.BlockSpec(memory_space=pltpu.SMEM)
    pre = pl.BlockSpec((GROUP_ROWS, wide), lambda group: (group, 0))
    param = pl.BlockSpec((2 * KERNEL, 3 * width), lambda group: (0, 0))
    narrow = pl.BlockSpec((GROUP_ROWS, width), lambda group: (group, 0))
    square = pl.BlockSpec((heads, GROUP_ROWS, HEAD_DIM), lambda group: (group, 0, 0))
    return layout, pre, param, narrow, square


def mixer_call(kernel, groups, width, in_specs, out_specs, out_shape):
    return pl.pallas_call(
        kernel,
        grid=(groups,),
        in_specs=in_specs,
        out_specs=out_specs,
        out_shape=out_shape,
        compiler_params=pltpu.CompilerParams(
            dimension_semantics=("arbitrary",), vmem_limit_bytes=48 * 2**20
        ),
        cost_estimate=pl.CostEstimate(
            flops=groups * width * 2**26, bytes_accessed=2**23, transcendentals=2**21
        ),
    )


def mixer_forward(layout, pre, params, width):
    groups = layout.shape[0]
    layout_spec, pre_spec, param_spec, narrow, square = mixer_specs(width)
    squares = jax.ShapeDtypeStruct((groups * width // HEAD_DIM, GROUP_ROWS, HEAD_DIM), f32)
    return mixer_call(
        mixer_forward_kernel,
        groups,
        width,
        [layout_spec, pre_spec, param_spec],
        [narrow] + [square] * 4,
        [jax.ShapeDtypeStruct((groups * GROUP_ROWS, width), bf)] + [squares] * 4,
    )(layout, pre, params)


def mixer_backward(layout, pre, params, d_mixer, kept, width):
    groups = layout.shape[0]
    layout_spec, pre_spec, param_spec, narrow, square = mixer_specs(width)
    return mixer_call(
        mixer_backward_kernel,
        groups,
        width,
        [layout_spec, pre_spec, param_spec, narrow] + [square] * 4,
        [pre_spec, param_spec],
        [
            jax.ShapeDtypeStruct(pre.shape, bf),
            jax.ShapeDtypeStruct(params.shape, f32),
        ],
    )(layout, pre, params, d_mixer, *kept)


def tie(value, *others):
    anywhere = pl.BlockSpec(memory_space=pl.ANY)
    return pl.pallas_call(
        lambda *refs: None,
        in_specs=[anywhere] * (1 + len(others)),
        out_specs=anywhere,
        out_shape=jax.ShapeDtypeStruct(value.shape, value.dtype),
        input_output_aliases={0: 0},
        cost_estimate=pl.CostEstimate(flops=0, bytes_accessed=0, transcendentals=0),
    )(value, *others)


def copy_columns(*refs):
    *sources, target = refs
    start = 0
    for source in sources:
        block = source[...].reshape(source.shape[-2:])
        columns = pl.ds(start, block.shape[1])
        if len(target.shape) == 3:
            target[0, :, columns] = block.astype(target.dtype)
        else:
            target[:, columns] = block.astype(target.dtype)
        start += block.shape[1]


def to_parts(sources, parts, dtype):
    rows = sources[0][0].shape[0]

    def spec(section, width):
        return pl.BlockSpec((rows, width), lambda p: (0, section * parts + p))

    total = sum(width for _, _, width in sources)
    return pl.pallas_call(
        copy_columns,
        grid=(parts,),
        in_specs=[spec(section, width) for _, section, width in sources],
        out_specs=pl.BlockSpec((1, rows, total), lambda p: (p, 0, 0)),
        out_shape=jax.ShapeDtypeStruct((parts, rows, total), dtype),
    )(*[array for array, _, _ in sources])


def from_parts(slabs, width, first, sections):
    parts, rows, _ = slabs.shape
    return pl.pallas_call(
        copy_columns,
        grid=(sections, parts),
        in_specs=[pl.BlockSpec((1, rows, width), lambda s, p: (p, 0, first + s))],
        out_specs=pl.BlockSpec((rows, width), lambda s, p: (0, s * parts + p)),
        out_shape=jax.ShapeDtypeStruct((rows, sections * parts * width), f32),
    )(slabs)


def total_of(own_ref, received_refs):
    total = own_ref[...]
    for ref in received_refs:
        total = total + ref[...].astype(f32)
    return total


def row_scale(values):
    return lax.rsqrt(jnp.mean(values * values, -1, keepdims=True) + 1e-06)


def norm_slope(values, scale, gain, grad):
    mean = jnp.mean(gain * grad * values, -1, keepdims=True)
    return scale * gain * grad - values * (scale * scale * scale * mean)


def hidden_kernel(own_ref, *refs):
    *received, input_ref, gain_ref, hidden_ref, normed_ref = refs
    hidden = input_ref[...].astype(f32) + total_of(own_ref, received)
    hidden_ref[...] = hidden
    normed_ref[...] = (hidden * row_scale(hidden) * gain_ref[...]).astype(bf)


def hidden_back_kernel(own_ref, *refs):
    *received, hidden_ref, gain_ref, cot_ref, d_hidden_ref, d_mixed_ref, d_gain_ref = refs
    grad = total_of(own_ref, received)
    hidden = hidden_ref[...]
    scale = row_scale(hidden)

    @pl.when(pl.program_id(0) == 0)
    def _():
        d_gain_ref[...] = jnp.zeros_like(d_gain_ref)

    d_gain_ref[...] += jnp.sum(grad * hidden * scale, 0, keepdims=True)
    d_hidden = cot_ref[...].astype(f32) + norm_slope(hidden, scale, gain_ref[...], grad)
    d_hidden_ref[...] = d_hidden
    d_mixed_ref[...] = d_hidden.astype(bf)


def input_back_kernel(own_ref, *refs):
    *received, input_ref, gain_ref, d_hidden_ref, out_ref = refs
    grad = total_of(own_ref, received)
    values = input_ref[...].astype(f32)
    slope = norm_slope(values, row_scale(values), gain_ref[...], grad)
    out_ref[...] = (d_hidden_ref[...] + slope).astype(bf)


def block_out_kernel(own_ref, *refs):
    *received, hidden_ref, out_ref = refs
    out_ref[...] = (hidden_ref[...] + total_of(own_ref, received)).astype(bf)


def by_rows(kernel, arrays, outs, block=32):
    def spec(shape):
        if shape[0] == 1:
            return pl.BlockSpec(shape, lambda i: (0, 0))
        return pl.BlockSpec((block, shape[1]), lambda i: (i, 0))

    return pl.pallas_call(
        kernel,
        grid=(GROUP_ROWS // block,),
        in_specs=[spec(array.shape) for array in arrays],
        out_specs=[spec(shape) for shape, _ in outs],
        out_shape=[jax.ShapeDtypeStruct(shape, dtype) for shape, dtype in outs],
        compiler_params=pltpu.CompilerParams(dimension_semantics=("arbitrary",)),
    )(*arrays)


def body(
    block_in,
    out_grad,
    norm1_gain,
    conv_weight,
    head_gain,
    qkv_weight,
    beta_weight,
    gate_weight,
    out_weight,
    norm2_gain,
    updown_weight,
    down_weight,
    seq_blocks,
    lead_blocks,
):
    devices = lax.axis_size("dp")
    parts = MODEL
    copies = devices // parts
    part = lax.axis_index("dp") // copies
    copy = lax.axis_index("dp") % copies
    rows_own = qkv_weight.shape[0]
    width = D // parts
    units = FF // parts
    heads_part = HEADS // parts
    wide = 4 * width + SMALL
    model_groups = [[m * copies + t for m in range(parts)] for t in range(copies)]
    copy_groups = [[m * copies + t for t in range(copies)] for m in range(parts)]

    def exchange(values):
        return lax.all_to_all(
            values, "dp", split_axis=0, concat_axis=0, axis_index_groups=model_groups, tiled=True
        )

    def shift(values, step):
        pairs = [
            (m * copies + t, (m + step) % parts * copies + t)
            for m in range(parts)
            for t in range(copies)
        ]
        return lax.ppermute(values, "dp", pairs)

    def exchange_apart(values):
        whole = values
        for step in range(1, parts):
            piece = lax.dynamic_index_in_dim(values, (part + step) % parts, 0, keepdims=False)
            piece = shift(piece, step)
            whole = lax.dynamic_update_index_in_dim(whole, piece, (part - step) % parts, 0)
        return whole

    def gather_rows(values):
        return [values] + [shift(values, step) for step in range(1, parts)]

    def scatter_rows(terms):
        others = [
            shift(terms[step * GROUP_ROWS :][:GROUP_ROWS].astype(bf), -step)
            for step in range(1, parts)
        ]
        return [terms] + others

    def gather_copies(values):
        return lax.all_gather(values, "dp", axis=0, axis_index_groups=copy_groups, tiled=True)

    def scatter_copies(values):
        return lax.psum_scatter(
            values.astype(bf),
            "dp",
            scatter_dimension=0,
            axis_index_groups=copy_groups,
            tiled=True,
        )

    def to_wire(values):
        return values.reshape(-1, parts, copies, rows_own).swapaxes(1, 2).reshape(-1, D)

    def from_wire(values):
        return values.reshape(-1, copies, parts, rows_own).swapaxes(1, 2).reshape(-1, D)

    strengths = beta_weight.reshape(rows_own, parts, heads_part)
    strengths = jnp.pad(strengths, ((0, 0), (0, 0), (0, SMALL - heads_part)))
    strengths = strengths.reshape(rows_own, parts * SMALL)
    pieces = [(qkv_weight, section, width) for section in range(3)]
    pieces = to_parts(pieces + [(gate_weight, 0, width), (strengths, 0, SMALL)], parts, bf)
    mixer_pieces = exchange(pieces)
    w_mixer = gather_copies(mixer_pieces.reshape(parts * rows_own, wide))
    w_out = gather_copies(to_wire(out_weight.astype(bf)))

    lanes = -(-3 * rows_own // 128) * 128
    numbers = jnp.concatenate([seq_blocks[0], lead_blocks]).astype(f32)
    small = [conv_weight.T, norm1_gain[None], head_gain[None], norm2_gain[None], numbers[None]]
    small = [jnp.pad(rows, ((0, 0), (0, lanes - rows.shape[1]))) for rows in small]
    small = jnp.pad(jnp.concatenate(small, 0).astype(bf), ((0, 2 * KERNEL), (0, 0)))
    small = jnp.broadcast_to(small[None], (devices,) + small.shape)
    small = lax.all_to_all(tie(small, mixer_pieces), "dp", 0, 0, tiled=True)
    taps = small[:, :KERNEL, : 3 * rows_own].swapaxes(0, 1).reshape(KERNEL, 3, parts, width)
    taps = lax.dynamic_index_in_dim(taps, part, 2, keepdims=False).reshape(KERNEL, 3 * width)
    gain_one, head_full, gain_two = (
        small[:, KERNEL + i, :rows_own].reshape(1, D).astype(f32) for i in range(3)
    )
    gain_one, gain_two = to_wire(gain_one), to_wire(gain_two)
    head_part = lax.dynamic_slice_in_dim(head_full, part * width, width, 1)
    params = jnp.concatenate([taps.astype(f32), jnp.pad(head_part, ((0, 0), (0, 2 * width)))], 0)
    params = jnp.pad(params, ((0, KERNEL - 1), (0, 0)))
    numbers = small[:, KERNEL + 3, :3].astype(f32).astype(jnp.int32)
    layouts = block_layouts(numbers[:, 0], numbers[:, 1], numbers[:, 2])
    layouts = layouts.reshape(parts, copies, 4)
    layouts = lax.dynamic_index_in_dim(layouts, copy, 1, keepdims=False)
    wanted = (part - jnp.arange(parts)) % parts
    wanted = (wanted[:, None] == jnp.arange(parts)).astype(f32)
    layouts = jnp.sum(wanted[:, :, None] * layouts, 1)

    inputs = to_wire(block_in)
    input_rows = gather_rows(tie(inputs, mixer_pieces))

    pieces = to_parts([(updown_weight, half, units) for half in range(2)], parts, bf)
    pieces = exchange_apart(tie(pieces, *input_rows[1:]))
    w_updown = gather_copies(pieces.reshape(parts * rows_own, 2 * units))
    w_down = gather_copies(to_wire(down_weight.astype(bf)))
    cotangent_own = to_wire(out_grad)
    cotangent = gather_rows(tie(cotangent_own, pieces))

    input_rows = jnp.concatenate(input_rows, 0).astype(f32)
    input_scale = row_scale(input_rows)
    normed = (input_rows * input_scale * gain_one).astype(bf)
    pre = plain_product(normed, w_mixer)
    mixed, *kept = mixer_forward(layouts, pre, params, width)
    stream = ((GROUP_ROWS, D), f32)
    narrow = ((GROUP_ROWS, D), bf)
    hidden, normed_two = by_rows(
        hidden_kernel,
        scatter_rows(plain_product(mixed, w_out)) + [inputs, tie(gain_two, *cotangent[1:])],
        [stream, narrow],
    )
    normed_two = jnp.concatenate(gather_rows(normed_two), 0)
    cotangent = jnp.concatenate(cotangent, 0)

    def swiglu_units(updown):
        return jax.nn.silu(updown[:, :units]) * updown[:, units:]

    updown = plain_product(normed_two, w_updown)
    active, swiglu_back = jax.vjp(swiglu_units, updown)
    active = active.astype(bf)
    d_active = transposed_product(cotangent, w_down)
    d_updown = swiglu_back(d_active)[0].astype(bf)
    d_normed_two = scatter_rows(transposed_product(d_updown, w_updown))
    updown_terms = rows_product(normed_two, tie(d_updown, *d_normed_two[:1])).astype(bf)
    down_terms = rows_product(active, cotangent).astype(bf)
    updown_grad = scatter_copies(updown_terms)
    down_grad = scatter_copies(tie(down_terms, updown_grad))

    gain_two_late = tie(gain_two, updown_terms, down_terms)
    d_hidden, d_mixed, gain_two_grad = by_rows(
        hidden_back_kernel,
        d_normed_two + [hidden, gain_two_late, cotangent_own],
        [stream, narrow, ((1, D), f32)],
    )
    d_mixed = jnp.concatenate(gather_rows(d_mixed), 0)
    d_mixer = transposed_product(d_mixed, w_out)
    block_out = scatter_rows(plain_product(tie(active, d_mixed), w_down))
    d_pre, d_params = mixer_backward(layouts, pre, params, d_mixer, kept, width)
    out_terms = rows_product(mixed, d_mixed).astype(bf)

    d_normed_terms = transposed_product(d_pre, w_mixer)
    gain_one_grad = jnp.sum(d_normed_terms * (input_rows * input_scale), 0, keepdims=True)
    here = (jnp.arange(parts) == part).astype(f32)[:, None]
    taps_grad = d_params[:KERNEL].reshape(KERNEL, 3, 1, width) * here
    taps_grad = taps_grad.reshape(KERNEL, parts, copies, 3, rows_own).transpose(3, 0, 2, 1, 4)
    head_grad = to_wire((d_params[KERNEL, :width] * here).reshape(1, D))
    columns = [taps_grad.reshape(3 * KERNEL, D), head_grad, gain_two_grad, gain_one_grad]
    columns = jnp.concatenate(columns, 0)
    columns = rows_product(columns, jnp.eye(columns.shape[0], dtype=f32))
    first = 4 * width + heads_part
    columns = jnp.pad(columns, ((0, 0), (first, wide - first - columns.shape[1])))
    mixer_terms = (rows_product(normed, d_pre) + columns).astype(bf)
    mixer_grad = scatter_copies(tie(mixer_terms, down_grad))
    out_shard = from_wire(scatter_copies(tie(out_terms, mixer_grad)).astype(f32))
    down_shard = from_wire(down_grad.astype(f32))
    mixer_grad = exchange(mixer_grad.reshape(parts, rows_own, wide))
    qkv_shard = from_parts(mixer_grad, width, 0, 3)
    gate_shard = from_parts(mixer_grad, width, 3, 1)
    beta_shard = mixer_grad[:, :, 4 * width : first].swapaxes(0, 1).reshape(rows_own, HEADS)
    sums = jnp.sum(mixer_grad[:, :, first:].astype(f32), 0)
    taps_width = 3 * KERNEL
    taps_shard = sums[:, :taps_width].reshape(rows_own, 3, KERNEL).swapaxes(0, 1)

    updown_grad = exchange_apart(updown_grad.reshape(parts, rows_own, 2 * units))
    updown_shard = from_parts(updown_grad, units, 0, 2)
    (input_grad,) = by_rows(
        input_back_kernel, scatter_rows(d_normed_terms) + [inputs, gain_one, d_hidden], [narrow]
    )
    (block_out,) = by_rows(block_out_kernel, block_out + [hidden], [narrow])
    return (
        from_wire(block_out),
        from_wire(input_grad),
        sums[:, taps_width + 2],
        taps_shard.reshape(-1, KERNEL),
        sums[:, taps_width],
        qkv_shard,
        beta_shard.astype(f32),
        gate_shard,
        out_shard,
        sums[:, taps_width + 1],
        updown_shard,
        down_shard,
    )


def solution(mesh):
    placed = (
        P("dp", None),
        P("dp", None),
        P("dp"),
        P("dp", None),
        P("dp"),
        P("dp", None),
        P("dp", None),
        P("dp", None),
        P("dp", None),
        P("dp"),
        P("dp", None),
        P("dp", None),
        P("dp", None),
        P("dp"),
    )
    return jax.shard_map(
        body,
        mesh=mesh,
        in_specs=placed,
        out_specs=(
            P("dp", None),
            P("dp", None),
            P("dp"),
            P("dp", None),
            P("dp"),
            P("dp", None),
            P("dp", None),
            P("dp", None),
            P("dp", None),
            P("dp"),
            P("dp", None),
            P("dp", None),
        ),
        check_vma=False,
    )
```

```python
import jax
import jax.numpy as jnp
from jax import lax
from jax.experimental import pallas as pl
from jax.experimental.pallas import tpu as pltpu
from jax.sharding import PartitionSpec as P

D = 2048
HEADS = 16
HEAD_DIM = 128
FF = 5632
KERNEL = 4
BLOCK_ROWS = 64
BLOCKS_DEV = 2
GROUP_ROWS = BLOCK_ROWS * BLOCKS_DEV
SMALL = 128
MODEL = 4

f32 = jnp.float32
bf = jnp.bfloat16


def block_layouts(first, second, lead):
    def doc(block):
        in_first = (block >= lead) & (block < lead + first)
        in_second = (block >= lead + first) & (block < lead + first + second)
        return jnp.where(in_first, 1, jnp.where(in_second, 2, 0))

    starts = (lead == 1) | (lead + first == 1) & (second > 0)
    columns = [doc(0) > 0, doc(1) > 0, doc(0) == doc(1), ~starts]
    return jnp.stack(columns, 1).astype(f32)


def plain_product(left, right):
    return jnp.dot(left, right, preferred_element_type=f32)


def rows_product(left, right):
    return lax.dot_general(left, right, (((0,), (0,)), ((), ())), preferred_element_type=f32)


def transposed_product(left, right):
    return lax.dot_general(left, right, (((1,), (1,)), ((), ())), preferred_element_type=f32)


def halves(values):
    high = values.astype(bf)
    return high, (values - high.astype(f32)).astype(bf)


def exact(left, right, left_dim, right_dim):
    left_high, left_low = left if isinstance(left, tuple) else halves(left)
    right_high, right_low = right if isinstance(right, tuple) else halves(right)
    return lax.dot_general(
        jnp.concatenate([left_high, left_high, left_low], left_dim),
        jnp.concatenate([right_high, right_low, right_high], right_dim),
        (((left_dim,), (right_dim,)), ((), ())),
        preferred_element_type=f32,
    )


def stacked(first, second):
    return tuple(jnp.concatenate([a, b], 0) for a, b in zip(first, second))


class Tile:
    def __init__(self, layout_ref, group):
        live_first, live_second, same, persist = (layout_ref[group, i] for i in range(4))
        shape = (GROUP_ROWS, HEAD_DIM)
        row = lax.broadcasted_iota(jnp.int32, shape, 0)
        col = lax.broadcasted_iota(jnp.int32, shape, 1)
        late = row >= BLOCK_ROWS
        self.row, self.col = row, col
        self.live = jnp.where(late, live_second, live_first)
        self.taps = [None] + [
            jnp.where(
                row < offset,
                0.0,
                jnp.where(late & (row < BLOCK_ROWS + offset), same, 1.0),
            )
            for offset in range(1, KERNEL)
        ]
        cross = jnp.where(late & (col < BLOCK_ROWS), persist, 1.0)
        self.lower = jnp.where(row > col, cross, 0.0)
        self.lower_full = jnp.where(row >= col, cross, 0.0)

    def earlier(self, values, offset):
        return pltpu.roll(values, offset, 0) * self.taps[offset]

    def later(self, values, offset):
        return pltpu.roll(values * self.taps[offset], GROUP_ROWS - offset, 0)


def convolve(tile, values, taps):
    total = values * taps[0]
    for offset in range(1, KERNEL):
        total = total + tile.earlier(values, offset) * taps[offset]
    return total


def unit_scale(values):
    return lax.rsqrt(jnp.sum(values * values, -1, keepdims=True) + 1e-06)


def head_columns(part_width, section, head):
    return pl.ds(section * part_width + head * HEAD_DIM, HEAD_DIM)


def unit_inverses(tile, lowers):
    eye = jnp.where(tile.row == tile.col, 1.0, 0.0)
    inverses = None
    size = 1
    while size < GROUP_ROWS:
        pair = tile.row // (2 * size) == tile.col // (2 * size)
        split = pair & (tile.row // size != tile.col // size)
        parts = [jnp.where(split, lower, 0.0) for lower in lowers]
        if inverses is None:
            inverses = [eye - part for part in parts]
        else:
            kept = [halves(inverse) for inverse in inverses]
            inner = [exact(part, known, 1, 0) for part, known in zip(parts, kept)]
            outer = [exact(known, value, 1, 0) for known, value in zip(kept, inner)]
            inverses = [inverse - value for inverse, value in zip(inverses, outer)]
        size *= 2
    return inverses


def mixer_forward_kernel(
    layout_ref, pre_ref, param_ref, mixed_ref, inverse_ref, score_ref, solved_ref, out_ref
):
    width = mixed_ref.shape[1]
    heads = range(width // HEAD_DIM)
    tile = Tile(layout_ref, pl.program_id(0))
    queries, keys, values, strengths = [], [], [], []
    for head in heads:
        parts = []
        for section in range(3):
            columns = head_columns(width, section, head)
            taps = [param_ref[offset : offset + 1, columns] for offset in range(KERNEL)]
            convolved = convolve(tile, pre_ref[:, columns], taps)
            parts.append(convolved * jax.nn.sigmoid(convolved))
        queries.append(parts[0] * (unit_scale(parts[0]) * HEAD_DIM**-0.5))
        keys.append(parts[1] * unit_scale(parts[1]))
        values.append(parts[2])
        start = 4 * width + head
        strengths.append(jax.nn.sigmoid(pre_ref[:, start : start + 1]) * tile.live)
    lowers, scores = [], []
    for head in heads:
        key_halves = halves(keys[head])
        both = exact(stacked(key_halves, halves(queries[head])), key_halves, 1, 1)
        lowers.append(both[:GROUP_ROWS] * strengths[head] * tile.lower)
        scores.append(both[GROUP_ROWS:] * tile.lower_full)
    inverses = unit_inverses(tile, lowers)
    solved = [exact(inverses[head], values[head] * strengths[head], 1, 0) for head in heads]
    outs = [exact(scores[head], solved[head], 1, 0) for head in heads]
    for head in heads:
        out = outs[head]
        scaled = out * lax.rsqrt(jnp.mean(out * out, -1, keepdims=True) + 1e-05)
        gate = pre_ref[:, head_columns(width, 3, head)]
        gain = param_ref[KERNEL : KERNEL + 1, head_columns(width, 0, head)]
        mixed = scaled * gain * (gate * jax.nn.sigmoid(gate)) * tile.live
        mixed_ref[:, head_columns(width, 0, head)] = mixed.astype(bf)
        inverse_ref[head] = inverses[head]
        score_ref[head] = scores[head]
        solved_ref[head] = solved[head]
        out_ref[head] = out


def mixer_backward_kernel(
    layout_ref,
    pre_ref,
    param_ref,
    grad_ref,
    inverse_ref,
    score_ref,
    solved_ref,
    out_ref,
    d_pre_ref,
    d_param_ref,
):
    width = grad_ref.shape[1]
    heads = range(width // HEAD_DIM)
    tile = Tile(layout_ref, pl.program_id(0))

    @pl.when(pl.program_id(0) == 0)
    def _():
        d_param_ref[...] = jnp.zeros_like(d_param_ref)

    def along(values):
        return jnp.sum(values, -1, keepdims=True)

    d_outs = []
    for head in heads:
        columns = head_columns(width, 0, head)
        d_mixed = grad_ref[:, columns] * tile.live
        out = out_ref[head]
        scale = lax.rsqrt(jnp.mean(out * out, -1, keepdims=True) + 1e-05)
        scaled = out * scale
        gate = pre_ref[:, head_columns(width, 3, head)]
        gate_open = jax.nn.sigmoid(gate)
        gain = param_ref[KERNEL : KERNEL + 1, columns]
        gated = d_mixed * (gate * gate_open)
        d_param_ref[KERNEL : KERNEL + 1, columns] += jnp.sum(gated * scaled, 0, keepdims=True)
        d_gate = d_mixed * scaled * gain * (gate_open * (1.0 + gate * (1.0 - gate_open)))
        d_pre_ref[:, head_columns(width, 3, head)] = d_gate.astype(bf)
        d_scaled = gated * gain
        mean = jnp.mean(d_scaled * out, -1, keepdims=True)
        d_outs.append(scale * d_scaled - out * (scale * scale * scale * mean))
    d_out_halves = [halves(value) for value in d_outs]
    solved_halves = [halves(solved_ref[head]) for head in heads]
    d_solved = [exact(score_ref[head], d_out_halves[head], 0, 0) for head in heads]
    d_scores = [
        exact(d_out_halves[head], solved_halves[head], 1, 1) * tile.lower_full for head in heads
    ]
    d_inner = [exact(inverse_ref[head], d_solved[head], 0, 0) for head in heads]
    d_lowers = [exact(d_inner[head], solved_halves[head], 1, 1) * -tile.lower for head in heads]
    d_beta = jnp.zeros((GROUP_ROWS, SMALL), f32)
    for head in heads:
        pres, convolved, opened, active = [], [], [], []
        for section in range(3):
            columns = head_columns(width, section, head)
            taps = [param_ref[offset : offset + 1, columns] for offset in range(KERNEL)]
            pres.append(pre_ref[:, columns])
            convolved.append(convolve(tile, pres[section], taps))
            opened.append(jax.nn.sigmoid(convolved[section]))
            active.append(convolved[section] * opened[section])
        query_scale = unit_scale(active[0])
        key_scale = unit_scale(active[1])
        query_unit = active[0] * query_scale
        key = active[1] * key_scale
        start = 4 * width + head
        opening = jax.nn.sigmoid(pre_ref[:, start : start + 1])
        strength = opening * tile.live
        d_both = stacked(halves(d_lowers[head]), halves(d_scores[head]))
        by_key = exact(d_both, key, 1, 0)
        d_query = by_key[GROUP_ROWS:] * HEAD_DIM**-0.5
        from_lower = by_key[:GROUP_ROWS]
        weighted = stacked(halves(key * strength), halves(query_unit * HEAD_DIM**-0.5))
        d_key = strength * from_lower + exact(d_both, weighted, 0, 0)
        d_strength = along(d_inner[head] * active[2] + from_lower * key)
        d_value = d_inner[head] * strength
        d_opening = d_strength * (opening * (1.0 - opening)) * tile.live
        d_beta = d_beta + jnp.where(tile.col == head, d_opening, 0.0)
        d_active = [
            (d_query - query_unit * along(query_unit * d_query)) * query_scale,
            (d_key - key * along(key * d_key)) * key_scale,
            d_value,
        ]
        for section in range(3):
            columns = head_columns(width, section, head)
            taps = [param_ref[offset : offset + 1, columns] for offset in range(KERNEL)]
            slope = opened[section] * (1.0 + convolved[section] * (1.0 - opened[section]))
            d_convolved = d_active[section] * slope
            d_pre = d_convolved * taps[0]
            sums = [jnp.sum(d_convolved * pres[section], 0, keepdims=True)]
            for offset in range(1, KERNEL):
                d_pre = d_pre + tile.later(d_convolved, offset) * taps[offset]
                sums.append(
                    jnp.sum(d_convolved * tile.earlier(pres[section], offset), 0, keepdims=True)
                )
            d_param_ref[0:KERNEL, columns] += jnp.concatenate(sums, 0)
            d_pre_ref[:, columns] = d_pre.astype(bf)
    d_pre_ref[:, 4 * width :] = d_beta.astype(bf)


def mixer_specs(width):
    wide = 4 * width + SMALL
    heads = width // HEAD_DIM
    layout = pl.BlockSpec(memory_space=pltpu.SMEM)
    pre = pl.BlockSpec((GROUP_ROWS, wide), lambda group: (group, 0))
    param = pl.BlockSpec((2 * KERNEL, 3 * width), lambda group: (0, 0))
    narrow = pl.BlockSpec((GROUP_ROWS, width), lambda group: (group, 0))
    square = pl.BlockSpec((heads, GROUP_ROWS, HEAD_DIM), lambda group: (group, 0, 0))
    return layout, pre, param, narrow, square


def mixer_call(kernel, groups, width, in_specs, out_specs, out_shape):
    return pl.pallas_call(
        kernel,
        grid=(groups,),
        in_specs=in_specs,
        out_specs=out_specs,
        out_shape=out_shape,
        compiler_params=pltpu.CompilerParams(
            dimension_semantics=("arbitrary",), vmem_limit_bytes=48 * 2**20
        ),
        cost_estimate=pl.CostEstimate(
            flops=groups * width * 2**26, bytes_accessed=2**23, transcendentals=2**21
        ),
    )


def mixer_forward(layout, pre, params, width):
    groups = layout.shape[0]
    layout_spec, pre_spec, param_spec, narrow, square = mixer_specs(width)
    squares = jax.ShapeDtypeStruct((groups * width // HEAD_DIM, GROUP_ROWS, HEAD_DIM), f32)
    return mixer_call(
        mixer_forward_kernel,
        groups,
        width,
        [layout_spec, pre_spec, param_spec],
        [narrow] + [square] * 4,
        [jax.ShapeDtypeStruct((groups * GROUP_ROWS, width), bf)] + [squares] * 4,
    )(layout, pre, params)


def mixer_backward(layout, pre, params, d_mixer, kept, width):
    groups = layout.shape[0]
    layout_spec, pre_spec, param_spec, narrow, square = mixer_specs(width)
    return mixer_call(
        mixer_backward_kernel,
        groups,
        width,
        [layout_spec, pre_spec, param_spec, narrow] + [square] * 4,
        [pre_spec, param_spec],
        [
            jax.ShapeDtypeStruct(pre.shape, bf),
            jax.ShapeDtypeStruct(params.shape, f32),
        ],
    )(layout, pre, params, d_mixer, *kept)


def tie_all(values, *others):
    anywhere = pl.BlockSpec(memory_space=pl.ANY)
    tied = pl.pallas_call(
        lambda *refs: None,
        in_specs=[anywhere] * (len(values) + len(others)),
        out_specs=[anywhere] * len(values),
        out_shape=[jax.ShapeDtypeStruct(value.shape, value.dtype) for value in values],
        input_output_aliases={i: i for i in range(len(values))},
        cost_estimate=pl.CostEstimate(flops=0, bytes_accessed=0, transcendentals=0),
    )(*values, *others)
    return list(tied)


def tie(value, *others):
    return tie_all([value], *others)[0]


def copy_columns(*refs):
    *sources, target = refs
    start = 0
    for source in sources:
        block = source[...].reshape(source.shape[-2:])
        columns = pl.ds(start, block.shape[1])
        if len(target.shape) == 3:
            target[0, :, columns] = block.astype(target.dtype)
        else:
            target[:, columns] = block.astype(target.dtype)
        start += block.shape[1]


def to_parts(sources, parts, dtype):
    rows = sources[0][0].shape[0]

    def spec(section, width):
        return pl.BlockSpec((rows, width), lambda p: (0, section * parts + p))

    total = sum(width for _, _, width in sources)
    return pl.pallas_call(
        copy_columns,
        grid=(parts,),
        in_specs=[spec(section, width) for _, section, width in sources],
        out_specs=pl.BlockSpec((1, rows, total), lambda p: (p, 0, 0)),
        out_shape=jax.ShapeDtypeStruct((parts, rows, total), dtype),
    )(*[array for array, _, _ in sources])


def updown_from_parts(slabs):
    parts, rows, width = slabs.shape
    units = width // 2

    def kernel(slabs_ref, out_ref):
        for p in range(parts):
            out_ref[:, p * units : (p + 1) * units] = slabs_ref[p].astype(f32)

    return pl.pallas_call(
        kernel,
        grid=(2,),
        in_specs=[pl.BlockSpec((parts, rows, units), lambda half: (0, 0, half))],
        out_specs=pl.BlockSpec((rows, parts * units), lambda half: (0, half)),
        out_shape=jax.ShapeDtypeStruct((rows, parts * width), f32),
        compiler_params=pltpu.CompilerParams(vmem_limit_bytes=32 * 2**20),
    )(slabs)


def mixer_from_parts(slabs, width):
    parts, rows, _ = slabs.shape

    def kernel(slabs_ref, qkv_ref, gate_ref, sum_ref, strength_ref):
        total = jnp.zeros(sum_ref.shape, f32)
        for p in range(parts):
            for section in range(4):
                block = slabs_ref[p, :, section * width : (section + 1) * width].astype(f32)
                if section < 3:
                    start = (section * parts + p) * width
                    qkv_ref[:, start : start + width] = block
                else:
                    gate_ref[:, p * width : (p + 1) * width] = block
            last = slabs_ref[p, :, 4 * width :].astype(f32)
            total = total + last
            strength_ref[:, p * SMALL : (p + 1) * SMALL] = last
        sum_ref[...] = total

    widths = [3 * parts * width, parts * width, SMALL, parts * SMALL]
    return pl.pallas_call(
        kernel,
        out_shape=[jax.ShapeDtypeStruct((rows, size), f32) for size in widths],
        compiler_params=pltpu.CompilerParams(vmem_limit_bytes=32 * 2**20),
    )(slabs)


def total_of(own_ref, received_refs):
    total = own_ref[...]
    for ref in received_refs:
        total = total + ref[...].astype(f32)
    return total


def row_scale(values):
    return lax.rsqrt(jnp.mean(values * values, -1, keepdims=True) + 1e-06)


def norm_slope(values, scale, gain, grad):
    mean = jnp.mean(gain * grad * values, -1, keepdims=True)
    return scale * gain * grad - values * (scale * scale * scale * mean)


def hidden_kernel(own_ref, *refs):
    *received, input_ref, gain_ref, hidden_ref, normed_ref = refs
    hidden = input_ref[...].astype(f32) + total_of(own_ref, received)
    hidden_ref[...] = hidden
    normed_ref[...] = (hidden * row_scale(hidden) * gain_ref[...]).astype(bf)


def hidden_back_kernel(own_ref, *refs):
    *received, hidden_ref, gain_ref, cot_ref, d_hidden_ref, d_mixed_ref, d_gain_ref = refs
    grad = total_of(own_ref, received)
    hidden = hidden_ref[...]
    scale = row_scale(hidden)

    @pl.when(pl.program_id(0) == 0)
    def _():
        d_gain_ref[...] = jnp.zeros_like(d_gain_ref)

    d_gain_ref[...] += jnp.sum(grad * hidden * scale, 0, keepdims=True)
    d_hidden = cot_ref[...].astype(f32) + norm_slope(hidden, scale, gain_ref[...], grad)
    d_hidden_ref[...] = d_hidden
    d_mixed_ref[...] = d_hidden.astype(bf)


def input_back_kernel(own_ref, *refs):
    *received, input_ref, gain_ref, d_hidden_ref, out_ref = refs
    grad = total_of(own_ref, received)
    values = input_ref[...].astype(f32)
    slope = norm_slope(values, row_scale(values), gain_ref[...], grad)
    out_ref[...] = (d_hidden_ref[...] + slope).astype(bf)


def block_out_kernel(own_ref, *refs):
    *received, hidden_ref, out_ref = refs
    out_ref[...] = (hidden_ref[...] + total_of(own_ref, received)).astype(bf)


def by_rows(kernel, arrays, outs, block=32):
    def spec(shape):
        if shape[0] == 1:
            return pl.BlockSpec(shape, lambda i: (0, 0))
        return pl.BlockSpec((block, shape[1]), lambda i: (i, 0))

    return pl.pallas_call(
        kernel,
        grid=(GROUP_ROWS // block,),
        in_specs=[spec(array.shape) for array in arrays],
        out_specs=[spec(shape) for shape, _ in outs],
        out_shape=[jax.ShapeDtypeStruct(shape, dtype) for shape, dtype in outs],
        compiler_params=pltpu.CompilerParams(dimension_semantics=("arbitrary",)),
    )(*arrays)


def body(
    block_in,
    out_grad,
    norm1_gain,
    conv_weight,
    head_gain,
    qkv_weight,
    beta_weight,
    gate_weight,
    out_weight,
    norm2_gain,
    updown_weight,
    down_weight,
    seq_blocks,
    lead_blocks,
):
    devices = lax.axis_size("dp")
    parts = MODEL
    copies = devices // parts
    part = lax.axis_index("dp") // copies
    copy = lax.axis_index("dp") % copies
    rows_own = qkv_weight.shape[0]
    width = D // parts
    units = FF // parts
    heads_part = HEADS // parts
    wide = 4 * width + SMALL
    model_groups = [[m * copies + t for m in range(parts)] for t in range(copies)]
    copy_groups = [[m * copies + t for t in range(copies)] for m in range(parts)]

    def exchange(values):
        return lax.all_to_all(
            values, "dp", split_axis=0, concat_axis=0, axis_index_groups=model_groups, tiled=True
        )

    def shift(values, step):
        pairs = [
            (m * copies + t, (m + step) % parts * copies + t)
            for m in range(parts)
            for t in range(copies)
        ]
        return lax.ppermute(values, "dp", pairs)

    def exchange_apart(values, *others):
        received = []
        for step in range(1, parts):
            piece = lax.dynamic_index_in_dim(values, (part + step) % parts, 0, keepdims=False)
            received.append(shift(piece, step))
        received = tie_all(received, *others)
        for step, piece in enumerate(received, 1):
            values = lax.dynamic_update_index_in_dim(values, piece, (part - step) % parts, 0)
        return values

    def gather_rows(values):
        return [values] + [shift(values, step) for step in range(1, parts)]

    def parcels(terms):
        return [
            terms[step * GROUP_ROWS :][:GROUP_ROWS].astype(bf) for step in range(1, parts)
        ]

    def scatter_rows(terms, sent):
        return [terms] + [shift(block, -step) for step, block in enumerate(sent, 1)]

    def gather_copies(values):
        return lax.all_gather(values, "dp", axis=0, axis_index_groups=copy_groups, tiled=True)

    def scatter_copies(values):
        return lax.psum_scatter(
            values.astype(bf),
            "dp",
            scatter_dimension=0,
            axis_index_groups=copy_groups,
            tiled=True,
        )

    def halve(values, bit, axis):
        pairs = [(i, i ^ (1 << bit)) for i in range(devices)]
        side = (copy >> bit) & 1
        own = lax.dynamic_index_in_dim(values, side, axis, keepdims=False)
        other = lax.dynamic_index_in_dim(values, 1 - side, axis, keepdims=False)
        return (own.astype(f32) + lax.ppermute(other, "dp", pairs).astype(f32)).astype(bf)

    by_halves = copies == 8

    def halve_cores(values):
        if not by_halves:
            return values
        rows, columns = values.shape
        return halve(values.reshape(2, 2, 2, rows // 8, columns), 0, 2)

    def halve_first(values):
        if not by_halves:
            return [values]
        middle = values.shape[-1] // 2
        return [halve(values[..., :middle], 1, 1), halve(values[..., middle:], 2, 0)]

    def halve_second(values):
        if not by_halves:
            return scatter_copies(values[0])
        return jnp.concatenate([halve(values[0], 2, 0), halve(values[1], 1, 0)], 1)

    def to_wire(values):
        return values.reshape(-1, parts, copies, rows_own).swapaxes(1, 2).reshape(-1, D)

    def from_wire(values):
        return values.reshape(-1, copies, parts, rows_own).swapaxes(1, 2).reshape(-1, D)

    strengths = beta_weight.reshape(rows_own, parts, heads_part)
    strengths = jnp.pad(strengths, ((0, 0), (0, 0), (0, SMALL - heads_part)))
    strengths = strengths.reshape(rows_own, parts * SMALL)
    pieces = [(qkv_weight, section, width) for section in range(3)]
    pieces = to_parts(pieces + [(gate_weight, 0, width), (strengths, 0, SMALL)], parts, bf)
    mixer_pieces = exchange(pieces)
    w_mixer = gather_copies(mixer_pieces.reshape(parts * rows_own, wide))
    w_out = gather_copies(to_wire(out_weight.astype(bf)))

    lanes = -(-3 * rows_own // 128) * 128
    numbers = jnp.concatenate([seq_blocks[0], lead_blocks]).astype(f32)
    small = [conv_weight.T, norm1_gain[None], head_gain[None], norm2_gain[None], numbers[None]]
    small = [jnp.pad(rows, ((0, 0), (0, lanes - rows.shape[1]))) for rows in small]
    small = jnp.pad(jnp.concatenate(small, 0).astype(bf), ((0, 2 * KERNEL), (0, 0)))
    small = jnp.broadcast_to(small[None], (devices,) + small.shape)
    small = lax.all_to_all(tie(small, mixer_pieces), "dp", 0, 0, tiled=True)
    taps = small[:, :KERNEL, : 3 * rows_own].swapaxes(0, 1).reshape(KERNEL, 3, parts, width)
    taps = lax.dynamic_index_in_dim(taps, part, 2, keepdims=False).reshape(KERNEL, 3 * width)
    gain_one, head_full, gain_two = (
        small[:, KERNEL + i, :rows_own].reshape(1, D).astype(f32) for i in range(3)
    )
    gain_one, gain_two = to_wire(gain_one), to_wire(gain_two)
    head_part = lax.dynamic_slice_in_dim(head_full, part * width, width, 1)
    params = jnp.concatenate([taps.astype(f32), jnp.pad(head_part, ((0, 0), (0, 2 * width)))], 0)
    params = jnp.pad(params, ((0, KERNEL - 1), (0, 0)))
    numbers = small[:, KERNEL + 3, :3].astype(f32).astype(jnp.int32)
    layouts = block_layouts(numbers[:, 0], numbers[:, 1], numbers[:, 2])
    layouts = layouts.reshape(parts, copies, 4)
    layouts = lax.dynamic_index_in_dim(layouts, copy, 1, keepdims=False)
    wanted = (part - jnp.arange(parts)) % parts
    wanted = (wanted[:, None] == jnp.arange(parts)).astype(f32)
    layouts = jnp.sum(wanted[:, :, None] * layouts, 1)

    inputs = to_wire(block_in)
    input_rows = gather_rows(tie(inputs, mixer_pieces))

    pieces = to_parts([(updown_weight, half, units) for half in range(2)], parts, bf)
    updown_pieces = tie(pieces, small, *input_rows[1:])
    w_down = gather_copies(to_wire(down_weight.astype(bf)))
    cotangent_own = to_wire(out_grad)

    input_rows = jnp.concatenate(input_rows, 0).astype(f32)
    input_scale = row_scale(input_rows)
    normed = (input_rows * input_scale * gain_one).astype(bf)
    pre = plain_product(normed, w_mixer)
    mixed, *kept = mixer_forward(layouts, pre, params, width)
    updown_pieces = exchange_apart(updown_pieces, mixed)
    w_updown = gather_copies(updown_pieces.reshape(parts * rows_own, 2 * units))
    cotangent = gather_rows(tie(cotangent_own, updown_pieces))
    stream = ((GROUP_ROWS, D), f32)
    narrow = ((GROUP_ROWS, D), bf)
    out_terms = plain_product(mixed, w_out)
    hidden, normed_two = by_rows(
        hidden_kernel,
        scatter_rows(out_terms, parcels(out_terms)) + [inputs, tie(gain_two, *cotangent[1:])],
        [stream, narrow],
    )
    normed_two = jnp.concatenate(gather_rows(normed_two), 0)
    cotangent = jnp.concatenate(cotangent, 0)

    def swiglu_units(updown):
        return jax.nn.silu(updown[:, :units]) * updown[:, units:]

    updown = plain_product(normed_two, w_updown)
    active, swiglu_back = jax.vjp(swiglu_units, updown)
    active = active.astype(bf)
    d_active = transposed_product(cotangent, w_down)
    d_updown = swiglu_back(d_active)[0].astype(bf)
    d_normed_two = transposed_product(d_updown, w_updown)
    sent = parcels(d_normed_two)
    d_normed_two = scatter_rows(d_normed_two, sent)
    updown_terms = rows_product(normed_two, tie(d_updown, *sent)).astype(bf)
    active = tie(active, *sent)
    down_terms = rows_product(active, cotangent).astype(bf)
    out_terms = plain_product(active, w_down)
    out_sent = parcels(out_terms)
    updown_grad = scatter_copies(updown_terms)
    down_grad = halve_cores(down_terms)

    gain_two_late = tie(gain_two, updown_terms, down_terms, *out_sent)
    d_hidden, d_mixed, gain_two_grad = by_rows(
        hidden_back_kernel,
        d_normed_two + [hidden, gain_two_late, cotangent_own],
        [stream, narrow, ((1, D), f32)],
    )
    d_mixed = gather_rows(d_mixed)
    down_grad = halve_first(down_grad)
    d_mixed = jnp.concatenate(d_mixed[:1] + tie_all(d_mixed[1:], *down_grad), 0)
    d_mixer = transposed_product(d_mixed, w_out)
    block_out = scatter_rows(out_terms, [tie(block, d_mixed) for block in out_sent])
    d_pre, d_params = mixer_backward(layouts, pre, params, d_mixer, kept, width)
    down_grad = halve_second(down_grad)
    out_grad_terms = rows_product(mixed, d_mixed).astype(bf)

    mixer_terms = rows_product(normed, d_pre)
    d_normed_terms = transposed_product(d_pre, w_mixer)
    gain_one_grad = jnp.sum(d_normed_terms * (input_rows * input_scale), 0, keepdims=True)
    here = (jnp.arange(parts) == part).astype(f32)[:, None]
    taps_grad = d_params[:KERNEL].reshape(KERNEL, 3, 1, width) * here
    taps_grad = taps_grad.reshape(KERNEL, parts, copies, 3, rows_own).transpose(3, 0, 2, 1, 4)
    head_grad = to_wire((d_params[KERNEL, :width] * here).reshape(1, D))
    columns = [taps_grad.reshape(3 * KERNEL, D), head_grad, gain_two_grad, gain_one_grad]
    columns = jnp.concatenate(columns, 0)
    columns = rows_product(columns, jnp.eye(columns.shape[0], dtype=f32))
    first = 4 * width + heads_part
    columns = jnp.pad(columns, ((0, 0), (first, wide - first - columns.shape[1])))
    mixer_grad = scatter_copies(tie((mixer_terms + columns).astype(bf), updown_grad))
    out_shard = halve_second(halve_first(halve_cores(out_grad_terms)))
    out_shard = from_wire(out_shard.astype(f32))
    down_shard = from_wire(down_grad.astype(f32))
    updown_grad = exchange_apart(updown_grad.reshape(parts, rows_own, 2 * units))
    updown_shard = updown_from_parts(updown_grad)
    mixer_grad = exchange(tie(mixer_grad, updown_grad).reshape(parts, rows_own, wide))
    qkv_shard, gate_shard, sums, strengths = mixer_from_parts(mixer_grad, width)
    beta_shard = strengths.reshape(rows_own, parts, SMALL)[:, :, :heads_part]
    sums = sums[:, heads_part:]
    taps_width = 3 * KERNEL
    taps_shard = sums[:, :taps_width].reshape(rows_own, 3, KERNEL).swapaxes(0, 1)

    sent = tie_all(parcels(d_normed_terms), down_grad, *block_out[1:])
    d_normed = scatter_rows(d_normed_terms, sent)
    (input_grad,) = by_rows(input_back_kernel, d_normed + [inputs, gain_one, d_hidden], [narrow])
    (block_out,) = by_rows(block_out_kernel, block_out + [hidden], [narrow])
    return (
        from_wire(block_out),
        from_wire(input_grad),
        sums[:, taps_width + 2],
        taps_shard.reshape(-1, KERNEL),
        sums[:, taps_width],
        qkv_shard,
        beta_shard.reshape(rows_own, HEADS),
        gate_shard,
        out_shard,
        sums[:, taps_width + 1],
        updown_shard,
        down_shard,
    )


def solution(mesh):
    placed = (
        P("dp", None),
        P("dp", None),
        P("dp"),
        P("dp", None),
        P("dp"),
        P("dp", None),
        P("dp", None),
        P("dp", None),
        P("dp", None),
        P("dp"),
        P("dp", None),
        P("dp", None),
        P("dp", None),
        P("dp"),
    )
    return jax.shard_map(
        body,
        mesh=mesh,
        in_specs=placed,
        out_specs=(
            P("dp", None),
            P("dp", None),
            P("dp"),
            P("dp", None),
            P("dp"),
            P("dp", None),
            P("dp", None),
            P("dp", None),
            P("dp", None),
            P("dp"),
            P("dp", None),
            P("dp", None),
        ),
        check_vma=False,
    )
```

```python
import functools

import jax
import jax.numpy as jnp
from jax import lax
from jax.experimental import pallas as pl
from jax.experimental.pallas import tpu as pltpu
from jax.sharding import PartitionSpec as P

D = 2048
HEADS = 16
HEAD_DIM = 128
FF = 5632
KERNEL = 4
BLOCK_ROWS = 64
BLOCKS_DEV = 2
GROUP_ROWS = BLOCK_ROWS * BLOCKS_DEV
SMALL = 128
MODEL = 4

f32 = jnp.float32
bf = jnp.bfloat16


def block_layouts(first, second, lead):
    def doc(block):
        in_first = (block >= lead) & (block < lead + first)
        in_second = (block >= lead + first) & (block < lead + first + second)
        return jnp.where(in_first, 1, jnp.where(in_second, 2, 0))

    starts = (lead == 1) | (lead + first == 1) & (second > 0)
    columns = [doc(0) > 0, doc(1) > 0, doc(0) == doc(1), ~starts]
    return jnp.stack(columns, 1).astype(f32)


def plain_product(left, right):
    return jnp.dot(left, right, preferred_element_type=f32)


def rows_product(left, right):
    return lax.dot_general(left, right, (((0,), (0,)), ((), ())), preferred_element_type=f32)


def transposed_product(left, right):
    return lax.dot_general(left, right, (((1,), (1,)), ((), ())), preferred_element_type=f32)


def halves(values):
    high = values.astype(bf)
    return high, (values - high.astype(f32)).astype(bf)


def exact(left, right, left_dim, right_dim):
    left_high, left_low = left if isinstance(left, tuple) else halves(left)
    right_high, right_low = right if isinstance(right, tuple) else halves(right)
    return lax.dot_general(
        jnp.concatenate([left_high, left_high, left_low], left_dim),
        jnp.concatenate([right_high, right_low, right_high], right_dim),
        (((left_dim,), (right_dim,)), ((), ())),
        preferred_element_type=f32,
    )


def stacked(first, second):
    return tuple(jnp.concatenate([a, b], 0) for a, b in zip(first, second))


class Tile:
    def __init__(self, layout_ref, group):
        live_first, live_second, same, persist = (layout_ref[group, i] for i in range(4))
        shape = (GROUP_ROWS, HEAD_DIM)
        row = lax.broadcasted_iota(jnp.int32, shape, 0)
        col = lax.broadcasted_iota(jnp.int32, shape, 1)
        late = row >= BLOCK_ROWS
        self.row, self.col = row, col
        self.live = jnp.where(late, live_second, live_first)
        self.taps = [None] + [
            jnp.where(
                row < offset,
                0.0,
                jnp.where(late & (row < BLOCK_ROWS + offset), same, 1.0),
            )
            for offset in range(1, KERNEL)
        ]
        cross = jnp.where(late & (col < BLOCK_ROWS), persist, 1.0)
        self.lower = jnp.where(row > col, cross, 0.0)
        self.lower_full = jnp.where(row >= col, cross, 0.0)

    def earlier(self, values, offset):
        return pltpu.roll(values, offset, 0) * self.taps[offset]

    def later(self, values, offset):
        return pltpu.roll(values * self.taps[offset], GROUP_ROWS - offset, 0)


def convolve(tile, values, taps):
    total = values * taps[0]
    for offset in range(1, KERNEL):
        total = total + tile.earlier(values, offset) * taps[offset]
    return total


def unit_scale(values):
    return lax.rsqrt(jnp.sum(values * values, -1, keepdims=True) + 1e-06)


def head_columns(part_width, section, head):
    return pl.ds(section * part_width + head * HEAD_DIM, HEAD_DIM)


def unit_inverses(tile, lowers):
    eye = jnp.where(tile.row == tile.col, 1.0, 0.0)
    inverses = None
    size = 1
    while size < GROUP_ROWS:
        pair = tile.row // (2 * size) == tile.col // (2 * size)
        split = pair & (tile.row // size != tile.col // size)
        parts = [jnp.where(split, lower, 0.0) for lower in lowers]
        if inverses is None:
            inverses = [eye - part for part in parts]
        else:
            kept = [halves(inverse) for inverse in inverses]
            inner = [exact(part, known, 1, 0) for part, known in zip(parts, kept)]
            outer = [exact(known, value, 1, 0) for known, value in zip(kept, inner)]
            inverses = [inverse - value for inverse, value in zip(inverses, outer)]
        size *= 2
    return inverses


def mixer_forward_kernel(
    group, layout_ref, pre_ref, param_ref, mixed_ref, inverse_ref, score_ref, solved_ref, out_ref
):
    width = mixed_ref.shape[1]
    heads = range(width // HEAD_DIM)
    tile = Tile(layout_ref, group)
    queries, keys, values, strengths = [], [], [], []
    for head in heads:
        parts = []
        for section in range(3):
            columns = head_columns(width, section, head)
            taps = [param_ref[offset : offset + 1, columns] for offset in range(KERNEL)]
            convolved = convolve(tile, pre_ref[:, columns], taps)
            parts.append(convolved * jax.nn.sigmoid(convolved))
        queries.append(parts[0] * (unit_scale(parts[0]) * HEAD_DIM**-0.5))
        keys.append(parts[1] * unit_scale(parts[1]))
        values.append(parts[2])
        start = 4 * width + head
        strengths.append(jax.nn.sigmoid(pre_ref[:, start : start + 1]) * tile.live)
    lowers, scores = [], []
    for head in heads:
        key_halves = halves(keys[head])
        both = exact(stacked(key_halves, halves(queries[head])), key_halves, 1, 1)
        lowers.append(both[:GROUP_ROWS] * strengths[head] * tile.lower)
        scores.append(both[GROUP_ROWS:] * tile.lower_full)
    inverses = unit_inverses(tile, lowers)
    solved = [exact(inverses[head], values[head] * strengths[head], 1, 0) for head in heads]
    outs = [exact(scores[head], solved[head], 1, 0) for head in heads]
    for head in heads:
        out = outs[head]
        scaled = out * lax.rsqrt(jnp.mean(out * out, -1, keepdims=True) + 1e-05)
        gate = pre_ref[:, head_columns(width, 3, head)]
        gain = param_ref[KERNEL : KERNEL + 1, head_columns(width, 0, head)]
        mixed = scaled * gain * (gate * jax.nn.sigmoid(gate)) * tile.live
        mixed_ref[:, head_columns(width, 0, head)] = mixed.astype(bf)
        inverse_ref[head] = inverses[head]
        score_ref[head] = scores[head]
        solved_ref[head] = solved[head]
        out_ref[head] = out


def mixer_backward_kernel(
    group,
    layout_ref,
    pre_ref,
    param_ref,
    grad_ref,
    inverse_ref,
    score_ref,
    solved_ref,
    out_ref,
    d_pre_ref,
    d_param_ref,
):
    width = grad_ref.shape[1]
    heads = range(width // HEAD_DIM)
    tile = Tile(layout_ref, group)

    d_param_ref[...] = jnp.zeros_like(d_param_ref)

    def along(values):
        return jnp.sum(values, -1, keepdims=True)

    d_outs = []
    for head in heads:
        columns = head_columns(width, 0, head)
        d_mixed = grad_ref[:, columns] * tile.live
        out = out_ref[head]
        scale = lax.rsqrt(jnp.mean(out * out, -1, keepdims=True) + 1e-05)
        scaled = out * scale
        gate = pre_ref[:, head_columns(width, 3, head)]
        gate_open = jax.nn.sigmoid(gate)
        gain = param_ref[KERNEL : KERNEL + 1, columns]
        gated = d_mixed * (gate * gate_open)
        d_param_ref[KERNEL : KERNEL + 1, columns] += jnp.sum(gated * scaled, 0, keepdims=True)
        d_gate = d_mixed * scaled * gain * (gate_open * (1.0 + gate * (1.0 - gate_open)))
        d_pre_ref[:, head_columns(width, 3, head)] = d_gate.astype(bf)
        d_scaled = gated * gain
        mean = jnp.mean(d_scaled * out, -1, keepdims=True)
        d_outs.append(scale * d_scaled - out * (scale * scale * scale * mean))
    d_out_halves = [halves(value) for value in d_outs]
    solved_halves = [halves(solved_ref[head]) for head in heads]
    d_solved = [exact(score_ref[head], d_out_halves[head], 0, 0) for head in heads]
    d_scores = [
        exact(d_out_halves[head], solved_halves[head], 1, 1) * tile.lower_full for head in heads
    ]
    d_inner = [exact(inverse_ref[head], d_solved[head], 0, 0) for head in heads]
    d_lowers = [exact(d_inner[head], solved_halves[head], 1, 1) * -tile.lower for head in heads]
    d_beta = jnp.zeros((GROUP_ROWS, SMALL), f32)
    for head in heads:
        pres, convolved, opened, active = [], [], [], []
        for section in range(3):
            columns = head_columns(width, section, head)
            taps = [param_ref[offset : offset + 1, columns] for offset in range(KERNEL)]
            pres.append(pre_ref[:, columns])
            convolved.append(convolve(tile, pres[section], taps))
            opened.append(jax.nn.sigmoid(convolved[section]))
            active.append(convolved[section] * opened[section])
        query_scale = unit_scale(active[0])
        key_scale = unit_scale(active[1])
        query_unit = active[0] * query_scale
        key = active[1] * key_scale
        start = 4 * width + head
        opening = jax.nn.sigmoid(pre_ref[:, start : start + 1])
        strength = opening * tile.live
        d_both = stacked(halves(d_lowers[head]), halves(d_scores[head]))
        by_key = exact(d_both, key, 1, 0)
        d_query = by_key[GROUP_ROWS:] * HEAD_DIM**-0.5
        from_lower = by_key[:GROUP_ROWS]
        weighted = stacked(halves(key * strength), halves(query_unit * HEAD_DIM**-0.5))
        d_key = strength * from_lower + exact(d_both, weighted, 0, 0)
        d_strength = along(d_inner[head] * active[2] + from_lower * key)
        d_value = d_inner[head] * strength
        d_opening = d_strength * (opening * (1.0 - opening)) * tile.live
        d_beta = d_beta + jnp.where(tile.col == head, d_opening, 0.0)
        d_active = [
            (d_query - query_unit * along(query_unit * d_query)) * query_scale,
            (d_key - key * along(key * d_key)) * key_scale,
            d_value,
        ]
        for section in range(3):
            columns = head_columns(width, section, head)
            taps = [param_ref[offset : offset + 1, columns] for offset in range(KERNEL)]
            slope = opened[section] * (1.0 + convolved[section] * (1.0 - opened[section]))
            d_convolved = d_active[section] * slope
            d_pre = d_convolved * taps[0]
            sums = [jnp.sum(d_convolved * pres[section], 0, keepdims=True)]
            for offset in range(1, KERNEL):
                d_pre = d_pre + tile.later(d_convolved, offset) * taps[offset]
                sums.append(
                    jnp.sum(d_convolved * tile.earlier(pres[section], offset), 0, keepdims=True)
                )
            d_param_ref[0:KERNEL, columns] += jnp.concatenate(sums, 0)
            d_pre_ref[:, columns] = d_pre.astype(bf)
    d_pre_ref[:, 4 * width :] = d_beta.astype(bf)


def mixer_call(kernel, group, operands, shapes):
    vmem = pl.BlockSpec(memory_space=pltpu.VMEM)
    return pl.pallas_call(
        functools.partial(kernel, group),
        in_specs=[pl.BlockSpec(memory_space=pltpu.SMEM)] + [vmem] * (len(operands) - 1),
        out_specs=[vmem] * len(shapes),
        out_shape=shapes,
        compiler_params=pltpu.CompilerParams(vmem_limit_bytes=32 * 2**20),
        cost_estimate=pl.CostEstimate(flops=2**32, bytes_accessed=2**21, transcendentals=2**19),
    )(*operands)


def mixer_forward(group, layout, pre, params, width):
    square = jax.ShapeDtypeStruct((width // HEAD_DIM, GROUP_ROWS, HEAD_DIM), f32)
    shapes = [jax.ShapeDtypeStruct((GROUP_ROWS, width), bf)] + [square] * 4
    return mixer_call(mixer_forward_kernel, group, [layout, pre, params], shapes)


def mixer_backward(group, layout, pre, params, d_mixer, kept, width):
    shapes = [jax.ShapeDtypeStruct(pre.shape, bf), jax.ShapeDtypeStruct(params.shape, f32)]
    operands = [layout, pre, params, d_mixer, *kept]
    return mixer_call(mixer_backward_kernel, group, operands, shapes)


def tie_all(values, *others):
    anywhere = pl.BlockSpec(memory_space=pl.ANY)
    tied = pl.pallas_call(
        lambda *refs: None,
        in_specs=[anywhere] * (len(values) + len(others)),
        out_specs=[anywhere] * len(values),
        out_shape=[jax.ShapeDtypeStruct(value.shape, value.dtype) for value in values],
        input_output_aliases={i: i for i in range(len(values))},
        cost_estimate=pl.CostEstimate(flops=0, bytes_accessed=0, transcendentals=0),
    )(*values, *others)
    return list(tied)


def tie(value, *others):
    return tie_all([value], *others)[0]


def assemble(part, values, received, others):
    parts = values.shape[0]

    def kernel(part_ref, values_ref, *refs):
        own = part_ref[0]
        out_ref = refs[-1]
        out_ref[own] = values_ref[own]
        for step in range(1, parts):
            out_ref[lax.rem(own + parts - step, parts)] = refs[step - 1][...]

    vmem = pl.BlockSpec(memory_space=pltpu.VMEM)
    anywhere = pl.BlockSpec(memory_space=pl.ANY)
    return pl.pallas_call(
        kernel,
        in_specs=[pl.BlockSpec(memory_space=pltpu.SMEM)]
        + [vmem] * parts
        + [anywhere] * len(others),
        out_specs=vmem,
        out_shape=jax.ShapeDtypeStruct(values.shape, values.dtype),
        compiler_params=pltpu.CompilerParams(vmem_limit_bytes=32 * 2**20),
    )(part.reshape(1).astype(jnp.int32), values, *received, *others)


def copy_columns(*refs):
    *sources, target = refs
    start = 0
    for source in sources:
        block = source[...].reshape(source.shape[-2:])
        columns = pl.ds(start, block.shape[1])
        if len(target.shape) == 3:
            target[0, :, columns] = block.astype(target.dtype)
        else:
            target[:, columns] = block.astype(target.dtype)
        start += block.shape[1]


def to_parts(sources, parts, dtype):
    rows = sources[0][0].shape[0]

    def spec(section, width):
        return pl.BlockSpec((rows, width), lambda p: (0, section * parts + p))

    total = sum(width for _, _, width in sources)
    return pl.pallas_call(
        copy_columns,
        grid=(parts,),
        in_specs=[spec(section, width) for _, section, width in sources],
        out_specs=pl.BlockSpec((1, rows, total), lambda p: (p, 0, 0)),
        out_shape=jax.ShapeDtypeStruct((parts, rows, total), dtype),
    )(*[array for array, _, _ in sources])


def updown_from_parts(slabs):
    parts, rows, width = slabs.shape
    units = width // 2

    def kernel(slabs_ref, out_ref):
        for p in range(parts):
            out_ref[:, p * units : (p + 1) * units] = slabs_ref[p].astype(f32)

    return pl.pallas_call(
        kernel,
        grid=(2,),
        in_specs=[pl.BlockSpec((parts, rows, units), lambda half: (0, 0, half))],
        out_specs=pl.BlockSpec((rows, parts * units), lambda half: (0, half)),
        out_shape=jax.ShapeDtypeStruct((rows, parts * width), f32),
        compiler_params=pltpu.CompilerParams(vmem_limit_bytes=32 * 2**20),
    )(slabs)


def mixer_from_parts(slabs, width):
    parts, rows, _ = slabs.shape

    def kernel(slabs_ref, qkv_ref, gate_ref, sum_ref, strength_ref):
        total = jnp.zeros(sum_ref.shape, f32)
        for p in range(parts):
            for section in range(4):
                block = slabs_ref[p, :, section * width : (section + 1) * width].astype(f32)
                if section < 3:
                    start = (section * parts + p) * width
                    qkv_ref[:, start : start + width] = block
                else:
                    gate_ref[:, p * width : (p + 1) * width] = block
            last = slabs_ref[p, :, 4 * width :].astype(f32)
            total = total + last
            strength_ref[:, p * SMALL : (p + 1) * SMALL] = last
        sum_ref[...] = total

    widths = [3 * parts * width, parts * width, SMALL, parts * SMALL]
    return pl.pallas_call(
        kernel,
        out_shape=[jax.ShapeDtypeStruct((rows, size), f32) for size in widths],
        compiler_params=pltpu.CompilerParams(vmem_limit_bytes=32 * 2**20),
    )(slabs)


def total_of(own_ref, received_refs):
    total = own_ref[...]
    for ref in received_refs:
        total = total + ref[...].astype(f32)
    return total


def row_scale(values):
    return lax.rsqrt(jnp.mean(values * values, -1, keepdims=True) + 1e-06)


def norm_slope(values, scale, gain, grad):
    mean = jnp.mean(gain * grad * values, -1, keepdims=True)
    return scale * gain * grad - values * (scale * scale * scale * mean)


def norm_kernel(values_ref, gain_ref, normed_ref):
    values = values_ref[...].astype(f32)
    normed_ref[...] = (values * row_scale(values) * gain_ref[...]).astype(bf)


def hidden_kernel(own_ref, *refs):
    *received, input_ref, gain_ref, hidden_ref, normed_ref = refs
    hidden = input_ref[...].astype(f32) + total_of(own_ref, received)
    hidden_ref[...] = hidden
    normed_ref[...] = (hidden * row_scale(hidden) * gain_ref[...]).astype(bf)


def hidden_back_kernel(own_ref, *refs):
    *received, hidden_ref, gain_ref, cot_ref, d_hidden_ref, d_mixed_ref, d_gain_ref = refs
    grad = total_of(own_ref, received)
    hidden = hidden_ref[...]
    scale = row_scale(hidden)

    @pl.when(pl.program_id(0) == 0)
    def _():
        d_gain_ref[...] = jnp.zeros_like(d_gain_ref)

    d_gain_ref[...] += jnp.sum(grad * hidden * scale, 0, keepdims=True)
    d_hidden = cot_ref[...].astype(f32) + norm_slope(hidden, scale, gain_ref[...], grad)
    d_hidden_ref[...] = d_hidden
    d_mixed_ref[...] = d_hidden.astype(bf)


def input_back_kernel(own_ref, *refs):
    *received, input_ref, gain_ref, d_hidden_ref, out_ref = refs
    grad = total_of(own_ref, received)
    values = input_ref[...].astype(f32)
    slope = norm_slope(values, row_scale(values), gain_ref[...], grad)
    out_ref[...] = (d_hidden_ref[...] + slope).astype(bf)


def block_out_kernel(own_ref, *refs):
    *received, hidden_ref, out_ref = refs
    out_ref[...] = (hidden_ref[...] + total_of(own_ref, received)).astype(bf)


def by_rows(kernel, arrays, outs, block=32):
    def spec(shape):
        if shape[0] == 1:
            return pl.BlockSpec(shape, lambda i: (0, 0))
        return pl.BlockSpec((block, shape[1]), lambda i: (i, 0))

    return pl.pallas_call(
        kernel,
        grid=(GROUP_ROWS // block,),
        in_specs=[spec(array.shape) for array in arrays],
        out_specs=[spec(shape) for shape, _ in outs],
        out_shape=[jax.ShapeDtypeStruct(shape, dtype) for shape, dtype in outs],
        compiler_params=pltpu.CompilerParams(dimension_semantics=("arbitrary",)),
    )(*arrays)


def body(
    block_in,
    out_grad,
    norm1_gain,
    conv_weight,
    head_gain,
    qkv_weight,
    beta_weight,
    gate_weight,
    out_weight,
    norm2_gain,
    updown_weight,
    down_weight,
    seq_blocks,
    lead_blocks,
):
    devices = lax.axis_size("dp")
    parts = MODEL
    copies = devices // parts
    part = lax.axis_index("dp") // copies
    copy = lax.axis_index("dp") % copies
    rows_own = qkv_weight.shape[0]
    width = D // parts
    units = FF // parts
    heads_part = HEADS // parts
    wide = 4 * width + SMALL
    model_groups = [[m * copies + t for m in range(parts)] for t in range(copies)]
    copy_groups = [[m * copies + t for t in range(copies)] for m in range(parts)]

    def exchange(values):
        return lax.all_to_all(
            values, "dp", split_axis=0, concat_axis=0, axis_index_groups=model_groups, tiled=True
        )

    def shift(values, step):
        pairs = [
            (m * copies + t, (m + step) % parts * copies + t)
            for m in range(parts)
            for t in range(copies)
        ]
        return lax.ppermute(values, "dp", pairs)

    def exchange_apart(values, *others):
        received = []
        for step in range(1, parts):
            piece = lax.dynamic_index_in_dim(values, (part + step) % parts, 0, keepdims=False)
            received.append(shift(piece, step))
        return assemble(part, values, received, others)

    def gather_rows(values):
        return [values] + [shift(values, step) for step in range(1, parts)]

    def send(terms, step):
        return shift(terms.astype(bf), -step)

    def gather_copies(values):
        return lax.all_gather(values, "dp", axis=0, axis_index_groups=copy_groups, tiled=True)

    def scatter_copies(values):
        return lax.psum_scatter(
            values.astype(bf),
            "dp",
            scatter_dimension=0,
            axis_index_groups=copy_groups,
            tiled=True,
        )

    def halve(values, bit, axis):
        pairs = [(i, i ^ (1 << bit)) for i in range(devices)]
        side = (copy >> bit) & 1
        own = lax.dynamic_index_in_dim(values, side, axis, keepdims=False)
        other = lax.dynamic_index_in_dim(values, 1 - side, axis, keepdims=False)
        return (own.astype(f32) + lax.ppermute(other, "dp", pairs).astype(f32)).astype(bf)

    by_halves = copies == 8

    def halve_cores(values):
        if not by_halves:
            return values
        rows, columns = values.shape
        return halve(values.reshape(2, 2, 2, rows // 8, columns), 0, 2)

    def halve_first(values):
        if not by_halves:
            return [values]
        middle = values.shape[-1] // 2
        return [halve(values[..., :middle], 1, 1), halve(values[..., middle:], 2, 0)]

    def halve_second(values):
        if not by_halves:
            return scatter_copies(values[0])
        return jnp.concatenate([halve(values[0], 2, 0), halve(values[1], 1, 0)], 1)

    def to_wire(values):
        return values.reshape(-1, parts, copies, rows_own).swapaxes(1, 2).reshape(-1, D)

    def from_wire(values):
        return values.reshape(-1, copies, parts, rows_own).swapaxes(1, 2).reshape(-1, D)

    w_out_own = to_wire(out_weight.astype(bf))
    w_out = gather_copies(w_out_own)
    strengths = beta_weight.reshape(rows_own, parts, heads_part)
    strengths = jnp.pad(strengths, ((0, 0), (0, 0), (0, SMALL - heads_part)))
    strengths = tie(strengths.reshape(rows_own, parts * SMALL), w_out_own)
    pieces = [(qkv_weight, section, width) for section in range(3)]
    pieces = to_parts(pieces + [(gate_weight, 0, width), (strengths, 0, SMALL)], parts, bf)
    mixer_pieces = tie(exchange(pieces), w_out)
    w_mixer = gather_copies(mixer_pieces.reshape(parts * rows_own, wide))
    inputs = tie(to_wire(block_in), mixer_pieces)
    input_rows = gather_rows(inputs)

    lanes = -(-3 * rows_own // 128) * 128
    numbers = jnp.concatenate([seq_blocks[0], lead_blocks]).astype(f32)
    small = [conv_weight.T, norm1_gain[None], head_gain[None], norm2_gain[None], numbers[None]]
    small = [jnp.pad(rows, ((0, 0), (0, lanes - rows.shape[1]))) for rows in small]
    small = jnp.pad(jnp.concatenate(small, 0).astype(bf), ((0, 2 * KERNEL), (0, 0)))
    small = jnp.broadcast_to(small[None], (devices,) + small.shape)
    small = lax.all_to_all(tie(small, inputs), "dp", 0, 0, tiled=True)
    taps = small[:, :KERNEL, : 3 * rows_own].swapaxes(0, 1).reshape(KERNEL, 3, parts, width)
    taps = lax.dynamic_index_in_dim(taps, part, 2, keepdims=False).reshape(KERNEL, 3 * width)
    gain_one, head_full, gain_two = (
        small[:, KERNEL + i, :rows_own].reshape(1, D).astype(f32) for i in range(3)
    )
    gain_one, gain_two = to_wire(gain_one), to_wire(gain_two)
    head_part = lax.dynamic_slice_in_dim(head_full, part * width, width, 1)
    params = jnp.concatenate([taps.astype(f32), jnp.pad(head_part, ((0, 0), (0, 2 * width)))], 0)
    params = jnp.pad(params, ((0, KERNEL - 1), (0, 0)))
    numbers = small[:, KERNEL + 3, :3].astype(f32).astype(jnp.int32)
    layouts = block_layouts(numbers[:, 0], numbers[:, 1], numbers[:, 2])
    layouts = layouts.reshape(parts, copies, 4)
    layouts = lax.dynamic_index_in_dim(layouts, copy, 1, keepdims=False)
    wanted = (part - jnp.arange(parts)) % parts
    wanted = (wanted[:, None] == jnp.arange(parts)).astype(f32)
    layouts = jnp.sum(wanted[:, :, None] * layouts, 1)

    pieces = to_parts([(updown_weight, half, units) for half in range(2)], parts, bf)
    updown_pieces = tie(pieces, small, *input_rows[1:])
    w_down_own = to_wire(down_weight.astype(bf))
    w_down = gather_copies(tie(w_down_own, *input_rows[1:]))
    cotangent_own = to_wire(out_grad)

    gain_first = tie(gain_one, w_down_own, cotangent_own)
    sums, normed, pre, mixed, kept = ([None] * parts for _ in range(5))
    order = list(range(1, parts)) + [0]
    ahead = gain_first
    for group in order:
        (normed[group],) = by_rows(norm_kernel, [input_rows[group], ahead], [((GROUP_ROWS, D), bf)])
        pre[group] = plain_product(normed[group], w_mixer)
        mixed[group], *kept[group] = mixer_forward(group, layouts, pre[group], params, width)
        sums[group] = plain_product(mixed[group], w_out)
        if group > 0:
            sums[group] = sums[group].astype(bf)
        ahead = tie(gain_first, sums[group])
        if group == 2:
            updown_pieces = exchange_apart(updown_pieces, sums[group])
        if group > 0:
            sums[group] = send(sums[group], group)
        if group == parts - 1:
            ahead = tie(ahead, sums[1])
    cotangent = gather_rows(tie(cotangent_own, mixed[0]))
    updown_pieces = tie(updown_pieces, w_down, mixed[0])
    w_updown = gather_copies(updown_pieces.reshape(parts * rows_own, 2 * units))
    stream = ((GROUP_ROWS, D), f32)
    narrow = ((GROUP_ROWS, D), bf)
    hidden, normed_two = by_rows(hidden_kernel, sums + [inputs, gain_two], [stream, narrow])

    def swiglu_units(updown):
        return jax.nn.silu(updown[:, :units]) * updown[:, units:]

    normed_two = gather_rows(normed_two)
    active, d_updown, sums = ([None] * parts for _ in range(3))
    ahead = None
    for group in range(parts):
        if ahead is not None:
            normed_two[group] = tie(normed_two[group], ahead)
        updown = plain_product(normed_two[group], w_updown)
        act, swiglu_back = jax.vjp(swiglu_units, updown)
        active[group] = act.astype(bf)
        d_active = transposed_product(cotangent[group], w_down)
        d_updown[group] = swiglu_back(d_active)[0].astype(bf)
        sums[group] = transposed_product(d_updown[group], w_updown)
        if group > 0:
            sums[group] = sums[group].astype(bf)
        ahead = sums[group]
        if group > 0:
            sums[group] = send(sums[group], group)
    normed_two = jnp.concatenate(normed_two, 0)
    cotangent = jnp.concatenate(cotangent, 0)
    d_updown = tie(jnp.concatenate(d_updown, 0), ahead)
    active = tie(jnp.concatenate(active, 0), ahead)
    updown_terms = rows_product(normed_two, d_updown).astype(bf)
    updown_grad = scatter_copies(updown_terms)
    d_hidden, d_mixed, gain_two_grad = by_rows(
        hidden_back_kernel,
        sums + [hidden, tie(gain_two, updown_terms), cotangent_own],
        [stream, narrow, ((1, D), f32)],
    )

    active = tie(active, d_mixed)
    down_terms = rows_product(active, cotangent).astype(bf)
    out_terms = plain_product(active, w_down)
    block_out = [out_terms[step * GROUP_ROWS :][:GROUP_ROWS] for step in range(parts)]
    block_out[1:] = [block.astype(bf) for block in block_out[1:]]
    down_grad = halve_cores(down_terms)
    d_mixed = gather_rows(d_mixed)
    sums, d_pre = ([None] * parts for _ in range(2))
    gain_one_grad, d_params = 0.0, 0.0
    for group in range(parts):
        if group == 1:
            d_mixed[group] = tie(d_mixed[group], ahead, down_grad, *block_out[1:])
            down_grad = halve_first(down_grad)
        if group > 1:
            d_mixed[group] = tie(d_mixed[group], ahead, *down_grad)
        d_mixer = transposed_product(d_mixed[group], w_out)
        d_pre[group], d_more = mixer_backward(
            group, layouts, pre[group], params, d_mixer, kept[group], width
        )
        d_params = d_params + d_more
        sums[group] = transposed_product(d_pre[group], w_mixer)
        values = input_rows[group].astype(f32)
        scaled = values * row_scale(values)
        gain_one_grad = gain_one_grad + jnp.sum(sums[group] * scaled, 0, keepdims=True)
        if group > 0:
            sums[group] = sums[group].astype(bf)
        ahead = sums[group]
        if group > 0:
            sums[group] = send(sums[group], group)
    block_out[1:] = [
        send(block, step) for step, block in enumerate(tie_all(block_out[1:], ahead), 1)
    ]
    normed = jnp.concatenate(normed, 0)
    mixer_terms = rows_product(normed, jnp.concatenate(d_pre, 0))
    d_params = tie(d_params, sums[1])

    here = (jnp.arange(parts) == part).astype(f32)[:, None]
    taps_grad = d_params[:KERNEL].reshape(KERNEL, 3, 1, width) * here
    taps_grad = taps_grad.reshape(KERNEL, parts, copies, 3, rows_own).transpose(3, 0, 2, 1, 4)
    head_grad = to_wire((d_params[KERNEL, :width] * here).reshape(1, D))
    columns = [taps_grad.reshape(3 * KERNEL, D), head_grad, gain_two_grad, gain_one_grad]
    columns = jnp.concatenate(columns, 0)
    columns = rows_product(columns, jnp.eye(columns.shape[0], dtype=f32))
    first = 4 * width + heads_part
    columns = jnp.pad(columns, ((0, 0), (first, wide - first - columns.shape[1])))
    mixer_terms = (mixer_terms + columns).astype(bf)
    mixer_grad = scatter_copies(tie(mixer_terms, updown_grad, sums[2]))

    late = tie(gain_one, mixer_terms)
    (input_grad,) = by_rows(input_back_kernel, sums + [inputs, late, d_hidden], [narrow])
    updown_grad = tie(updown_grad, input_grad).reshape(parts, rows_own, 2 * units)
    mixed = tie(jnp.concatenate(mixed, 0), input_grad)
    out_shard = rows_product(mixed, jnp.concatenate(d_mixed, 0)).astype(bf)
    out_shard = halve_second(halve_first(halve_cores(out_shard)))
    out_shard = from_wire(out_shard.astype(f32))
    down_shard = from_wire(halve_second(tie_all(down_grad, input_grad)).astype(f32))
    updown_shard = updown_from_parts(exchange_apart(updown_grad))
    (block_out,) = by_rows(block_out_kernel, block_out + [hidden], [narrow])
    mixer_grad = exchange(mixer_grad.reshape(parts, rows_own, wide))
    qkv_shard, gate_shard, sums, strengths = mixer_from_parts(mixer_grad, width)
    beta_shard = strengths.reshape(rows_own, parts, SMALL)[:, :, :heads_part]
    sums = sums[:, heads_part:]
    taps_width = 3 * KERNEL
    taps_shard = sums[:, :taps_width].reshape(rows_own, 3, KERNEL).swapaxes(0, 1)
    return (
        from_wire(block_out),
        from_wire(input_grad),
        sums[:, taps_width + 2],
        taps_shard.reshape(-1, KERNEL),
        sums[:, taps_width],
        qkv_shard,
        beta_shard.reshape(rows_own, HEADS),
        gate_shard,
        out_shard,
        sums[:, taps_width + 1],
        updown_shard,
        down_shard,
    )


def solution(mesh):
    placed = (
        P("dp", None),
        P("dp", None),
        P("dp"),
        P("dp", None),
        P("dp"),
        P("dp", None),
        P("dp", None),
        P("dp", None),
        P("dp", None),
        P("dp"),
        P("dp", None),
        P("dp", None),
        P("dp", None),
        P("dp"),
    )
    return jax.shard_map(
        body,
        mesh=mesh,
        in_specs=placed,
        out_specs=(
            P("dp", None),
            P("dp", None),
            P("dp"),
            P("dp", None),
            P("dp"),
            P("dp", None),
            P("dp", None),
            P("dp", None),
            P("dp", None),
            P("dp"),
            P("dp", None),
            P("dp", None),
        ),
        check_vma=False,
    )
```

```python
import functools

import jax
import jax.numpy as jnp
from jax import lax
from jax.experimental import pallas as pl
from jax.experimental.pallas import tpu as pltpu
from jax.sharding import PartitionSpec as P

D = 2048
HEADS = 16
HEAD_DIM = 128
FF = 5632
KERNEL = 4
BLOCK_ROWS = 64
BLOCKS_DEV = 2
GROUP_ROWS = BLOCK_ROWS * BLOCKS_DEV
SMALL = 128
MODEL = 4

f32 = jnp.float32
bf = jnp.bfloat16


def block_layouts(first, second, lead):
    def doc(block):
        in_first = (block >= lead) & (block < lead + first)
        in_second = (block >= lead + first) & (block < lead + first + second)
        return jnp.where(in_first, 1, jnp.where(in_second, 2, 0))

    starts = (lead == 1) | (lead + first == 1) & (second > 0)
    columns = [doc(0) > 0, doc(1) > 0, doc(0) == doc(1), ~starts]
    return jnp.stack(columns, 1).astype(f32)


def plain_product(left, right):
    return jnp.dot(left, right, preferred_element_type=f32)


def rows_product(left, right):
    return lax.dot_general(left, right, (((0,), (0,)), ((), ())), preferred_element_type=f32)


def transposed_product(left, right):
    return lax.dot_general(left, right, (((1,), (1,)), ((), ())), preferred_element_type=f32)


def halves(values):
    high = values.astype(bf)
    return high, (values - high.astype(f32)).astype(bf)


def exact(left, right, left_dim, right_dim):
    left_high, left_low = left if isinstance(left, tuple) else halves(left)
    right_high, right_low = right if isinstance(right, tuple) else halves(right)
    return lax.dot_general(
        jnp.concatenate([left_high, left_high, left_low], left_dim),
        jnp.concatenate([right_high, right_low, right_high], right_dim),
        (((left_dim,), (right_dim,)), ((), ())),
        preferred_element_type=f32,
    )


def stacked(first, second):
    return tuple(jnp.concatenate([a, b], 0) for a, b in zip(first, second))


class Tile:
    def __init__(self, layout_ref, group):
        live_first, live_second, same, persist = (layout_ref[group, i] for i in range(4))
        shape = (GROUP_ROWS, HEAD_DIM)
        row = lax.broadcasted_iota(jnp.int32, shape, 0)
        col = lax.broadcasted_iota(jnp.int32, shape, 1)
        late = row >= BLOCK_ROWS
        self.row, self.col = row, col
        self.live = jnp.where(late, live_second, live_first)
        self.taps = [None] + [
            jnp.where(
                row < offset,
                0.0,
                jnp.where(late & (row < BLOCK_ROWS + offset), same, 1.0),
            )
            for offset in range(1, KERNEL)
        ]
        cross = jnp.where(late & (col < BLOCK_ROWS), persist, 1.0)
        self.lower = jnp.where(row > col, cross, 0.0)
        self.lower_full = jnp.where(row >= col, cross, 0.0)

    def earlier(self, values, offset):
        return pltpu.roll(values, offset, 0) * self.taps[offset]

    def later(self, values, offset):
        return pltpu.roll(values * self.taps[offset], GROUP_ROWS - offset, 0)


def convolve(tile, values, taps):
    total = values * taps[0]
    for offset in range(1, KERNEL):
        total = total + tile.earlier(values, offset) * taps[offset]
    return total


def unit_scale(values):
    return lax.rsqrt(jnp.sum(values * values, -1, keepdims=True) + 1e-06)


def head_columns(part_width, section, head):
    return pl.ds(section * part_width + head * HEAD_DIM, HEAD_DIM)


def unit_inverses(tile, lowers):
    eye = jnp.where(tile.row == tile.col, 1.0, 0.0)
    inverses = None
    size = 1
    while size < GROUP_ROWS:
        pair = tile.row // (2 * size) == tile.col // (2 * size)
        split = pair & (tile.row // size != tile.col // size)
        parts = [jnp.where(split, lower, 0.0) for lower in lowers]
        if inverses is None:
            inverses = [eye - part for part in parts]
        else:
            kept = [halves(inverse) for inverse in inverses]
            inner = [exact(part, known, 1, 0) for part, known in zip(parts, kept)]
            outer = [exact(known, value, 1, 0) for known, value in zip(kept, inner)]
            inverses = [inverse - value for inverse, value in zip(inverses, outer)]
        size *= 2
    return inverses


def mixer_forward_kernel(
    layout_ref, pre_ref, param_ref, mixed_ref, inverse_ref, score_ref, solved_ref, out_ref
):
    width = mixed_ref.shape[1]
    heads = range(width // HEAD_DIM)
    tile = Tile(layout_ref, pl.program_id(0))
    queries, keys, values, strengths = [], [], [], []
    for head in heads:
        parts = []
        for section in range(3):
            columns = head_columns(width, section, head)
            taps = [param_ref[offset : offset + 1, columns] for offset in range(KERNEL)]
            convolved = convolve(tile, pre_ref[:, columns], taps)
            parts.append(convolved * jax.nn.sigmoid(convolved))
        queries.append(parts[0] * (unit_scale(parts[0]) * HEAD_DIM**-0.5))
        keys.append(parts[1] * unit_scale(parts[1]))
        values.append(parts[2])
        start = 4 * width + head
        strengths.append(jax.nn.sigmoid(pre_ref[:, start : start + 1]) * tile.live)
    lowers, scores = [], []
    for head in heads:
        key_halves = halves(keys[head])
        both = exact(stacked(key_halves, halves(queries[head])), key_halves, 1, 1)
        lowers.append(both[:GROUP_ROWS] * strengths[head] * tile.lower)
        scores.append(both[GROUP_ROWS:] * tile.lower_full)
    inverses = unit_inverses(tile, lowers)
    solved = [exact(inverses[head], values[head] * strengths[head], 1, 0) for head in heads]
    outs = [exact(scores[head], solved[head], 1, 0) for head in heads]
    for head in heads:
        out = outs[head]
        scaled = out * lax.rsqrt(jnp.mean(out * out, -1, keepdims=True) + 1e-05)
        gate = pre_ref[:, head_columns(width, 3, head)]
        gain = param_ref[KERNEL : KERNEL + 1, head_columns(width, 0, head)]
        mixed = scaled * gain * (gate * jax.nn.sigmoid(gate)) * tile.live
        mixed_ref[:, head_columns(width, 0, head)] = mixed.astype(bf)
        inverse_ref[head] = inverses[head]
        score_ref[head] = scores[head]
        solved_ref[head] = solved[head]
        out_ref[head] = out


def mixer_backward_kernel(
    group,
    layout_ref,
    pre_ref,
    param_ref,
    grad_ref,
    inverse_ref,
    score_ref,
    solved_ref,
    out_ref,
    earlier_ref,
    *refs,
):
    d_pre_ref, d_param_ref = refs[-2:]
    width = grad_ref.shape[1]
    heads = range(width // HEAD_DIM)
    tile = Tile(layout_ref, group)

    d_param_ref[...] = earlier_ref[...]

    def along(values):
        return jnp.sum(values, -1, keepdims=True)

    d_outs = []
    for head in heads:
        columns = head_columns(width, 0, head)
        d_mixed = grad_ref[:, columns] * tile.live
        out = out_ref[head]
        scale = lax.rsqrt(jnp.mean(out * out, -1, keepdims=True) + 1e-05)
        scaled = out * scale
        gate = pre_ref[:, head_columns(width, 3, head)]
        gate_open = jax.nn.sigmoid(gate)
        gain = param_ref[KERNEL : KERNEL + 1, columns]
        gated = d_mixed * (gate * gate_open)
        d_param_ref[KERNEL : KERNEL + 1, columns] += jnp.sum(gated * scaled, 0, keepdims=True)
        d_gate = d_mixed * scaled * gain * (gate_open * (1.0 + gate * (1.0 - gate_open)))
        d_pre_ref[:, head_columns(width, 3, head)] = d_gate.astype(bf)
        d_scaled = gated * gain
        mean = jnp.mean(d_scaled * out, -1, keepdims=True)
        d_outs.append(scale * d_scaled - out * (scale * scale * scale * mean))
    d_out_halves = [halves(value) for value in d_outs]
    solved_halves = [halves(solved_ref[head]) for head in heads]
    d_solved = [exact(score_ref[head], d_out_halves[head], 0, 0) for head in heads]
    d_scores = [
        exact(d_out_halves[head], solved_halves[head], 1, 1) * tile.lower_full for head in heads
    ]
    d_inner = [exact(inverse_ref[head], d_solved[head], 0, 0) for head in heads]
    d_lowers = [exact(d_inner[head], solved_halves[head], 1, 1) * -tile.lower for head in heads]
    d_beta = jnp.zeros((GROUP_ROWS, SMALL), f32)
    for head in heads:
        pres, convolved, opened, active = [], [], [], []
        for section in range(3):
            columns = head_columns(width, section, head)
            taps = [param_ref[offset : offset + 1, columns] for offset in range(KERNEL)]
            pres.append(pre_ref[:, columns])
            convolved.append(convolve(tile, pres[section], taps))
            opened.append(jax.nn.sigmoid(convolved[section]))
            active.append(convolved[section] * opened[section])
        query_scale = unit_scale(active[0])
        key_scale = unit_scale(active[1])
        query_unit = active[0] * query_scale
        key = active[1] * key_scale
        start = 4 * width + head
        opening = jax.nn.sigmoid(pre_ref[:, start : start + 1])
        strength = opening * tile.live
        d_both = stacked(halves(d_lowers[head]), halves(d_scores[head]))
        by_key = exact(d_both, key, 1, 0)
        d_query = by_key[GROUP_ROWS:] * HEAD_DIM**-0.5
        from_lower = by_key[:GROUP_ROWS]
        weighted = stacked(halves(key * strength), halves(query_unit * HEAD_DIM**-0.5))
        d_key = strength * from_lower + exact(d_both, weighted, 0, 0)
        d_strength = along(d_inner[head] * active[2] + from_lower * key)
        d_value = d_inner[head] * strength
        d_opening = d_strength * (opening * (1.0 - opening)) * tile.live
        d_beta = d_beta + jnp.where(tile.col == head, d_opening, 0.0)
        d_active = [
            (d_query - query_unit * along(query_unit * d_query)) * query_scale,
            (d_key - key * along(key * d_key)) * key_scale,
            d_value,
        ]
        for section in range(3):
            columns = head_columns(width, section, head)
            taps = [param_ref[offset : offset + 1, columns] for offset in range(KERNEL)]
            slope = opened[section] * (1.0 + convolved[section] * (1.0 - opened[section]))
            d_convolved = d_active[section] * slope
            d_pre = d_convolved * taps[0]
            sums = [jnp.sum(d_convolved * pres[section], 0, keepdims=True)]
            for offset in range(1, KERNEL):
                d_pre = d_pre + tile.later(d_convolved, offset) * taps[offset]
                sums.append(
                    jnp.sum(d_convolved * tile.earlier(pres[section], offset), 0, keepdims=True)
                )
            d_param_ref[0:KERNEL, columns] += jnp.concatenate(sums, 0)
            d_pre_ref[:, columns] = d_pre.astype(bf)
    d_pre_ref[:, 4 * width :] = d_beta.astype(bf)


def mixer_specs(width, group_of):
    wide = 4 * width + SMALL
    heads = width // HEAD_DIM
    layout = pl.BlockSpec(memory_space=pltpu.SMEM)
    pre = pl.BlockSpec((GROUP_ROWS, wide), lambda i: (group_of(i), 0))
    param = pl.BlockSpec((2 * KERNEL, 3 * width), lambda i: (0, 0))
    narrow = pl.BlockSpec((GROUP_ROWS, width), lambda i: (group_of(i), 0))
    square = pl.BlockSpec((heads, GROUP_ROWS, HEAD_DIM), lambda i: (group_of(i), 0, 0))
    return layout, pre, param, narrow, square


def mixer_params(steps):
    return {
        "grid": (steps,),
        "compiler_params": pltpu.CompilerParams(
            dimension_semantics=("arbitrary",), vmem_limit_bytes=48 * 2**20
        ),
        "cost_estimate": pl.CostEstimate(
            flops=steps * 2**32, bytes_accessed=steps * 2**21, transcendentals=steps * 2**19
        ),
    }


def mixer_forward(layout, pre, params, width):
    groups = layout.shape[0]
    layout_spec, pre_spec, param_spec, narrow, square = mixer_specs(width, lambda i: i)
    squares = jax.ShapeDtypeStruct((groups * width // HEAD_DIM, GROUP_ROWS, HEAD_DIM), f32)
    return pl.pallas_call(
        mixer_forward_kernel,
        in_specs=[layout_spec, pre_spec, param_spec],
        out_specs=[narrow] + [square] * 4,
        out_shape=[jax.ShapeDtypeStruct((groups * GROUP_ROWS, width), bf)] + [squares] * 4,
        **mixer_params(groups),
    )(layout, pre, params)


def mixer_backward(group, layout, pre, params, d_mixer, kept, d_params, d_pre, width):
    layout_spec, pre_spec, param_spec, _, square = mixer_specs(width, lambda i: group)
    whole = pl.BlockSpec(d_mixer.shape, lambda i: (0, 0))
    operands = [layout, pre, params, d_mixer, *kept, d_params]
    in_specs = [layout_spec, pre_spec, param_spec, whole] + [square] * 4 + [param_spec]
    aliases = {}
    if d_pre is not None:
        aliases = {len(operands): 0}
        operands.append(d_pre)
        in_specs.append(pl.BlockSpec(memory_space=pl.ANY))
    return pl.pallas_call(
        functools.partial(mixer_backward_kernel, group),
        in_specs=in_specs,
        out_specs=[pre_spec, param_spec],
        out_shape=[
            jax.ShapeDtypeStruct(pre.shape, bf),
            jax.ShapeDtypeStruct(params.shape, f32),
        ],
        input_output_aliases=aliases,
        **mixer_params(1),
    )(*operands)


def tie_all(values, *others):
    anywhere = pl.BlockSpec(memory_space=pl.ANY)
    tied = pl.pallas_call(
        lambda *refs: None,
        in_specs=[anywhere] * (len(values) + len(others)),
        out_specs=[anywhere] * len(values),
        out_shape=[jax.ShapeDtypeStruct(value.shape, value.dtype) for value in values],
        input_output_aliases={i: i for i in range(len(values))},
        cost_estimate=pl.CostEstimate(flops=0, bytes_accessed=0, transcendentals=0),
    )(*values, *others)
    return list(tied)


def tie(value, *others):
    return tie_all([value], *others)[0]


def assemble(part, values, received, others):
    parts = values.shape[0]

    def kernel(part_ref, values_ref, *refs):
        own = part_ref[0]
        out_ref = refs[-1]
        out_ref[own] = values_ref[own]
        for step in range(1, parts):
            out_ref[lax.rem(own + parts - step, parts)] = refs[step - 1][...]

    vmem = pl.BlockSpec(memory_space=pltpu.VMEM)
    anywhere = pl.BlockSpec(memory_space=pl.ANY)
    return pl.pallas_call(
        kernel,
        in_specs=[pl.BlockSpec(memory_space=pltpu.SMEM)]
        + [vmem] * parts
        + [anywhere] * len(others),
        out_specs=vmem,
        out_shape=jax.ShapeDtypeStruct(values.shape, values.dtype),
        compiler_params=pltpu.CompilerParams(vmem_limit_bytes=32 * 2**20),
    )(part.reshape(1).astype(jnp.int32), values, *received, *others)


def copy_columns(*refs):
    *sources, target = refs
    start = 0
    for source in sources:
        block = source[...].reshape(source.shape[-2:])
        columns = pl.ds(start, block.shape[1])
        if len(target.shape) == 3:
            target[0, :, columns] = block.astype(target.dtype)
        else:
            target[:, columns] = block.astype(target.dtype)
        start += block.shape[1]


def to_parts(sources, parts, dtype):
    rows = sources[0][0].shape[0]

    def spec(section, width):
        return pl.BlockSpec((rows, width), lambda p: (0, section * parts + p))

    total = sum(width for _, _, width in sources)
    return pl.pallas_call(
        copy_columns,
        grid=(parts,),
        in_specs=[spec(section, width) for _, section, width in sources],
        out_specs=pl.BlockSpec((1, rows, total), lambda p: (p, 0, 0)),
        out_shape=jax.ShapeDtypeStruct((parts, rows, total), dtype),
    )(*[array for array, _, _ in sources])


def updown_from_parts(slabs):
    parts, rows, width = slabs.shape
    units = width // 2

    def kernel(slabs_ref, out_ref):
        for p in range(parts):
            out_ref[:, p * units : (p + 1) * units] = slabs_ref[p].astype(f32)

    return pl.pallas_call(
        kernel,
        grid=(2,),
        in_specs=[pl.BlockSpec((parts, rows, units), lambda half: (0, 0, half))],
        out_specs=pl.BlockSpec((rows, parts * units), lambda half: (0, half)),
        out_shape=jax.ShapeDtypeStruct((rows, parts * width), f32),
        compiler_params=pltpu.CompilerParams(vmem_limit_bytes=32 * 2**20),
    )(slabs)


def mixer_from_parts(slabs, width):
    parts, rows, _ = slabs.shape

    def kernel(slabs_ref, qkv_ref, gate_ref, strength_ref):
        for p in range(parts):
            for section in range(4):
                block = slabs_ref[p, :, section * width : (section + 1) * width].astype(f32)
                if section < 3:
                    start = (section * parts + p) * width
                    qkv_ref[:, start : start + width] = block
                else:
                    gate_ref[:, p * width : (p + 1) * width] = block
            last = slabs_ref[p, :, 4 * width :].astype(f32)
            strength_ref[:, p * SMALL : (p + 1) * SMALL] = last

    widths = [3 * parts * width, parts * width, parts * SMALL]
    return pl.pallas_call(
        kernel,
        out_shape=[jax.ShapeDtypeStruct((rows, size), f32) for size in widths],
        compiler_params=pltpu.CompilerParams(vmem_limit_bytes=32 * 2**20),
    )(slabs)


def total_of(own_ref, received_refs):
    total = own_ref[...]
    for ref in received_refs:
        total = total + ref[...].astype(f32)
    return total


def row_scale(values):
    return lax.rsqrt(jnp.mean(values * values, -1, keepdims=True) + 1e-06)


def norm_slope(values, scale, gain, grad):
    mean = jnp.mean(gain * grad * values, -1, keepdims=True)
    return scale * gain * grad - values * (scale * scale * scale * mean)


def hidden_kernel(own_ref, *refs):
    *received, input_ref, gain_ref, hidden_ref, normed_ref = refs
    hidden = input_ref[...].astype(f32) + total_of(own_ref, received)
    hidden_ref[...] = hidden
    normed_ref[...] = (hidden * row_scale(hidden) * gain_ref[...]).astype(bf)


def hidden_back_kernel(own_ref, *refs):
    *received, hidden_ref, gain_ref, cot_ref, d_hidden_ref, d_mixed_ref, d_gain_ref = refs
    grad = total_of(own_ref, received)
    hidden = hidden_ref[...]
    scale = row_scale(hidden)

    @pl.when(pl.program_id(0) == 0)
    def _():
        d_gain_ref[...] = jnp.zeros_like(d_gain_ref)

    d_gain_ref[...] += jnp.sum(grad * hidden * scale, 0, keepdims=True)
    d_hidden = cot_ref[...].astype(f32) + norm_slope(hidden, scale, gain_ref[...], grad)
    d_hidden_ref[...] = d_hidden
    d_mixed_ref[...] = d_hidden.astype(bf)


def input_back_kernel(own_ref, *refs):
    *received, input_ref, gain_ref, d_hidden_ref, out_ref = refs
    grad = total_of(own_ref, received)
    values = input_ref[...].astype(f32)
    slope = norm_slope(values, row_scale(values), gain_ref[...], grad)
    out_ref[...] = (d_hidden_ref[...] + slope).astype(bf)


def block_out_kernel(own_ref, *refs):
    *received, hidden_ref, out_ref = refs
    out_ref[...] = (hidden_ref[...] + total_of(own_ref, received)).astype(bf)


def by_rows(kernel, arrays, outs, block=32):
    def spec(shape):
        if shape[0] == 1:
            return pl.BlockSpec(shape, lambda i: (0, 0))
        return pl.BlockSpec((block, shape[1]), lambda i: (i, 0))

    return pl.pallas_call(
        kernel,
        grid=(GROUP_ROWS // block,),
        in_specs=[spec(array.shape) for array in arrays],
        out_specs=[spec(shape) for shape, _ in outs],
        out_shape=[jax.ShapeDtypeStruct(shape, dtype) for shape, dtype in outs],
        compiler_params=pltpu.CompilerParams(dimension_semantics=("arbitrary",)),
    )(*arrays)


def body(
    block_in,
    out_grad,
    norm1_gain,
    conv_weight,
    head_gain,
    qkv_weight,
    beta_weight,
    gate_weight,
    out_weight,
    norm2_gain,
    updown_weight,
    down_weight,
    seq_blocks,
    lead_blocks,
):
    devices = lax.axis_size("dp")
    parts = MODEL
    copies = devices // parts
    part = lax.axis_index("dp") // copies
    copy = lax.axis_index("dp") % copies
    rows_own = qkv_weight.shape[0]
    width = D // parts
    units = FF // parts
    heads_part = HEADS // parts
    wide = 4 * width + SMALL
    model_groups = [[m * copies + t for m in range(parts)] for t in range(copies)]
    copy_groups = [[m * copies + t for t in range(copies)] for m in range(parts)]

    def exchange(values):
        return lax.all_to_all(
            values, "dp", split_axis=0, concat_axis=0, axis_index_groups=model_groups, tiled=True
        )

    def shift(values, step):
        pairs = [
            (m * copies + t, (m + step) % parts * copies + t)
            for m in range(parts)
            for t in range(copies)
        ]
        return lax.ppermute(values, "dp", pairs)

    def exchange_apart(values, *others):
        received = []
        for step in range(1, parts):
            piece = lax.dynamic_index_in_dim(values, (part + step) % parts, 0, keepdims=False)
            received.append(shift(piece, step))
        return assemble(part, values, received, others)

    def gather_rows(values):
        return [values] + [shift(values, step) for step in range(1, parts)]

    def parcels(terms):
        return [
            terms[step * GROUP_ROWS :][:GROUP_ROWS].astype(bf) for step in range(1, parts)
        ]

    def scatter_rows(terms, sent):
        return [terms] + [shift(block, -step) for step, block in enumerate(sent, 1)]

    def gather_copies(values):
        return lax.all_gather(values, "dp", axis=0, axis_index_groups=copy_groups, tiled=True)

    def scatter_copies(values):
        return lax.psum_scatter(
            values.astype(bf),
            "dp",
            scatter_dimension=0,
            axis_index_groups=copy_groups,
            tiled=True,
        )

    def halve(values, bit, axis):
        pairs = [(i, i ^ (1 << bit)) for i in range(devices)]
        side = (copy >> bit) & 1
        own = lax.dynamic_index_in_dim(values, side, axis, keepdims=False)
        other = lax.dynamic_index_in_dim(values, 1 - side, axis, keepdims=False)
        return (own.astype(f32) + lax.ppermute(other, "dp", pairs).astype(f32)).astype(bf)

    by_halves = copies == 8

    def halve_cores(values):
        if not by_halves:
            return values
        rows, columns = values.shape
        return halve(values.reshape(2, 2, 2, rows // 8, columns), 0, 2)

    def halve_first(values):
        if not by_halves:
            return [values]
        middle = values.shape[-1] // 2
        return [halve(values[..., :middle], 1, 1), halve(values[..., middle:], 2, 0)]

    def halve_second(values):
        if not by_halves:
            return scatter_copies(values[0])
        return jnp.concatenate([halve(values[0], 2, 0), halve(values[1], 1, 0)], 1)

    def to_wire(values):
        return values.reshape(-1, parts, copies, rows_own).swapaxes(1, 2).reshape(-1, D)

    def from_wire(values):
        return values.reshape(-1, copies, parts, rows_own).swapaxes(1, 2).reshape(-1, D)

    w_out_own = to_wire(out_weight.astype(bf))
    w_out = gather_copies(w_out_own)
    strengths = beta_weight.reshape(rows_own, parts, heads_part)
    strengths = jnp.pad(strengths, ((0, 0), (0, 0), (0, SMALL - heads_part)))
    strengths = tie(strengths.reshape(rows_own, parts * SMALL), w_out_own)
    pieces = [(qkv_weight, section, width) for section in range(3)]
    pieces = to_parts(pieces + [(gate_weight, 0, width), (strengths, 0, SMALL)], parts, bf)
    mixer_pieces = tie(exchange(pieces), w_out)
    w_mixer = gather_copies(mixer_pieces.reshape(parts * rows_own, wide))
    inputs = tie(to_wire(block_in), mixer_pieces)
    input_rows = gather_rows(inputs)

    lanes = -(-3 * rows_own // 128) * 128
    numbers = jnp.concatenate([seq_blocks[0], lead_blocks]).astype(f32)
    small = [conv_weight.T, norm1_gain[None], head_gain[None], norm2_gain[None], numbers[None]]
    small = [jnp.pad(rows, ((0, 0), (0, lanes - rows.shape[1]))) for rows in small]
    small = jnp.pad(jnp.concatenate(small, 0).astype(bf), ((0, 2 * KERNEL), (0, 0)))
    small = jnp.broadcast_to(small[None], (devices,) + small.shape)
    small = lax.all_to_all(tie(small, inputs), "dp", 0, 0, tiled=True)
    taps = small[:, :KERNEL, : 3 * rows_own].swapaxes(0, 1).reshape(KERNEL, 3, parts, width)
    taps = lax.dynamic_index_in_dim(taps, part, 2, keepdims=False).reshape(KERNEL, 3 * width)
    gain_one, head_full, gain_two = (
        small[:, KERNEL + i, :rows_own].reshape(1, D).astype(f32) for i in range(3)
    )
    gain_one, gain_two = to_wire(gain_one), to_wire(gain_two)
    head_part = lax.dynamic_slice_in_dim(head_full, part * width, width, 1)
    params = jnp.concatenate([taps.astype(f32), jnp.pad(head_part, ((0, 0), (0, 2 * width)))], 0)
    params = jnp.pad(params, ((0, KERNEL - 1), (0, 0)))
    numbers = small[:, KERNEL + 3, :3].astype(f32).astype(jnp.int32)
    layouts = block_layouts(numbers[:, 0], numbers[:, 1], numbers[:, 2])
    layouts = layouts.reshape(parts, copies, 4)
    layouts = lax.dynamic_index_in_dim(layouts, copy, 1, keepdims=False)
    wanted = (part - jnp.arange(parts)) % parts
    wanted = (wanted[:, None] == jnp.arange(parts)).astype(f32)
    layouts = jnp.sum(wanted[:, :, None] * layouts, 1)

    pieces = to_parts([(updown_weight, half, units) for half in range(2)], parts, bf)
    updown_pieces = tie(pieces, small, *input_rows[1:])
    w_down_own = to_wire(down_weight.astype(bf))
    w_down = gather_copies(tie(w_down_own, *input_rows[1:]))
    cotangent_own = to_wire(out_grad)

    input_rows = jnp.concatenate(input_rows, 0).astype(f32)
    input_scale = row_scale(input_rows)
    gain_first = tie(gain_one, w_down_own, cotangent_own)
    normed = (input_rows * input_scale * gain_first).astype(bf)
    pre = plain_product(normed, w_mixer)
    mixed, *kept = mixer_forward(layouts, pre, params, width)
    updown_pieces = exchange_apart(updown_pieces, mixed)
    w_updown = gather_copies(updown_pieces.reshape(parts * rows_own, 2 * units))
    stream = ((GROUP_ROWS, D), f32)
    narrow = ((GROUP_ROWS, D), bf)
    out_terms = plain_product(mixed, w_out)
    hidden, normed_two = by_rows(
        hidden_kernel,
        scatter_rows(out_terms, parcels(out_terms)) + [inputs, gain_two],
        [stream, narrow],
    )
    cotangent = jnp.concatenate(gather_rows(tie(cotangent_own, normed_two)), 0)
    normed_two = jnp.concatenate(gather_rows(normed_two), 0)

    def swiglu_units(updown):
        return jax.nn.silu(updown[:, :units]) * updown[:, units:]

    updown = plain_product(normed_two, w_updown)
    active, swiglu_back = jax.vjp(swiglu_units, updown)
    active = active.astype(bf)
    d_active = transposed_product(cotangent, w_down)
    d_updown = swiglu_back(d_active)[0].astype(bf)
    d_normed_two = transposed_product(d_updown, w_updown)
    sent = parcels(d_normed_two)
    d_normed_two = scatter_rows(d_normed_two, sent)
    updown_terms = rows_product(normed_two, tie(d_updown, *sent)).astype(bf)
    updown_grad = scatter_copies(updown_terms)
    active = tie(active, *sent)
    down_terms = rows_product(active, cotangent).astype(bf)
    gain_two_late = tie(gain_two, updown_terms, down_terms)
    d_hidden, d_mixed, gain_two_grad = by_rows(
        hidden_back_kernel,
        d_normed_two + [hidden, gain_two_late, cotangent_own],
        [stream, narrow, ((1, D), f32)],
    )

    out_terms = plain_product(tie(active, d_mixed), w_down)
    out_sent = parcels(out_terms)
    down_grad = halve_cores(tie(down_terms, d_mixed))
    d_mixed = gather_rows(d_mixed)
    d_pre = None
    d_params = jnp.zeros(params.shape, f32)
    for group in range(parts):
        if group == 1:
            d_mixed[group] = tie(d_mixed[group], down_grad, d_params, *out_sent)
            down_grad = halve_first(down_grad)
        elif group > 1:
            d_mixed[group] = tie(d_mixed[group], d_params)
        d_mixer = transposed_product(d_mixed[group], w_out)
        d_pre, d_params = mixer_backward(
            group, layouts, pre, params, d_mixer, kept, d_params, d_pre, width
        )
    out_sent = tie_all(out_sent, d_mixed[-1])
    block_out = scatter_rows(out_terms, out_sent)
    mixer_terms = tie(rows_product(normed, d_pre).astype(bf), updown_grad)
    mixer_grad = scatter_copies(mixer_terms)

    d_normed_terms = transposed_product(tie(d_pre, mixer_terms), w_mixer)
    d_normed = scatter_rows(d_normed_terms, parcels(d_normed_terms))
    gain_one_grad = jnp.sum(d_normed_terms * (input_rows * input_scale), 0, keepdims=True)

    here = (jnp.arange(parts) == part).astype(f32)[:, None]
    taps_grad = d_params[:KERNEL].reshape(KERNEL, 3, 1, width) * here
    taps_grad = taps_grad.reshape(KERNEL, parts, copies, 3, rows_own).transpose(1, 2, 3, 0, 4)
    taps_grad = taps_grad.reshape(devices, 3 * KERNEL, rows_own)
    head_grad = (d_params[KERNEL, :width] * here).reshape(devices, 1, rows_own)
    gain_grads = [
        grad.reshape(copies, parts, 1, rows_own).swapaxes(0, 1).reshape(devices, 1, rows_own)
        for grad in (gain_one_grad, gain_two_grad)
    ]
    small_grad = jnp.concatenate([taps_grad, head_grad] + gain_grads, 1)
    small_grad = jnp.pad(small_grad, ((0, 0), (0, 1), (0, 128 - rows_own)))
    small_grad = jnp.sum(lax.all_to_all(small_grad, "dp", 0, 0, tiled=True), 0)[:, :rows_own]
    taps_shard = small_grad[: 3 * KERNEL].reshape(3, KERNEL, rows_own).swapaxes(1, 2)
    taps_shard = taps_shard.reshape(3 * rows_own, KERNEL)
    head_shard, gain_one_shard, gain_two_shard = small_grad[3 * KERNEL : 3 * KERNEL + 3]

    (block_out,) = by_rows(block_out_kernel, block_out + [hidden], [narrow])
    (input_grad,) = by_rows(input_back_kernel, d_normed + [inputs, gain_one, d_hidden], [narrow])
    updown_grad = tie(updown_grad, d_normed_terms).reshape(parts, rows_own, 2 * units)
    updown_shard = updown_from_parts(exchange_apart(updown_grad))
    mixed = tie(mixed, block_out)
    out_shard = rows_product(mixed, jnp.concatenate(d_mixed, 0)).astype(bf)
    out_shard = halve_second(halve_first(halve_cores(out_shard)))
    out_shard = from_wire(out_shard.astype(f32))
    down_shard = from_wire(halve_second(tie_all(down_grad, block_out)).astype(f32))
    mixer_grad = exchange(mixer_grad.reshape(parts, rows_own, wide))
    qkv_shard, gate_shard, strengths = mixer_from_parts(mixer_grad, width)
    beta_shard = strengths.reshape(rows_own, parts, SMALL)[:, :, :heads_part]
    return (
        from_wire(block_out),
        from_wire(input_grad),
        gain_one_shard,
        taps_shard,
        head_shard,
        qkv_shard,
        beta_shard.reshape(rows_own, HEADS),
        gate_shard,
        out_shard,
        gain_two_shard,
        updown_shard,
        down_shard,
    )


def solution(mesh):
    placed = (
        P("dp", None),
        P("dp", None),
        P("dp"),
        P("dp", None),
        P("dp"),
        P("dp", None),
        P("dp", None),
        P("dp", None),
        P("dp", None),
        P("dp"),
        P("dp", None),
        P("dp", None),
        P("dp", None),
        P("dp"),
    )
    return jax.shard_map(
        body,
        mesh=mesh,
        in_specs=placed,
        out_specs=(
            P("dp", None),
            P("dp", None),
            P("dp"),
            P("dp", None),
            P("dp"),
            P("dp", None),
            P("dp", None),
            P("dp", None),
            P("dp", None),
            P("dp"),
            P("dp", None),
            P("dp", None),
        ),
        check_vma=False,
    )
```

```python
import jax
import jax.numpy as jnp
from jax import lax
from jax.experimental import pallas as pl
from jax.experimental.pallas import tpu as pltpu
from jax.sharding import PartitionSpec as P

D = 2048
HEADS = 16
HEAD_DIM = 128
FF = 5632
KERNEL = 4
BLOCK_ROWS = 64
BLOCKS_DEV = 2
GROUP_ROWS = BLOCK_ROWS * BLOCKS_DEV
SMALL = 128
MODEL = 4

f32 = jnp.float32
bf = jnp.bfloat16


def block_layouts(first, second, lead):
    def doc(block):
        in_first = (block >= lead) & (block < lead + first)
        in_second = (block >= lead + first) & (block < lead + first + second)
        return jnp.where(in_first, 1, jnp.where(in_second, 2, 0))

    starts = (lead == 1) | (lead + first == 1) & (second > 0)
    columns = [doc(0) > 0, doc(1) > 0, doc(0) == doc(1), ~starts]
    return jnp.stack(columns, 1).astype(f32)


def plain_product(left, right):
    return jnp.dot(left, right, preferred_element_type=f32)


def rows_product(left, right):
    return lax.dot_general(left, right, (((0,), (0,)), ((), ())), preferred_element_type=f32)


def transposed_product(left, right):
    return lax.dot_general(left, right, (((1,), (1,)), ((), ())), preferred_element_type=f32)


def halves(values):
    high = values.astype(bf)
    return high, (values - high.astype(f32)).astype(bf)


def exact(left, right, left_dim, right_dim):
    left_high, left_low = left if isinstance(left, tuple) else halves(left)
    right_high, right_low = right if isinstance(right, tuple) else halves(right)
    return lax.dot_general(
        jnp.concatenate([left_high, left_high, left_low], left_dim),
        jnp.concatenate([right_high, right_low, right_high], right_dim),
        (((left_dim,), (right_dim,)), ((), ())),
        preferred_element_type=f32,
    )


def stacked(first, second):
    return tuple(jnp.concatenate([a, b], 0) for a, b in zip(first, second))


class Tile:
    def __init__(self, layout_ref, group):
        live_first, live_second, same, persist = (layout_ref[group, i] for i in range(4))
        shape = (GROUP_ROWS, HEAD_DIM)
        row = lax.broadcasted_iota(jnp.int32, shape, 0)
        col = lax.broadcasted_iota(jnp.int32, shape, 1)
        late = row >= BLOCK_ROWS
        self.row, self.col = row, col
        self.live = jnp.where(late, live_second, live_first)
        self.taps = [None] + [
            jnp.where(
                row < offset,
                0.0,
                jnp.where(late & (row < BLOCK_ROWS + offset), same, 1.0),
            )
            for offset in range(1, KERNEL)
        ]
        cross = jnp.where(late & (col < BLOCK_ROWS), persist, 1.0)
        self.lower = jnp.where(row > col, cross, 0.0)
        self.lower_full = jnp.where(row >= col, cross, 0.0)

    def earlier(self, values, offset):
        return pltpu.roll(values, offset, 0) * self.taps[offset]

    def later(self, values, offset):
        return pltpu.roll(values * self.taps[offset], GROUP_ROWS - offset, 0)


def convolve(tile, values, taps):
    total = values * taps[0]
    for offset in range(1, KERNEL):
        total = total + tile.earlier(values, offset) * taps[offset]
    return total


def unit_scale(values):
    return lax.rsqrt(jnp.sum(values * values, -1, keepdims=True) + 1e-06)


def head_columns(part_width, section, head):
    return pl.ds(section * part_width + head * HEAD_DIM, HEAD_DIM)


def unit_inverses(tile, lowers):
    eye = jnp.where(tile.row == tile.col, 1.0, 0.0)
    inverses = None
    size = 1
    while size < GROUP_ROWS:
        pair = tile.row // (2 * size) == tile.col // (2 * size)
        split = pair & (tile.row // size != tile.col // size)
        parts = [jnp.where(split, lower, 0.0) for lower in lowers]
        if inverses is None:
            inverses = [eye - part for part in parts]
        else:
            kept = [halves(inverse) for inverse in inverses]
            inner = [exact(part, known, 1, 0) for part, known in zip(parts, kept)]
            outer = [exact(known, value, 1, 0) for known, value in zip(kept, inner)]
            inverses = [inverse - value for inverse, value in zip(inverses, outer)]
        size *= 2
    return inverses


def mixer_forward_kernel(
    layout_ref, pre_ref, param_ref, mixed_ref, inverse_ref, score_ref, solved_ref, out_ref
):
    width = mixed_ref.shape[1]
    heads = range(width // HEAD_DIM)
    tile = Tile(layout_ref, pl.program_id(0))
    queries, keys, values, strengths = [], [], [], []
    for head in heads:
        parts = []
        for section in range(3):
            columns = head_columns(width, section, head)
            taps = [param_ref[offset : offset + 1, columns] for offset in range(KERNEL)]
            convolved = convolve(tile, pre_ref[:, columns], taps)
            parts.append(convolved * jax.nn.sigmoid(convolved))
        queries.append(parts[0] * (unit_scale(parts[0]) * HEAD_DIM**-0.5))
        keys.append(parts[1] * unit_scale(parts[1]))
        values.append(parts[2])
        start = 4 * width + head
        strengths.append(jax.nn.sigmoid(pre_ref[:, start : start + 1]) * tile.live)
    lowers, scores = [], []
    for head in heads:
        key_halves = halves(keys[head])
        both = exact(stacked(key_halves, halves(queries[head])), key_halves, 1, 1)
        lowers.append(both[:GROUP_ROWS] * strengths[head] * tile.lower)
        scores.append(both[GROUP_ROWS:] * tile.lower_full)
    inverses = unit_inverses(tile, lowers)
    solved = [exact(inverses[head], values[head] * strengths[head], 1, 0) for head in heads]
    outs = [exact(scores[head], solved[head], 1, 0) for head in heads]
    for head in heads:
        out = outs[head]
        scaled = out * lax.rsqrt(jnp.mean(out * out, -1, keepdims=True) + 1e-05)
        gate = pre_ref[:, head_columns(width, 3, head)]
        gain = param_ref[KERNEL : KERNEL + 1, head_columns(width, 0, head)]
        mixed = scaled * gain * (gate * jax.nn.sigmoid(gate)) * tile.live
        mixed_ref[:, head_columns(width, 0, head)] = mixed.astype(bf)
        inverse_ref[head] = inverses[head]
        score_ref[head] = scores[head]
        solved_ref[head] = solved[head]
        out_ref[head] = out


def mixer_backward_kernel(
    layout_ref,
    pre_ref,
    param_ref,
    weight_ref,
    inverse_ref,
    score_ref,
    solved_ref,
    out_ref,
    *refs,
):
    *mixed_refs, d_pre_ref, d_param_ref, grad_ref = refs
    width = grad_ref.shape[1]
    heads = range(width // HEAD_DIM)
    tile = Tile(layout_ref, pl.program_id(0))
    for group, mixed_ref in enumerate(mixed_refs):

        @pl.when(pl.program_id(0) == group)
        def _():
            grad_ref[...] = transposed_product(mixed_ref[...], weight_ref[...])

    @pl.when(pl.program_id(0) == 0)
    def _():
        d_param_ref[...] = jnp.zeros_like(d_param_ref)

    def along(values):
        return jnp.sum(values, -1, keepdims=True)

    d_outs = []
    for head in heads:
        columns = head_columns(width, 0, head)
        d_mixed = grad_ref[:, columns] * tile.live
        out = out_ref[head]
        scale = lax.rsqrt(jnp.mean(out * out, -1, keepdims=True) + 1e-05)
        scaled = out * scale
        gate = pre_ref[:, head_columns(width, 3, head)]
        gate_open = jax.nn.sigmoid(gate)
        gain = param_ref[KERNEL : KERNEL + 1, columns]
        gated = d_mixed * (gate * gate_open)
        d_param_ref[KERNEL : KERNEL + 1, columns] += jnp.sum(gated * scaled, 0, keepdims=True)
        d_gate = d_mixed * scaled * gain * (gate_open * (1.0 + gate * (1.0 - gate_open)))
        d_pre_ref[:, head_columns(width, 3, head)] = d_gate.astype(bf)
        d_scaled = gated * gain
        mean = jnp.mean(d_scaled * out, -1, keepdims=True)
        d_outs.append(scale * d_scaled - out * (scale * scale * scale * mean))
    d_out_halves = [halves(value) for value in d_outs]
    solved_halves = [halves(solved_ref[head]) for head in heads]
    d_solved = [exact(score_ref[head], d_out_halves[head], 0, 0) for head in heads]
    d_scores = [
        exact(d_out_halves[head], solved_halves[head], 1, 1) * tile.lower_full for head in heads
    ]
    d_inner = [exact(inverse_ref[head], d_solved[head], 0, 0) for head in heads]
    d_lowers = [exact(d_inner[head], solved_halves[head], 1, 1) * -tile.lower for head in heads]
    d_beta = jnp.zeros((GROUP_ROWS, SMALL), f32)
    for head in heads:
        pres, convolved, opened, active = [], [], [], []
        for section in range(3):
            columns = head_columns(width, section, head)
            taps = [param_ref[offset : offset + 1, columns] for offset in range(KERNEL)]
            pres.append(pre_ref[:, columns])
            convolved.append(convolve(tile, pres[section], taps))
            opened.append(jax.nn.sigmoid(convolved[section]))
            active.append(convolved[section] * opened[section])
        query_scale = unit_scale(active[0])
        key_scale = unit_scale(active[1])
        query_unit = active[0] * query_scale
        key = active[1] * key_scale
        start = 4 * width + head
        opening = jax.nn.sigmoid(pre_ref[:, start : start + 1])
        strength = opening * tile.live
        d_both = stacked(halves(d_lowers[head]), halves(d_scores[head]))
        by_key = exact(d_both, key, 1, 0)
        d_query = by_key[GROUP_ROWS:] * HEAD_DIM**-0.5
        from_lower = by_key[:GROUP_ROWS]
        weighted = stacked(halves(key * strength), halves(query_unit * HEAD_DIM**-0.5))
        d_key = strength * from_lower + exact(d_both, weighted, 0, 0)
        d_strength = along(d_inner[head] * active[2] + from_lower * key)
        d_value = d_inner[head] * strength
        d_opening = d_strength * (opening * (1.0 - opening)) * tile.live
        d_beta = d_beta + jnp.where(tile.col == head, d_opening, 0.0)
        d_active = [
            (d_query - query_unit * along(query_unit * d_query)) * query_scale,
            (d_key - key * along(key * d_key)) * key_scale,
            d_value,
        ]
        for section in range(3):
            columns = head_columns(width, section, head)
            taps = [param_ref[offset : offset + 1, columns] for offset in range(KERNEL)]
            slope = opened[section] * (1.0 + convolved[section] * (1.0 - opened[section]))
            d_convolved = d_active[section] * slope
            d_pre = d_convolved * taps[0]
            sums = [jnp.sum(d_convolved * pres[section], 0, keepdims=True)]
            for offset in range(1, KERNEL):
                d_pre = d_pre + tile.later(d_convolved, offset) * taps[offset]
                sums.append(
                    jnp.sum(d_convolved * tile.earlier(pres[section], offset), 0, keepdims=True)
                )
            d_param_ref[0:KERNEL, columns] += jnp.concatenate(sums, 0)
            d_pre_ref[:, columns] = d_pre.astype(bf)
    d_pre_ref[:, 4 * width :] = d_beta.astype(bf)


NO_COST = pl.CostEstimate(flops=0, bytes_accessed=0, transcendentals=0)


def call(kernel, operands, in_specs, out_specs, out_shape, grid=(), scratch=()):
    results = pl.pallas_call(
        kernel,
        grid=grid,
        in_specs=in_specs,
        out_specs=out_specs,
        out_shape=out_shape,
        scratch_shapes=scratch,
        compiler_params=pltpu.CompilerParams(
            dimension_semantics=("arbitrary",) * len(grid), vmem_limit_bytes=48 * 2**20
        ),
        cost_estimate=NO_COST,
    )(*operands)
    return list(results)


def whole(array):
    return pl.BlockSpec(array.shape, lambda *step: (0,) * len(array.shape))


def mixer_specs(width):
    wide = 4 * width + SMALL
    heads = width // HEAD_DIM
    layout = pl.BlockSpec(memory_space=pltpu.SMEM)
    pre = pl.BlockSpec((GROUP_ROWS, wide), lambda group: (group, 0))
    param = pl.BlockSpec((2 * KERNEL, 3 * width), lambda group: (0, 0))
    narrow = pl.BlockSpec((GROUP_ROWS, width), lambda group: (group, 0))
    square = pl.BlockSpec((heads, GROUP_ROWS, HEAD_DIM), lambda group: (group, 0, 0))
    return layout, pre, param, narrow, square


def mixer_forward(layout, pre, params, width):
    groups = layout.shape[0]
    layout_spec, pre_spec, param_spec, narrow, square = mixer_specs(width)
    squares = jax.ShapeDtypeStruct((groups * width // HEAD_DIM, GROUP_ROWS, HEAD_DIM), f32)
    return call(
        mixer_forward_kernel,
        [layout, pre, params],
        [layout_spec, pre_spec, param_spec],
        [narrow] + [square] * 4,
        [jax.ShapeDtypeStruct((groups * GROUP_ROWS, width), bf)] + [squares] * 4,
        (groups,),
    )


def mixer_backward(layout, pre, params, weight, d_mixed, kept, width):
    groups = layout.shape[0]
    layout_spec, pre_spec, param_spec, _, square = mixer_specs(width)
    return call(
        mixer_backward_kernel,
        [layout, pre, params, weight, *kept, *d_mixed],
        [layout_spec, pre_spec, param_spec, whole(weight)]
        + [square] * 4
        + [whole(block) for block in d_mixed],
        [pre_spec, param_spec],
        [jax.ShapeDtypeStruct(pre.shape, bf), jax.ShapeDtypeStruct(params.shape, f32)],
        (groups,),
        [pltpu.VMEM((GROUP_ROWS, width), f32)],
    )


def first_kernel(gain_ref, weight_ref, *refs):
    *value_refs, normed_ref, out_ref, scale_ref, total_ref = refs
    step, depth = pl.program_id(0), weight_ref.shape[0]

    @pl.when(step == 0)
    def _():
        for group, ref in enumerate(value_refs):
            values = ref[...].astype(f32)
            scale = lax.rsqrt(jnp.mean(values * values, -1, keepdims=True) + 1e-06)
            rows = pl.ds(group * GROUP_ROWS, GROUP_ROWS)
            scale_ref[rows, :] = jnp.broadcast_to(scale, (GROUP_ROWS, 128))
        total_ref[...] = jnp.zeros_like(total_ref)

    columns = pl.ds(pl.multiple_of(step * depth, depth), depth)
    for group, ref in enumerate(value_refs):
        rows = pl.ds(group * GROUP_ROWS, GROUP_ROWS)
        values = ref[:, columns].astype(f32) * scale_ref[rows, :1] * gain_ref[...]
        normed_ref[rows, :] = values.astype(bf)
    total_ref[...] += plain_product(normed_ref[...], weight_ref[...])

    @pl.when(step == pl.num_programs(0) - 1)
    def _():
        out_ref[...] = total_ref[...]


def normed_product(blocks, gain, weight, depth=512):
    rows, (features, columns) = len(blocks) * GROUP_ROWS, weight.shape
    return call(
        first_kernel,
        [gain, weight, *blocks],
        [
            pl.BlockSpec((1, depth), lambda step: (0, step)),
            pl.BlockSpec((depth, columns), lambda step: (step, 0)),
        ]
        + [whole(block) for block in blocks],
        [
            pl.BlockSpec((rows, depth), lambda step: (0, step)),
            pl.BlockSpec((rows, columns), lambda step: (0, 0)),
        ],
        [
            jax.ShapeDtypeStruct((rows, features), bf),
            jax.ShapeDtypeStruct((rows, columns), f32),
        ],
        (features // depth,),
        [pltpu.VMEM((rows, 128), f32), pltpu.VMEM((rows, columns), f32)],
    )


def product_blocks(left, right, transposed=False, block=512):
    product = transposed_product if transposed else plain_product
    columns = right.shape[0] if transposed else right.shape[1]
    groups = left.shape[0] // GROUP_ROWS

    def kernel(left_ref, right_ref, *out_refs):
        total = product(left_ref[...], right_ref[...])
        for group, ref in enumerate(out_refs):
            ref[...] = total[group * GROUP_ROWS : (group + 1) * GROUP_ROWS].astype(ref.dtype)

    if transposed:
        right_spec = pl.BlockSpec((block, right.shape[1]), lambda step: (step, 0))
    else:
        right_spec = pl.BlockSpec((right.shape[0], block), lambda step: (0, step))
    return call(
        kernel,
        [left, right],
        [whole(left), right_spec],
        [pl.BlockSpec((GROUP_ROWS, block), lambda step: (0, step))] * groups,
        [
            jax.ShapeDtypeStruct((GROUP_ROWS, columns), bf if group else f32)
            for group in range(groups)
        ],
        (columns // block,),
    )


def grad_product(left, right, block=256):
    rows, features = left.shape
    if features % block:
        block = 128

    def kernel(left_ref, right_ref, out_ref):
        out_ref[...] = rows_product(left_ref[...], right_ref[...]).astype(bf)

    return call(
        kernel,
        [left, right],
        [pl.BlockSpec((rows, block), lambda step: (0, step)), whole(right)],
        [pl.BlockSpec((block, right.shape[1]), lambda step: (step, 0))],
        [jax.ShapeDtypeStruct((features, right.shape[1]), bf)],
        (features // block,),
    )[0]


def tie_all(values, *others):
    anywhere = pl.BlockSpec(memory_space=pl.ANY)
    tied = pl.pallas_call(
        lambda *refs: None,
        in_specs=[anywhere] * (len(values) + len(others)),
        out_specs=[anywhere] * len(values),
        out_shape=[jax.ShapeDtypeStruct(value.shape, value.dtype) for value in values],
        input_output_aliases={i: i for i in range(len(values))},
        cost_estimate=NO_COST,
    )(*values, *others)
    return list(tied)


def tie(value, *others):
    return tie_all([value], *others)[0]


def assemble(part, values, received, others):
    parts = values.shape[0]

    def kernel(part_ref, values_ref, *refs):
        own = part_ref[0]
        out_ref = refs[-1]
        out_ref[own] = values_ref[own]
        for step in range(1, parts):
            out_ref[lax.rem(own + parts - step, parts)] = refs[step - 1][...]

    vmem = pl.BlockSpec(memory_space=pltpu.VMEM)
    anywhere = pl.BlockSpec(memory_space=pl.ANY)
    return pl.pallas_call(
        kernel,
        in_specs=[pl.BlockSpec(memory_space=pltpu.SMEM)]
        + [vmem] * parts
        + [anywhere] * len(others),
        out_specs=vmem,
        out_shape=jax.ShapeDtypeStruct(values.shape, values.dtype),
        compiler_params=pltpu.CompilerParams(vmem_limit_bytes=32 * 2**20),
        cost_estimate=NO_COST,
    )(part.reshape(1).astype(jnp.int32), values, *received, *others)


def copy_columns(*refs):
    *sources, target = refs
    start = 0
    for source in sources:
        block = source[...].reshape(source.shape[-2:])
        columns = pl.ds(start, block.shape[1])
        if len(target.shape) == 3:
            target[0, :, columns] = block.astype(target.dtype)
        else:
            target[:, columns] = block.astype(target.dtype)
        start += block.shape[1]


def to_parts(sources, parts, dtype):
    rows = sources[0][0].shape[0]

    def spec(section, width):
        return pl.BlockSpec((rows, width), lambda p: (0, section * parts + p))

    total = sum(width for _, _, width in sources)
    return pl.pallas_call(
        copy_columns,
        grid=(parts,),
        in_specs=[spec(section, width) for _, section, width in sources],
        out_specs=pl.BlockSpec((1, rows, total), lambda p: (p, 0, 0)),
        out_shape=jax.ShapeDtypeStruct((parts, rows, total), dtype),
    )(*[array for array, _, _ in sources])


def updown_from_parts(slabs):
    parts, rows, width = slabs.shape
    units = width // 2

    def kernel(slabs_ref, out_ref):
        for p in range(parts):
            out_ref[:, p * units : (p + 1) * units] = slabs_ref[p].astype(f32)

    return pl.pallas_call(
        kernel,
        grid=(2,),
        in_specs=[pl.BlockSpec((parts, rows, units), lambda half: (0, 0, half))],
        out_specs=pl.BlockSpec((rows, parts * units), lambda half: (0, half)),
        out_shape=jax.ShapeDtypeStruct((rows, parts * width), f32),
        compiler_params=pltpu.CompilerParams(vmem_limit_bytes=32 * 2**20),
        cost_estimate=NO_COST,
    )(slabs)


def mixer_from_parts(slabs, width):
    parts, rows, _ = slabs.shape

    def kernel(slabs_ref, qkv_ref, gate_ref, strength_ref):
        for p in range(parts):
            for section in range(4):
                block = slabs_ref[p, :, section * width : (section + 1) * width].astype(f32)
                if section < 3:
                    start = (section * parts + p) * width
                    qkv_ref[:, start : start + width] = block
                else:
                    gate_ref[:, p * width : (p + 1) * width] = block
            last = slabs_ref[p, :, 4 * width :].astype(f32)
            strength_ref[:, p * SMALL : (p + 1) * SMALL] = last

    widths = [3 * parts * width, parts * width, parts * SMALL]
    return pl.pallas_call(
        kernel,
        out_shape=[jax.ShapeDtypeStruct((rows, size), f32) for size in widths],
        compiler_params=pltpu.CompilerParams(vmem_limit_bytes=32 * 2**20),
        cost_estimate=NO_COST,
    )(slabs)


def total_of(own_ref, received_refs):
    total = own_ref[...]
    for ref in received_refs:
        total = total + ref[...].astype(f32)
    return total


def row_scale(values):
    return lax.rsqrt(jnp.mean(values * values, -1, keepdims=True) + 1e-06)


def norm_slope(values, scale, gain, grad):
    mean = jnp.mean(gain * grad * values, -1, keepdims=True)
    return scale * gain * grad - values * (scale * scale * scale * mean)


def hidden_kernel(own_ref, *refs):
    *received, input_ref, gain_ref, hidden_ref, normed_ref = refs
    hidden = input_ref[...].astype(f32) + total_of(own_ref, received)
    hidden_ref[...] = hidden
    normed_ref[...] = (hidden * row_scale(hidden) * gain_ref[...]).astype(bf)


def hidden_back_kernel(own_ref, *refs):
    *received, hidden_ref, gain_ref, cot_ref, d_hidden_ref, d_mixed_ref, d_gain_ref = refs
    grad = total_of(own_ref, received)
    hidden = hidden_ref[...]
    scale = row_scale(hidden)

    @pl.when(pl.program_id(0) == 0)
    def _():
        d_gain_ref[...] = jnp.zeros_like(d_gain_ref)

    d_gain_ref[...] += jnp.sum(grad * hidden * scale, 0, keepdims=True)
    d_hidden = cot_ref[...].astype(f32) + norm_slope(hidden, scale, gain_ref[...], grad)
    d_hidden_ref[...] = d_hidden
    d_mixed_ref[...] = d_hidden.astype(bf)


def input_back_kernel(own_ref, *refs):
    *received, input_ref, gain_ref, d_hidden_ref, out_ref = refs
    grad = total_of(own_ref, received)
    values = input_ref[...].astype(f32)
    slope = norm_slope(values, row_scale(values), gain_ref[...], grad)
    out_ref[...] = (d_hidden_ref[...] + slope).astype(bf)


def block_out_kernel(own_ref, *refs):
    *received, hidden_ref, out_ref = refs
    out_ref[...] = (hidden_ref[...] + total_of(own_ref, received)).astype(bf)


def by_rows(kernel, arrays, outs, block=32):
    def spec(shape):
        if shape[0] == 1:
            return pl.BlockSpec(shape, lambda i: (0, 0))
        return pl.BlockSpec((block, shape[1]), lambda i: (i, 0))

    return pl.pallas_call(
        kernel,
        grid=(GROUP_ROWS // block,),
        in_specs=[spec(array.shape) for array in arrays],
        out_specs=[spec(shape) for shape, _ in outs],
        out_shape=[jax.ShapeDtypeStruct(shape, dtype) for shape, dtype in outs],
        compiler_params=pltpu.CompilerParams(dimension_semantics=("arbitrary",)),
        cost_estimate=NO_COST,
    )(*arrays)


def body(
    block_in,
    out_grad,
    norm1_gain,
    conv_weight,
    head_gain,
    qkv_weight,
    beta_weight,
    gate_weight,
    out_weight,
    norm2_gain,
    updown_weight,
    down_weight,
    seq_blocks,
    lead_blocks,
):
    devices = lax.axis_size("dp")
    parts = MODEL
    copies = devices // parts
    part = lax.axis_index("dp") // copies
    copy = lax.axis_index("dp") % copies
    rows_own = qkv_weight.shape[0]
    width = D // parts
    units = FF // parts
    heads_part = HEADS // parts
    wide = 4 * width + SMALL
    model_groups = [[m * copies + t for m in range(parts)] for t in range(copies)]
    copy_groups = [[m * copies + t for t in range(copies)] for m in range(parts)]

    def exchange(values):
        return lax.all_to_all(
            values, "dp", split_axis=0, concat_axis=0, axis_index_groups=model_groups, tiled=True
        )

    def shift(values, step):
        pairs = [
            (m * copies + t, (m + step) % parts * copies + t)
            for m in range(parts)
            for t in range(copies)
        ]
        return lax.ppermute(values, "dp", pairs)

    def exchange_apart(values, before, after=()):
        cut = [
            lax.dynamic_index_in_dim(values, (part + step) % parts, 0, keepdims=False)
            for step in range(1, parts)
        ]
        received = [shift(piece, step) for step, piece in enumerate(tie_all(cut, *before), 1)]
        return assemble(part, values, received, after)

    def gather_rows(values):
        return [values] + [shift(values, step) for step in range(1, parts)]

    def scatter_rows(terms):
        return [terms[0]] + [shift(block, -step) for step, block in enumerate(terms[1:], 1)]

    def gather_copies(values):
        return lax.all_gather(values, "dp", axis=0, axis_index_groups=copy_groups, tiled=True)

    def scatter_copies(values):
        return lax.psum_scatter(
            values.astype(bf),
            "dp",
            scatter_dimension=0,
            axis_index_groups=copy_groups,
            tiled=True,
        )

    def halve(values, bit, axis):
        pairs = [(i, i ^ (1 << bit)) for i in range(devices)]
        side = (copy >> bit) & 1
        own = lax.dynamic_index_in_dim(values, side, axis, keepdims=False)
        other = lax.dynamic_index_in_dim(values, 1 - side, axis, keepdims=False)
        return (own.astype(f32) + lax.ppermute(other, "dp", pairs).astype(f32)).astype(bf)

    by_halves = copies == 8

    def halve_cores(values):
        if not by_halves:
            return values
        rows, columns = values.shape
        return halve(values.reshape(2, 2, 2, rows // 8, columns), 0, 2)

    def halve_first(values):
        if not by_halves:
            return [values]
        middle = values.shape[-1] // 2
        return [halve(values[..., :middle], 1, 1), halve(values[..., middle:], 2, 0)]

    def halve_second(values):
        if not by_halves:
            return scatter_copies(values[0])
        return jnp.concatenate([halve(values[0], 2, 0), halve(values[1], 1, 0)], 1)

    def to_wire(values):
        return values.reshape(-1, parts, copies, rows_own).swapaxes(1, 2).reshape(-1, D)

    def from_wire(values):
        return values.reshape(-1, copies, parts, rows_own).swapaxes(1, 2).reshape(-1, D)

    w_out_own = to_wire(out_weight.astype(bf))
    w_out = gather_copies(w_out_own)
    strengths = beta_weight.reshape(rows_own, parts, heads_part)
    strengths = jnp.pad(strengths, ((0, 0), (0, 0), (0, SMALL - heads_part)))
    strengths = tie(strengths.reshape(rows_own, parts * SMALL), w_out_own)
    pieces = [(qkv_weight, section, width) for section in range(3)]
    pieces = to_parts(pieces + [(gate_weight, 0, width), (strengths, 0, SMALL)], parts, bf)
    mixer_pieces = tie(exchange(pieces), w_out)
    w_mixer = gather_copies(mixer_pieces.reshape(parts * rows_own, wide))
    inputs = tie(to_wire(block_in), mixer_pieces)
    input_rows = gather_rows(inputs)

    lanes = -(-3 * rows_own // 128) * 128
    numbers = jnp.concatenate([seq_blocks[0], lead_blocks]).astype(f32)
    small = [conv_weight.T, norm1_gain[None], head_gain[None], norm2_gain[None], numbers[None]]
    small = [jnp.pad(rows, ((0, 0), (0, lanes - rows.shape[1]))) for rows in small]
    small = jnp.pad(jnp.concatenate(small, 0).astype(bf), ((0, 2 * KERNEL), (0, 0)))
    small = jnp.broadcast_to(small[None], (devices,) + small.shape)
    small = lax.all_to_all(tie(small, inputs), "dp", 0, 0, tiled=True)
    taps = small[:, :KERNEL, : 3 * rows_own].swapaxes(0, 1).reshape(KERNEL, 3, parts, width)
    taps = lax.dynamic_index_in_dim(taps, part, 2, keepdims=False).reshape(KERNEL, 3 * width)
    gain_one, head_full, gain_two = (
        small[:, KERNEL + i, :rows_own].reshape(1, D).astype(f32) for i in range(3)
    )
    gain_one, gain_two = to_wire(gain_one), to_wire(gain_two)
    head_part = lax.dynamic_slice_in_dim(head_full, part * width, width, 1)
    params = jnp.concatenate([taps.astype(f32), jnp.pad(head_part, ((0, 0), (0, 2 * width)))], 0)
    params = jnp.pad(params, ((0, KERNEL - 1), (0, 0)))
    numbers = small[:, KERNEL + 3, :3].astype(f32).astype(jnp.int32)
    layouts = block_layouts(numbers[:, 0], numbers[:, 1], numbers[:, 2])
    layouts = layouts.reshape(parts, copies, 4)
    layouts = lax.dynamic_index_in_dim(layouts, copy, 1, keepdims=False)
    wanted = (part - jnp.arange(parts)) % parts
    wanted = (wanted[:, None] == jnp.arange(parts)).astype(f32)
    layouts = jnp.sum(wanted[:, :, None] * layouts, 1)

    pieces = [(updown_weight, half, units) for half in range(2)]
    updown_pieces = to_parts(pieces, parts, bf)
    w_down_own = to_wire(down_weight.astype(bf))
    w_down = gather_copies(tie(w_down_own, *input_rows[1:]))
    cotangent_own = to_wire(out_grad)

    gain_first = tie(gain_one, w_down_own, cotangent_own, updown_pieces)
    normed, pre = normed_product(input_rows, gain_first, w_mixer)
    mixed, *kept = mixer_forward(layouts, pre, params, width)
    updown_pieces = exchange_apart(updown_pieces, input_rows[1:] + [small], [mixed])
    w_updown = gather_copies(updown_pieces.reshape(parts * rows_own, 2 * units))
    stream = ((GROUP_ROWS, D), f32)
    narrow = ((GROUP_ROWS, D), bf)
    hidden, normed_two = by_rows(
        hidden_kernel,
        scatter_rows(product_blocks(mixed, w_out)) + [inputs, gain_two],
        [stream, narrow],
    )
    cotangent = jnp.concatenate(gather_rows(tie(cotangent_own, normed_two)), 0)
    normed_two = jnp.concatenate(gather_rows(normed_two), 0)

    def swiglu_units(updown):
        return jax.nn.silu(updown[:, :units]) * updown[:, units:]

    updown = plain_product(normed_two, w_updown)
    active, swiglu_back = jax.vjp(swiglu_units, updown)
    active = active.astype(bf)
    d_active = transposed_product(cotangent, w_down)
    d_updown = swiglu_back(d_active)[0].astype(bf)
    d_normed_two = product_blocks(d_updown, w_updown, transposed=True)
    updown_terms = grad_product(normed_two, tie(d_updown, *d_normed_two[1:]))
    active = tie(active, *d_normed_two[1:])
    down_terms = grad_product(active, tie(cotangent, updown_terms))
    d_hidden, d_mixed, gain_two_grad = by_rows(
        hidden_back_kernel,
        scatter_rows(d_normed_two) + [hidden, tie(gain_two, down_terms), cotangent_own],
        [stream, narrow, ((1, D), f32)],
    )

    updown_grad = scatter_copies(tie(updown_terms, d_mixed))

    out_terms = product_blocks(tie(active, d_mixed), w_down)
    down_grad = halve_cores(tie(down_terms, d_mixed))
    d_mixed = gather_rows(d_mixed)
    late = tie(params, down_grad, *out_terms)
    d_pre, d_params = mixer_backward(layouts, pre, late, w_out, d_mixed, kept, width)
    mixer_terms = tie(grad_product(normed, d_pre), updown_grad)
    mixer_grad = scatter_copies(mixer_terms)

    d_normed_terms = product_blocks(tie(d_pre, mixer_terms), w_mixer, transposed=True)
    out_terms[1:] = tie_all(out_terms[1:], *d_normed_terms[1:])
    d_normed, block_out = scatter_rows(d_normed_terms), scatter_rows(out_terms)
    gain_one_grad = 0.0
    for values, terms in zip(input_rows, d_normed_terms):
        values = values.astype(f32)
        terms = terms.astype(f32) * (values * row_scale(values))
        gain_one_grad = gain_one_grad + jnp.sum(terms, 0, keepdims=True)

    here = (jnp.arange(parts) == part).astype(f32)[:, None]
    taps_grad = d_params[:KERNEL].reshape(KERNEL, 3, 1, width) * here
    taps_grad = taps_grad.reshape(KERNEL, parts, copies, 3, rows_own).transpose(1, 2, 3, 0, 4)
    taps_grad = taps_grad.reshape(devices, 3 * KERNEL, rows_own)
    head_grad = (d_params[KERNEL, :width] * here).reshape(devices, 1, rows_own)
    gain_grads = [
        grad.reshape(copies, parts, 1, rows_own).swapaxes(0, 1).reshape(devices, 1, rows_own)
        for grad in (gain_one_grad, gain_two_grad)
    ]
    small_grad = jnp.concatenate([taps_grad, head_grad] + gain_grads, 1)
    small_grad = jnp.pad(small_grad, ((0, 0), (0, 1), (0, 128 - rows_own)))
    small_grad = jnp.sum(lax.all_to_all(small_grad, "dp", 0, 0, tiled=True), 0)[:, :rows_own]
    taps_shard = small_grad[: 3 * KERNEL].reshape(3, KERNEL, rows_own).swapaxes(1, 2)
    taps_shard = taps_shard.reshape(3 * rows_own, KERNEL)
    head_shard, gain_one_shard, gain_two_shard = small_grad[3 * KERNEL : 3 * KERNEL + 3]

    (input_grad,) = by_rows(input_back_kernel, d_normed + [inputs, gain_one, d_hidden], [narrow])
    updown_grad = updown_grad.reshape(parts, rows_own, 2 * units)
    updown_shard = updown_from_parts(exchange_apart(updown_grad, d_normed_terms[1:], [input_grad]))
    hidden = tie(hidden, input_grad)
    (block_out,) = by_rows(block_out_kernel, block_out + [hidden], [narrow])
    out_shard = grad_product(tie(mixed, input_grad), jnp.concatenate(d_mixed, 0))
    out_shard = halve_second(halve_first(halve_cores(out_shard)))
    out_shard = from_wire(out_shard.astype(f32))
    down_shard = halve_second(halve_first(tie(down_grad, input_grad)))
    down_shard = from_wire(down_shard.astype(f32))
    mixer_grad = exchange(mixer_grad.reshape(parts, rows_own, wide))
    qkv_shard, gate_shard, strengths = mixer_from_parts(mixer_grad, width)
    beta_shard = strengths.reshape(rows_own, parts, SMALL)[:, :, :heads_part]
    return (
        from_wire(block_out),
        from_wire(input_grad),
        gain_one_shard,
        taps_shard,
        head_shard,
        qkv_shard,
        beta_shard.reshape(rows_own, HEADS),
        gate_shard,
        out_shard,
        gain_two_shard,
        updown_shard,
        down_shard,
    )


def solution(mesh):
    placed = (
        P("dp", None),
        P("dp", None),
        P("dp"),
        P("dp", None),
        P("dp"),
        P("dp", None),
        P("dp", None),
        P("dp", None),
        P("dp", None),
        P("dp"),
        P("dp", None),
        P("dp", None),
        P("dp", None),
        P("dp"),
    )
    return jax.shard_map(
        body,
        mesh=mesh,
        in_specs=placed,
        out_specs=(
            P("dp", None),
            P("dp", None),
            P("dp"),
            P("dp", None),
            P("dp"),
            P("dp", None),
            P("dp", None),
            P("dp", None),
            P("dp", None),
            P("dp"),
            P("dp", None),
            P("dp", None),
        ),
        check_vma=False,
    )
```

```python
import jax
import jax.numpy as jnp
from jax import lax
from jax.experimental import pallas as pl
from jax.experimental.pallas import tpu as pltpu
from jax.sharding import PartitionSpec as P

D = 2048
HEADS = 16
HEAD_DIM = 128
FF = 5632
KERNEL = 4
BLOCK_ROWS = 64
BLOCKS_DEV = 2
GROUP_ROWS = BLOCK_ROWS * BLOCKS_DEV
SMALL = 128
MODEL = 4

f32 = jnp.float32
bf = jnp.bfloat16


def block_layouts(first, second, lead):
    def doc(block):
        in_first = (block >= lead) & (block < lead + first)
        in_second = (block >= lead + first) & (block < lead + first + second)
        return jnp.where(in_first, 1, jnp.where(in_second, 2, 0))

    starts = (lead == 1) | (lead + first == 1) & (second > 0)
    columns = [doc(0) > 0, doc(1) > 0, doc(0) == doc(1), ~starts]
    return jnp.stack(columns, 1).astype(f32)


def plain_product(left, right):
    return jnp.dot(left, right, preferred_element_type=f32)


def rows_product(left, right):
    return lax.dot_general(left, right, (((0,), (0,)), ((), ())), preferred_element_type=f32)


def transposed_product(left, right):
    return lax.dot_general(left, right, (((1,), (1,)), ((), ())), preferred_element_type=f32)


def halves(values):
    high = values.astype(bf)
    return high, (values - high.astype(f32)).astype(bf)


def exact(left, right, left_dim, right_dim):
    left_high, left_low = left if isinstance(left, tuple) else halves(left)
    right_high, right_low = right if isinstance(right, tuple) else halves(right)
    return lax.dot_general(
        jnp.concatenate([left_high, left_high, left_low], left_dim),
        jnp.concatenate([right_high, right_low, right_high], right_dim),
        (((left_dim,), (right_dim,)), ((), ())),
        preferred_element_type=f32,
    )


def stacked(first, second):
    return tuple(jnp.concatenate([a, b], 0) for a, b in zip(first, second))


class Tile:
    def __init__(self, layout_ref, group):
        live_first, live_second, same, persist = (layout_ref[group, i] for i in range(4))
        shape = (GROUP_ROWS, HEAD_DIM)
        row = lax.broadcasted_iota(jnp.int32, shape, 0)
        col = lax.broadcasted_iota(jnp.int32, shape, 1)
        late = row >= BLOCK_ROWS
        self.row, self.col = row, col
        self.live = jnp.where(late, live_second, live_first)
        self.taps = [None] + [
            jnp.where(
                row < offset,
                0.0,
                jnp.where(late & (row < BLOCK_ROWS + offset), same, 1.0),
            )
            for offset in range(1, KERNEL)
        ]
        cross = jnp.where(late & (col < BLOCK_ROWS), persist, 1.0)
        self.lower = jnp.where(row > col, cross, 0.0)
        self.lower_full = jnp.where(row >= col, cross, 0.0)

    def earlier(self, values, offset):
        return pltpu.roll(values, offset, 0) * self.taps[offset]

    def later(self, values, offset):
        return pltpu.roll(values * self.taps[offset], GROUP_ROWS - offset, 0)


def convolve(tile, values, taps):
    total = values * taps[0]
    for offset in range(1, KERNEL):
        total = total + tile.earlier(values, offset) * taps[offset]
    return total


def unit_scale(values):
    return lax.rsqrt(jnp.sum(values * values, -1, keepdims=True) + 1e-06)


def head_columns(part_width, section, head):
    return pl.ds(section * part_width + head * HEAD_DIM, HEAD_DIM)


def unit_inverses(tile, lowers):
    eye = jnp.where(tile.row == tile.col, 1.0, 0.0)
    inverses = None
    size = 1
    while size < GROUP_ROWS:
        pair = tile.row // (2 * size) == tile.col // (2 * size)
        split = pair & (tile.row // size != tile.col // size)
        parts = [jnp.where(split, lower, 0.0) for lower in lowers]
        if inverses is None:
            inverses = [eye - part for part in parts]
        else:
            kept = [halves(inverse) for inverse in inverses]
            inner = [exact(part, known, 1, 0) for part, known in zip(parts, kept)]
            outer = [exact(known, value, 1, 0) for known, value in zip(kept, inner)]
            inverses = [inverse - value for inverse, value in zip(inverses, outer)]
        size *= 2
    return inverses


def mixer_forward_kernel(
    layout_ref, pre_ref, param_ref, mixed_ref, inverse_ref, score_ref, solved_ref, out_ref
):
    width = mixed_ref.shape[1]
    heads = range(width // HEAD_DIM)
    tile = Tile(layout_ref, pl.program_id(0))
    queries, keys, values, strengths = [], [], [], []
    for head in heads:
        parts = []
        for section in range(3):
            columns = head_columns(width, section, head)
            taps = [param_ref[offset : offset + 1, columns] for offset in range(KERNEL)]
            convolved = convolve(tile, pre_ref[:, columns], taps)
            parts.append(convolved * jax.nn.sigmoid(convolved))
        queries.append(parts[0] * (unit_scale(parts[0]) * HEAD_DIM**-0.5))
        keys.append(parts[1] * unit_scale(parts[1]))
        values.append(parts[2])
        start = 4 * width + head
        strengths.append(jax.nn.sigmoid(pre_ref[:, start : start + 1]) * tile.live)
    lowers, scores = [], []
    for head in heads:
        key_halves = halves(keys[head])
        both = exact(stacked(key_halves, halves(queries[head])), key_halves, 1, 1)
        lowers.append(both[:GROUP_ROWS] * strengths[head] * tile.lower)
        scores.append(both[GROUP_ROWS:] * tile.lower_full)
    inverses = unit_inverses(tile, lowers)
    solved = [exact(inverses[head], values[head] * strengths[head], 1, 0) for head in heads]
    outs = [exact(scores[head], solved[head], 1, 0) for head in heads]
    for head in heads:
        out = outs[head]
        scaled = out * lax.rsqrt(jnp.mean(out * out, -1, keepdims=True) + 1e-05)
        gate = pre_ref[:, head_columns(width, 3, head)]
        gain = param_ref[KERNEL : KERNEL + 1, head_columns(width, 0, head)]
        mixed = scaled * gain * (gate * jax.nn.sigmoid(gate)) * tile.live
        mixed_ref[:, head_columns(width, 0, head)] = mixed.astype(bf)
        inverse_ref[head] = inverses[head]
        score_ref[head] = scores[head]
        solved_ref[head] = solved[head]
        out_ref[head] = out


def mixer_backward_kernel(
    layout_ref,
    pre_ref,
    param_ref,
    weight_ref,
    inverse_ref,
    score_ref,
    solved_ref,
    out_ref,
    *refs,
):
    *mixed_refs, d_pre_ref, d_param_ref, grad_ref = refs
    width = grad_ref.shape[1]
    heads = range(width // HEAD_DIM)
    tile = Tile(layout_ref, pl.program_id(0))
    for group, mixed_ref in enumerate(mixed_refs):

        @pl.when(pl.program_id(0) == group)
        def _():
            grad_ref[...] = transposed_product(mixed_ref[...], weight_ref[...])

    @pl.when(pl.program_id(0) == 0)
    def _():
        d_param_ref[...] = jnp.zeros_like(d_param_ref)

    def along(values):
        return jnp.sum(values, -1, keepdims=True)

    d_outs = []
    for head in heads:
        columns = head_columns(width, 0, head)
        d_mixed = grad_ref[:, columns] * tile.live
        out = out_ref[head]
        scale = lax.rsqrt(jnp.mean(out * out, -1, keepdims=True) + 1e-05)
        scaled = out * scale
        gate = pre_ref[:, head_columns(width, 3, head)]
        gate_open = jax.nn.sigmoid(gate)
        gain = param_ref[KERNEL : KERNEL + 1, columns]
        gated = d_mixed * (gate * gate_open)
        d_param_ref[KERNEL : KERNEL + 1, columns] += jnp.sum(gated * scaled, 0, keepdims=True)
        d_gate = d_mixed * scaled * gain * (gate_open * (1.0 + gate * (1.0 - gate_open)))
        d_pre_ref[:, head_columns(width, 3, head)] = d_gate.astype(bf)
        d_scaled = gated * gain
        mean = jnp.mean(d_scaled * out, -1, keepdims=True)
        d_outs.append(scale * d_scaled - out * (scale * scale * scale * mean))
    d_out_halves = [halves(value) for value in d_outs]
    solved_halves = [halves(solved_ref[head]) for head in heads]
    d_solved = [exact(score_ref[head], d_out_halves[head], 0, 0) for head in heads]
    d_scores = [
        exact(d_out_halves[head], solved_halves[head], 1, 1) * tile.lower_full for head in heads
    ]
    d_inner = [exact(inverse_ref[head], d_solved[head], 0, 0) for head in heads]
    d_lowers = [exact(d_inner[head], solved_halves[head], 1, 1) * -tile.lower for head in heads]
    d_beta = jnp.zeros((GROUP_ROWS, SMALL), f32)
    for head in heads:
        pres, convolved, opened, active = [], [], [], []
        for section in range(3):
            columns = head_columns(width, section, head)
            taps = [param_ref[offset : offset + 1, columns] for offset in range(KERNEL)]
            pres.append(pre_ref[:, columns])
            convolved.append(convolve(tile, pres[section], taps))
            opened.append(jax.nn.sigmoid(convolved[section]))
            active.append(convolved[section] * opened[section])
        query_scale = unit_scale(active[0])
        key_scale = unit_scale(active[1])
        query_unit = active[0] * query_scale
        key = active[1] * key_scale
        start = 4 * width + head
        opening = jax.nn.sigmoid(pre_ref[:, start : start + 1])
        strength = opening * tile.live
        d_both = stacked(halves(d_lowers[head]), halves(d_scores[head]))
        by_key = exact(d_both, key, 1, 0)
        d_query = by_key[GROUP_ROWS:] * HEAD_DIM**-0.5
        from_lower = by_key[:GROUP_ROWS]
        weighted = stacked(halves(key * strength), halves(query_unit * HEAD_DIM**-0.5))
        d_key = strength * from_lower + exact(d_both, weighted, 0, 0)
        d_strength = along(d_inner[head] * active[2] + from_lower * key)
        d_value = d_inner[head] * strength
        d_opening = d_strength * (opening * (1.0 - opening)) * tile.live
        d_beta = d_beta + jnp.where(tile.col == head, d_opening, 0.0)
        d_active = [
            (d_query - query_unit * along(query_unit * d_query)) * query_scale,
            (d_key - key * along(key * d_key)) * key_scale,
            d_value,
        ]
        for section in range(3):
            columns = head_columns(width, section, head)
            taps = [param_ref[offset : offset + 1, columns] for offset in range(KERNEL)]
            slope = opened[section] * (1.0 + convolved[section] * (1.0 - opened[section]))
            d_convolved = d_active[section] * slope
            d_pre = d_convolved * taps[0]
            sums = [jnp.sum(d_convolved * pres[section], 0, keepdims=True)]
            for offset in range(1, KERNEL):
                d_pre = d_pre + tile.later(d_convolved, offset) * taps[offset]
                sums.append(
                    jnp.sum(d_convolved * tile.earlier(pres[section], offset), 0, keepdims=True)
                )
            d_param_ref[0:KERNEL, columns] += jnp.concatenate(sums, 0)
            d_pre_ref[:, columns] = d_pre.astype(bf)
    d_pre_ref[:, 4 * width :] = d_beta.astype(bf)


NO_COST = pl.CostEstimate(flops=0, bytes_accessed=0, transcendentals=0)


def call(kernel, operands, in_specs, out_specs, out_shape, grid=(), scratch=()):
    results = pl.pallas_call(
        kernel,
        grid=grid,
        in_specs=in_specs,
        out_specs=out_specs,
        out_shape=out_shape,
        scratch_shapes=scratch,
        compiler_params=pltpu.CompilerParams(
            dimension_semantics=("arbitrary",) * len(grid), vmem_limit_bytes=48 * 2**20
        ),
        cost_estimate=NO_COST,
    )(*operands)
    return list(results)


def whole(array):
    return pl.BlockSpec(array.shape, lambda *step: (0,) * len(array.shape))


def mixer_specs(width):
    wide = 4 * width + SMALL
    heads = width // HEAD_DIM
    layout = pl.BlockSpec(memory_space=pltpu.SMEM)
    pre = pl.BlockSpec((GROUP_ROWS, wide), lambda group: (group, 0))
    param = pl.BlockSpec((2 * KERNEL, 3 * width), lambda group: (0, 0))
    narrow = pl.BlockSpec((GROUP_ROWS, width), lambda group: (group, 0))
    square = pl.BlockSpec((heads, GROUP_ROWS, HEAD_DIM), lambda group: (group, 0, 0))
    return layout, pre, param, narrow, square


def mixer_forward(layout, pre, params, width):
    groups = layout.shape[0]
    layout_spec, pre_spec, param_spec, narrow, square = mixer_specs(width)
    squares = jax.ShapeDtypeStruct((groups * width // HEAD_DIM, GROUP_ROWS, HEAD_DIM), f32)
    return call(
        mixer_forward_kernel,
        [layout, pre, params],
        [layout_spec, pre_spec, param_spec],
        [narrow] + [square] * 4,
        [jax.ShapeDtypeStruct((groups * GROUP_ROWS, width), bf)] + [squares] * 4,
        (groups,),
    )


def mixer_backward(layout, pre, params, weight, d_mixed, kept, width):
    groups = layout.shape[0]
    layout_spec, pre_spec, param_spec, _, square = mixer_specs(width)
    return call(
        mixer_backward_kernel,
        [layout, pre, params, weight, *kept, *d_mixed],
        [layout_spec, pre_spec, param_spec, whole(weight)]
        + [square] * 4
        + [whole(block) for block in d_mixed],
        [pre_spec, param_spec],
        [jax.ShapeDtypeStruct(pre.shape, bf), jax.ShapeDtypeStruct(params.shape, f32)],
        (groups,),
        [pltpu.VMEM((GROUP_ROWS, width), f32)],
    )


def first_kernel(gain_ref, weight_ref, *refs):
    *value_refs, normed_ref, out_ref, scale_ref, total_ref = refs
    step, depth = pl.program_id(0), weight_ref.shape[0]

    @pl.when(step == 0)
    def _():
        for group, ref in enumerate(value_refs):
            values = ref[...].astype(f32)
            scale = lax.rsqrt(jnp.mean(values * values, -1, keepdims=True) + 1e-06)
            rows = pl.ds(group * GROUP_ROWS, GROUP_ROWS)
            scale_ref[rows, :] = jnp.broadcast_to(scale, (GROUP_ROWS, 128))
        total_ref[...] = jnp.zeros_like(total_ref)

    columns = pl.ds(pl.multiple_of(step * depth, depth), depth)
    for group, ref in enumerate(value_refs):
        rows = pl.ds(group * GROUP_ROWS, GROUP_ROWS)
        values = ref[:, columns].astype(f32) * scale_ref[rows, :1] * gain_ref[...]
        normed_ref[rows, :] = values.astype(bf)
    total_ref[...] += plain_product(normed_ref[...], weight_ref[...])

    @pl.when(step == pl.num_programs(0) - 1)
    def _():
        out_ref[...] = total_ref[...]


def normed_product(blocks, gain, weight, depth=512):
    rows, (features, columns) = len(blocks) * GROUP_ROWS, weight.shape
    return call(
        first_kernel,
        [gain, weight, *blocks],
        [
            pl.BlockSpec((1, depth), lambda step: (0, step)),
            pl.BlockSpec((depth, columns), lambda step: (step, 0)),
        ]
        + [whole(block) for block in blocks],
        [
            pl.BlockSpec((rows, depth), lambda step: (0, step)),
            pl.BlockSpec((rows, columns), lambda step: (0, 0)),
        ],
        [
            jax.ShapeDtypeStruct((rows, features), bf),
            jax.ShapeDtypeStruct((rows, columns), f32),
        ],
        (features // depth,),
        [pltpu.VMEM((rows, 128), f32), pltpu.VMEM((rows, columns), f32)],
    )


def product_blocks(left, right, transposed=False, block=512):
    product = transposed_product if transposed else plain_product
    columns = right.shape[0] if transposed else right.shape[1]
    groups = left.shape[0] // GROUP_ROWS

    def kernel(left_ref, right_ref, *out_refs):
        total = product(left_ref[...], right_ref[...])
        for group, ref in enumerate(out_refs):
            ref[...] = total[group * GROUP_ROWS : (group + 1) * GROUP_ROWS].astype(ref.dtype)

    if transposed:
        right_spec = pl.BlockSpec((block, right.shape[1]), lambda step: (step, 0))
    else:
        right_spec = pl.BlockSpec((right.shape[0], block), lambda step: (0, step))
    return call(
        kernel,
        [left, right],
        [whole(left), right_spec],
        [pl.BlockSpec((GROUP_ROWS, block), lambda step: (0, step))] * groups,
        [
            jax.ShapeDtypeStruct((GROUP_ROWS, columns), bf if group else f32)
            for group in range(groups)
        ],
        (columns // block,),
    )


def grad_product(left, right, block=256):
    rows, features = left.shape
    if features % block:
        block = 128

    def kernel(left_ref, right_ref, out_ref):
        out_ref[...] = rows_product(left_ref[...], right_ref[...]).astype(bf)

    return call(
        kernel,
        [left, right],
        [pl.BlockSpec((rows, block), lambda step: (0, step)), whole(right)],
        [pl.BlockSpec((block, right.shape[1]), lambda step: (step, 0))],
        [jax.ShapeDtypeStruct((features, right.shape[1]), bf)],
        (features // block,),
    )[0]


def tie_all(values, *others):
    anywhere = pl.BlockSpec(memory_space=pl.ANY)
    tied = pl.pallas_call(
        lambda *refs: None,
        in_specs=[anywhere] * (len(values) + len(others)),
        out_specs=[anywhere] * len(values),
        out_shape=[jax.ShapeDtypeStruct(value.shape, value.dtype) for value in values],
        input_output_aliases={i: i for i in range(len(values))},
        cost_estimate=NO_COST,
    )(*values, *others)
    return list(tied)


def tie(value, *others):
    return tie_all([value], *others)[0]


def assemble(part, values, received, others):
    parts = values.shape[0]

    def kernel(part_ref, values_ref, *refs):
        own = part_ref[0]
        out_ref = refs[-1]
        out_ref[own] = values_ref[own]
        for step in range(1, parts):
            out_ref[lax.rem(own + parts - step, parts)] = refs[step - 1][...]

    vmem = pl.BlockSpec(memory_space=pltpu.VMEM)
    anywhere = pl.BlockSpec(memory_space=pl.ANY)
    return pl.pallas_call(
        kernel,
        in_specs=[pl.BlockSpec(memory_space=pltpu.SMEM)]
        + [vmem] * parts
        + [anywhere] * len(others),
        out_specs=vmem,
        out_shape=jax.ShapeDtypeStruct(values.shape, values.dtype),
        compiler_params=pltpu.CompilerParams(vmem_limit_bytes=32 * 2**20),
        cost_estimate=NO_COST,
    )(part.reshape(1).astype(jnp.int32), values, *received, *others)


def copy_columns(*refs):
    *sources, target = refs
    start = 0
    for source in sources:
        block = source[...].reshape(source.shape[-2:])
        columns = pl.ds(start, block.shape[1])
        if len(target.shape) == 3:
            target[0, :, columns] = block.astype(target.dtype)
        else:
            target[:, columns] = block.astype(target.dtype)
        start += block.shape[1]


def to_parts(sources, parts, dtype):
    rows = sources[0][0].shape[0]

    def spec(section, width):
        return pl.BlockSpec((rows, width), lambda p: (0, section * parts + p))

    total = sum(width for _, _, width in sources)
    return pl.pallas_call(
        copy_columns,
        grid=(parts,),
        in_specs=[spec(section, width) for _, section, width in sources],
        out_specs=pl.BlockSpec((1, rows, total), lambda p: (p, 0, 0)),
        out_shape=jax.ShapeDtypeStruct((parts, rows, total), dtype),
    )(*[array for array, _, _ in sources])


def updown_from_parts(slabs):
    parts, rows, width = slabs.shape
    units = width // 2

    def kernel(slabs_ref, out_ref):
        for p in range(parts):
            out_ref[:, p * units : (p + 1) * units] = slabs_ref[p].astype(f32)

    return pl.pallas_call(
        kernel,
        grid=(2,),
        in_specs=[pl.BlockSpec((parts, rows, units), lambda half: (0, 0, half))],
        out_specs=pl.BlockSpec((rows, parts * units), lambda half: (0, half)),
        out_shape=jax.ShapeDtypeStruct((rows, parts * width), f32),
        compiler_params=pltpu.CompilerParams(vmem_limit_bytes=32 * 2**20),
        cost_estimate=NO_COST,
    )(slabs)


def mixer_from_parts(slabs, width):
    parts, rows, _ = slabs.shape

    def kernel(slabs_ref, qkv_ref, gate_ref, strength_ref):
        for p in range(parts):
            for section in range(4):
                block = slabs_ref[p, :, section * width : (section + 1) * width].astype(f32)
                if section < 3:
                    start = (section * parts + p) * width
                    qkv_ref[:, start : start + width] = block
                else:
                    gate_ref[:, p * width : (p + 1) * width] = block
            last = slabs_ref[p, :, 4 * width :].astype(f32)
            strength_ref[:, p * SMALL : (p + 1) * SMALL] = last

    widths = [3 * parts * width, parts * width, parts * SMALL]
    return pl.pallas_call(
        kernel,
        out_shape=[jax.ShapeDtypeStruct((rows, size), f32) for size in widths],
        compiler_params=pltpu.CompilerParams(vmem_limit_bytes=32 * 2**20),
        cost_estimate=NO_COST,
    )(slabs)


def total_of(own_ref, received_refs):
    total = own_ref[...]
    for ref in received_refs:
        total = total + ref[...].astype(f32)
    return total


def row_scale(values):
    return lax.rsqrt(jnp.mean(values * values, -1, keepdims=True) + 1e-06)


def norm_slope(values, scale, gain, grad):
    mean = jnp.mean(gain * grad * values, -1, keepdims=True)
    return scale * gain * grad - values * (scale * scale * scale * mean)


def hidden_kernel(own_ref, *refs):
    *received, input_ref, gain_ref, hidden_ref, normed_ref = refs
    hidden = input_ref[...].astype(f32) + total_of(own_ref, received)
    hidden_ref[...] = hidden
    normed_ref[...] = (hidden * row_scale(hidden) * gain_ref[...]).astype(bf)


def hidden_back_kernel(own_ref, *refs):
    *received, hidden_ref, gain_ref, cot_ref, d_hidden_ref, d_mixed_ref, d_gain_ref = refs
    grad = total_of(own_ref, received)
    hidden = hidden_ref[...]
    scale = row_scale(hidden)

    @pl.when(pl.program_id(0) == 0)
    def _():
        d_gain_ref[...] = jnp.zeros_like(d_gain_ref)

    d_gain_ref[...] += jnp.sum(grad * hidden * scale, 0, keepdims=True)
    d_hidden = cot_ref[...].astype(f32) + norm_slope(hidden, scale, gain_ref[...], grad)
    d_hidden_ref[...] = d_hidden
    d_mixed_ref[...] = d_hidden.astype(bf)


def input_back_kernel(own_ref, *refs):
    *received, input_ref, gain_ref, d_hidden_ref, out_ref = refs
    grad = total_of(own_ref, received)
    values = input_ref[...].astype(f32)
    slope = norm_slope(values, row_scale(values), gain_ref[...], grad)
    out_ref[...] = (d_hidden_ref[...] + slope).astype(bf)


def block_out_kernel(own_ref, *refs):
    *received, hidden_ref, out_ref = refs
    out_ref[...] = (hidden_ref[...] + total_of(own_ref, received)).astype(bf)


def by_rows(kernel, arrays, outs, block=64):
    def spec(shape):
        if shape[0] == 1:
            return pl.BlockSpec(shape, lambda i: (0, 0))
        return pl.BlockSpec((block, shape[1]), lambda i: (i, 0))

    return pl.pallas_call(
        kernel,
        grid=(GROUP_ROWS // block,),
        in_specs=[spec(array.shape) for array in arrays],
        out_specs=[spec(shape) for shape, _ in outs],
        out_shape=[jax.ShapeDtypeStruct(shape, dtype) for shape, dtype in outs],
        compiler_params=pltpu.CompilerParams(dimension_semantics=("arbitrary",)),
        cost_estimate=NO_COST,
    )(*arrays)


def body(
    block_in,
    out_grad,
    norm1_gain,
    conv_weight,
    head_gain,
    qkv_weight,
    beta_weight,
    gate_weight,
    out_weight,
    norm2_gain,
    updown_weight,
    down_weight,
    seq_blocks,
    lead_blocks,
):
    devices = lax.axis_size("dp")
    parts = MODEL
    copies = devices // parts
    part = lax.axis_index("dp") // copies
    copy = lax.axis_index("dp") % copies
    rows_own = qkv_weight.shape[0]
    width = D // parts
    units = FF // parts
    heads_part = HEADS // parts
    wide = 4 * width + SMALL
    model_groups = [[m * copies + t for m in range(parts)] for t in range(copies)]
    copy_groups = [[m * copies + t for t in range(copies)] for m in range(parts)]

    def exchange(values):
        return lax.all_to_all(
            values, "dp", split_axis=0, concat_axis=0, axis_index_groups=model_groups, tiled=True
        )

    def shift(values, step):
        pairs = [
            (m * copies + t, (m + step) % parts * copies + t)
            for m in range(parts)
            for t in range(copies)
        ]
        return lax.ppermute(values, "dp", pairs)

    def exchange_apart(values, before, after=()):
        cut = [
            lax.dynamic_index_in_dim(values, (part + step) % parts, 0, keepdims=False)
            for step in range(1, parts)
        ]
        received = [shift(piece, step) for step, piece in enumerate(tie_all(cut, *before), 1)]
        return assemble(part, values, received, after)

    def gather_rows(values):
        return [values] + [shift(values, step) for step in range(1, parts)]

    def scatter_rows(terms):
        return [terms[0]] + [shift(block, -step) for step, block in enumerate(terms[1:], 1)]

    def gather_copies(values):
        return lax.all_gather(values, "dp", axis=0, axis_index_groups=copy_groups, tiled=True)

    def scatter_copies(values):
        return lax.psum_scatter(
            values.astype(bf),
            "dp",
            scatter_dimension=0,
            axis_index_groups=copy_groups,
            tiled=True,
        )

    def halve(values, bit, axis):
        pairs = [(i, i ^ (1 << bit)) for i in range(devices)]
        side = (copy >> bit) & 1
        own = lax.dynamic_index_in_dim(values, side, axis, keepdims=False)
        other = lax.dynamic_index_in_dim(values, 1 - side, axis, keepdims=False)
        return (own.astype(f32) + lax.ppermute(other, "dp", pairs).astype(f32)).astype(bf)

    by_halves = copies == 8

    def halve_cores(values):
        if not by_halves:
            return values
        rows, columns = values.shape
        return halve(values.reshape(2, 2, 2, rows // 8, columns), 0, 2)

    def halve_first(values):
        if not by_halves:
            return [values]
        middle = values.shape[-1] // 2
        return [halve(values[..., :middle], 1, 1), halve(values[..., middle:], 2, 0)]

    def halve_second(values):
        if not by_halves:
            return scatter_copies(values[0])
        return jnp.concatenate([halve(values[0], 2, 0), halve(values[1], 1, 0)], 1)

    def to_wire(values):
        return values.reshape(-1, parts, copies, rows_own).swapaxes(1, 2).reshape(-1, D)

    def from_wire(values):
        return values.reshape(-1, copies, parts, rows_own).swapaxes(1, 2).reshape(-1, D)

    w_out_own = to_wire(out_weight.astype(bf))
    w_out = gather_copies(w_out_own)
    strengths = beta_weight.reshape(rows_own, parts, heads_part)
    strengths = jnp.pad(strengths, ((0, 0), (0, 0), (0, SMALL - heads_part)))
    strengths = tie(strengths.reshape(rows_own, parts * SMALL), w_out_own)
    pieces = [(qkv_weight, section, width) for section in range(3)]
    pieces = to_parts(pieces + [(gate_weight, 0, width), (strengths, 0, SMALL)], parts, bf)
    mixer_pieces = tie(exchange(pieces), w_out)
    w_mixer = gather_copies(mixer_pieces.reshape(parts * rows_own, wide))
    inputs = tie(to_wire(block_in), mixer_pieces)
    input_rows = gather_rows(inputs)

    lanes = -(-3 * rows_own // 128) * 128
    numbers = jnp.concatenate([seq_blocks[0], lead_blocks]).astype(f32)
    small = [conv_weight.T, norm1_gain[None], head_gain[None], norm2_gain[None], numbers[None]]
    small = [jnp.pad(rows, ((0, 0), (0, lanes - rows.shape[1]))) for rows in small]
    small = jnp.pad(jnp.concatenate(small, 0).astype(bf), ((0, 2 * KERNEL), (0, 0)))
    small = jnp.broadcast_to(small[None], (devices,) + small.shape)
    small = lax.all_to_all(tie(small, inputs), "dp", 0, 0, tiled=True)
    taps = small[:, :KERNEL, : 3 * rows_own].swapaxes(0, 1).reshape(KERNEL, 3, parts, width)
    taps = lax.dynamic_index_in_dim(taps, part, 2, keepdims=False).reshape(KERNEL, 3 * width)
    gain_one, head_full, gain_two = (
        small[:, KERNEL + i, :rows_own].reshape(1, D).astype(f32) for i in range(3)
    )
    gain_one, gain_two = to_wire(gain_one), to_wire(gain_two)
    head_part = lax.dynamic_slice_in_dim(head_full, part * width, width, 1)
    params = jnp.concatenate([taps.astype(f32), jnp.pad(head_part, ((0, 0), (0, 2 * width)))], 0)
    params = jnp.pad(params, ((0, KERNEL - 1), (0, 0)))
    numbers = small[:, KERNEL + 3, :3].astype(f32).astype(jnp.int32)
    layouts = block_layouts(numbers[:, 0], numbers[:, 1], numbers[:, 2])
    layouts = layouts.reshape(parts, copies, 4)
    layouts = lax.dynamic_index_in_dim(layouts, copy, 1, keepdims=False)
    wanted = (part - jnp.arange(parts)) % parts
    wanted = (wanted[:, None] == jnp.arange(parts)).astype(f32)
    layouts = jnp.sum(wanted[:, :, None] * layouts, 1)

    pieces = [(updown_weight, half, units) for half in range(2)]
    updown_pieces = to_parts(pieces, parts, bf)
    w_down_own = to_wire(down_weight.astype(bf))
    w_down = gather_copies(tie(w_down_own, *input_rows[1:]))
    cotangent_own = to_wire(out_grad)

    gain_first = tie(gain_one, w_down_own, cotangent_own, updown_pieces)
    normed, pre = normed_product(input_rows, gain_first, w_mixer)
    mixed, *kept = mixer_forward(layouts, pre, params, width)
    out_terms = product_blocks(mixed, w_out)
    updown_pieces = exchange_apart(updown_pieces, [pre], out_terms[1:])
    w_updown = gather_copies(updown_pieces.reshape(parts * rows_own, 2 * units))
    stream = ((GROUP_ROWS, D), f32)
    narrow = ((GROUP_ROWS, D), bf)
    hidden, normed_two = by_rows(
        hidden_kernel,
        scatter_rows(out_terms) + [inputs, gain_two],
        [stream, narrow],
    )
    cotangent = jnp.concatenate(gather_rows(tie(cotangent_own, normed_two)), 0)
    normed_two = jnp.concatenate(gather_rows(normed_two), 0)

    def swiglu_units(updown):
        return jax.nn.silu(updown[:, :units]) * updown[:, units:]

    updown = plain_product(normed_two, w_updown)
    active, swiglu_back = jax.vjp(swiglu_units, updown)
    active = active.astype(bf)
    d_active = transposed_product(cotangent, w_down)
    d_updown = swiglu_back(d_active)[0].astype(bf)
    d_normed_two = product_blocks(d_updown, w_updown, transposed=True)
    updown_terms = grad_product(normed_two, tie(d_updown, *d_normed_two[1:]))
    active = tie(active, *d_normed_two[1:])
    down_terms = grad_product(active, tie(cotangent, updown_terms))
    d_normed_two = scatter_rows(d_normed_two)
    updown_grad = scatter_copies(tie(updown_terms, *d_normed_two[1:]))
    d_hidden, d_mixed, gain_two_grad = by_rows(
        hidden_back_kernel,
        d_normed_two + [hidden, tie(gain_two, down_terms), cotangent_own],
        [stream, narrow, ((1, D), f32)],
    )


    out_terms = product_blocks(tie(active, d_mixed), w_down)
    down_grad = halve_cores(tie(down_terms, d_mixed))
    d_mixed = gather_rows(d_mixed)
    late = tie(params, down_grad, *out_terms)
    out_terms[1:] = tie_all(out_terms[1:], *d_mixed[1:])
    (block_out,) = by_rows(block_out_kernel, scatter_rows(out_terms) + [hidden], [narrow])
    d_pre, d_params = mixer_backward(layouts, pre, late, w_out, d_mixed, kept, width)
    mixer_terms = tie(grad_product(normed, d_pre), updown_grad)
    mixer_grad = scatter_copies(mixer_terms)

    d_normed_terms = product_blocks(
        tie(d_pre, mixer_terms, block_out), w_mixer, transposed=True
    )
    d_normed = scatter_rows(d_normed_terms)
    down_grad = halve_first(tie(down_grad, *d_normed_terms[1:]))
    gain_one_grad = 0.0
    for values, terms in zip(input_rows, d_normed_terms):
        values = values.astype(f32)
        terms = terms.astype(f32) * (values * row_scale(values))
        gain_one_grad = gain_one_grad + jnp.sum(terms, 0, keepdims=True)

    here = (jnp.arange(parts) == part).astype(f32)[:, None]
    taps_grad = d_params[:KERNEL].reshape(KERNEL, 3, 1, width) * here
    taps_grad = taps_grad.reshape(KERNEL, parts, copies, 3, rows_own).transpose(1, 2, 3, 0, 4)
    taps_grad = taps_grad.reshape(devices, 3 * KERNEL, rows_own)
    head_grad = (d_params[KERNEL, :width] * here).reshape(devices, 1, rows_own)
    gain_grads = [
        grad.reshape(copies, parts, 1, rows_own).swapaxes(0, 1).reshape(devices, 1, rows_own)
        for grad in (gain_one_grad, gain_two_grad)
    ]
    small_grad = jnp.concatenate([taps_grad, head_grad] + gain_grads, 1)
    small_grad = jnp.pad(small_grad, ((0, 0), (0, 1), (0, 128 - rows_own)))
    small_grad = jnp.sum(lax.all_to_all(small_grad, "dp", 0, 0, tiled=True), 0)[:, :rows_own]
    taps_shard = small_grad[: 3 * KERNEL].reshape(3, KERNEL, rows_own).swapaxes(1, 2)
    taps_shard = taps_shard.reshape(3 * rows_own, KERNEL)
    head_shard, gain_one_shard, gain_two_shard = small_grad[3 * KERNEL : 3 * KERNEL + 3]

    (input_grad,) = by_rows(input_back_kernel, d_normed + [inputs, gain_one, d_hidden], [narrow])
    updown_grad = updown_grad.reshape(parts, rows_own, 2 * units)
    updown_shard = updown_from_parts(exchange_apart(updown_grad, [input_grad]))
    out_shard = grad_product(tie(mixed, input_grad), jnp.concatenate(d_mixed, 0))
    out_shard = halve_second(halve_first(halve_cores(out_shard)))
    out_shard = from_wire(out_shard.astype(f32))
    down_shard = from_wire(halve_second(tie_all(down_grad, input_grad)).astype(f32))
    mixer_grad = exchange(mixer_grad.reshape(parts, rows_own, wide))
    qkv_shard, gate_shard, strengths = mixer_from_parts(mixer_grad, width)
    beta_shard = strengths.reshape(rows_own, parts, SMALL)[:, :, :heads_part]
    return (
        from_wire(block_out),
        from_wire(input_grad),
        gain_one_shard,
        taps_shard,
        head_shard,
        qkv_shard,
        beta_shard.reshape(rows_own, HEADS),
        gate_shard,
        out_shard,
        gain_two_shard,
        updown_shard,
        down_shard,
    )


def solution(mesh):
    placed = (
        P("dp", None),
        P("dp", None),
        P("dp"),
        P("dp", None),
        P("dp"),
        P("dp", None),
        P("dp", None),
        P("dp", None),
        P("dp", None),
        P("dp"),
        P("dp", None),
        P("dp", None),
        P("dp", None),
        P("dp"),
    )
    return jax.shard_map(
        body,
        mesh=mesh,
        in_specs=placed,
        out_specs=(
            P("dp", None),
            P("dp", None),
            P("dp"),
            P("dp", None),
            P("dp"),
            P("dp", None),
            P("dp", None),
            P("dp", None),
            P("dp", None),
            P("dp"),
            P("dp", None),
            P("dp", None),
        ),
        check_vma=False,
    )
```

```python
import jax
import jax.numpy as jnp
from jax import lax
from jax.experimental import pallas as pl
from jax.experimental.pallas import tpu as pltpu
from jax.sharding import PartitionSpec as P

D = 2048
HEADS = 16
HEAD_DIM = 128
FF = 5632
KERNEL = 4
BLOCK_ROWS = 64
BLOCKS_DEV = 2
GROUP_ROWS = BLOCK_ROWS * BLOCKS_DEV
SMALL = 128
MODEL = 4

f32 = jnp.float32
bf = jnp.bfloat16


def block_layouts(first, second, lead):
    def doc(block):
        in_first = (block >= lead) & (block < lead + first)
        in_second = (block >= lead + first) & (block < lead + first + second)
        return jnp.where(in_first, 1, jnp.where(in_second, 2, 0))

    starts = (lead == 1) | (lead + first == 1) & (second > 0)
    columns = [doc(0) > 0, doc(1) > 0, doc(0) == doc(1), ~starts]
    return jnp.stack(columns, 1).astype(f32)


def plain_product(left, right):
    return jnp.dot(left, right, preferred_element_type=f32)


def rows_product(left, right):
    return lax.dot_general(left, right, (((0,), (0,)), ((), ())), preferred_element_type=f32)


def transposed_product(left, right):
    return lax.dot_general(left, right, (((1,), (1,)), ((), ())), preferred_element_type=f32)


def halves(values):
    high = values.astype(bf)
    return high, (values - high.astype(f32)).astype(bf)


def exact(left, right, left_dim, right_dim):
    left_high, left_low = left if isinstance(left, tuple) else halves(left)
    right_high, right_low = right if isinstance(right, tuple) else halves(right)
    return lax.dot_general(
        jnp.concatenate([left_high, left_high, left_low], left_dim),
        jnp.concatenate([right_high, right_low, right_high], right_dim),
        (((left_dim,), (right_dim,)), ((), ())),
        preferred_element_type=f32,
    )


def stacked(first, second):
    return tuple(jnp.concatenate([a, b], 0) for a, b in zip(first, second))


class Tile:
    def __init__(self, layout_ref, group):
        live_first, live_second, same, persist = (layout_ref[group, i] for i in range(4))
        shape = (GROUP_ROWS, HEAD_DIM)
        row = lax.broadcasted_iota(jnp.int32, shape, 0)
        col = lax.broadcasted_iota(jnp.int32, shape, 1)
        late = row >= BLOCK_ROWS
        self.row, self.col = row, col
        self.live = jnp.where(late, live_second, live_first)
        self.taps = [None] + [
            jnp.where(
                row < offset,
                0.0,
                jnp.where(late & (row < BLOCK_ROWS + offset), same, 1.0),
            )
            for offset in range(1, KERNEL)
        ]
        cross = jnp.where(late & (col < BLOCK_ROWS), persist, 1.0)
        self.lower = jnp.where(row > col, cross, 0.0)
        self.lower_full = jnp.where(row >= col, cross, 0.0)

    def earlier(self, values, offset):
        return pltpu.roll(values, offset, 0) * self.taps[offset]

    def later(self, values, offset):
        return pltpu.roll(values * self.taps[offset], GROUP_ROWS - offset, 0)


def convolve(tile, values, taps):
    total = values * taps[0]
    for offset in range(1, KERNEL):
        total = total + tile.earlier(values, offset) * taps[offset]
    return total


def unit_scale(values):
    return lax.rsqrt(jnp.sum(values * values, -1, keepdims=True) + 1e-06)


def head_columns(part_width, section, head):
    return pl.ds(section * part_width + head * HEAD_DIM, HEAD_DIM)


def unit_inverses(tile, lowers):
    eye = jnp.where(tile.row == tile.col, 1.0, 0.0)
    inverses = None
    size = 1
    while size < GROUP_ROWS:
        pair = tile.row // (2 * size) == tile.col // (2 * size)
        split = pair & (tile.row // size != tile.col // size)
        parts = [jnp.where(split, lower, 0.0) for lower in lowers]
        if inverses is None:
            inverses = [eye - part for part in parts]
        else:
            kept = [halves(inverse) for inverse in inverses]
            inner = [exact(part, known, 1, 0) for part, known in zip(parts, kept)]
            outer = [exact(known, value, 1, 0) for known, value in zip(kept, inner)]
            inverses = [inverse - value for inverse, value in zip(inverses, outer)]
        size *= 2
    return inverses


def mixer_forward_kernel(
    layout_ref, pre_ref, param_ref, mixed_ref, inverse_ref, score_ref, solved_ref, out_ref
):
    width = mixed_ref.shape[1]
    heads = range(width // HEAD_DIM)
    tile = Tile(layout_ref, pl.program_id(0))
    queries, keys, values, strengths = [], [], [], []
    for head in heads:
        parts = []
        for section in range(3):
            columns = head_columns(width, section, head)
            taps = [param_ref[offset : offset + 1, columns] for offset in range(KERNEL)]
            convolved = convolve(tile, pre_ref[:, columns], taps)
            parts.append(convolved * jax.nn.sigmoid(convolved))
        queries.append(parts[0] * (unit_scale(parts[0]) * HEAD_DIM**-0.5))
        keys.append(parts[1] * unit_scale(parts[1]))
        values.append(parts[2])
        start = 4 * width + head
        strengths.append(jax.nn.sigmoid(pre_ref[:, start : start + 1]) * tile.live)
    lowers, scores = [], []
    for head in heads:
        key_halves = halves(keys[head])
        both = exact(stacked(key_halves, halves(queries[head])), key_halves, 1, 1)
        lowers.append(both[:GROUP_ROWS] * strengths[head] * tile.lower)
        scores.append(both[GROUP_ROWS:] * tile.lower_full)
    inverses = unit_inverses(tile, lowers)
    solved = [exact(inverses[head], values[head] * strengths[head], 1, 0) for head in heads]
    outs = [exact(scores[head], solved[head], 1, 0) for head in heads]
    for head in heads:
        out = outs[head]
        scaled = out * lax.rsqrt(jnp.mean(out * out, -1, keepdims=True) + 1e-05)
        gate = pre_ref[:, head_columns(width, 3, head)]
        gain = param_ref[KERNEL : KERNEL + 1, head_columns(width, 0, head)]
        mixed = scaled * gain * (gate * jax.nn.sigmoid(gate)) * tile.live
        mixed_ref[:, head_columns(width, 0, head)] = mixed.astype(bf)
        inverse_ref[head] = inverses[head]
        score_ref[head] = scores[head]
        solved_ref[head] = solved[head]
        out_ref[head] = out


def mixer_backward_kernel(
    layout_ref,
    pre_ref,
    param_ref,
    weight_ref,
    inverse_ref,
    score_ref,
    solved_ref,
    out_ref,
    *refs,
):
    *mixed_refs, d_pre_ref, d_param_ref, grad_ref = refs
    width = grad_ref.shape[1]
    heads = range(width // HEAD_DIM)
    tile = Tile(layout_ref, pl.program_id(0))
    for group, mixed_ref in enumerate(mixed_refs):

        @pl.when(pl.program_id(0) == group)
        def _():
            grad_ref[...] = transposed_product(mixed_ref[...], weight_ref[...])

    @pl.when(pl.program_id(0) == 0)
    def _():
        d_param_ref[...] = jnp.zeros_like(d_param_ref)

    def along(values):
        return jnp.sum(values, -1, keepdims=True)

    d_outs = []
    for head in heads:
        columns = head_columns(width, 0, head)
        d_mixed = grad_ref[:, columns] * tile.live
        out = out_ref[head]
        scale = lax.rsqrt(jnp.mean(out * out, -1, keepdims=True) + 1e-05)
        scaled = out * scale
        gate = pre_ref[:, head_columns(width, 3, head)]
        gate_open = jax.nn.sigmoid(gate)
        gain = param_ref[KERNEL : KERNEL + 1, columns]
        gated = d_mixed * (gate * gate_open)
        d_param_ref[KERNEL : KERNEL + 1, columns] += jnp.sum(gated * scaled, 0, keepdims=True)
        d_gate = d_mixed * scaled * gain * (gate_open * (1.0 + gate * (1.0 - gate_open)))
        d_pre_ref[:, head_columns(width, 3, head)] = d_gate.astype(bf)
        d_scaled = gated * gain
        mean = jnp.mean(d_scaled * out, -1, keepdims=True)
        d_outs.append(scale * d_scaled - out * (scale * scale * scale * mean))
    d_out_halves = [halves(value) for value in d_outs]
    solved_halves = [halves(solved_ref[head]) for head in heads]
    d_solved = [exact(score_ref[head], d_out_halves[head], 0, 0) for head in heads]
    d_scores = [
        exact(d_out_halves[head], solved_halves[head], 1, 1) * tile.lower_full for head in heads
    ]
    d_inner = [exact(inverse_ref[head], d_solved[head], 0, 0) for head in heads]
    d_lowers = [exact(d_inner[head], solved_halves[head], 1, 1) * -tile.lower for head in heads]
    d_beta = jnp.zeros((GROUP_ROWS, SMALL), f32)
    for head in heads:
        pres, convolved, opened, active = [], [], [], []
        for section in range(3):
            columns = head_columns(width, section, head)
            taps = [param_ref[offset : offset + 1, columns] for offset in range(KERNEL)]
            pres.append(pre_ref[:, columns])
            convolved.append(convolve(tile, pres[section], taps))
            opened.append(jax.nn.sigmoid(convolved[section]))
            active.append(convolved[section] * opened[section])
        query_scale = unit_scale(active[0])
        key_scale = unit_scale(active[1])
        query_unit = active[0] * query_scale
        key = active[1] * key_scale
        start = 4 * width + head
        opening = jax.nn.sigmoid(pre_ref[:, start : start + 1])
        strength = opening * tile.live
        d_both = stacked(halves(d_lowers[head]), halves(d_scores[head]))
        by_key = exact(d_both, key, 1, 0)
        d_query = by_key[GROUP_ROWS:] * HEAD_DIM**-0.5
        from_lower = by_key[:GROUP_ROWS]
        weighted = stacked(halves(key * strength), halves(query_unit * HEAD_DIM**-0.5))
        d_key = strength * from_lower + exact(d_both, weighted, 0, 0)
        d_strength = along(d_inner[head] * active[2] + from_lower * key)
        d_value = d_inner[head] * strength
        d_opening = d_strength * (opening * (1.0 - opening)) * tile.live
        d_beta = d_beta + jnp.where(tile.col == head, d_opening, 0.0)
        d_active = [
            (d_query - query_unit * along(query_unit * d_query)) * query_scale,
            (d_key - key * along(key * d_key)) * key_scale,
            d_value,
        ]
        for section in range(3):
            columns = head_columns(width, section, head)
            taps = [param_ref[offset : offset + 1, columns] for offset in range(KERNEL)]
            slope = opened[section] * (1.0 + convolved[section] * (1.0 - opened[section]))
            d_convolved = d_active[section] * slope
            d_pre = d_convolved * taps[0]
            sums = [jnp.sum(d_convolved * pres[section], 0, keepdims=True)]
            for offset in range(1, KERNEL):
                d_pre = d_pre + tile.later(d_convolved, offset) * taps[offset]
                sums.append(
                    jnp.sum(d_convolved * tile.earlier(pres[section], offset), 0, keepdims=True)
                )
            d_param_ref[0:KERNEL, columns] += jnp.concatenate(sums, 0)
            d_pre_ref[:, columns] = d_pre.astype(bf)
    d_pre_ref[:, 4 * width :] = d_beta.astype(bf)


NO_COST = pl.CostEstimate(flops=0, bytes_accessed=0, transcendentals=0)


def call(kernel, operands, in_specs, out_specs, out_shape, grid=(), scratch=(), micros=0):
    results = pl.pallas_call(
        kernel,
        grid=grid,
        in_specs=in_specs,
        out_specs=out_specs,
        out_shape=out_shape,
        scratch_shapes=scratch,
        compiler_params=pltpu.CompilerParams(
            dimension_semantics=("arbitrary",) * len(grid), vmem_limit_bytes=48 * 2**20
        ),
        cost_estimate=pl.CostEstimate(
            flops=micros * 10**9, bytes_accessed=0, transcendentals=0
        ),
    )(*operands)
    return list(results)


def whole(array):
    return pl.BlockSpec(array.shape, lambda *step: (0,) * len(array.shape))


def mixer_specs(width):
    wide = 4 * width + SMALL
    heads = width // HEAD_DIM
    layout = pl.BlockSpec(memory_space=pltpu.SMEM)
    pre = pl.BlockSpec((GROUP_ROWS, wide), lambda group: (group, 0))
    param = pl.BlockSpec((2 * KERNEL, 3 * width), lambda group: (0, 0))
    narrow = pl.BlockSpec((GROUP_ROWS, width), lambda group: (group, 0))
    square = pl.BlockSpec((heads, GROUP_ROWS, HEAD_DIM), lambda group: (group, 0, 0))
    return layout, pre, param, narrow, square


def mixer_forward(layout, pre, params, width):
    groups = layout.shape[0]
    layout_spec, pre_spec, param_spec, narrow, square = mixer_specs(width)
    squares = pltpu.HBM((groups * width // HEAD_DIM, GROUP_ROWS, HEAD_DIM), f32)
    return call(
        mixer_forward_kernel,
        [layout, pre, params],
        [layout_spec, pre_spec, param_spec],
        [narrow] + [square] * 4,
        [jax.ShapeDtypeStruct((groups * GROUP_ROWS, width), bf)] + [squares] * 4,
        (groups,),
    )


def mixer_backward(layout, pre, params, weight, d_mixed, kept, width):
    groups = layout.shape[0]
    layout_spec, pre_spec, param_spec, _, square = mixer_specs(width)
    return call(
        mixer_backward_kernel,
        [layout, pre, params, weight, *kept, *d_mixed],
        [layout_spec, pre_spec, param_spec, whole(weight)]
        + [square] * 4
        + [whole(block) for block in d_mixed],
        [pre_spec, param_spec],
        [jax.ShapeDtypeStruct(pre.shape, bf), jax.ShapeDtypeStruct(params.shape, f32)],
        (groups,),
        [pltpu.VMEM((GROUP_ROWS, width), f32)],
        micros=60,
    )


def first_kernel(gain_ref, weight_ref, *refs):
    *value_refs, normed_ref, out_ref, scale_ref, total_ref = refs
    step, depth = pl.program_id(0), weight_ref.shape[0]

    @pl.when(step == 0)
    def _():
        for group, ref in enumerate(value_refs):
            values = ref[...].astype(f32)
            scale = lax.rsqrt(jnp.mean(values * values, -1, keepdims=True) + 1e-06)
            rows = pl.ds(group * GROUP_ROWS, GROUP_ROWS)
            scale_ref[rows, :] = jnp.broadcast_to(scale, (GROUP_ROWS, 128))
        total_ref[...] = jnp.zeros_like(total_ref)

    columns = pl.ds(pl.multiple_of(step * depth, depth), depth)
    for group, ref in enumerate(value_refs):
        rows = pl.ds(group * GROUP_ROWS, GROUP_ROWS)
        values = ref[:, columns].astype(f32) * scale_ref[rows, :1] * gain_ref[...]
        normed_ref[rows, :] = values.astype(bf)
    total_ref[...] += plain_product(normed_ref[...], weight_ref[...])

    @pl.when(step == pl.num_programs(0) - 1)
    def _():
        out_ref[...] = total_ref[...]


def normed_product(blocks, gain, weight, depth=512):
    rows, (features, columns) = len(blocks) * GROUP_ROWS, weight.shape
    return call(
        first_kernel,
        [gain, weight, *blocks],
        [
            pl.BlockSpec((1, depth), lambda step: (0, step)),
            pl.BlockSpec((depth, columns), lambda step: (step, 0)),
        ]
        + [whole(block) for block in blocks],
        [
            pl.BlockSpec((rows, depth), lambda step: (0, step)),
            pl.BlockSpec((rows, columns), lambda step: (0, 0)),
        ],
        [
            jax.ShapeDtypeStruct((rows, features), bf),
            jax.ShapeDtypeStruct((rows, columns), f32),
        ],
        (features // depth,),
        [pltpu.VMEM((rows, 128), f32), pltpu.VMEM((rows, columns), f32)],
    )


def product_blocks(left, right, transposed=False, block=512, micros=0):
    product = transposed_product if transposed else plain_product
    columns = right.shape[0] if transposed else right.shape[1]
    groups = left.shape[0] // GROUP_ROWS

    def kernel(left_ref, right_ref, *out_refs):
        total = product(left_ref[...], right_ref[...])
        for group, ref in enumerate(out_refs):
            ref[...] = total[group * GROUP_ROWS : (group + 1) * GROUP_ROWS].astype(ref.dtype)

    if transposed:
        right_spec = pl.BlockSpec((block, right.shape[1]), lambda step: (step, 0))
    else:
        right_spec = pl.BlockSpec((right.shape[0], block), lambda step: (0, step))
    return call(
        kernel,
        [left, right],
        [whole(left), right_spec],
        [pl.BlockSpec((GROUP_ROWS, block), lambda step: (0, step))] * groups,
        [
            jax.ShapeDtypeStruct((GROUP_ROWS, columns), bf if group else f32)
            for group in range(groups)
        ],
        (columns // block,),
        micros=micros,
    )


def grad_product(left, right, block=256, micros=0):
    rows, features = left.shape
    if features % block:
        block = 128

    def kernel(left_ref, right_ref, out_ref):
        out_ref[...] = rows_product(left_ref[...], right_ref[...]).astype(bf)

    return call(
        kernel,
        [left, right],
        [pl.BlockSpec((rows, block), lambda step: (0, step)), whole(right)],
        [pl.BlockSpec((block, right.shape[1]), lambda step: (step, 0))],
        [pltpu.HBM((features, right.shape[1]), bf)],
        (features // block,),
        micros=micros,
    )[0]


def from_own(part, values):
    groups = values.shape[0] // GROUP_ROWS

    def kernel(part_ref, values_ref, out_ref):
        for step in range(groups):
            source = lax.rem(part_ref[0] + groups - step, groups) * GROUP_ROWS
            rows = pl.ds(pl.multiple_of(source, GROUP_ROWS), GROUP_ROWS)
            out_ref[step * GROUP_ROWS : (step + 1) * GROUP_ROWS] = values_ref[rows]

    return call(
        kernel,
        [part.reshape(1).astype(jnp.int32), values],
        [pl.BlockSpec(memory_space=pltpu.SMEM), whole(values)],
        [whole(values)],
        [jax.ShapeDtypeStruct(values.shape, values.dtype)],
        (1,),
    )[0]


def tie_all(values, *others):
    anywhere = pl.BlockSpec(memory_space=pl.ANY)
    tied = pl.pallas_call(
        lambda *refs: None,
        in_specs=[anywhere] * (len(values) + len(others)),
        out_specs=[anywhere] * len(values),
        out_shape=[jax.ShapeDtypeStruct(value.shape, value.dtype) for value in values],
        input_output_aliases={i: i for i in range(len(values))},
        cost_estimate=NO_COST,
    )(*values, *others)
    return list(tied)


def tie(value, *others):
    return tie_all([value], *others)[0]


def assemble(part, values, received, others):
    parts = values.shape[0]

    def kernel(part_ref, values_ref, *refs):
        own = part_ref[0]
        out_ref = refs[-1]
        out_ref[own] = values_ref[own]
        for step in range(1, parts):
            out_ref[lax.rem(own + parts - step, parts)] = refs[step - 1][...]

    vmem = pl.BlockSpec(memory_space=pltpu.VMEM)
    anywhere = pl.BlockSpec(memory_space=pl.ANY)
    return pl.pallas_call(
        kernel,
        in_specs=[pl.BlockSpec(memory_space=pltpu.SMEM)]
        + [vmem] * parts
        + [anywhere] * len(others),
        out_specs=vmem,
        out_shape=jax.ShapeDtypeStruct(values.shape, values.dtype),
        compiler_params=pltpu.CompilerParams(vmem_limit_bytes=32 * 2**20),
        cost_estimate=NO_COST,
    )(part.reshape(1).astype(jnp.int32), values, *received, *others)


def copy_columns(*refs):
    *sources, target = refs
    start = 0
    for source in sources:
        block = source[...].reshape(source.shape[-2:])
        columns = pl.ds(start, block.shape[1])
        if len(target.shape) == 3:
            target[0, :, columns] = block.astype(target.dtype)
        else:
            target[:, columns] = block.astype(target.dtype)
        start += block.shape[1]


def to_parts(sources, parts, dtype):
    rows = sources[0][0].shape[0]

    def spec(section, width):
        return pl.BlockSpec((rows, width), lambda p: (0, section * parts + p))

    total = sum(width for _, _, width in sources)
    return pl.pallas_call(
        copy_columns,
        grid=(parts,),
        in_specs=[spec(section, width) for _, section, width in sources],
        out_specs=pl.BlockSpec((1, rows, total), lambda p: (p, 0, 0)),
        out_shape=jax.ShapeDtypeStruct((parts, rows, total), dtype),
    )(*[array for array, _, _ in sources])


def updown_from_parts(slabs):
    parts, rows, width = slabs.shape
    units = width // 2

    def kernel(slabs_ref, out_ref):
        for p in range(parts):
            out_ref[:, p * units : (p + 1) * units] = slabs_ref[p].astype(f32)

    return pl.pallas_call(
        kernel,
        grid=(2,),
        in_specs=[pl.BlockSpec((parts, rows, units), lambda half: (0, 0, half))],
        out_specs=pl.BlockSpec((rows, parts * units), lambda half: (0, half)),
        out_shape=jax.ShapeDtypeStruct((rows, parts * width), f32),
        compiler_params=pltpu.CompilerParams(vmem_limit_bytes=32 * 2**20),
        cost_estimate=NO_COST,
    )(slabs)


def mixer_from_parts(slabs, width):
    parts, rows, _ = slabs.shape

    def kernel(slabs_ref, qkv_ref, gate_ref, strength_ref):
        for p in range(parts):
            for section in range(4):
                block = slabs_ref[p, :, section * width : (section + 1) * width].astype(f32)
                if section < 3:
                    start = (section * parts + p) * width
                    qkv_ref[:, start : start + width] = block
                else:
                    gate_ref[:, p * width : (p + 1) * width] = block
            last = slabs_ref[p, :, 4 * width :].astype(f32)
            strength_ref[:, p * SMALL : (p + 1) * SMALL] = last

    widths = [3 * parts * width, parts * width, parts * SMALL]
    return pl.pallas_call(
        kernel,
        out_shape=[jax.ShapeDtypeStruct((rows, size), f32) for size in widths],
        compiler_params=pltpu.CompilerParams(vmem_limit_bytes=32 * 2**20),
        cost_estimate=NO_COST,
    )(slabs)


def total_of(own_ref, received_refs):
    total = own_ref[...]
    for ref in received_refs:
        total = total + ref[...].astype(f32)
    return total


def row_scale(values):
    return lax.rsqrt(jnp.mean(values * values, -1, keepdims=True) + 1e-06)


def norm_slope(values, scale, gain, grad):
    mean = jnp.mean(gain * grad * values, -1, keepdims=True)
    return scale * gain * grad - values * (scale * scale * scale * mean)


def hidden_kernel(own_ref, *refs):
    *received, input_ref, gain_ref, hidden_ref, normed_ref = refs
    hidden = input_ref[...].astype(f32) + total_of(own_ref, received)
    hidden_ref[...] = hidden
    normed_ref[...] = (hidden * row_scale(hidden) * gain_ref[...]).astype(bf)


def hidden_back_kernel(own_ref, *refs):
    *received, hidden_ref, gain_ref, cot_ref, d_hidden_ref, d_mixed_ref, d_gain_ref = refs
    grad = total_of(own_ref, received)
    hidden = hidden_ref[...]
    scale = row_scale(hidden)

    @pl.when(pl.program_id(0) == 0)
    def _():
        d_gain_ref[...] = jnp.zeros_like(d_gain_ref)

    d_gain_ref[...] += jnp.sum(grad * hidden * scale, 0, keepdims=True)
    d_hidden = cot_ref[...].astype(f32) + norm_slope(hidden, scale, gain_ref[...], grad)
    d_hidden_ref[...] = d_hidden
    d_mixed_ref[...] = d_hidden.astype(bf)


def input_back_kernel(own_ref, *refs):
    *received, input_ref, gain_ref, d_hidden_ref, out_ref = refs
    grad = total_of(own_ref, received)
    values = input_ref[...].astype(f32)
    slope = norm_slope(values, row_scale(values), gain_ref[...], grad)
    out_ref[...] = (d_hidden_ref[...] + slope).astype(bf)


def block_out_kernel(own_ref, *refs):
    *received, hidden_ref, out_ref = refs
    out_ref[...] = (hidden_ref[...] + total_of(own_ref, received)).astype(bf)


def by_rows(kernel, arrays, outs, block=64):
    def spec(shape):
        if shape[0] == 1:
            return pl.BlockSpec(shape, lambda i: (0, 0))
        return pl.BlockSpec((block, shape[1]), lambda i: (i, 0))

    return pl.pallas_call(
        kernel,
        grid=(GROUP_ROWS // block,),
        in_specs=[spec(array.shape) for array in arrays],
        out_specs=[spec(shape) for shape, _ in outs],
        out_shape=[jax.ShapeDtypeStruct(shape, dtype) for shape, dtype in outs],
        compiler_params=pltpu.CompilerParams(dimension_semantics=("arbitrary",)),
        cost_estimate=NO_COST,
    )(*arrays)


def body(
    block_in,
    out_grad,
    norm1_gain,
    conv_weight,
    head_gain,
    qkv_weight,
    beta_weight,
    gate_weight,
    out_weight,
    norm2_gain,
    updown_weight,
    down_weight,
    seq_blocks,
    lead_blocks,
):
    devices = lax.axis_size("dp")
    parts = MODEL
    copies = devices // parts
    part = lax.axis_index("dp") // copies
    copy = lax.axis_index("dp") % copies
    rows_own = qkv_weight.shape[0]
    width = D // parts
    units = FF // parts
    heads_part = HEADS // parts
    wide = 4 * width + SMALL
    model_groups = [[m * copies + t for m in range(parts)] for t in range(copies)]
    copy_groups = [[m * copies + t for t in range(copies)] for m in range(parts)]

    def exchange(values):
        return lax.all_to_all(
            values, "dp", split_axis=0, concat_axis=0, axis_index_groups=model_groups, tiled=True
        )

    def shift(values, step):
        pairs = [
            (m * copies + t, (m + step) % parts * copies + t)
            for m in range(parts)
            for t in range(copies)
        ]
        return lax.ppermute(values, "dp", pairs)

    def exchange_apart(values, before, after=()):
        cut = [
            lax.dynamic_index_in_dim(values, (part + step) % parts, 0, keepdims=False)
            for step in range(1, parts)
        ]
        received = [shift(piece, step) for step, piece in enumerate(tie_all(cut, *before), 1)]
        return assemble(part, values, received, after)

    def gather_rows(values):
        return [values] + [shift(values, step) for step in range(1, parts)]

    def scatter_rows(terms):
        return [terms[0]] + [shift(block, -step) for step, block in enumerate(terms[1:], 1)]

    def gather_copies(values):
        return lax.all_gather(values, "dp", axis=0, axis_index_groups=copy_groups, tiled=True)

    def scatter_copies(values):
        return lax.psum_scatter(
            values.astype(bf),
            "dp",
            scatter_dimension=0,
            axis_index_groups=copy_groups,
            tiled=True,
        )

    def halve(values, bit, axis):
        pairs = [(i, i ^ (1 << bit)) for i in range(devices)]
        side = (copy >> bit) & 1
        own = lax.dynamic_index_in_dim(values, side, axis, keepdims=False)
        other = lax.dynamic_index_in_dim(values, 1 - side, axis, keepdims=False)
        return (own.astype(f32) + lax.ppermute(other, "dp", pairs).astype(f32)).astype(bf)

    by_halves = copies == 8

    def halve_cores(values):
        if not by_halves:
            return values
        rows, columns = values.shape
        return halve(values.reshape(2, 2, 2, rows // 8, columns), 0, 2)

    def halve_first(values):
        if not by_halves:
            return [values]
        middle = values.shape[-1] // 2
        return [halve(values[..., :middle], 1, 1), halve(values[..., middle:], 2, 0)]

    def halve_second(values):
        if not by_halves:
            return scatter_copies(values[0])
        return jnp.concatenate([halve(values[0], 2, 0), halve(values[1], 1, 0)], 1)

    def to_wire(values):
        return values.reshape(-1, parts, copies, rows_own).swapaxes(1, 2).reshape(-1, D)

    def from_wire(values):
        return values.reshape(-1, copies, parts, rows_own).swapaxes(1, 2).reshape(-1, D)

    w_out_own = to_wire(out_weight.astype(bf))
    w_out = gather_copies(w_out_own)
    strengths = beta_weight.reshape(rows_own, parts, heads_part)
    strengths = jnp.pad(strengths, ((0, 0), (0, 0), (0, SMALL - heads_part)))
    strengths = tie(strengths.reshape(rows_own, parts * SMALL), w_out_own)
    pieces = [(qkv_weight, section, width) for section in range(3)]
    pieces = to_parts(pieces + [(gate_weight, 0, width), (strengths, 0, SMALL)], parts, bf)
    mixer_pieces = tie(exchange(pieces), w_out)
    w_mixer = gather_copies(mixer_pieces.reshape(parts * rows_own, wide))
    inputs = tie(to_wire(block_in), mixer_pieces)
    input_rows = gather_rows(inputs)

    lanes = -(-3 * rows_own // 128) * 128
    numbers = jnp.concatenate([seq_blocks[0], lead_blocks]).astype(f32)
    small = [conv_weight.T, norm1_gain[None], head_gain[None], norm2_gain[None], numbers[None]]
    small = [jnp.pad(rows, ((0, 0), (0, lanes - rows.shape[1]))) for rows in small]
    small = jnp.pad(jnp.concatenate(small, 0).astype(bf), ((0, 2 * KERNEL), (0, 0)))
    small = jnp.broadcast_to(small[None], (devices,) + small.shape)
    small = lax.all_to_all(tie(small, inputs), "dp", 0, 0, tiled=True)
    taps = small[:, :KERNEL, : 3 * rows_own].swapaxes(0, 1).reshape(KERNEL, 3, parts, width)
    taps = lax.dynamic_index_in_dim(taps, part, 2, keepdims=False).reshape(KERNEL, 3 * width)
    gain_one, head_full, gain_two = (
        small[:, KERNEL + i, :rows_own].reshape(1, D).astype(f32) for i in range(3)
    )
    gain_one, gain_two = to_wire(gain_one), to_wire(gain_two)
    head_part = lax.dynamic_slice_in_dim(head_full, part * width, width, 1)
    params = jnp.concatenate([taps.astype(f32), jnp.pad(head_part, ((0, 0), (0, 2 * width)))], 0)
    params = jnp.pad(params, ((0, KERNEL - 1), (0, 0)))
    numbers = small[:, KERNEL + 3, :3].astype(f32).astype(jnp.int32)
    layouts = block_layouts(numbers[:, 0], numbers[:, 1], numbers[:, 2])
    layouts = layouts.reshape(parts, copies, 4)
    layouts = lax.dynamic_index_in_dim(layouts, copy, 1, keepdims=False)
    wanted = (part - jnp.arange(parts)) % parts
    wanted = (wanted[:, None] == jnp.arange(parts)).astype(f32)
    layouts = jnp.sum(wanted[:, :, None] * layouts, 1)

    pieces = [(updown_weight, half, units) for half in range(2)]
    updown_pieces = to_parts(pieces, parts, bf)
    w_down_own = to_wire(down_weight.astype(bf))
    w_down = gather_copies(tie(w_down_own, *input_rows[1:]))
    cotangent_own = to_wire(out_grad)

    cotangent = lax.all_gather(
        tie(cotangent_own, small), "dp", axis=0, axis_index_groups=model_groups, tiled=True
    )
    gain_first = tie(gain_one, w_down_own, cotangent_own, updown_pieces)
    normed, pre = normed_product(input_rows, gain_first, w_mixer)
    mixed, *kept = mixer_forward(layouts, pre, params, width)
    out_terms = product_blocks(mixed, w_out)
    updown_pieces = exchange_apart(updown_pieces, [pre], out_terms[1:])
    w_updown = gather_copies(updown_pieces.reshape(parts * rows_own, 2 * units))
    stream = ((GROUP_ROWS, D), f32)
    narrow = ((GROUP_ROWS, D), bf)
    hidden, normed_two = by_rows(
        hidden_kernel,
        scatter_rows(out_terms) + [inputs, gain_two],
        [stream, narrow],
    )
    cotangent = from_own(part, cotangent)
    normed_two = jnp.concatenate(gather_rows(normed_two), 0)

    def swiglu_units(updown):
        return jax.nn.silu(updown[:, :units]) * updown[:, units:]

    updown = plain_product(normed_two, w_updown)
    active, swiglu_back = jax.vjp(swiglu_units, updown)
    active = active.astype(bf)
    d_active = transposed_product(cotangent, w_down)
    d_updown = swiglu_back(d_active)[0].astype(bf)
    d_normed_two = product_blocks(d_updown, w_updown, transposed=True)
    active = tie(active, *d_normed_two[1:])
    down_terms = grad_product(active, cotangent)
    updown_terms = grad_product(normed_two, tie(d_updown, down_terms))
    gain_late = tie(gain_two, updown_terms)
    d_normed_two = scatter_rows(d_normed_two)
    updown_grad = scatter_copies(tie(updown_terms, gain_late, *d_normed_two[1:]))
    d_hidden, d_mixed, gain_two_grad = by_rows(
        hidden_back_kernel,
        d_normed_two + [hidden, gain_late, cotangent_own],
        [stream, narrow, ((1, D), f32)],
    )


    out_terms = product_blocks(tie(active, d_mixed), w_down)
    down_grad = halve_cores(tie(down_terms, d_mixed))
    d_mixed = gather_rows(d_mixed)
    late = tie(params, down_grad, *out_terms)
    out_terms[1:] = tie_all(out_terms[1:], *d_mixed[1:])
    (block_out,) = by_rows(block_out_kernel, scatter_rows(out_terms) + [hidden], [narrow])
    d_pre, d_params = mixer_backward(layouts, pre, late, w_out, d_mixed, kept, width)
    mixer_terms = tie(grad_product(normed, d_pre, micros=20), updown_grad)
    mixer_grad = scatter_copies(mixer_terms)

    d_normed_terms = product_blocks(
        tie(d_pre, mixer_terms), w_mixer, transposed=True, micros=150
    )
    d_normed_terms[1:] = tie_all(d_normed_terms[1:], block_out)
    d_normed = scatter_rows(d_normed_terms)
    down_grad = halve_first(tie(down_grad, *d_normed_terms[1:]))
    gain_one_grad = 0.0
    for values, terms in zip(input_rows, d_normed_terms):
        values = values.astype(f32)
        terms = terms.astype(f32) * (values * row_scale(values))
        gain_one_grad = gain_one_grad + jnp.sum(terms, 0, keepdims=True)

    here = (jnp.arange(parts) == part).astype(f32)[:, None]
    taps_grad = d_params[:KERNEL].reshape(KERNEL, 3, 1, width) * here
    taps_grad = taps_grad.reshape(KERNEL, parts, copies, 3, rows_own).transpose(1, 2, 3, 0, 4)
    taps_grad = taps_grad.reshape(devices, 3 * KERNEL, rows_own)
    head_grad = (d_params[KERNEL, :width] * here).reshape(devices, 1, rows_own)
    gain_grads = [
        grad.reshape(copies, parts, 1, rows_own).swapaxes(0, 1).reshape(devices, 1, rows_own)
        for grad in (gain_one_grad, gain_two_grad)
    ]
    small_grad = jnp.concatenate([taps_grad, head_grad] + gain_grads, 1)
    small_grad = jnp.pad(small_grad, ((0, 0), (0, 1), (0, 128 - rows_own)))
    small_grad = jnp.sum(lax.all_to_all(small_grad, "dp", 0, 0, tiled=True), 0)[:, :rows_own]
    taps_shard = small_grad[: 3 * KERNEL].reshape(3, KERNEL, rows_own).swapaxes(1, 2)
    taps_shard = taps_shard.reshape(3 * rows_own, KERNEL)
    head_shard, gain_one_shard, gain_two_shard = small_grad[3 * KERNEL : 3 * KERNEL + 3]

    (input_grad,) = by_rows(input_back_kernel, d_normed + [inputs, gain_one, d_hidden], [narrow])
    updown_grad = updown_grad.reshape(parts, rows_own, 2 * units)
    updown_shard = updown_from_parts(exchange_apart(updown_grad, [input_grad]))
    out_shard = grad_product(tie(mixed, input_grad), jnp.concatenate(d_mixed, 0))
    out_shard = halve_second(halve_first(halve_cores(out_shard)))
    out_shard = from_wire(out_shard.astype(f32))
    down_shard = from_wire(halve_second(tie_all(down_grad, input_grad)).astype(f32))
    mixer_grad = exchange(mixer_grad.reshape(parts, rows_own, wide))
    qkv_shard, gate_shard, strengths = mixer_from_parts(mixer_grad, width)
    beta_shard = strengths.reshape(rows_own, parts, SMALL)[:, :, :heads_part]
    return (
        from_wire(block_out),
        from_wire(input_grad),
        gain_one_shard,
        taps_shard,
        head_shard,
        qkv_shard,
        beta_shard.reshape(rows_own, HEADS),
        gate_shard,
        out_shard,
        gain_two_shard,
        updown_shard,
        down_shard,
    )


def solution(mesh):
    placed = (
        P("dp", None),
        P("dp", None),
        P("dp"),
        P("dp", None),
        P("dp"),
        P("dp", None),
        P("dp", None),
        P("dp", None),
        P("dp", None),
        P("dp"),
        P("dp", None),
        P("dp", None),
        P("dp", None),
        P("dp"),
    )
    return jax.shard_map(
        body,
        mesh=mesh,
        in_specs=placed,
        out_specs=(
            P("dp", None),
            P("dp", None),
            P("dp"),
            P("dp", None),
            P("dp"),
            P("dp", None),
            P("dp", None),
            P("dp", None),
            P("dp", None),
            P("dp"),
            P("dp", None),
            P("dp", None),
        ),
        check_vma=False,
    )
```

```python
import functools

import jax
import jax.numpy as jnp
from jax import lax
from jax.experimental import pallas as pl
from jax.experimental.pallas import tpu as pltpu
from jax.sharding import PartitionSpec as P

D = 2048
HEADS = 16
HEAD_DIM = 128
FF = 5632
KERNEL = 4
BLOCK_ROWS = 64
BLOCKS_DEV = 2
GROUP_ROWS = BLOCK_ROWS * BLOCKS_DEV
SMALL = 128
MODEL = 4

f32 = jnp.float32
bf = jnp.bfloat16


def block_layouts(first, second, lead):
    def doc(block):
        in_first = (block >= lead) & (block < lead + first)
        in_second = (block >= lead + first) & (block < lead + first + second)
        return jnp.where(in_first, 1, jnp.where(in_second, 2, 0))

    starts = (lead == 1) | (lead + first == 1) & (second > 0)
    columns = [doc(0) > 0, doc(1) > 0, doc(0) == doc(1), ~starts]
    return jnp.stack(columns, 1).astype(f32)


def plain_product(left, right):
    return jnp.dot(left, right, preferred_element_type=f32)


def rows_product(left, right):
    return lax.dot_general(left, right, (((0,), (0,)), ((), ())), preferred_element_type=f32)


def transposed_product(left, right):
    return lax.dot_general(left, right, (((1,), (1,)), ((), ())), preferred_element_type=f32)


def halves(values):
    high = values.astype(bf)
    return high, (values - high.astype(f32)).astype(bf)


def exact(left, right, left_dim, right_dim):
    left_high, left_low = left if isinstance(left, tuple) else halves(left)
    right_high, right_low = right if isinstance(right, tuple) else halves(right)
    return lax.dot_general(
        jnp.concatenate([left_high, left_high, left_low], left_dim),
        jnp.concatenate([right_high, right_low, right_high], right_dim),
        (((left_dim,), (right_dim,)), ((), ())),
        preferred_element_type=f32,
    )


def stacked(first, second):
    return tuple(jnp.concatenate([a, b], 0) for a, b in zip(first, second))


class Tile:
    def __init__(self, layout_ref, group):
        live_first, live_second, same, persist = (layout_ref[group, i] for i in range(4))
        shape = (GROUP_ROWS, HEAD_DIM)
        row = lax.broadcasted_iota(jnp.int32, shape, 0)
        col = lax.broadcasted_iota(jnp.int32, shape, 1)
        late = row >= BLOCK_ROWS
        self.row, self.col = row, col
        self.live = jnp.where(late, live_second, live_first)
        self.taps = [None] + [
            jnp.where(
                row < offset,
                0.0,
                jnp.where(late & (row < BLOCK_ROWS + offset), same, 1.0),
            )
            for offset in range(1, KERNEL)
        ]
        cross = jnp.where(late & (col < BLOCK_ROWS), persist, 1.0)
        self.lower = jnp.where(row > col, cross, 0.0)
        self.lower_full = jnp.where(row >= col, cross, 0.0)

    def earlier(self, values, offset):
        return pltpu.roll(values, offset, 0) * self.taps[offset]

    def later(self, values, offset):
        return pltpu.roll(values * self.taps[offset], GROUP_ROWS - offset, 0)


def convolve(tile, values, taps):
    total = values * taps[0]
    for offset in range(1, KERNEL):
        total = total + tile.earlier(values, offset) * taps[offset]
    return total


def unit_scale(values):
    return lax.rsqrt(jnp.sum(values * values, -1, keepdims=True) + 1e-06)


def head_columns(part_width, section, head):
    return pl.ds(section * part_width + head * HEAD_DIM, HEAD_DIM)


def unit_inverses(tile, lowers):
    eye = jnp.where(tile.row == tile.col, 1.0, 0.0)
    inverses = None
    size = 1
    while size < GROUP_ROWS:
        pair = tile.row // (2 * size) == tile.col // (2 * size)
        split = pair & (tile.row // size != tile.col // size)
        parts = [jnp.where(split, lower, 0.0) for lower in lowers]
        if inverses is None:
            inverses = [eye - part for part in parts]
        else:
            kept = [halves(inverse) for inverse in inverses]
            inner = [exact(part, known, 1, 0) for part, known in zip(parts, kept)]
            outer = [exact(known, value, 1, 0) for known, value in zip(kept, inner)]
            inverses = [inverse - value for inverse, value in zip(inverses, outer)]
        size *= 2
    return inverses


def mixer_forward_kernel(
    layout_ref, pre_ref, param_ref, mixed_ref, inverse_ref, score_ref, solved_ref, out_ref
):
    width = mixed_ref.shape[1]
    heads = range(width // HEAD_DIM)
    tile = Tile(layout_ref, pl.program_id(0))
    queries, keys, values, strengths = [], [], [], []
    for head in heads:
        parts = []
        for section in range(3):
            columns = head_columns(width, section, head)
            taps = [param_ref[offset : offset + 1, columns] for offset in range(KERNEL)]
            convolved = convolve(tile, pre_ref[:, columns], taps)
            parts.append(convolved * jax.nn.sigmoid(convolved))
        queries.append(parts[0] * (unit_scale(parts[0]) * HEAD_DIM**-0.5))
        keys.append(parts[1] * unit_scale(parts[1]))
        values.append(parts[2])
        start = 4 * width + head
        strengths.append(jax.nn.sigmoid(pre_ref[:, start : start + 1]) * tile.live)
    lowers, scores = [], []
    for head in heads:
        key_halves = halves(keys[head])
        both = exact(stacked(key_halves, halves(queries[head])), key_halves, 1, 1)
        lowers.append(both[:GROUP_ROWS] * strengths[head] * tile.lower)
        scores.append(both[GROUP_ROWS:] * tile.lower_full)
    inverses = unit_inverses(tile, lowers)
    solved = [exact(inverses[head], values[head] * strengths[head], 1, 0) for head in heads]
    outs = [exact(scores[head], solved[head], 1, 0) for head in heads]
    for head in heads:
        out = outs[head]
        scaled = out * lax.rsqrt(jnp.mean(out * out, -1, keepdims=True) + 1e-05)
        gate = pre_ref[:, head_columns(width, 3, head)]
        gain = param_ref[KERNEL : KERNEL + 1, head_columns(width, 0, head)]
        mixed = scaled * gain * (gate * jax.nn.sigmoid(gate)) * tile.live
        mixed_ref[:, head_columns(width, 0, head)] = mixed.astype(bf)
        inverse_ref[head] = inverses[head]
        score_ref[head] = scores[head]
        solved_ref[head] = solved[head]
        out_ref[head] = out


def mixer_backward_kernel(
    layout_ref,
    pre_ref,
    param_ref,
    weight_ref,
    inverse_ref,
    score_ref,
    solved_ref,
    out_ref,
    *refs,
):
    *mixed_refs, d_pre_ref, d_param_ref, grad_ref = refs
    width = grad_ref.shape[1]
    heads = range(width // HEAD_DIM)
    tile = Tile(layout_ref, pl.program_id(0))
    for group, mixed_ref in enumerate(mixed_refs):

        @pl.when(pl.program_id(0) == group)
        def _():
            grad_ref[...] = transposed_product(mixed_ref[...], weight_ref[...])

    @pl.when(pl.program_id(0) == 0)
    def _():
        d_param_ref[...] = jnp.zeros_like(d_param_ref)

    def along(values):
        return jnp.sum(values, -1, keepdims=True)

    d_outs = []
    for head in heads:
        columns = head_columns(width, 0, head)
        d_mixed = grad_ref[:, columns] * tile.live
        out = out_ref[head]
        scale = lax.rsqrt(jnp.mean(out * out, -1, keepdims=True) + 1e-05)
        scaled = out * scale
        gate = pre_ref[:, head_columns(width, 3, head)]
        gate_open = jax.nn.sigmoid(gate)
        gain = param_ref[KERNEL : KERNEL + 1, columns]
        gated = d_mixed * (gate * gate_open)
        d_param_ref[KERNEL : KERNEL + 1, columns] += jnp.sum(gated * scaled, 0, keepdims=True)
        d_gate = d_mixed * scaled * gain * (gate_open * (1.0 + gate * (1.0 - gate_open)))
        d_pre_ref[:, head_columns(width, 3, head)] = d_gate.astype(bf)
        d_scaled = gated * gain
        mean = jnp.mean(d_scaled * out, -1, keepdims=True)
        d_outs.append(scale * d_scaled - out * (scale * scale * scale * mean))
    d_out_halves = [halves(value) for value in d_outs]
    solved_halves = [halves(solved_ref[head]) for head in heads]
    d_solved = [exact(score_ref[head], d_out_halves[head], 0, 0) for head in heads]
    d_scores = [
        exact(d_out_halves[head], solved_halves[head], 1, 1) * tile.lower_full for head in heads
    ]
    d_inner = [exact(inverse_ref[head], d_solved[head], 0, 0) for head in heads]
    d_lowers = [exact(d_inner[head], solved_halves[head], 1, 1) * -tile.lower for head in heads]
    d_beta = jnp.zeros((GROUP_ROWS, SMALL), f32)
    for head in heads:
        pres, convolved, opened, active = [], [], [], []
        for section in range(3):
            columns = head_columns(width, section, head)
            taps = [param_ref[offset : offset + 1, columns] for offset in range(KERNEL)]
            pres.append(pre_ref[:, columns])
            convolved.append(convolve(tile, pres[section], taps))
            opened.append(jax.nn.sigmoid(convolved[section]))
            active.append(convolved[section] * opened[section])
        query_scale = unit_scale(active[0])
        key_scale = unit_scale(active[1])
        query_unit = active[0] * query_scale
        key = active[1] * key_scale
        start = 4 * width + head
        opening = jax.nn.sigmoid(pre_ref[:, start : start + 1])
        strength = opening * tile.live
        d_both = stacked(halves(d_lowers[head]), halves(d_scores[head]))
        by_key = exact(d_both, key, 1, 0)
        d_query = by_key[GROUP_ROWS:] * HEAD_DIM**-0.5
        from_lower = by_key[:GROUP_ROWS]
        weighted = stacked(halves(key * strength), halves(query_unit * HEAD_DIM**-0.5))
        d_key = strength * from_lower + exact(d_both, weighted, 0, 0)
        d_strength = along(d_inner[head] * active[2] + from_lower * key)
        d_value = d_inner[head] * strength
        d_opening = d_strength * (opening * (1.0 - opening)) * tile.live
        d_beta = d_beta + jnp.where(tile.col == head, d_opening, 0.0)
        d_active = [
            (d_query - query_unit * along(query_unit * d_query)) * query_scale,
            (d_key - key * along(key * d_key)) * key_scale,
            d_value,
        ]
        for section in range(3):
            columns = head_columns(width, section, head)
            taps = [param_ref[offset : offset + 1, columns] for offset in range(KERNEL)]
            slope = opened[section] * (1.0 + convolved[section] * (1.0 - opened[section]))
            d_convolved = d_active[section] * slope
            d_pre = d_convolved * taps[0]
            sums = [jnp.sum(d_convolved * pres[section], 0, keepdims=True)]
            for offset in range(1, KERNEL):
                d_pre = d_pre + tile.later(d_convolved, offset) * taps[offset]
                sums.append(
                    jnp.sum(d_convolved * tile.earlier(pres[section], offset), 0, keepdims=True)
                )
            d_param_ref[0:KERNEL, columns] += jnp.concatenate(sums, 0)
            d_pre_ref[:, columns] = d_pre.astype(bf)
    d_pre_ref[:, 4 * width :] = d_beta.astype(bf)


NO_COST = pl.CostEstimate(flops=0, bytes_accessed=0, transcendentals=0)


def call(kernel, operands, in_specs, out_specs, out_shape, grid=(), scratch=(), micros=0):
    results = pl.pallas_call(
        kernel,
        grid=grid,
        in_specs=in_specs,
        out_specs=out_specs,
        out_shape=out_shape,
        scratch_shapes=scratch,
        compiler_params=pltpu.CompilerParams(
            dimension_semantics=("arbitrary",) * len(grid), vmem_limit_bytes=48 * 2**20
        ),
        cost_estimate=pl.CostEstimate(
            flops=micros * 10**9, bytes_accessed=0, transcendentals=0
        ),
    )(*operands)
    return list(results)


def whole(array):
    return pl.BlockSpec(array.shape, lambda *step: (0,) * len(array.shape))


def mixer_specs(width):
    wide = 4 * width + SMALL
    heads = width // HEAD_DIM
    layout = pl.BlockSpec(memory_space=pltpu.SMEM)
    pre = pl.BlockSpec((GROUP_ROWS, wide), lambda group: (group, 0))
    param = pl.BlockSpec((2 * KERNEL, 3 * width), lambda group: (0, 0))
    narrow = pl.BlockSpec((GROUP_ROWS, width), lambda group: (group, 0))
    square = pl.BlockSpec((heads, GROUP_ROWS, HEAD_DIM), lambda group: (group, 0, 0))
    return layout, pre, param, narrow, square


def mixer_forward(layout, pre, params, width):
    groups = layout.shape[0]
    layout_spec, pre_spec, param_spec, narrow, square = mixer_specs(width)
    squares = pltpu.HBM((groups * width // HEAD_DIM, GROUP_ROWS, HEAD_DIM), f32)
    return call(
        mixer_forward_kernel,
        [layout, pre, params],
        [layout_spec, pre_spec, param_spec],
        [narrow] + [square] * 4,
        [jax.ShapeDtypeStruct((groups * GROUP_ROWS, width), bf)] + [squares] * 4,
        (groups,),
    )


def mixer_backward(layout, pre, params, weight, d_mixed, kept, width):
    groups = layout.shape[0]
    layout_spec, pre_spec, param_spec, _, square = mixer_specs(width)
    kept = [pltpu.with_memory_space_constraint(array, pltpu.HBM) for array in kept]
    return call(
        mixer_backward_kernel,
        [layout, pre, params, weight, *kept, *d_mixed],
        [layout_spec, pre_spec, param_spec, whole(weight)]
        + [square] * 4
        + [whole(block) for block in d_mixed],
        [pre_spec, param_spec],
        [jax.ShapeDtypeStruct(pre.shape, bf), jax.ShapeDtypeStruct(params.shape, f32)],
        (groups,),
        [pltpu.VMEM((GROUP_ROWS, width), f32)],
        micros=60,
    )


def first_kernel(gain_ref, weight_ref, *refs):
    *value_refs, normed_ref, out_ref, scale_ref, total_ref = refs
    step, depth = pl.program_id(0), weight_ref.shape[0]

    @pl.when(step == 0)
    def _():
        for group, ref in enumerate(value_refs):
            values = ref[...].astype(f32)
            scale = lax.rsqrt(jnp.mean(values * values, -1, keepdims=True) + 1e-06)
            rows = pl.ds(group * GROUP_ROWS, GROUP_ROWS)
            scale_ref[rows, :] = jnp.broadcast_to(scale, (GROUP_ROWS, 128))
        total_ref[...] = jnp.zeros_like(total_ref)

    columns = pl.ds(pl.multiple_of(step * depth, depth), depth)
    for group, ref in enumerate(value_refs):
        rows = pl.ds(group * GROUP_ROWS, GROUP_ROWS)
        values = ref[:, columns].astype(f32) * scale_ref[rows, :1] * gain_ref[...]
        normed_ref[rows, :] = values.astype(bf)
    total_ref[...] += plain_product(normed_ref[...], weight_ref[...])

    @pl.when(step == pl.num_programs(0) - 1)
    def _():
        out_ref[...] = total_ref[...]


def normed_product(blocks, gain, weight, depth=512):
    rows, (features, columns) = len(blocks) * GROUP_ROWS, weight.shape
    return call(
        first_kernel,
        [gain, weight, *blocks],
        [
            pl.BlockSpec((1, depth), lambda step: (0, step)),
            pl.BlockSpec((depth, columns), lambda step: (step, 0)),
        ]
        + [whole(block) for block in blocks],
        [
            pl.BlockSpec((rows, depth), lambda step: (0, step)),
            pl.BlockSpec((rows, columns), lambda step: (0, 0)),
        ],
        [
            jax.ShapeDtypeStruct((rows, features), bf),
            jax.ShapeDtypeStruct((rows, columns), f32),
        ],
        (features // depth,),
        [pltpu.VMEM((rows, 128), f32), pltpu.VMEM((rows, columns), f32)],
    )


def product_blocks(left, right, transposed=False, block=512, micros=0):
    product = transposed_product if transposed else plain_product
    columns = right.shape[0] if transposed else right.shape[1]
    groups = left.shape[0] // GROUP_ROWS

    def kernel(left_ref, right_ref, *out_refs):
        total = product(left_ref[...], right_ref[...])
        for group, ref in enumerate(out_refs):
            ref[...] = total[group * GROUP_ROWS : (group + 1) * GROUP_ROWS].astype(ref.dtype)

    if transposed:
        right_spec = pl.BlockSpec((block, right.shape[1]), lambda step: (step, 0))
    else:
        right_spec = pl.BlockSpec((right.shape[0], block), lambda step: (0, step))
    return call(
        kernel,
        [left, right],
        [whole(left), right_spec],
        [pl.BlockSpec((GROUP_ROWS, block), lambda step: (0, step))] * groups,
        [
            jax.ShapeDtypeStruct((GROUP_ROWS, columns), bf if group else f32)
            for group in range(groups)
        ],
        (columns // block,),
        micros=micros,
    )


def grad_product(left, right, block=256, micros=0):
    rows, features = left.shape
    if features % block:
        block = 128

    def kernel(left_ref, right_ref, out_ref):
        out_ref[...] = rows_product(left_ref[...], right_ref[...]).astype(bf)

    return call(
        kernel,
        [left, right],
        [pl.BlockSpec((rows, block), lambda step: (0, step)), whole(right)],
        [pl.BlockSpec((block, right.shape[1]), lambda step: (step, 0))],
        [pltpu.HBM((features, right.shape[1]), bf)],
        (features // block,),
        micros=micros,
    )[0]


def from_own(part, values):
    groups = values.shape[0] // GROUP_ROWS

    def kernel(part_ref, values_ref, out_ref):
        for step in range(groups):
            source = lax.rem(part_ref[0] + groups - step, groups) * GROUP_ROWS
            rows = pl.ds(pl.multiple_of(source, GROUP_ROWS), GROUP_ROWS)
            out_ref[step * GROUP_ROWS : (step + 1) * GROUP_ROWS] = values_ref[rows]

    return call(
        kernel,
        [part.reshape(1).astype(jnp.int32), values],
        [pl.BlockSpec(memory_space=pltpu.SMEM), whole(values)],
        [whole(values)],
        [jax.ShapeDtypeStruct(values.shape, values.dtype)],
        (1,),
    )[0]


def tie_all(values, *others):
    anywhere = pl.BlockSpec(memory_space=pl.ANY)
    tied = pl.pallas_call(
        lambda *refs: None,
        in_specs=[anywhere] * (len(values) + len(others)),
        out_specs=[anywhere] * len(values),
        out_shape=[jax.ShapeDtypeStruct(value.shape, value.dtype) for value in values],
        input_output_aliases={i: i for i in range(len(values))},
        cost_estimate=NO_COST,
    )(*values, *others)
    return list(tied)


def tie(value, *others):
    return tie_all([value], *others)[0]


def assemble(part, values, received, others):
    parts = values.shape[0]

    def kernel(part_ref, values_ref, *refs):
        own = part_ref[0]
        out_ref = refs[-1]
        out_ref[own] = values_ref[own]
        for step in range(1, parts):
            out_ref[lax.rem(own + parts - step, parts)] = refs[step - 1][...]

    vmem = pl.BlockSpec(memory_space=pltpu.VMEM)
    anywhere = pl.BlockSpec(memory_space=pl.ANY)
    return pl.pallas_call(
        kernel,
        in_specs=[pl.BlockSpec(memory_space=pltpu.SMEM)]
        + [vmem] * parts
        + [anywhere] * len(others),
        out_specs=vmem,
        out_shape=jax.ShapeDtypeStruct(values.shape, values.dtype),
        compiler_params=pltpu.CompilerParams(vmem_limit_bytes=32 * 2**20),
        cost_estimate=NO_COST,
    )(part.reshape(1).astype(jnp.int32), values, *received, *others)


def copy_columns(count, *refs):
    target = refs[-1]
    start = 0
    for source in refs[:count]:
        block = source[...].reshape(source.shape[-2:])
        columns = pl.ds(start, block.shape[1])
        if len(target.shape) == 3:
            target[0, :, columns] = block.astype(target.dtype)
        else:
            target[:, columns] = block.astype(target.dtype)
        start += block.shape[1]


def to_parts(sources, parts, dtype, others=()):
    rows = sources[0][0].shape[0]

    def spec(section, width):
        return pl.BlockSpec((rows, width), lambda p: (0, section * parts + p))

    total = sum(width for _, _, width in sources)
    return pl.pallas_call(
        functools.partial(copy_columns, len(sources)),
        grid=(parts,),
        in_specs=[spec(section, width) for _, section, width in sources]
        + [pl.BlockSpec(memory_space=pl.ANY)] * len(others),
        out_specs=pl.BlockSpec((1, rows, total), lambda p: (p, 0, 0)),
        out_shape=jax.ShapeDtypeStruct((parts, rows, total), dtype),
        cost_estimate=NO_COST,
    )(*[array for array, _, _ in sources], *others)


def updown_from_parts(slabs):
    parts, rows, width = slabs.shape
    units = width // 2

    def kernel(slabs_ref, out_ref):
        for p in range(parts):
            out_ref[:, p * units : (p + 1) * units] = slabs_ref[p].astype(f32)

    return pl.pallas_call(
        kernel,
        grid=(2,),
        in_specs=[pl.BlockSpec((parts, rows, units), lambda half: (0, 0, half))],
        out_specs=pl.BlockSpec((rows, parts * units), lambda half: (0, half)),
        out_shape=jax.ShapeDtypeStruct((rows, parts * width), f32),
        compiler_params=pltpu.CompilerParams(vmem_limit_bytes=32 * 2**20),
        cost_estimate=NO_COST,
    )(slabs)


def mixer_from_parts(slabs, width):
    parts, rows, _ = slabs.shape

    def kernel(slabs_ref, qkv_ref, gate_ref, strength_ref):
        for p in range(parts):
            for section in range(4):
                block = slabs_ref[p, :, section * width : (section + 1) * width].astype(f32)
                if section < 3:
                    start = (section * parts + p) * width
                    qkv_ref[:, start : start + width] = block
                else:
                    gate_ref[:, p * width : (p + 1) * width] = block
            last = slabs_ref[p, :, 4 * width :].astype(f32)
            strength_ref[:, p * SMALL : (p + 1) * SMALL] = last

    widths = [3 * parts * width, parts * width, parts * SMALL]
    return pl.pallas_call(
        kernel,
        out_shape=[jax.ShapeDtypeStruct((rows, size), f32) for size in widths],
        compiler_params=pltpu.CompilerParams(vmem_limit_bytes=32 * 2**20),
        cost_estimate=NO_COST,
    )(slabs)


def total_of(own_ref, received_refs):
    total = own_ref[...]
    for ref in received_refs:
        total = total + ref[...].astype(f32)
    return total


def row_scale(values):
    return lax.rsqrt(jnp.mean(values * values, -1, keepdims=True) + 1e-06)


def norm_slope(values, scale, gain, grad):
    mean = jnp.mean(gain * grad * values, -1, keepdims=True)
    return scale * gain * grad - values * (scale * scale * scale * mean)


def hidden_kernel(own_ref, *refs):
    *received, input_ref, gain_ref, hidden_ref, normed_ref = refs
    hidden = input_ref[...].astype(f32) + total_of(own_ref, received)
    hidden_ref[...] = hidden
    normed_ref[...] = (hidden * row_scale(hidden) * gain_ref[...]).astype(bf)


def hidden_back_kernel(own_ref, *refs):
    *received, hidden_ref, gain_ref, cot_ref, d_hidden_ref, d_mixed_ref, d_gain_ref = refs
    grad = total_of(own_ref, received)
    hidden = hidden_ref[...]
    scale = row_scale(hidden)

    @pl.when(pl.program_id(0) == 0)
    def _():
        d_gain_ref[...] = jnp.zeros_like(d_gain_ref)

    d_gain_ref[...] += jnp.sum(grad * hidden * scale, 0, keepdims=True)
    d_hidden = cot_ref[...].astype(f32) + norm_slope(hidden, scale, gain_ref[...], grad)
    d_hidden_ref[...] = d_hidden
    d_mixed_ref[...] = d_hidden.astype(bf)


def input_back_kernel(own_ref, *refs):
    *received, input_ref, gain_ref, d_hidden_ref, out_ref = refs
    grad = total_of(own_ref, received)
    values = input_ref[...].astype(f32)
    slope = norm_slope(values, row_scale(values), gain_ref[...], grad)
    out_ref[...] = (d_hidden_ref[...] + slope).astype(bf)


def block_out_kernel(own_ref, *refs):
    *received, hidden_ref, out_ref = refs
    out_ref[...] = (hidden_ref[...] + total_of(own_ref, received)).astype(bf)


def by_rows(kernel, arrays, outs, block=64):
    def spec(shape):
        if shape[0] == 1:
            return pl.BlockSpec(shape, lambda i: (0, 0))
        return pl.BlockSpec((block, shape[1]), lambda i: (i, 0))

    return pl.pallas_call(
        kernel,
        grid=(GROUP_ROWS // block,),
        in_specs=[spec(array.shape) for array in arrays],
        out_specs=[spec(shape) for shape, _ in outs],
        out_shape=[jax.ShapeDtypeStruct(shape, dtype) for shape, dtype in outs],
        compiler_params=pltpu.CompilerParams(dimension_semantics=("arbitrary",)),
        cost_estimate=NO_COST,
    )(*arrays)


def body(
    block_in,
    out_grad,
    norm1_gain,
    conv_weight,
    head_gain,
    qkv_weight,
    beta_weight,
    gate_weight,
    out_weight,
    norm2_gain,
    updown_weight,
    down_weight,
    seq_blocks,
    lead_blocks,
):
    devices = lax.axis_size("dp")
    parts = MODEL
    copies = devices // parts
    part = lax.axis_index("dp") // copies
    copy = lax.axis_index("dp") % copies
    rows_own = qkv_weight.shape[0]
    width = D // parts
    units = FF // parts
    heads_part = HEADS // parts
    wide = 4 * width + SMALL
    model_groups = [[m * copies + t for m in range(parts)] for t in range(copies)]
    copy_groups = [[m * copies + t for t in range(copies)] for m in range(parts)]

    def exchange(values):
        return lax.all_to_all(
            values, "dp", split_axis=0, concat_axis=0, axis_index_groups=model_groups, tiled=True
        )

    def shift(values, step):
        pairs = [
            (m * copies + t, (m + step) % parts * copies + t)
            for m in range(parts)
            for t in range(copies)
        ]
        return lax.ppermute(values, "dp", pairs)

    def exchange_apart(values, before, after=()):
        cut = [
            lax.dynamic_index_in_dim(values, (part + step) % parts, 0, keepdims=False)
            for step in range(1, parts)
        ]
        received = [shift(piece, step) for step, piece in enumerate(tie_all(cut, *before), 1)]
        return assemble(part, values, received, after)

    def gather_rows(values):
        return [values] + [shift(values, step) for step in range(1, parts)]

    def scatter_rows(terms):
        return [terms[0]] + [shift(block, -step) for step, block in enumerate(terms[1:], 1)]

    def gather_copies(values):
        return lax.all_gather(values, "dp", axis=0, axis_index_groups=copy_groups, tiled=True)

    def scatter_copies(values):
        return lax.psum_scatter(
            values.astype(bf),
            "dp",
            scatter_dimension=0,
            axis_index_groups=copy_groups,
            tiled=True,
        )

    def halves_across(values, bit, axis):
        pairs = [(i, i ^ (1 << bit)) for i in range(devices)]
        side = (copy >> bit) & 1
        own = lax.dynamic_index_in_dim(values, side, axis, keepdims=False)
        other = lax.dynamic_index_in_dim(values, 1 - side, axis, keepdims=False)
        return own, lax.ppermute(other, "dp", pairs)

    def halve(values, bit, axis, *others):
        own, received = halves_across(values, bit, axis)
        if others:
            received = tie(received, *others)
        return (own.astype(f32) + received.astype(f32)).astype(bf)

    by_halves = copies == 8

    def halve_cores(values, *others):
        if not by_halves:
            return values
        rows, columns = values.shape
        return halve(values.reshape(2, 2, 2, rows // 8, columns), 0, 2, *others)

    def halve_first(values):
        if not by_halves:
            return [values]
        middle = values.shape[-1] // 2
        return [halve(values[..., :middle], 1, 1), halve(values[..., middle:], 2, 0)]

    def halve_second(values):
        if not by_halves:
            return scatter_copies(values[0])
        return jnp.concatenate([halve(values[0], 2, 0), halve(values[1], 1, 0)], 1)

    def to_wire(values):
        return values.reshape(-1, parts, copies, rows_own).swapaxes(1, 2).reshape(-1, D)

    def from_wire(values):
        return values.reshape(-1, copies, parts, rows_own).swapaxes(1, 2).reshape(-1, D)

    w_out_own = to_wire(out_weight.astype(bf))
    w_out = gather_copies(w_out_own)
    strengths = beta_weight.reshape(rows_own, parts, heads_part)
    strengths = jnp.pad(strengths, ((0, 0), (0, 0), (0, SMALL - heads_part)))
    strengths = tie(strengths.reshape(rows_own, parts * SMALL), w_out_own)
    pieces = [(qkv_weight, section, width) for section in range(3)]
    pieces = to_parts(pieces + [(gate_weight, 0, width), (strengths, 0, SMALL)], parts, bf)
    mixer_pieces = tie(exchange(pieces), w_out)
    w_mixer = gather_copies(mixer_pieces.reshape(parts * rows_own, wide))
    inputs = tie(to_wire(block_in), mixer_pieces)
    input_rows = gather_rows(inputs)

    lanes = -(-3 * rows_own // 128) * 128
    numbers = jnp.concatenate([seq_blocks[0], lead_blocks]).astype(f32)
    small = [conv_weight.T, norm1_gain[None], head_gain[None], norm2_gain[None], numbers[None]]
    small = [jnp.pad(rows, ((0, 0), (0, lanes - rows.shape[1]))) for rows in small]
    small = jnp.pad(jnp.concatenate(small, 0).astype(bf), ((0, 2 * KERNEL), (0, 0)))
    small = jnp.broadcast_to(small[None], (devices,) + small.shape)
    small = lax.all_to_all(tie(small, input_rows[1]), "dp", 0, 0, tiled=True)
    taps = small[:, :KERNEL, : 3 * rows_own].swapaxes(0, 1).reshape(KERNEL, 3, parts, width)
    taps = lax.dynamic_index_in_dim(taps, part, 2, keepdims=False).reshape(KERNEL, 3 * width)
    gain_one, head_full, gain_two = (
        small[:, KERNEL + i, :rows_own].reshape(1, D).astype(f32) for i in range(3)
    )
    gain_one, gain_two = to_wire(gain_one), to_wire(gain_two)
    head_part = lax.dynamic_slice_in_dim(head_full, part * width, width, 1)
    params = jnp.concatenate([taps.astype(f32), jnp.pad(head_part, ((0, 0), (0, 2 * width)))], 0)
    params = jnp.pad(params, ((0, KERNEL - 1), (0, 0)))
    numbers = small[:, KERNEL + 3, :3].astype(f32).astype(jnp.int32)
    layouts = block_layouts(numbers[:, 0], numbers[:, 1], numbers[:, 2])
    layouts = layouts.reshape(parts, copies, 4)
    layouts = lax.dynamic_index_in_dim(layouts, copy, 1, keepdims=False)
    wanted = (part - jnp.arange(parts)) % parts
    wanted = (wanted[:, None] == jnp.arange(parts)).astype(f32)
    layouts = jnp.sum(wanted[:, :, None] * layouts, 1)

    pieces = [(updown_weight, half, units) for half in range(2)]
    updown_pieces = to_parts(pieces, parts, bf, input_rows[1:] + [small])
    w_down_own = to_wire(down_weight.astype(bf))
    w_down = gather_copies(tie(w_down_own, *input_rows[1:]))
    cotangent_own = to_wire(out_grad)

    cotangent = lax.all_gather(
        tie(cotangent_own, small), "dp", axis=0, axis_index_groups=model_groups, tiled=True
    )
    gain_first = tie(gain_one, w_down_own, cotangent_own, updown_pieces)
    normed, pre = normed_product(input_rows, gain_first, w_mixer)
    mixed, *kept = mixer_forward(layouts, pre, params, width)
    out_terms = product_blocks(mixed, w_out)
    updown_pieces = exchange_apart(updown_pieces, [pre], out_terms[1:])
    w_updown = gather_copies(updown_pieces.reshape(parts * rows_own, 2 * units))
    stream = ((GROUP_ROWS, D), f32)
    narrow = ((GROUP_ROWS, D), bf)
    hidden, normed_two = by_rows(
        hidden_kernel,
        scatter_rows(out_terms) + [inputs, gain_two],
        [stream, narrow],
    )
    cotangent = from_own(part, cotangent)
    normed_two = jnp.concatenate(gather_rows(normed_two), 0)

    def swiglu_units(updown):
        return jax.nn.silu(updown[:, :units]) * updown[:, units:]

    updown = plain_product(normed_two, w_updown)
    active, swiglu_back = jax.vjp(swiglu_units, updown)
    active = active.astype(bf)
    d_active = transposed_product(cotangent, w_down)
    d_updown = swiglu_back(d_active)[0].astype(bf)
    d_normed_two = product_blocks(d_updown, w_updown, transposed=True)
    active = tie(active, *d_normed_two[1:])
    down_terms = grad_product(active, cotangent)
    updown_terms = grad_product(normed_two, tie(d_updown, down_terms))
    gain_late = tie(gain_two, updown_terms)
    d_normed_two = scatter_rows(d_normed_two)
    updown_grad = scatter_copies(tie(updown_terms, gain_late, *d_normed_two[1:]))
    d_hidden, d_mixed, gain_two_grad = by_rows(
        hidden_back_kernel,
        d_normed_two + [hidden, gain_late, cotangent_own],
        [stream, narrow, ((1, D), f32)],
    )


    out_terms = product_blocks(tie(active, d_mixed), w_down)
    down_terms = tie(down_terms, *out_terms[1:])
    d_mixed = gather_rows(d_mixed)
    late = tie(params, *out_terms)
    out_terms[1:] = tie_all(out_terms[1:], *d_mixed[1:])
    d_pre, d_params = mixer_backward(layouts, pre, late, w_out, d_mixed, kept, width)
    mixer_terms = tie(grad_product(normed, d_pre, micros=20), updown_grad)
    mixer_grad = scatter_copies(mixer_terms)

    d_normed_terms = product_blocks(
        tie(d_pre, mixer_terms), w_mixer, transposed=True, micros=150
    )
    hidden = tie(hidden, d_normed_terms[0])
    (block_out,) = by_rows(block_out_kernel, scatter_rows(out_terms) + [hidden], [narrow])
    d_normed_terms[1:] = tie_all(d_normed_terms[1:], block_out)
    d_normed = scatter_rows(d_normed_terms)
    down_grad = halve_first(halve_cores(down_terms, *d_normed_terms[1:]))
    gain_one_grad = 0.0
    for values, terms in zip(input_rows, d_normed_terms):
        values = values.astype(f32)
        terms = terms.astype(f32) * (values * row_scale(values))
        gain_one_grad = gain_one_grad + jnp.sum(terms, 0, keepdims=True)

    here = (jnp.arange(parts) == part).astype(f32)[:, None]
    taps_grad = d_params[:KERNEL].reshape(KERNEL, 3, 1, width) * here
    taps_grad = taps_grad.reshape(KERNEL, parts, copies, 3, rows_own).transpose(1, 2, 3, 0, 4)
    taps_grad = taps_grad.reshape(devices, 3 * KERNEL, rows_own)
    head_grad = (d_params[KERNEL, :width] * here).reshape(devices, 1, rows_own)
    gain_grads = [
        grad.reshape(copies, parts, 1, rows_own).swapaxes(0, 1).reshape(devices, 1, rows_own)
        for grad in (gain_one_grad, gain_two_grad)
    ]
    small_grad = jnp.concatenate([taps_grad, head_grad] + gain_grads, 1)
    small_grad = jnp.pad(small_grad, ((0, 0), (0, 1), (0, 128 - rows_own)))
    small_grad = jnp.sum(lax.all_to_all(small_grad, "dp", 0, 0, tiled=True), 0)[:, :rows_own]
    taps_shard = small_grad[: 3 * KERNEL].reshape(3, KERNEL, rows_own).swapaxes(1, 2)
    taps_shard = taps_shard.reshape(3 * rows_own, KERNEL)
    head_shard, gain_one_shard, gain_two_shard = small_grad[3 * KERNEL : 3 * KERNEL + 3]

    (input_grad,) = by_rows(input_back_kernel, d_normed + [inputs, gain_one, d_hidden], [narrow])
    updown_grad = updown_grad.reshape(parts, rows_own, 2 * units)
    updown_shard = updown_from_parts(exchange_apart(updown_grad, [mixer_terms], [input_grad]))
    out_shard = grad_product(tie(mixed, input_grad), jnp.concatenate(d_mixed, 0))
    out_shard = halve_second(halve_first(halve_cores(out_shard)))
    out_shard = from_wire(out_shard.astype(f32))
    down_shard = from_wire(halve_second(tie_all(down_grad, input_grad)).astype(f32))
    mixer_grad = exchange(mixer_grad.reshape(parts, rows_own, wide))
    qkv_shard, gate_shard, strengths = mixer_from_parts(mixer_grad, width)
    beta_shard = strengths.reshape(rows_own, parts, SMALL)[:, :, :heads_part]
    return (
        from_wire(block_out),
        from_wire(input_grad),
        gain_one_shard,
        taps_shard,
        head_shard,
        qkv_shard,
        beta_shard.reshape(rows_own, HEADS),
        gate_shard,
        out_shard,
        gain_two_shard,
        updown_shard,
        down_shard,
    )


def solution(mesh):
    placed = (
        P("dp", None),
        P("dp", None),
        P("dp"),
        P("dp", None),
        P("dp"),
        P("dp", None),
        P("dp", None),
        P("dp", None),
        P("dp", None),
        P("dp"),
        P("dp", None),
        P("dp", None),
        P("dp", None),
        P("dp"),
    )
    return jax.shard_map(
        body,
        mesh=mesh,
        in_specs=placed,
        out_specs=(
            P("dp", None),
            P("dp", None),
            P("dp"),
            P("dp", None),
            P("dp"),
            P("dp", None),
            P("dp", None),
            P("dp", None),
            P("dp", None),
            P("dp"),
            P("dp", None),
            P("dp", None),
        ),
        check_vma=False,
    )
```

```python
import functools

import jax
import jax.numpy as jnp
from jax import lax
from jax.experimental import pallas as pl
from jax.experimental.pallas import tpu as pltpu
from jax.sharding import PartitionSpec as P

D = 2048
HEADS = 16
HEAD_DIM = 128
FF = 5632
KERNEL = 4
BLOCK_ROWS = 64
BLOCKS_DEV = 2
GROUP_ROWS = BLOCK_ROWS * BLOCKS_DEV
SMALL = 128
MODEL = 4

f32 = jnp.float32
bf = jnp.bfloat16


def block_layouts(first, second, lead):
    def doc(block):
        in_first = (block >= lead) & (block < lead + first)
        in_second = (block >= lead + first) & (block < lead + first + second)
        return jnp.where(in_first, 1, jnp.where(in_second, 2, 0))

    starts = (lead == 1) | (lead + first == 1) & (second > 0)
    columns = [doc(0) > 0, doc(1) > 0, doc(0) == doc(1), ~starts]
    return jnp.stack(columns, 1).astype(f32)


def plain_product(left, right):
    return jnp.dot(left, right, preferred_element_type=f32)


def rows_product(left, right):
    return lax.dot_general(left, right, (((0,), (0,)), ((), ())), preferred_element_type=f32)


def transposed_product(left, right):
    return lax.dot_general(left, right, (((1,), (1,)), ((), ())), preferred_element_type=f32)


def halves(values):
    high = values.astype(bf)
    return high, (values - high.astype(f32)).astype(bf)


def exact(left, right, left_dim, right_dim):
    left_high, left_low = left if isinstance(left, tuple) else halves(left)
    right_high, right_low = right if isinstance(right, tuple) else halves(right)
    return lax.dot_general(
        jnp.concatenate([left_high, left_high, left_low], left_dim),
        jnp.concatenate([right_high, right_low, right_high], right_dim),
        (((left_dim,), (right_dim,)), ((), ())),
        preferred_element_type=f32,
    )


def stacked(first, second):
    return tuple(jnp.concatenate([a, b], 0) for a, b in zip(first, second))


class Tile:
    def __init__(self, layout_ref, group):
        live_first, live_second, same, persist = (layout_ref[group, i] for i in range(4))
        shape = (GROUP_ROWS, HEAD_DIM)
        row = lax.broadcasted_iota(jnp.int32, shape, 0)
        col = lax.broadcasted_iota(jnp.int32, shape, 1)
        late = row >= BLOCK_ROWS
        self.row, self.col = row, col
        self.live = jnp.where(late, live_second, live_first)
        self.taps = [None] + [
            jnp.where(
                row < offset,
                0.0,
                jnp.where(late & (row < BLOCK_ROWS + offset), same, 1.0),
            )
            for offset in range(1, KERNEL)
        ]
        cross = jnp.where(late & (col < BLOCK_ROWS), persist, 1.0)
        self.lower = jnp.where(row > col, cross, 0.0)
        self.lower_full = jnp.where(row >= col, cross, 0.0)

    def earlier(self, values, offset):
        return pltpu.roll(values, offset, 0) * self.taps[offset]

    def later(self, values, offset):
        return pltpu.roll(values * self.taps[offset], GROUP_ROWS - offset, 0)


def convolve(tile, values, taps):
    total = values * taps[0]
    for offset in range(1, KERNEL):
        total = total + tile.earlier(values, offset) * taps[offset]
    return total


def unit_scale(values):
    return lax.rsqrt(jnp.sum(values * values, -1, keepdims=True) + 1e-06)


def head_columns(part_width, section, head):
    return pl.ds(section * part_width + head * HEAD_DIM, HEAD_DIM)


def unit_inverses(tile, lowers):
    eye = jnp.where(tile.row == tile.col, 1.0, 0.0)
    inverses = None
    size = 1
    while size < GROUP_ROWS:
        pair = tile.row // (2 * size) == tile.col // (2 * size)
        split = pair & (tile.row // size != tile.col // size)
        parts = [jnp.where(split, lower, 0.0) for lower in lowers]
        if inverses is None:
            inverses = [eye - part for part in parts]
        else:
            kept = [halves(inverse) for inverse in inverses]
            inner = [exact(part, known, 1, 0) for part, known in zip(parts, kept)]
            outer = [exact(known, value, 1, 0) for known, value in zip(kept, inner)]
            inverses = [inverse - value for inverse, value in zip(inverses, outer)]
        size *= 2
    return inverses


def mixer_forward_kernel(
    layout_ref, pre_ref, param_ref, mixed_ref, inverse_ref, score_ref, solved_ref, out_ref
):
    width = mixed_ref.shape[1]
    heads = range(width // HEAD_DIM)
    tile = Tile(layout_ref, pl.program_id(0))
    queries, keys, values, strengths = [], [], [], []
    for head in heads:
        parts = []
        for section in range(3):
            columns = head_columns(width, section, head)
            taps = [param_ref[offset : offset + 1, columns] for offset in range(KERNEL)]
            convolved = convolve(tile, pre_ref[:, columns], taps)
            parts.append(convolved * jax.nn.sigmoid(convolved))
        queries.append(parts[0] * (unit_scale(parts[0]) * HEAD_DIM**-0.5))
        keys.append(parts[1] * unit_scale(parts[1]))
        values.append(parts[2])
        start = 4 * width + head
        strengths.append(jax.nn.sigmoid(pre_ref[:, start : start + 1]) * tile.live)
    lowers, scores = [], []
    for head in heads:
        key_halves = halves(keys[head])
        both = exact(stacked(key_halves, halves(queries[head])), key_halves, 1, 1)
        lowers.append(both[:GROUP_ROWS] * strengths[head] * tile.lower)
        scores.append(both[GROUP_ROWS:] * tile.lower_full)
    inverses = unit_inverses(tile, lowers)
    solved = [exact(inverses[head], values[head] * strengths[head], 1, 0) for head in heads]
    outs = [exact(scores[head], solved[head], 1, 0) for head in heads]
    for head in heads:
        out = outs[head]
        scaled = out * lax.rsqrt(jnp.mean(out * out, -1, keepdims=True) + 1e-05)
        gate = pre_ref[:, head_columns(width, 3, head)]
        gain = param_ref[KERNEL : KERNEL + 1, head_columns(width, 0, head)]
        mixed = scaled * gain * (gate * jax.nn.sigmoid(gate)) * tile.live
        mixed_ref[:, head_columns(width, 0, head)] = mixed.astype(bf)
        inverse_ref[head] = inverses[head]
        score_ref[head] = scores[head]
        solved_ref[head] = solved[head]
        out_ref[head] = out


def mixer_backward_kernel(
    layout_ref,
    pre_ref,
    param_ref,
    weight_ref,
    inverse_ref,
    score_ref,
    solved_ref,
    out_ref,
    *refs,
):
    *mixed_refs, d_pre_ref, d_param_ref, grad_ref = refs
    width = grad_ref.shape[1]
    heads = range(width // HEAD_DIM)
    tile = Tile(layout_ref, pl.program_id(0))
    for group, mixed_ref in enumerate(mixed_refs):

        @pl.when(pl.program_id(0) == group)
        def _():
            grad_ref[...] = transposed_product(mixed_ref[...], weight_ref[...])

    @pl.when(pl.program_id(0) == 0)
    def _():
        d_param_ref[...] = jnp.zeros_like(d_param_ref)

    def along(values):
        return jnp.sum(values, -1, keepdims=True)

    d_outs = []
    for head in heads:
        columns = head_columns(width, 0, head)
        d_mixed = grad_ref[:, columns] * tile.live
        out = out_ref[head]
        scale = lax.rsqrt(jnp.mean(out * out, -1, keepdims=True) + 1e-05)
        scaled = out * scale
        gate = pre_ref[:, head_columns(width, 3, head)]
        gate_open = jax.nn.sigmoid(gate)
        gain = param_ref[KERNEL : KERNEL + 1, columns]
        gated = d_mixed * (gate * gate_open)
        d_param_ref[KERNEL : KERNEL + 1, columns] += jnp.sum(gated * scaled, 0, keepdims=True)
        d_gate = d_mixed * scaled * gain * (gate_open * (1.0 + gate * (1.0 - gate_open)))
        d_pre_ref[:, head_columns(width, 3, head)] = d_gate.astype(bf)
        d_scaled = gated * gain
        mean = jnp.mean(d_scaled * out, -1, keepdims=True)
        d_outs.append(scale * d_scaled - out * (scale * scale * scale * mean))
    d_out_halves = [halves(value) for value in d_outs]
    solved_halves = [halves(solved_ref[head]) for head in heads]
    d_solved = [exact(score_ref[head], d_out_halves[head], 0, 0) for head in heads]
    d_scores = [
        exact(d_out_halves[head], solved_halves[head], 1, 1) * tile.lower_full for head in heads
    ]
    d_inner = [exact(inverse_ref[head], d_solved[head], 0, 0) for head in heads]
    d_lowers = [exact(d_inner[head], solved_halves[head], 1, 1) * -tile.lower for head in heads]
    d_beta = jnp.zeros((GROUP_ROWS, SMALL), f32)
    for head in heads:
        pres, convolved, opened, active = [], [], [], []
        for section in range(3):
            columns = head_columns(width, section, head)
            taps = [param_ref[offset : offset + 1, columns] for offset in range(KERNEL)]
            pres.append(pre_ref[:, columns])
            convolved.append(convolve(tile, pres[section], taps))
            opened.append(jax.nn.sigmoid(convolved[section]))
            active.append(convolved[section] * opened[section])
        query_scale = unit_scale(active[0])
        key_scale = unit_scale(active[1])
        query_unit = active[0] * query_scale
        key = active[1] * key_scale
        start = 4 * width + head
        opening = jax.nn.sigmoid(pre_ref[:, start : start + 1])
        strength = opening * tile.live
        d_both = stacked(halves(d_lowers[head]), halves(d_scores[head]))
        by_key = exact(d_both, key, 1, 0)
        d_query = by_key[GROUP_ROWS:] * HEAD_DIM**-0.5
        from_lower = by_key[:GROUP_ROWS]
        weighted = stacked(halves(key * strength), halves(query_unit * HEAD_DIM**-0.5))
        d_key = strength * from_lower + exact(d_both, weighted, 0, 0)
        d_strength = along(d_inner[head] * active[2] + from_lower * key)
        d_value = d_inner[head] * strength
        d_opening = d_strength * (opening * (1.0 - opening)) * tile.live
        d_beta = d_beta + jnp.where(tile.col == head, d_opening, 0.0)
        d_active = [
            (d_query - query_unit * along(query_unit * d_query)) * query_scale,
            (d_key - key * along(key * d_key)) * key_scale,
            d_value,
        ]
        for section in range(3):
            columns = head_columns(width, section, head)
            taps = [param_ref[offset : offset + 1, columns] for offset in range(KERNEL)]
            slope = opened[section] * (1.0 + convolved[section] * (1.0 - opened[section]))
            d_convolved = d_active[section] * slope
            d_pre = d_convolved * taps[0]
            sums = [jnp.sum(d_convolved * pres[section], 0, keepdims=True)]
            for offset in range(1, KERNEL):
                d_pre = d_pre + tile.later(d_convolved, offset) * taps[offset]
                sums.append(
                    jnp.sum(d_convolved * tile.earlier(pres[section], offset), 0, keepdims=True)
                )
            d_param_ref[0:KERNEL, columns] += jnp.concatenate(sums, 0)
            d_pre_ref[:, columns] = d_pre.astype(bf)
    d_pre_ref[:, 4 * width :] = d_beta.astype(bf)


NO_COST = pl.CostEstimate(flops=0, bytes_accessed=0, transcendentals=0)


def call(kernel, operands, in_specs, out_specs, out_shape, grid=(), scratch=(), micros=0):
    results = pl.pallas_call(
        kernel,
        grid=grid,
        in_specs=in_specs,
        out_specs=out_specs,
        out_shape=out_shape,
        scratch_shapes=scratch,
        compiler_params=pltpu.CompilerParams(
            dimension_semantics=("arbitrary",) * len(grid), vmem_limit_bytes=48 * 2**20
        ),
        cost_estimate=pl.CostEstimate(
            flops=micros * 10**9, bytes_accessed=0, transcendentals=0
        ),
    )(*operands)
    return list(results)


def whole(array):
    return pl.BlockSpec(array.shape, lambda *step: (0,) * len(array.shape))


def mixer_specs(width):
    wide = 4 * width + SMALL
    heads = width // HEAD_DIM
    layout = pl.BlockSpec(memory_space=pltpu.SMEM)
    pre = pl.BlockSpec((GROUP_ROWS, wide), lambda group: (group, 0))
    param = pl.BlockSpec((2 * KERNEL, 3 * width), lambda group: (0, 0))
    narrow = pl.BlockSpec((GROUP_ROWS, width), lambda group: (group, 0))
    square = pl.BlockSpec((heads, GROUP_ROWS, HEAD_DIM), lambda group: (group, 0, 0))
    return layout, pre, param, narrow, square


def mixer_forward(layout, pre, params, width):
    groups = layout.shape[0]
    layout_spec, pre_spec, param_spec, narrow, square = mixer_specs(width)
    squares = pltpu.HBM((groups * width // HEAD_DIM, GROUP_ROWS, HEAD_DIM), f32)
    return call(
        mixer_forward_kernel,
        [layout, pre, params],
        [layout_spec, pre_spec, param_spec],
        [narrow] + [square] * 4,
        [jax.ShapeDtypeStruct((groups * GROUP_ROWS, width), bf)] + [squares] * 4,
        (groups,),
    )


def mixer_backward(layout, pre, params, weight, d_mixed, kept, width):
    groups = layout.shape[0]
    layout_spec, pre_spec, param_spec, _, square = mixer_specs(width)
    kept = [pltpu.with_memory_space_constraint(array, pltpu.HBM) for array in kept]
    return call(
        mixer_backward_kernel,
        [layout, pre, params, weight, *kept, *d_mixed],
        [layout_spec, pre_spec, param_spec, whole(weight)]
        + [square] * 4
        + [whole(block) for block in d_mixed],
        [pre_spec, param_spec],
        [jax.ShapeDtypeStruct(pre.shape, bf), jax.ShapeDtypeStruct(params.shape, f32)],
        (groups,),
        [pltpu.VMEM((GROUP_ROWS, width), f32)],
        micros=400,
    )


def first_kernel(gain_ref, weight_ref, *refs):
    *value_refs, normed_ref, out_ref, scale_ref, total_ref = refs
    step, depth = pl.program_id(0), weight_ref.shape[0]

    @pl.when(step == 0)
    def _():
        for group, ref in enumerate(value_refs):
            values = ref[...].astype(f32)
            scale = lax.rsqrt(jnp.mean(values * values, -1, keepdims=True) + 1e-06)
            rows = pl.ds(group * GROUP_ROWS, GROUP_ROWS)
            scale_ref[rows, :] = jnp.broadcast_to(scale, (GROUP_ROWS, 128))
        total_ref[...] = jnp.zeros_like(total_ref)

    columns = pl.ds(pl.multiple_of(step * depth, depth), depth)
    for group, ref in enumerate(value_refs):
        rows = pl.ds(group * GROUP_ROWS, GROUP_ROWS)
        values = ref[:, columns].astype(f32) * scale_ref[rows, :1] * gain_ref[...]
        normed_ref[rows, :] = values.astype(bf)
    total_ref[...] += plain_product(normed_ref[...], weight_ref[...])

    @pl.when(step == pl.num_programs(0) - 1)
    def _():
        out_ref[...] = total_ref[...]


def normed_product(blocks, gain, weight, depth=512):
    rows, (features, columns) = len(blocks) * GROUP_ROWS, weight.shape
    return call(
        first_kernel,
        [gain, weight, *blocks],
        [
            pl.BlockSpec((1, depth), lambda step: (0, step)),
            pl.BlockSpec((depth, columns), lambda step: (step, 0)),
        ]
        + [whole(block) for block in blocks],
        [
            pl.BlockSpec((rows, depth), lambda step: (0, step)),
            pl.BlockSpec((rows, columns), lambda step: (0, 0)),
        ],
        [
            jax.ShapeDtypeStruct((rows, features), bf),
            jax.ShapeDtypeStruct((rows, columns), f32),
        ],
        (features // depth,),
        [pltpu.VMEM((rows, 128), f32), pltpu.VMEM((rows, columns), f32)],
    )


def product_blocks(left, right, transposed=False, block=512, micros=0):
    product = transposed_product if transposed else plain_product
    columns = right.shape[0] if transposed else right.shape[1]
    groups = left.shape[0] // GROUP_ROWS

    def kernel(left_ref, right_ref, *out_refs):
        total = product(left_ref[...], right_ref[...])
        for group, ref in enumerate(out_refs):
            ref[...] = total[group * GROUP_ROWS : (group + 1) * GROUP_ROWS].astype(ref.dtype)

    if transposed:
        right_spec = pl.BlockSpec((block, right.shape[1]), lambda step: (step, 0))
    else:
        right_spec = pl.BlockSpec((right.shape[0], block), lambda step: (0, step))
    return call(
        kernel,
        [left, right],
        [whole(left), right_spec],
        [pl.BlockSpec((GROUP_ROWS, block), lambda step: (0, step))] * groups,
        [
            jax.ShapeDtypeStruct((GROUP_ROWS, columns), bf if group else f32)
            for group in range(groups)
        ],
        (columns // block,),
        micros=micros,
    )


def grad_product(left, right, block=256, micros=0):
    rows, features = left.shape
    if features % block:
        block = 128

    def kernel(left_ref, right_ref, out_ref):
        out_ref[...] = rows_product(left_ref[...], right_ref[...]).astype(bf)

    return call(
        kernel,
        [left, right],
        [pl.BlockSpec((rows, block), lambda step: (0, step)), whole(right)],
        [pl.BlockSpec((block, right.shape[1]), lambda step: (step, 0))],
        [pltpu.HBM((features, right.shape[1]), bf)],
        (features // block,),
        micros=micros,
    )[0]


def from_own(part, values):
    groups = values.shape[0] // GROUP_ROWS

    def kernel(part_ref, values_ref, out_ref):
        for step in range(groups):
            source = lax.rem(part_ref[0] + groups - step, groups) * GROUP_ROWS
            rows = pl.ds(pl.multiple_of(source, GROUP_ROWS), GROUP_ROWS)
            out_ref[step * GROUP_ROWS : (step + 1) * GROUP_ROWS] = values_ref[rows]

    return call(
        kernel,
        [part.reshape(1).astype(jnp.int32), values],
        [pl.BlockSpec(memory_space=pltpu.SMEM), whole(values)],
        [whole(values)],
        [jax.ShapeDtypeStruct(values.shape, values.dtype)],
        (1,),
    )[0]


def tie_all(values, *others):
    anywhere = pl.BlockSpec(memory_space=pl.ANY)
    others = [
        pltpu.with_memory_space_constraint(other, pltpu.HBM) if other.size > 2**21 else other
        for other in others
    ]
    tied = pl.pallas_call(
        lambda *refs: None,
        in_specs=[anywhere] * (len(values) + len(others)),
        out_specs=[anywhere] * len(values),
        out_shape=[
            (pltpu.HBM if value.size > 2**21 else jax.ShapeDtypeStruct)(value.shape, value.dtype)
            for value in values
        ],
        input_output_aliases={i: i for i in range(len(values))},
        cost_estimate=NO_COST,
    )(*values, *others)
    return list(tied)


def tie(value, *others):
    return tie_all([value], *others)[0]


def assemble(part, values, received, others):
    parts = values.shape[0]

    def kernel(part_ref, values_ref, *refs):
        own = part_ref[0]
        out_ref = refs[-1]
        out_ref[own] = values_ref[own]
        for step in range(1, parts):
            out_ref[lax.rem(own + parts - step, parts)] = refs[step - 1][...]

    vmem = pl.BlockSpec(memory_space=pltpu.VMEM)
    anywhere = pl.BlockSpec(memory_space=pl.ANY)
    return pl.pallas_call(
        kernel,
        in_specs=[pl.BlockSpec(memory_space=pltpu.SMEM)]
        + [vmem] * parts
        + [anywhere] * len(others),
        out_specs=vmem,
        out_shape=jax.ShapeDtypeStruct(values.shape, values.dtype),
        compiler_params=pltpu.CompilerParams(vmem_limit_bytes=32 * 2**20),
        cost_estimate=NO_COST,
    )(part.reshape(1).astype(jnp.int32), values, *received, *others)


def copy_columns(count, *refs):
    target = refs[-1]
    start = 0
    for source in refs[:count]:
        block = source[...].reshape(source.shape[-2:])
        columns = pl.ds(start, block.shape[1])
        if len(target.shape) == 3:
            target[0, :, columns] = block.astype(target.dtype)
        else:
            target[:, columns] = block.astype(target.dtype)
        start += block.shape[1]


def to_parts(sources, parts, dtype, others=()):
    rows = sources[0][0].shape[0]

    def spec(section, width):
        return pl.BlockSpec((rows, width), lambda p: (0, section * parts + p))

    total = sum(width for _, _, width in sources)
    return pl.pallas_call(
        functools.partial(copy_columns, len(sources)),
        grid=(parts,),
        in_specs=[spec(section, width) for _, section, width in sources]
        + [pl.BlockSpec(memory_space=pl.ANY)] * len(others),
        out_specs=pl.BlockSpec((1, rows, total), lambda p: (p, 0, 0)),
        out_shape=jax.ShapeDtypeStruct((parts, rows, total), dtype),
        cost_estimate=NO_COST,
    )(*[array for array, _, _ in sources], *others)


def updown_from_parts(slabs):
    parts, rows, width = slabs.shape
    units = width // 2

    def kernel(slabs_ref, out_ref):
        for p in range(parts):
            out_ref[:, p * units : (p + 1) * units] = slabs_ref[p].astype(f32)

    return pl.pallas_call(
        kernel,
        grid=(2,),
        in_specs=[pl.BlockSpec((parts, rows, units), lambda half: (0, 0, half))],
        out_specs=pl.BlockSpec((rows, parts * units), lambda half: (0, half)),
        out_shape=jax.ShapeDtypeStruct((rows, parts * width), f32),
        compiler_params=pltpu.CompilerParams(vmem_limit_bytes=32 * 2**20),
        cost_estimate=NO_COST,
    )(slabs)


def mixer_from_parts(slabs, width):
    parts, rows, _ = slabs.shape

    def kernel(slabs_ref, qkv_ref, gate_ref, strength_ref):
        for p in range(parts):
            for section in range(4):
                block = slabs_ref[p, :, section * width : (section + 1) * width].astype(f32)
                if section < 3:
                    start = (section * parts + p) * width
                    qkv_ref[:, start : start + width] = block
                else:
                    gate_ref[:, p * width : (p + 1) * width] = block
            last = slabs_ref[p, :, 4 * width :].astype(f32)
            strength_ref[:, p * SMALL : (p + 1) * SMALL] = last

    widths = [3 * parts * width, parts * width, parts * SMALL]
    return pl.pallas_call(
        kernel,
        out_shape=[jax.ShapeDtypeStruct((rows, size), f32) for size in widths],
        compiler_params=pltpu.CompilerParams(vmem_limit_bytes=32 * 2**20),
        cost_estimate=NO_COST,
    )(slabs)


def total_of(own_ref, received_refs):
    total = own_ref[...]
    for ref in received_refs:
        total = total + ref[...].astype(f32)
    return total


def row_scale(values):
    return lax.rsqrt(jnp.mean(values * values, -1, keepdims=True) + 1e-06)


def norm_slope(values, scale, gain, grad):
    mean = jnp.mean(gain * grad * values, -1, keepdims=True)
    return scale * gain * grad - values * (scale * scale * scale * mean)


def hidden_kernel(own_ref, *refs):
    *received, input_ref, gain_ref, hidden_ref, normed_ref = refs
    hidden = input_ref[...].astype(f32) + total_of(own_ref, received)
    hidden_ref[...] = hidden
    normed_ref[...] = (hidden * row_scale(hidden) * gain_ref[...]).astype(bf)


def hidden_back_kernel(own_ref, *refs):
    *received, hidden_ref, gain_ref, cot_ref, d_hidden_ref, d_mixed_ref, d_gain_ref = refs
    grad = total_of(own_ref, received)
    hidden = hidden_ref[...]
    scale = row_scale(hidden)

    @pl.when(pl.program_id(0) == 0)
    def _():
        d_gain_ref[...] = jnp.zeros_like(d_gain_ref)

    d_gain_ref[...] += jnp.sum(grad * hidden * scale, 0, keepdims=True)
    d_hidden = cot_ref[...].astype(f32) + norm_slope(hidden, scale, gain_ref[...], grad)
    d_hidden_ref[...] = d_hidden
    d_mixed_ref[...] = d_hidden.astype(bf)


def input_back_kernel(own_ref, *refs):
    *received, input_ref, gain_ref, d_hidden_ref, out_ref = refs
    grad = total_of(own_ref, received)
    values = input_ref[...].astype(f32)
    slope = norm_slope(values, row_scale(values), gain_ref[...], grad)
    out_ref[...] = (d_hidden_ref[...] + slope).astype(bf)


def block_out_kernel(own_ref, *refs):
    *received, hidden_ref, out_ref = refs
    out_ref[...] = (hidden_ref[...] + total_of(own_ref, received)).astype(bf)


def by_rows(kernel, arrays, outs, block=64):
    def spec(shape):
        if shape[0] == 1:
            return pl.BlockSpec(shape, lambda i: (0, 0))
        return pl.BlockSpec((block, shape[1]), lambda i: (i, 0))

    return pl.pallas_call(
        kernel,
        grid=(GROUP_ROWS // block,),
        in_specs=[spec(array.shape) for array in arrays],
        out_specs=[spec(shape) for shape, _ in outs],
        out_shape=[jax.ShapeDtypeStruct(shape, dtype) for shape, dtype in outs],
        compiler_params=pltpu.CompilerParams(dimension_semantics=("arbitrary",)),
        cost_estimate=NO_COST,
    )(*arrays)


def body(
    block_in,
    out_grad,
    norm1_gain,
    conv_weight,
    head_gain,
    qkv_weight,
    beta_weight,
    gate_weight,
    out_weight,
    norm2_gain,
    updown_weight,
    down_weight,
    seq_blocks,
    lead_blocks,
):
    devices = lax.axis_size("dp")
    parts = MODEL
    copies = devices // parts
    part = lax.axis_index("dp") // copies
    copy = lax.axis_index("dp") % copies
    rows_own = qkv_weight.shape[0]
    width = D // parts
    units = FF // parts
    heads_part = HEADS // parts
    wide = 4 * width + SMALL
    model_groups = [[m * copies + t for m in range(parts)] for t in range(copies)]
    copy_groups = [[m * copies + t for t in range(copies)] for m in range(parts)]

    def exchange(values):
        return lax.all_to_all(
            values, "dp", split_axis=0, concat_axis=0, axis_index_groups=model_groups, tiled=True
        )

    def shift(values, step):
        pairs = [
            (m * copies + t, (m + step) % parts * copies + t)
            for m in range(parts)
            for t in range(copies)
        ]
        return lax.ppermute(values, "dp", pairs)

    def send_apart(values, *others):
        cut = [
            lax.dynamic_index_in_dim(values, (part + step) % parts, 0, keepdims=False)
            for step in range(1, parts)
        ]
        cut = tie_all(cut, *others)
        return cut, [shift(piece, step) for step, piece in enumerate(cut, 1)]

    def gather_rows(values):
        return [values] + [shift(values, step) for step in range(1, parts)]

    def scatter_rows(terms):
        return [terms[0]] + [shift(block, -step) for step, block in enumerate(terms[1:], 1)]

    def gather_copies(values):
        return lax.all_gather(values, "dp", axis=0, axis_index_groups=copy_groups, tiled=True)

    def scatter_copies(values):
        return lax.psum_scatter(
            values.astype(bf),
            "dp",
            scatter_dimension=0,
            axis_index_groups=copy_groups,
            tiled=True,
        )

    by_cores = copies % 2 == 0

    def core_sides(values):
        rows, columns = values.shape
        if not by_cores:
            return [values.reshape(copies, rows // copies, columns)] * 2
        values = values.reshape(copies // 2, 2, rows // copies, columns)
        side = copy % 2
        own = lax.dynamic_index_in_dim(values, side, 1, keepdims=False)
        return own, lax.dynamic_index_in_dim(values, 1 - side, 1, keepdims=False)

    def core_sum(own, other, *others):
        if not by_cores:
            return own
        other = lax.ppermute(other, "dp", [(i, i ^ 1) for i in range(devices)])
        other = tie(other, *others)
        return (own.astype(f32) + other.astype(f32)).astype(bf)

    def plane_blocks(values, stride):
        groups = [
            [m * copies + t for t in range(first, copies, stride)]
            for m in range(parts)
            for first in range(stride)
        ]
        return lax.all_to_all(values, "dp", 0, 0, axis_index_groups=groups, tiled=True)

    def to_wire(values):
        return values.reshape(-1, parts, copies, rows_own).swapaxes(1, 2).reshape(-1, D)

    def from_wire(values):
        return values.reshape(-1, copies, parts, rows_own).swapaxes(1, 2).reshape(-1, D)

    w_out_own = to_wire(out_weight.astype(bf))
    w_out = gather_copies(w_out_own)
    strengths = beta_weight.reshape(rows_own, parts, heads_part)
    strengths = jnp.pad(strengths, ((0, 0), (0, 0), (0, SMALL - heads_part)))
    strengths = tie(strengths.reshape(rows_own, parts * SMALL), w_out_own)
    pieces = [(qkv_weight, section, width) for section in range(3)]
    pieces = to_parts(pieces + [(gate_weight, 0, width), (strengths, 0, SMALL)], parts, bf)
    mixer_pieces = tie(exchange(pieces), w_out)
    w_mixer = gather_copies(mixer_pieces.reshape(parts * rows_own, wide))
    inputs = tie(to_wire(block_in), mixer_pieces)
    input_rows = gather_rows(inputs)

    lanes = -(-3 * rows_own // 128) * 128
    numbers = jnp.concatenate([seq_blocks[0], lead_blocks]).astype(f32)
    small = [conv_weight.T, norm1_gain[None], head_gain[None], norm2_gain[None], numbers[None]]
    small = [jnp.pad(rows, ((0, 0), (0, lanes - rows.shape[1]))) for rows in small]
    small = jnp.pad(jnp.concatenate(small, 0).astype(bf), ((0, 2 * KERNEL), (0, 0)))
    small = jnp.broadcast_to(small[None], (devices,) + small.shape)
    small = lax.all_to_all(tie(small, *input_rows[1:]), "dp", 0, 0, tiled=True)
    taps = small[:, :KERNEL, : 3 * rows_own].swapaxes(0, 1).reshape(KERNEL, 3, parts, width)
    taps = lax.dynamic_index_in_dim(taps, part, 2, keepdims=False).reshape(KERNEL, 3 * width)
    gain_one, head_full, gain_two = (
        small[:, KERNEL + i, :rows_own].reshape(1, D).astype(f32) for i in range(3)
    )
    gain_one, gain_two = to_wire(gain_one), to_wire(gain_two)
    head_part = lax.dynamic_slice_in_dim(head_full, part * width, width, 1)
    params = jnp.concatenate([taps.astype(f32), jnp.pad(head_part, ((0, 0), (0, 2 * width)))], 0)
    params = jnp.pad(params, ((0, KERNEL - 1), (0, 0)))
    numbers = small[:, KERNEL + 3, :3].astype(f32).astype(jnp.int32)
    layouts = block_layouts(numbers[:, 0], numbers[:, 1], numbers[:, 2])
    layouts = layouts.reshape(parts, copies, 4)
    layouts = lax.dynamic_index_in_dim(layouts, copy, 1, keepdims=False)
    wanted = (part - jnp.arange(parts)) % parts
    wanted = (wanted[:, None] == jnp.arange(parts)).astype(f32)
    layouts = jnp.sum(wanted[:, :, None] * layouts, 1)

    pieces = [(updown_weight, half, units) for half in range(2)]
    updown_pieces = to_parts(pieces, parts, bf, input_rows[1:] + [small])
    w_down_own = to_wire(down_weight.astype(bf))
    w_down = gather_copies(tie(w_down_own, *input_rows[1:]))
    cotangent_own = to_wire(out_grad)

    cotangent = lax.all_gather(
        tie(cotangent_own, small), "dp", axis=0, axis_index_groups=model_groups, tiled=True
    )
    gain_first = tie(gain_one, w_down_own, cotangent_own, updown_pieces)
    normed, pre = normed_product(input_rows, gain_first, w_mixer)
    mixed, *kept = mixer_forward(layouts, pre, params, width)
    out_terms = product_blocks(mixed, w_out)
    _, received = send_apart(updown_pieces, pre)
    updown_pieces = assemble(part, updown_pieces, received, out_terms[1:])
    w_updown = gather_copies(updown_pieces.reshape(parts * rows_own, 2 * units))
    stream = ((GROUP_ROWS, D), f32)
    narrow = ((GROUP_ROWS, D), bf)
    hidden, normed_two = by_rows(
        hidden_kernel,
        scatter_rows(out_terms) + [inputs, gain_two],
        [stream, narrow],
    )
    cotangent = from_own(part, cotangent)
    normed_two = jnp.concatenate(gather_rows(normed_two), 0)

    def swiglu_units(updown):
        return jax.nn.silu(updown[:, :units]) * updown[:, units:]

    updown = plain_product(normed_two, w_updown)
    active, swiglu_back = jax.vjp(swiglu_units, updown)
    active = active.astype(bf)
    d_active = transposed_product(cotangent, w_down)
    d_updown = swiglu_back(d_active)[0].astype(bf)
    d_normed_two = product_blocks(d_updown, w_updown, transposed=True)
    active = tie(active, *d_normed_two[1:])
    down_terms = grad_product(active, cotangent)
    updown_terms = grad_product(normed_two, tie(d_updown, down_terms))
    gain_late = tie(gain_two, updown_terms)
    d_normed_two = scatter_rows(d_normed_two)
    updown_grad = scatter_copies(tie(updown_terms, gain_late))
    d_hidden, d_mixed, gain_two_grad = by_rows(
        hidden_back_kernel,
        d_normed_two + [hidden, gain_late, cotangent_own],
        [stream, narrow, ((1, D), f32)],
    )


    out_terms = product_blocks(tie(active, d_mixed), w_down)
    down_own, down_other = core_sides(tie(down_terms, *out_terms[1:]))
    d_mixed = gather_rows(d_mixed)
    late = tie(params, *out_terms)
    out_terms[1:] = tie_all(out_terms[1:], *d_mixed[1:])
    d_pre, d_params = mixer_backward(layouts, pre, late, w_out, d_mixed, kept, width)
    mixer_terms = tie(grad_product(normed, d_pre, micros=20), updown_grad)
    mixer_grad = scatter_copies(mixer_terms)

    d_normed_terms = product_blocks(
        tie(d_pre, mixer_terms), w_mixer, transposed=True, micros=150
    )
    hidden = tie(hidden, d_normed_terms[0])
    (block_out,) = by_rows(block_out_kernel, scatter_rows(out_terms) + [hidden], [narrow])
    d_normed_terms[1:] = tie_all(d_normed_terms[1:], block_out)
    d_normed = scatter_rows(d_normed_terms)
    d_mixed = jnp.concatenate([tie(d_mixed[0], block_out)] + d_mixed[1:], 0)
    out_grads = grad_product(mixed, d_mixed)
    down_grad = core_sum(down_own, down_other, *d_normed_terms[1:])
    down_blocks = plane_blocks(down_grad, 2 if by_cores else 1)
    gain_one_grad = 0.0
    for values, terms in zip(input_rows, d_normed_terms):
        values = values.astype(f32)
        terms = terms.astype(f32) * (values * row_scale(values))
        gain_one_grad = gain_one_grad + jnp.sum(terms, 0, keepdims=True)

    here = (jnp.arange(parts) == part).astype(f32)[:, None]
    taps_grad = d_params[:KERNEL].reshape(KERNEL, 3, 1, width) * here
    taps_grad = taps_grad.reshape(KERNEL, parts, copies, 3, rows_own).transpose(1, 2, 3, 0, 4)
    taps_grad = taps_grad.reshape(devices, 3 * KERNEL, rows_own)
    head_grad = (d_params[KERNEL, :width] * here).reshape(devices, 1, rows_own)
    gain_grads = [
        grad.reshape(copies, parts, 1, rows_own).swapaxes(0, 1).reshape(devices, 1, rows_own)
        for grad in (gain_one_grad, gain_two_grad)
    ]
    small_grad = jnp.concatenate([taps_grad, head_grad] + gain_grads, 1)
    small_grad = jnp.pad(small_grad, ((0, 0), (0, 1), (0, 128 - rows_own)))
    small_grad = jnp.sum(lax.all_to_all(small_grad, "dp", 0, 0, tiled=True), 0)[:, :rows_own]
    taps_shard = small_grad[: 3 * KERNEL].reshape(3, KERNEL, rows_own).swapaxes(1, 2)
    taps_shard = taps_shard.reshape(3 * rows_own, KERNEL)
    head_shard, gain_one_shard, gain_two_shard = small_grad[3 * KERNEL : 3 * KERNEL + 3]

    late = tie(gain_one, out_grads, down_grad)
    (input_grad,) = by_rows(input_back_kernel, d_normed + [inputs, late, d_hidden], [narrow])
    updown_grad = updown_grad.reshape(parts, rows_own, 2 * units)
    cut, received = send_apart(updown_grad, input_grad)
    down_shard = from_wire(jnp.sum(tie(down_blocks, *cut).astype(f32), 0))
    mixer_grad = tie(mixer_grad, *cut)
    mixer_slabs = exchange(mixer_grad.reshape(parts, rows_own, wide))
    updown_shard = updown_from_parts(assemble(part, updown_grad, received, [mixer_grad]))
    out_blocks = plane_blocks(tie(out_grads, mixer_grad).reshape(copies, rows_own, D), 1)
    out_shard = from_wire(jnp.sum(out_blocks.astype(f32), 0))
    mixer_grad = mixer_slabs
    qkv_shard, gate_shard, strengths = mixer_from_parts(mixer_grad, width)
    beta_shard = strengths.reshape(rows_own, parts, SMALL)[:, :, :heads_part]
    return (
        from_wire(block_out),
        from_wire(input_grad),
        gain_one_shard,
        taps_shard,
        head_shard,
        qkv_shard,
        beta_shard.reshape(rows_own, HEADS),
        gate_shard,
        out_shard,
        gain_two_shard,
        updown_shard,
        down_shard,
    )


def solution(mesh):
    placed = (
        P("dp", None),
        P("dp", None),
        P("dp"),
        P("dp", None),
        P("dp"),
        P("dp", None),
        P("dp", None),
        P("dp", None),
        P("dp", None),
        P("dp"),
        P("dp", None),
        P("dp", None),
        P("dp", None),
        P("dp"),
    )
    return jax.shard_map(
        body,
        mesh=mesh,
        in_specs=placed,
        out_specs=(
            P("dp", None),
            P("dp", None),
            P("dp"),
            P("dp", None),
            P("dp"),
            P("dp", None),
            P("dp", None),
            P("dp", None),
            P("dp", None),
            P("dp"),
            P("dp", None),
            P("dp", None),
        ),
        check_vma=False,
    )
```

```python
import functools

import jax
import jax.numpy as jnp
from jax import lax
from jax.experimental import pallas as pl
from jax.experimental.pallas import tpu as pltpu
from jax.sharding import PartitionSpec as P

D = 2048
HEADS = 16
HEAD_DIM = 128
FF = 5632
KERNEL = 4
BLOCK_ROWS = 64
BLOCKS_DEV = 2
GROUP_ROWS = BLOCK_ROWS * BLOCKS_DEV
SMALL = 128
MODEL = 4

f32 = jnp.float32
bf = jnp.bfloat16


def block_layouts(first, second, lead):
    def doc(block):
        in_first = (block >= lead) & (block < lead + first)
        in_second = (block >= lead + first) & (block < lead + first + second)
        return jnp.where(in_first, 1, jnp.where(in_second, 2, 0))

    starts = (lead == 1) | (lead + first == 1) & (second > 0)
    columns = [doc(0) > 0, doc(1) > 0, doc(0) == doc(1), ~starts]
    return jnp.stack(columns, 1).astype(f32)


def plain_product(left, right):
    return jnp.dot(left, right, preferred_element_type=f32)


def rows_product(left, right):
    return lax.dot_general(left, right, (((0,), (0,)), ((), ())), preferred_element_type=f32)


def transposed_product(left, right):
    return lax.dot_general(left, right, (((1,), (1,)), ((), ())), preferred_element_type=f32)


def halves(values):
    high = values.astype(bf)
    return high, (values - high.astype(f32)).astype(bf)


def exact(left, right, left_dim, right_dim):
    left_high, left_low = left if isinstance(left, tuple) else halves(left)
    right_high, right_low = right if isinstance(right, tuple) else halves(right)
    return lax.dot_general(
        jnp.concatenate([left_high, left_high, left_low], left_dim),
        jnp.concatenate([right_high, right_low, right_high], right_dim),
        (((left_dim,), (right_dim,)), ((), ())),
        preferred_element_type=f32,
    )


def stacked(first, second):
    return tuple(jnp.concatenate([a, b], 0) for a, b in zip(first, second))


class Tile:
    def __init__(self, layout_ref, group):
        live_first, live_second, same, persist = (layout_ref[group, i] for i in range(4))
        shape = (GROUP_ROWS, HEAD_DIM)
        row = lax.broadcasted_iota(jnp.int32, shape, 0)
        col = lax.broadcasted_iota(jnp.int32, shape, 1)
        late = row >= BLOCK_ROWS
        self.row, self.col = row, col
        self.live = jnp.where(late, live_second, live_first)
        self.taps = [None] + [
            jnp.where(
                row < offset,
                0.0,
                jnp.where(late & (row < BLOCK_ROWS + offset), same, 1.0),
            )
            for offset in range(1, KERNEL)
        ]
        cross = jnp.where(late & (col < BLOCK_ROWS), persist, 1.0)
        self.lower = jnp.where(row > col, cross, 0.0)
        self.lower_full = jnp.where(row >= col, cross, 0.0)

    def earlier(self, values, offset):
        return pltpu.roll(values, offset, 0) * self.taps[offset]

    def later(self, values, offset):
        return pltpu.roll(values * self.taps[offset], GROUP_ROWS - offset, 0)


def convolve(tile, values, taps):
    total = values * taps[0]
    for offset in range(1, KERNEL):
        total = total + tile.earlier(values, offset) * taps[offset]
    return total


def unit_scale(values):
    return lax.rsqrt(jnp.sum(values * values, -1, keepdims=True) + 1e-06)


def head_columns(part_width, section, head):
    return pl.ds(section * part_width + head * HEAD_DIM, HEAD_DIM)


def unit_inverses(tile, lowers):
    eye = jnp.where(tile.row == tile.col, 1.0, 0.0)
    inverses = None
    size = 1
    while size < GROUP_ROWS:
        pair = tile.row // (2 * size) == tile.col // (2 * size)
        split = pair & (tile.row // size != tile.col // size)
        parts = [jnp.where(split, lower, 0.0) for lower in lowers]
        if inverses is None:
            inverses = [eye - part for part in parts]
        else:
            kept = [halves(inverse) for inverse in inverses]
            inner = [exact(part, known, 1, 0) for part, known in zip(parts, kept)]
            outer = [exact(known, value, 1, 0) for known, value in zip(kept, inner)]
            inverses = [inverse - value for inverse, value in zip(inverses, outer)]
        size *= 2
    return inverses


def mixer_forward_kernel(
    layout_ref, pre_ref, param_ref, mixed_ref, inverse_ref, score_ref, solved_ref, out_ref
):
    width = mixed_ref.shape[1]
    heads = range(width // HEAD_DIM)
    tile = Tile(layout_ref, pl.program_id(0))
    queries, keys, values, strengths = [], [], [], []
    for head in heads:
        parts = []
        for section in range(3):
            columns = head_columns(width, section, head)
            taps = [param_ref[offset : offset + 1, columns] for offset in range(KERNEL)]
            convolved = convolve(tile, pre_ref[:, columns], taps)
            parts.append(convolved * jax.nn.sigmoid(convolved))
        queries.append(parts[0] * (unit_scale(parts[0]) * HEAD_DIM**-0.5))
        keys.append(parts[1] * unit_scale(parts[1]))
        values.append(parts[2])
        start = 4 * width + head
        strengths.append(jax.nn.sigmoid(pre_ref[:, start : start + 1]) * tile.live)
    lowers, scores = [], []
    for head in heads:
        key_halves = halves(keys[head])
        both = exact(stacked(key_halves, halves(queries[head])), key_halves, 1, 1)
        lowers.append(both[:GROUP_ROWS] * strengths[head] * tile.lower)
        scores.append(both[GROUP_ROWS:] * tile.lower_full)
    inverses = unit_inverses(tile, lowers)
    solved = [exact(inverses[head], values[head] * strengths[head], 1, 0) for head in heads]
    outs = [exact(scores[head], solved[head], 1, 0) for head in heads]
    for head in heads:
        out = outs[head]
        scaled = out * lax.rsqrt(jnp.mean(out * out, -1, keepdims=True) + 1e-05)
        gate = pre_ref[:, head_columns(width, 3, head)]
        gain = param_ref[KERNEL : KERNEL + 1, head_columns(width, 0, head)]
        mixed = scaled * gain * (gate * jax.nn.sigmoid(gate)) * tile.live
        mixed_ref[:, head_columns(width, 0, head)] = mixed.astype(bf)
        inverse_ref[head] = inverses[head]
        score_ref[head] = scores[head]
        solved_ref[head] = solved[head]
        out_ref[head] = out


def mixer_backward_kernel(
    layout_ref,
    pre_ref,
    param_ref,
    weight_ref,
    inverse_ref,
    score_ref,
    solved_ref,
    out_ref,
    *refs,
):
    *mixed_refs, d_pre_ref, d_param_ref, grad_ref = refs
    width = grad_ref.shape[1]
    heads = range(width // HEAD_DIM)
    tile = Tile(layout_ref, pl.program_id(0))
    for group, mixed_ref in enumerate(mixed_refs):

        @pl.when(pl.program_id(0) == group)
        def _():
            grad_ref[...] = transposed_product(mixed_ref[...], weight_ref[...])

    @pl.when(pl.program_id(0) == 0)
    def _():
        d_param_ref[...] = jnp.zeros_like(d_param_ref)

    def along(values):
        return jnp.sum(values, -1, keepdims=True)

    d_outs = []
    for head in heads:
        columns = head_columns(width, 0, head)
        d_mixed = grad_ref[:, columns] * tile.live
        out = out_ref[head]
        scale = lax.rsqrt(jnp.mean(out * out, -1, keepdims=True) + 1e-05)
        scaled = out * scale
        gate = pre_ref[:, head_columns(width, 3, head)]
        gate_open = jax.nn.sigmoid(gate)
        gain = param_ref[KERNEL : KERNEL + 1, columns]
        gated = d_mixed * (gate * gate_open)
        d_param_ref[KERNEL : KERNEL + 1, columns] += jnp.sum(gated * scaled, 0, keepdims=True)
        d_gate = d_mixed * scaled * gain * (gate_open * (1.0 + gate * (1.0 - gate_open)))
        d_pre_ref[:, head_columns(width, 3, head)] = d_gate.astype(bf)
        d_scaled = gated * gain
        mean = jnp.mean(d_scaled * out, -1, keepdims=True)
        d_outs.append(scale * d_scaled - out * (scale * scale * scale * mean))
    d_out_halves = [halves(value) for value in d_outs]
    solved_halves = [halves(solved_ref[head]) for head in heads]
    d_solved = [exact(score_ref[head], d_out_halves[head], 0, 0) for head in heads]
    d_scores = [
        exact(d_out_halves[head], solved_halves[head], 1, 1) * tile.lower_full for head in heads
    ]
    d_inner = [exact(inverse_ref[head], d_solved[head], 0, 0) for head in heads]
    d_lowers = [exact(d_inner[head], solved_halves[head], 1, 1) * -tile.lower for head in heads]
    d_beta = jnp.zeros((GROUP_ROWS, SMALL), f32)
    for head in heads:
        pres, convolved, opened, active = [], [], [], []
        for section in range(3):
            columns = head_columns(width, section, head)
            taps = [param_ref[offset : offset + 1, columns] for offset in range(KERNEL)]
            pres.append(pre_ref[:, columns])
            convolved.append(convolve(tile, pres[section], taps))
            opened.append(jax.nn.sigmoid(convolved[section]))
            active.append(convolved[section] * opened[section])
        query_scale = unit_scale(active[0])
        key_scale = unit_scale(active[1])
        query_unit = active[0] * query_scale
        key = active[1] * key_scale
        start = 4 * width + head
        opening = jax.nn.sigmoid(pre_ref[:, start : start + 1])
        strength = opening * tile.live
        d_both = stacked(halves(d_lowers[head]), halves(d_scores[head]))
        by_key = exact(d_both, key, 1, 0)
        d_query = by_key[GROUP_ROWS:] * HEAD_DIM**-0.5
        from_lower = by_key[:GROUP_ROWS]
        weighted = stacked(halves(key * strength), halves(query_unit * HEAD_DIM**-0.5))
        d_key = strength * from_lower + exact(d_both, weighted, 0, 0)
        d_strength = along(d_inner[head] * active[2] + from_lower * key)
        d_value = d_inner[head] * strength
        d_opening = d_strength * (opening * (1.0 - opening)) * tile.live
        d_beta = d_beta + jnp.where(tile.col == head, d_opening, 0.0)
        d_active = [
            (d_query - query_unit * along(query_unit * d_query)) * query_scale,
            (d_key - key * along(key * d_key)) * key_scale,
            d_value,
        ]
        for section in range(3):
            columns = head_columns(width, section, head)
            taps = [param_ref[offset : offset + 1, columns] for offset in range(KERNEL)]
            slope = opened[section] * (1.0 + convolved[section] * (1.0 - opened[section]))
            d_convolved = d_active[section] * slope
            d_pre = d_convolved * taps[0]
            sums = [jnp.sum(d_convolved * pres[section], 0, keepdims=True)]
            for offset in range(1, KERNEL):
                d_pre = d_pre + tile.later(d_convolved, offset) * taps[offset]
                sums.append(
                    jnp.sum(d_convolved * tile.earlier(pres[section], offset), 0, keepdims=True)
                )
            d_param_ref[0:KERNEL, columns] += jnp.concatenate(sums, 0)
            d_pre_ref[:, columns] = d_pre.astype(bf)
    d_pre_ref[:, 4 * width :] = d_beta.astype(bf)


NO_COST = pl.CostEstimate(flops=0, bytes_accessed=0, transcendentals=0)


def call(kernel, operands, in_specs, out_specs, out_shape, grid=(), scratch=(), micros=0):
    results = pl.pallas_call(
        kernel,
        grid=grid,
        in_specs=in_specs,
        out_specs=out_specs,
        out_shape=out_shape,
        scratch_shapes=scratch,
        compiler_params=pltpu.CompilerParams(
            dimension_semantics=("arbitrary",) * len(grid), vmem_limit_bytes=48 * 2**20
        ),
        cost_estimate=pl.CostEstimate(
            flops=micros * 10**9, bytes_accessed=0, transcendentals=0
        ),
    )(*operands)
    return list(results)


def whole(array):
    return pl.BlockSpec(array.shape, lambda *step: (0,) * len(array.shape))


def mixer_specs(width):
    wide = 4 * width + SMALL
    heads = width // HEAD_DIM
    layout = pl.BlockSpec(memory_space=pltpu.SMEM)
    pre = pl.BlockSpec((GROUP_ROWS, wide), lambda group: (group, 0))
    param = pl.BlockSpec((2 * KERNEL, 3 * width), lambda group: (0, 0))
    narrow = pl.BlockSpec((GROUP_ROWS, width), lambda group: (group, 0))
    square = pl.BlockSpec((heads, GROUP_ROWS, HEAD_DIM), lambda group: (group, 0, 0))
    return layout, pre, param, narrow, square


def mixer_forward(layout, pre, params, width):
    groups = layout.shape[0]
    layout_spec, pre_spec, param_spec, narrow, square = mixer_specs(width)
    squares = pltpu.HBM((groups * width // HEAD_DIM, GROUP_ROWS, HEAD_DIM), f32)
    return call(
        mixer_forward_kernel,
        [layout, pre, params],
        [layout_spec, pre_spec, param_spec],
        [narrow] + [square] * 4,
        [jax.ShapeDtypeStruct((groups * GROUP_ROWS, width), bf)] + [squares] * 4,
        (groups,),
    )


def mixer_backward(layout, pre, params, weight, d_mixed, kept, width):
    groups = layout.shape[0]
    layout_spec, pre_spec, param_spec, _, square = mixer_specs(width)
    kept = [pltpu.with_memory_space_constraint(array, pltpu.HBM) for array in kept]
    return call(
        mixer_backward_kernel,
        [layout, pre, params, weight, *kept, *d_mixed],
        [layout_spec, pre_spec, param_spec, whole(weight)]
        + [square] * 4
        + [whole(block) for block in d_mixed],
        [pre_spec, param_spec],
        [jax.ShapeDtypeStruct(pre.shape, bf), jax.ShapeDtypeStruct(params.shape, f32)],
        (groups,),
        [pltpu.VMEM((GROUP_ROWS, width), f32)],
        micros=60,
    )


def first_kernel(gain_ref, weight_ref, *refs):
    *value_refs, normed_ref, out_ref, scale_ref, total_ref = refs
    step, depth = pl.program_id(0), weight_ref.shape[0]

    @pl.when(step == 0)
    def _():
        for group, ref in enumerate(value_refs):
            values = ref[...].astype(f32)
            scale = lax.rsqrt(jnp.mean(values * values, -1, keepdims=True) + 1e-06)
            rows = pl.ds(group * GROUP_ROWS, GROUP_ROWS)
            scale_ref[rows, :] = jnp.broadcast_to(scale, (GROUP_ROWS, 128))
        total_ref[...] = jnp.zeros_like(total_ref)

    columns = pl.ds(pl.multiple_of(step * depth, depth), depth)
    for group, ref in enumerate(value_refs):
        rows = pl.ds(group * GROUP_ROWS, GROUP_ROWS)
        values = ref[:, columns].astype(f32) * scale_ref[rows, :1] * gain_ref[...]
        normed_ref[rows, :] = values.astype(bf)
    total_ref[...] += plain_product(normed_ref[...], weight_ref[...])

    @pl.when(step == pl.num_programs(0) - 1)
    def _():
        out_ref[...] = total_ref[...]


def normed_product(blocks, gain, weight, depth=512):
    rows, (features, columns) = len(blocks) * GROUP_ROWS, weight.shape
    return call(
        first_kernel,
        [gain, weight, *blocks],
        [
            pl.BlockSpec((1, depth), lambda step: (0, step)),
            pl.BlockSpec((depth, columns), lambda step: (step, 0)),
        ]
        + [whole(block) for block in blocks],
        [
            pl.BlockSpec((rows, depth), lambda step: (0, step)),
            pl.BlockSpec((rows, columns), lambda step: (0, 0)),
        ],
        [
            jax.ShapeDtypeStruct((rows, features), bf),
            jax.ShapeDtypeStruct((rows, columns), f32),
        ],
        (features // depth,),
        [pltpu.VMEM((rows, 128), f32), pltpu.VMEM((rows, columns), f32)],
    )


def product_blocks(left, right, transposed=False, block=512, micros=0):
    product = transposed_product if transposed else plain_product
    columns = right.shape[0] if transposed else right.shape[1]
    groups = left.shape[0] // GROUP_ROWS

    def kernel(left_ref, right_ref, *out_refs):
        total = product(left_ref[...], right_ref[...])
        for group, ref in enumerate(out_refs):
            ref[...] = total[group * GROUP_ROWS : (group + 1) * GROUP_ROWS].astype(ref.dtype)

    if transposed:
        right_spec = pl.BlockSpec((block, right.shape[1]), lambda step: (step, 0))
    else:
        right_spec = pl.BlockSpec((right.shape[0], block), lambda step: (0, step))
    return call(
        kernel,
        [left, right],
        [whole(left), right_spec],
        [pl.BlockSpec((GROUP_ROWS, block), lambda step: (0, step))] * groups,
        [
            jax.ShapeDtypeStruct((GROUP_ROWS, columns), bf if group else f32)
            for group in range(groups)
        ],
        (columns // block,),
        micros=micros,
    )


def grad_product(left, right, block=256, micros=0):
    rows, features = left.shape
    if features % block:
        block = 128

    def kernel(left_ref, right_ref, out_ref):
        out_ref[...] = rows_product(left_ref[...], right_ref[...]).astype(bf)

    return call(
        kernel,
        [left, right],
        [pl.BlockSpec((rows, block), lambda step: (0, step)), whole(right)],
        [pl.BlockSpec((block, right.shape[1]), lambda step: (step, 0))],
        [pltpu.HBM((features, right.shape[1]), bf)],
        (features // block,),
        micros=micros,
    )[0]


def from_own(part, values):
    groups = values.shape[0] // GROUP_ROWS

    def kernel(part_ref, values_ref, out_ref):
        for step in range(groups):
            source = lax.rem(part_ref[0] + groups - step, groups) * GROUP_ROWS
            rows = pl.ds(pl.multiple_of(source, GROUP_ROWS), GROUP_ROWS)
            out_ref[step * GROUP_ROWS : (step + 1) * GROUP_ROWS] = values_ref[rows]

    return call(
        kernel,
        [part.reshape(1).astype(jnp.int32), values],
        [pl.BlockSpec(memory_space=pltpu.SMEM), whole(values)],
        [whole(values)],
        [jax.ShapeDtypeStruct(values.shape, values.dtype)],
        (1,),
    )[0]


def tie_all(values, *others):
    anywhere = pl.BlockSpec(memory_space=pl.ANY)
    others = [
        pltpu.with_memory_space_constraint(other, pltpu.HBM) if other.size > 2**21 else other
        for other in others
    ]
    tied = pl.pallas_call(
        lambda *refs: None,
        in_specs=[anywhere] * (len(values) + len(others)),
        out_specs=[anywhere] * len(values),
        out_shape=[
            (pltpu.HBM if value.size > 2**21 else jax.ShapeDtypeStruct)(value.shape, value.dtype)
            for value in values
        ],
        input_output_aliases={i: i for i in range(len(values))},
        cost_estimate=NO_COST,
    )(*values, *others)
    return list(tied)


def tie(value, *others):
    return tie_all([value], *others)[0]


def assemble(part, values, received, others):
    parts = values.shape[0]

    def kernel(part_ref, values_ref, *refs):
        own = part_ref[0]
        out_ref = refs[-1]
        out_ref[own] = values_ref[own]
        for step in range(1, parts):
            out_ref[lax.rem(own + parts - step, parts)] = refs[step - 1][...]

    vmem = pl.BlockSpec(memory_space=pltpu.VMEM)
    anywhere = pl.BlockSpec(memory_space=pl.ANY)
    return pl.pallas_call(
        kernel,
        in_specs=[pl.BlockSpec(memory_space=pltpu.SMEM)]
        + [vmem] * parts
        + [anywhere] * len(others),
        out_specs=vmem,
        out_shape=jax.ShapeDtypeStruct(values.shape, values.dtype),
        compiler_params=pltpu.CompilerParams(vmem_limit_bytes=32 * 2**20),
        cost_estimate=NO_COST,
    )(part.reshape(1).astype(jnp.int32), values, *received, *others)


def copy_columns(count, *refs):
    target = refs[-1]
    start = 0
    for source in refs[:count]:
        block = source[...].reshape(source.shape[-2:])
        columns = pl.ds(start, block.shape[1])
        if len(target.shape) == 3:
            target[0, :, columns] = block.astype(target.dtype)
        else:
            target[:, columns] = block.astype(target.dtype)
        start += block.shape[1]


def to_parts(sources, parts, dtype, others=()):
    rows = sources[0][0].shape[0]

    def spec(section, width):
        return pl.BlockSpec((rows, width), lambda p: (0, section * parts + p))

    total = sum(width for _, _, width in sources)
    return pl.pallas_call(
        functools.partial(copy_columns, len(sources)),
        grid=(parts,),
        in_specs=[spec(section, width) for _, section, width in sources]
        + [pl.BlockSpec(memory_space=pl.ANY)] * len(others),
        out_specs=pl.BlockSpec((1, rows, total), lambda p: (p, 0, 0)),
        out_shape=jax.ShapeDtypeStruct((parts, rows, total), dtype),
        cost_estimate=NO_COST,
    )(*[array for array, _, _ in sources], *others)


def updown_from_parts(slabs):
    parts, rows, width = slabs.shape
    units = width // 2

    def kernel(slabs_ref, out_ref):
        for p in range(parts):
            out_ref[:, p * units : (p + 1) * units] = slabs_ref[p].astype(f32)

    return pl.pallas_call(
        kernel,
        grid=(2,),
        in_specs=[pl.BlockSpec((parts, rows, units), lambda half: (0, 0, half))],
        out_specs=pl.BlockSpec((rows, parts * units), lambda half: (0, half)),
        out_shape=jax.ShapeDtypeStruct((rows, parts * width), f32),
        compiler_params=pltpu.CompilerParams(vmem_limit_bytes=32 * 2**20),
        cost_estimate=NO_COST,
    )(slabs)


def mixer_from_parts(slabs, width):
    parts, rows, _ = slabs.shape

    def kernel(slabs_ref, qkv_ref, gate_ref, strength_ref):
        for p in range(parts):
            for section in range(4):
                block = slabs_ref[p, :, section * width : (section + 1) * width].astype(f32)
                if section < 3:
                    start = (section * parts + p) * width
                    qkv_ref[:, start : start + width] = block
                else:
                    gate_ref[:, p * width : (p + 1) * width] = block
            last = slabs_ref[p, :, 4 * width :].astype(f32)
            strength_ref[:, p * SMALL : (p + 1) * SMALL] = last

    widths = [3 * parts * width, parts * width, parts * SMALL]
    return pl.pallas_call(
        kernel,
        out_shape=[jax.ShapeDtypeStruct((rows, size), f32) for size in widths],
        compiler_params=pltpu.CompilerParams(vmem_limit_bytes=32 * 2**20),
        cost_estimate=NO_COST,
    )(slabs)


def total_of(own_ref, received_refs):
    total = own_ref[...]
    for ref in received_refs:
        total = total + ref[...].astype(f32)
    return total


def row_scale(values):
    return lax.rsqrt(jnp.mean(values * values, -1, keepdims=True) + 1e-06)


def norm_slope(values, scale, gain, grad):
    mean = jnp.mean(gain * grad * values, -1, keepdims=True)
    return scale * gain * grad - values * (scale * scale * scale * mean)


def hidden_kernel(own_ref, *refs):
    *received, input_ref, gain_ref, hidden_ref, normed_ref = refs
    hidden = input_ref[...].astype(f32) + total_of(own_ref, received)
    hidden_ref[...] = hidden
    normed_ref[...] = (hidden * row_scale(hidden) * gain_ref[...]).astype(bf)


def hidden_back_kernel(own_ref, *refs):
    *received, hidden_ref, gain_ref, cot_ref, d_hidden_ref, d_mixed_ref, d_gain_ref = refs
    grad = total_of(own_ref, received)
    hidden = hidden_ref[...]
    scale = row_scale(hidden)

    @pl.when(pl.program_id(0) == 0)
    def _():
        d_gain_ref[...] = jnp.zeros_like(d_gain_ref)

    d_gain_ref[...] += jnp.sum(grad * hidden * scale, 0, keepdims=True)
    d_hidden = cot_ref[...].astype(f32) + norm_slope(hidden, scale, gain_ref[...], grad)
    d_hidden_ref[...] = d_hidden
    d_mixed_ref[...] = d_hidden.astype(bf)


def input_back_kernel(own_ref, *refs):
    *received, input_ref, gain_ref, d_hidden_ref, out_ref = refs
    grad = total_of(own_ref, received)
    values = input_ref[...].astype(f32)
    slope = norm_slope(values, row_scale(values), gain_ref[...], grad)
    out_ref[...] = (d_hidden_ref[...] + slope).astype(bf)


def block_out_kernel(own_ref, *refs):
    *received, hidden_ref, out_ref = refs
    out_ref[...] = (hidden_ref[...] + total_of(own_ref, received)).astype(bf)


def by_rows(kernel, arrays, outs, block=64):
    def spec(shape):
        if shape[0] == 1:
            return pl.BlockSpec(shape, lambda i: (0, 0))
        return pl.BlockSpec((block, shape[1]), lambda i: (i, 0))

    return pl.pallas_call(
        kernel,
        grid=(GROUP_ROWS // block,),
        in_specs=[spec(array.shape) for array in arrays],
        out_specs=[spec(shape) for shape, _ in outs],
        out_shape=[jax.ShapeDtypeStruct(shape, dtype) for shape, dtype in outs],
        compiler_params=pltpu.CompilerParams(dimension_semantics=("arbitrary",)),
        cost_estimate=NO_COST,
    )(*arrays)


def body(
    block_in,
    out_grad,
    norm1_gain,
    conv_weight,
    head_gain,
    qkv_weight,
    beta_weight,
    gate_weight,
    out_weight,
    norm2_gain,
    updown_weight,
    down_weight,
    seq_blocks,
    lead_blocks,
):
    devices = lax.axis_size("dp")
    parts = MODEL
    copies = devices // parts
    part = lax.axis_index("dp") // copies
    copy = lax.axis_index("dp") % copies
    rows_own = qkv_weight.shape[0]
    width = D // parts
    units = FF // parts
    heads_part = HEADS // parts
    wide = 4 * width + SMALL
    model_groups = [[m * copies + t for m in range(parts)] for t in range(copies)]
    copy_groups = [[m * copies + t for t in range(copies)] for m in range(parts)]

    def exchange(values):
        return lax.all_to_all(
            values, "dp", split_axis=0, concat_axis=0, axis_index_groups=model_groups, tiled=True
        )

    def shift(values, step):
        pairs = [
            (m * copies + t, (m + step) % parts * copies + t)
            for m in range(parts)
            for t in range(copies)
        ]
        return lax.ppermute(values, "dp", pairs)

    def exchange_apart(values, before, after=()):
        cut = [
            lax.dynamic_index_in_dim(values, (part + step) % parts, 0, keepdims=False)
            for step in range(1, parts)
        ]
        received = [shift(piece, step) for step, piece in enumerate(tie_all(cut, *before), 1)]
        return assemble(part, values, received, after)

    def gather_rows(values):
        return [values] + [shift(values, step) for step in range(1, parts)]

    def scatter_rows(terms):
        return [terms[0]] + [shift(block, -step) for step, block in enumerate(terms[1:], 1)]

    def gather_copies(values):
        return lax.all_gather(values, "dp", axis=0, axis_index_groups=copy_groups, tiled=True)

    def scatter_copies(values):
        return lax.psum_scatter(
            values.astype(bf),
            "dp",
            scatter_dimension=0,
            axis_index_groups=copy_groups,
            tiled=True,
        )

    def halves_across(values, bit, axis):
        pairs = [(i, i ^ (1 << bit)) for i in range(devices)]
        side = (copy >> bit) & 1
        own = lax.dynamic_index_in_dim(values, side, axis, keepdims=False)
        other = lax.dynamic_index_in_dim(values, 1 - side, axis, keepdims=False)
        return own, lax.ppermute(other, "dp", pairs)

    def halve(values, bit, axis, *others):
        own, received = halves_across(values, bit, axis)
        if others:
            received = tie(received, *others)
        return (own.astype(f32) + received.astype(f32)).astype(bf)

    by_halves = copies == 8

    def halve_cores(values, *others):
        if not by_halves:
            return values
        rows, columns = values.shape
        return halve(values.reshape(2, 2, 2, rows // 8, columns), 0, 2, *others)

    def halve_first(values):
        if not by_halves:
            return [values]
        middle = values.shape[-1] // 2
        return [halve(values[..., :middle], 1, 1), halve(values[..., middle:], 2, 0)]

    def halve_second(values):
        if not by_halves:
            return scatter_copies(values[0])
        return jnp.concatenate([halve(values[0], 2, 0), halve(values[1], 1, 0)], 1)

    def to_wire(values):
        return values.reshape(-1, parts, copies, rows_own).swapaxes(1, 2).reshape(-1, D)

    def from_wire(values):
        return values.reshape(-1, copies, parts, rows_own).swapaxes(1, 2).reshape(-1, D)

    w_out_own = to_wire(out_weight.astype(bf))
    w_out = gather_copies(w_out_own)
    strengths = beta_weight.reshape(rows_own, parts, heads_part)
    strengths = jnp.pad(strengths, ((0, 0), (0, 0), (0, SMALL - heads_part)))
    strengths = tie(strengths.reshape(rows_own, parts * SMALL), w_out_own)
    pieces = [(qkv_weight, section, width) for section in range(3)]
    pieces = to_parts(pieces + [(gate_weight, 0, width), (strengths, 0, SMALL)], parts, bf)
    mixer_pieces = tie(exchange(pieces), w_out)
    w_mixer = gather_copies(mixer_pieces.reshape(parts * rows_own, wide))
    inputs = tie(to_wire(block_in), mixer_pieces)
    input_rows = gather_rows(inputs)

    lanes = -(-3 * rows_own // 128) * 128
    numbers = jnp.concatenate([seq_blocks[0], lead_blocks]).astype(f32)
    small = [conv_weight.T, norm1_gain[None], head_gain[None], norm2_gain[None], numbers[None]]
    small = [jnp.pad(rows, ((0, 0), (0, lanes - rows.shape[1]))) for rows in small]
    small = jnp.pad(jnp.concatenate(small, 0).astype(bf), ((0, 2 * KERNEL), (0, 0)))
    small = jnp.broadcast_to(small[None], (devices,) + small.shape)
    small = lax.all_to_all(tie(small, *input_rows[1:]), "dp", 0, 0, tiled=True)
    taps = small[:, :KERNEL, : 3 * rows_own].swapaxes(0, 1).reshape(KERNEL, 3, parts, width)
    taps = lax.dynamic_index_in_dim(taps, part, 2, keepdims=False).reshape(KERNEL, 3 * width)
    gain_one, head_full, gain_two = (
        small[:, KERNEL + i, :rows_own].reshape(1, D).astype(f32) for i in range(3)
    )
    gain_one, gain_two = to_wire(gain_one), to_wire(gain_two)
    head_part = lax.dynamic_slice_in_dim(head_full, part * width, width, 1)
    params = jnp.concatenate([taps.astype(f32), jnp.pad(head_part, ((0, 0), (0, 2 * width)))], 0)
    params = jnp.pad(params, ((0, KERNEL - 1), (0, 0)))
    numbers = small[:, KERNEL + 3, :3].astype(f32).astype(jnp.int32)
    layouts = block_layouts(numbers[:, 0], numbers[:, 1], numbers[:, 2])
    layouts = layouts.reshape(parts, copies, 4)
    layouts = lax.dynamic_index_in_dim(layouts, copy, 1, keepdims=False)
    wanted = (part - jnp.arange(parts)) % parts
    wanted = (wanted[:, None] == jnp.arange(parts)).astype(f32)
    layouts = jnp.sum(wanted[:, :, None] * layouts, 1)

    pieces = [(updown_weight, half, units) for half in range(2)]
    updown_pieces = to_parts(pieces, parts, bf, [mixer_pieces])
    w_down_own = to_wire(down_weight.astype(bf))
    w_down = gather_copies(tie(w_down_own, *input_rows[1:]))
    cotangent_own = to_wire(out_grad)

    cotangent = lax.all_gather(
        tie(cotangent_own, *input_rows[1:]), "dp", axis=0, axis_index_groups=model_groups, tiled=True
    )
    gain_first = tie(gain_one, w_down_own, cotangent_own, updown_pieces)
    normed, pre = normed_product(input_rows, gain_first, w_mixer)
    mixed, *kept = mixer_forward(layouts, pre, params, width)
    out_terms = product_blocks(mixed, w_out)
    updown_pieces = exchange_apart(updown_pieces, input_rows[1:], out_terms[1:])
    w_updown = gather_copies(updown_pieces.reshape(parts * rows_own, 2 * units))
    stream = ((GROUP_ROWS, D), f32)
    narrow = ((GROUP_ROWS, D), bf)
    hidden, normed_two = by_rows(
        hidden_kernel,
        scatter_rows(out_terms) + [inputs, gain_two],
        [stream, narrow],
    )
    cotangent = from_own(part, cotangent)
    normed_two = jnp.concatenate(gather_rows(normed_two), 0)

    def swiglu_units(updown):
        return jax.nn.silu(updown[:, :units]) * updown[:, units:]

    updown = plain_product(normed_two, w_updown)
    active, swiglu_back = jax.vjp(swiglu_units, updown)
    active = active.astype(bf)
    d_active = transposed_product(cotangent, w_down)
    d_updown = swiglu_back(d_active)[0].astype(bf)
    d_normed_two = product_blocks(d_updown, w_updown, transposed=True)
    active = tie(active, *d_normed_two[1:])
    down_terms = grad_product(active, cotangent)
    updown_terms = grad_product(normed_two, tie(d_updown, down_terms))
    gain_late = tie(gain_two, updown_terms)
    d_normed_two = scatter_rows(d_normed_two)
    updown_grad = scatter_copies(tie(updown_terms, gain_late, *d_normed_two[1:]))
    d_hidden, d_mixed, gain_two_grad = by_rows(
        hidden_back_kernel,
        d_normed_two + [hidden, gain_late, cotangent_own],
        [stream, narrow, ((1, D), f32)],
    )


    out_terms = product_blocks(tie(active, d_mixed), w_down)
    down_terms = tie(down_terms, *out_terms[1:])
    d_mixed = gather_rows(d_mixed)
    late = tie(params, *out_terms)
    out_terms[1:] = tie_all(out_terms[1:], *d_mixed[1:])
    d_pre, d_params = mixer_backward(layouts, pre, late, w_out, d_mixed, kept, width)
    mixer_terms = tie(grad_product(normed, d_pre, micros=20), updown_grad)
    mixer_grad = scatter_copies(mixer_terms)

    d_normed_terms = product_blocks(
        tie(d_pre, mixer_terms), w_mixer, transposed=True, micros=150
    )
    hidden = tie(hidden, d_normed_terms[0])
    (block_out,) = by_rows(block_out_kernel, scatter_rows(out_terms) + [hidden], [narrow])
    d_normed_terms[1:] = tie_all(d_normed_terms[1:], block_out)
    d_normed = scatter_rows(d_normed_terms)
    down_grad = halve_first(halve_cores(down_terms, *d_normed_terms[1:]))
    gain_one_grad = 0.0
    for values, terms in zip(input_rows, d_normed_terms):
        values = values.astype(f32)
        terms = terms.astype(f32) * (values * row_scale(values))
        gain_one_grad = gain_one_grad + jnp.sum(terms, 0, keepdims=True)

    here = (jnp.arange(parts) == part).astype(f32)[:, None]
    taps_grad = d_params[:KERNEL].reshape(KERNEL, 3, 1, width) * here
    taps_grad = taps_grad.reshape(KERNEL, parts, copies, 3, rows_own).transpose(1, 2, 3, 0, 4)
    taps_grad = taps_grad.reshape(devices, 3 * KERNEL, rows_own)
    head_grad = (d_params[KERNEL, :width] * here).reshape(devices, 1, rows_own)
    gain_grads = [
        grad.reshape(copies, parts, 1, rows_own).swapaxes(0, 1).reshape(devices, 1, rows_own)
        for grad in (gain_one_grad, gain_two_grad)
    ]
    small_grad = jnp.concatenate([taps_grad, head_grad] + gain_grads, 1)
    small_grad = jnp.pad(small_grad, ((0, 0), (0, 1), (0, 128 - rows_own)))
    small_grad = jnp.sum(lax.all_to_all(small_grad, "dp", 0, 0, tiled=True), 0)[:, :rows_own]
    taps_shard = small_grad[: 3 * KERNEL].reshape(3, KERNEL, rows_own).swapaxes(1, 2)
    taps_shard = taps_shard.reshape(3 * rows_own, KERNEL)
    head_shard, gain_one_shard, gain_two_shard = small_grad[3 * KERNEL : 3 * KERNEL + 3]

    (input_grad,) = by_rows(input_back_kernel, d_normed + [inputs, gain_one, d_hidden], [narrow])
    updown_grad = updown_grad.reshape(parts, rows_own, 2 * units)
    updown_shard = updown_from_parts(exchange_apart(updown_grad, [mixer_terms], [input_grad]))
    out_shard = grad_product(tie(mixed, d_normed_terms[0]), jnp.concatenate(d_mixed, 0))
    out_shard = halve_second(halve_first(halve_cores(tie(out_shard, mixer_grad))))
    out_shard = from_wire(out_shard.astype(f32))
    down_shard = from_wire(halve_second(tie_all(down_grad, mixer_grad)).astype(f32))
    mixer_grad = exchange(mixer_grad.reshape(parts, rows_own, wide))
    qkv_shard, gate_shard, strengths = mixer_from_parts(mixer_grad, width)
    beta_shard = strengths.reshape(rows_own, parts, SMALL)[:, :, :heads_part]
    return (
        from_wire(block_out),
        from_wire(input_grad),
        gain_one_shard,
        taps_shard,
        head_shard,
        qkv_shard,
        beta_shard.reshape(rows_own, HEADS),
        gate_shard,
        out_shard,
        gain_two_shard,
        updown_shard,
        down_shard,
    )


def solution(mesh):
    placed = (
        P("dp", None),
        P("dp", None),
        P("dp"),
        P("dp", None),
        P("dp"),
        P("dp", None),
        P("dp", None),
        P("dp", None),
        P("dp", None),
        P("dp"),
        P("dp", None),
        P("dp", None),
        P("dp", None),
        P("dp"),
    )
    return jax.shard_map(
        body,
        mesh=mesh,
        in_specs=placed,
        out_specs=(
            P("dp", None),
            P("dp", None),
            P("dp"),
            P("dp", None),
            P("dp"),
            P("dp", None),
            P("dp", None),
            P("dp", None),
            P("dp", None),
            P("dp"),
            P("dp", None),
            P("dp", None),
        ),
        check_vma=False,
    )
```

```python
import functools

import jax
import jax.numpy as jnp
from jax import lax
from jax.experimental import pallas as pl
from jax.experimental.pallas import tpu as pltpu
from jax.sharding import PartitionSpec as P

D = 2048
HEADS = 16
HEAD_DIM = 128
FF = 5632
KERNEL = 4
BLOCK_ROWS = 64
BLOCKS_DEV = 2
GROUP_ROWS = BLOCK_ROWS * BLOCKS_DEV
SMALL = 128
MODEL = 4

f32 = jnp.float32
bf = jnp.bfloat16


def block_layouts(first, second, lead):
    def doc(block):
        in_first = (block >= lead) & (block < lead + first)
        in_second = (block >= lead + first) & (block < lead + first + second)
        return jnp.where(in_first, 1, jnp.where(in_second, 2, 0))

    starts = (lead == 1) | (lead + first == 1) & (second > 0)
    columns = [doc(0) > 0, doc(1) > 0, doc(0) == doc(1), ~starts]
    return jnp.stack(columns, 1).astype(f32)


def plain_product(left, right):
    return jnp.dot(left, right, preferred_element_type=f32)


def rows_product(left, right):
    return lax.dot_general(left, right, (((0,), (0,)), ((), ())), preferred_element_type=f32)


def transposed_product(left, right):
    return lax.dot_general(left, right, (((1,), (1,)), ((), ())), preferred_element_type=f32)


def halves(values):
    high = values.astype(bf)
    return high, (values - high.astype(f32)).astype(bf)


def exact(left, right, left_dim, right_dim):
    left_high, left_low = left if isinstance(left, tuple) else halves(left)
    right_high, right_low = right if isinstance(right, tuple) else halves(right)
    return lax.dot_general(
        jnp.concatenate([left_high, left_high, left_low], left_dim),
        jnp.concatenate([right_high, right_low, right_high], right_dim),
        (((left_dim,), (right_dim,)), ((), ())),
        preferred_element_type=f32,
    )


def stacked(first, second):
    return tuple(jnp.concatenate([a, b], 0) for a, b in zip(first, second))


class Tile:
    def __init__(self, layout_ref, group):
        live_first, live_second, same, persist = (layout_ref[group, i] for i in range(4))
        shape = (GROUP_ROWS, HEAD_DIM)
        row = lax.broadcasted_iota(jnp.int32, shape, 0)
        col = lax.broadcasted_iota(jnp.int32, shape, 1)
        late = row >= BLOCK_ROWS
        self.row, self.col = row, col
        self.live = jnp.where(late, live_second, live_first)
        self.taps = [None] + [
            jnp.where(
                row < offset,
                0.0,
                jnp.where(late & (row < BLOCK_ROWS + offset), same, 1.0),
            )
            for offset in range(1, KERNEL)
        ]
        cross = jnp.where(late & (col < BLOCK_ROWS), persist, 1.0)
        self.lower = jnp.where(row > col, cross, 0.0)
        self.lower_full = jnp.where(row >= col, cross, 0.0)

    def earlier(self, values, offset):
        return pltpu.roll(values, offset, 0) * self.taps[offset]

    def later(self, values, offset):
        return pltpu.roll(values * self.taps[offset], GROUP_ROWS - offset, 0)


def convolve(tile, values, taps):
    total = values * taps[0]
    for offset in range(1, KERNEL):
        total = total + tile.earlier(values, offset) * taps[offset]
    return total


def unit_scale(values):
    return lax.rsqrt(jnp.sum(values * values, -1, keepdims=True) + 1e-06)


def head_columns(part_width, section, head):
    return pl.ds(section * part_width + head * HEAD_DIM, HEAD_DIM)


def unit_inverses(tile, lowers):
    eye = jnp.where(tile.row == tile.col, 1.0, 0.0)
    inverses = None
    size = 1
    while size < GROUP_ROWS:
        pair = tile.row // (2 * size) == tile.col // (2 * size)
        split = pair & (tile.row // size != tile.col // size)
        parts = [jnp.where(split, lower, 0.0) for lower in lowers]
        if inverses is None:
            inverses = [eye - part for part in parts]
        else:
            kept = [halves(inverse) for inverse in inverses]
            inner = [exact(part, known, 1, 0) for part, known in zip(parts, kept)]
            outer = [exact(known, value, 1, 0) for known, value in zip(kept, inner)]
            inverses = [inverse - value for inverse, value in zip(inverses, outer)]
        size *= 2
    return inverses


def mixer_forward_kernel(
    layout_ref, pre_ref, param_ref, mixed_ref, inverse_ref, score_ref, solved_ref, out_ref
):
    width = mixed_ref.shape[1]
    heads = range(width // HEAD_DIM)
    tile = Tile(layout_ref, pl.program_id(0))
    queries, keys, values, strengths = [], [], [], []
    for head in heads:
        parts = []
        for section in range(3):
            columns = head_columns(width, section, head)
            taps = [param_ref[offset : offset + 1, columns] for offset in range(KERNEL)]
            convolved = convolve(tile, pre_ref[:, columns], taps)
            parts.append(convolved * jax.nn.sigmoid(convolved))
        queries.append(parts[0] * (unit_scale(parts[0]) * HEAD_DIM**-0.5))
        keys.append(parts[1] * unit_scale(parts[1]))
        values.append(parts[2])
        start = 4 * width + head
        strengths.append(jax.nn.sigmoid(pre_ref[:, start : start + 1]) * tile.live)
    lowers, scores = [], []
    for head in heads:
        key_halves = halves(keys[head])
        both = exact(stacked(key_halves, halves(queries[head])), key_halves, 1, 1)
        lowers.append(both[:GROUP_ROWS] * strengths[head] * tile.lower)
        scores.append(both[GROUP_ROWS:] * tile.lower_full)
    inverses = unit_inverses(tile, lowers)
    solved = [exact(inverses[head], values[head] * strengths[head], 1, 0) for head in heads]
    outs = [exact(scores[head], solved[head], 1, 0) for head in heads]
    for head in heads:
        out = outs[head]
        scaled = out * lax.rsqrt(jnp.mean(out * out, -1, keepdims=True) + 1e-05)
        gate = pre_ref[:, head_columns(width, 3, head)]
        gain = param_ref[KERNEL : KERNEL + 1, head_columns(width, 0, head)]
        mixed = scaled * gain * (gate * jax.nn.sigmoid(gate)) * tile.live
        mixed_ref[:, head_columns(width, 0, head)] = mixed.astype(bf)
        inverse_ref[head] = inverses[head]
        score_ref[head] = scores[head]
        solved_ref[head] = solved[head]
        out_ref[head] = out


def mixer_backward_kernel(
    layout_ref,
    pre_ref,
    param_ref,
    weight_ref,
    inverse_ref,
    score_ref,
    solved_ref,
    out_ref,
    *refs,
):
    *mixed_refs, d_pre_ref, d_param_ref, grad_ref = refs
    width = grad_ref.shape[1]
    heads = range(width // HEAD_DIM)
    tile = Tile(layout_ref, pl.program_id(0))
    for group, mixed_ref in enumerate(mixed_refs):

        @pl.when(pl.program_id(0) == group)
        def _():
            grad_ref[...] = transposed_product(mixed_ref[...], weight_ref[...])

    @pl.when(pl.program_id(0) == 0)
    def _():
        d_param_ref[...] = jnp.zeros_like(d_param_ref)

    def along(values):
        return jnp.sum(values, -1, keepdims=True)

    d_outs = []
    for head in heads:
        columns = head_columns(width, 0, head)
        d_mixed = grad_ref[:, columns] * tile.live
        out = out_ref[head]
        scale = lax.rsqrt(jnp.mean(out * out, -1, keepdims=True) + 1e-05)
        scaled = out * scale
        gate = pre_ref[:, head_columns(width, 3, head)]
        gate_open = jax.nn.sigmoid(gate)
        gain = param_ref[KERNEL : KERNEL + 1, columns]
        gated = d_mixed * (gate * gate_open)
        d_param_ref[KERNEL : KERNEL + 1, columns] += jnp.sum(gated * scaled, 0, keepdims=True)
        d_gate = d_mixed * scaled * gain * (gate_open * (1.0 + gate * (1.0 - gate_open)))
        d_pre_ref[:, head_columns(width, 3, head)] = d_gate.astype(bf)
        d_scaled = gated * gain
        mean = jnp.mean(d_scaled * out, -1, keepdims=True)
        d_outs.append(scale * d_scaled - out * (scale * scale * scale * mean))
    d_out_halves = [halves(value) for value in d_outs]
    solved_halves = [halves(solved_ref[head]) for head in heads]
    d_solved = [exact(score_ref[head], d_out_halves[head], 0, 0) for head in heads]
    d_scores = [
        exact(d_out_halves[head], solved_halves[head], 1, 1) * tile.lower_full for head in heads
    ]
    d_inner = [exact(inverse_ref[head], d_solved[head], 0, 0) for head in heads]
    d_lowers = [exact(d_inner[head], solved_halves[head], 1, 1) * -tile.lower for head in heads]
    d_beta = jnp.zeros((GROUP_ROWS, SMALL), f32)
    for head in heads:
        pres, convolved, opened, active = [], [], [], []
        for section in range(3):
            columns = head_columns(width, section, head)
            taps = [param_ref[offset : offset + 1, columns] for offset in range(KERNEL)]
            pres.append(pre_ref[:, columns])
            convolved.append(convolve(tile, pres[section], taps))
            opened.append(jax.nn.sigmoid(convolved[section]))
            active.append(convolved[section] * opened[section])
        query_scale = unit_scale(active[0])
        key_scale = unit_scale(active[1])
        query_unit = active[0] * query_scale
        key = active[1] * key_scale
        start = 4 * width + head
        opening = jax.nn.sigmoid(pre_ref[:, start : start + 1])
        strength = opening * tile.live
        d_both = stacked(halves(d_lowers[head]), halves(d_scores[head]))
        by_key = exact(d_both, key, 1, 0)
        d_query = by_key[GROUP_ROWS:] * HEAD_DIM**-0.5
        from_lower = by_key[:GROUP_ROWS]
        weighted = stacked(halves(key * strength), halves(query_unit * HEAD_DIM**-0.5))
        d_key = strength * from_lower + exact(d_both, weighted, 0, 0)
        d_strength = along(d_inner[head] * active[2] + from_lower * key)
        d_value = d_inner[head] * strength
        d_opening = d_strength * (opening * (1.0 - opening)) * tile.live
        d_beta = d_beta + jnp.where(tile.col == head, d_opening, 0.0)
        d_active = [
            (d_query - query_unit * along(query_unit * d_query)) * query_scale,
            (d_key - key * along(key * d_key)) * key_scale,
            d_value,
        ]
        for section in range(3):
            columns = head_columns(width, section, head)
            taps = [param_ref[offset : offset + 1, columns] for offset in range(KERNEL)]
            slope = opened[section] * (1.0 + convolved[section] * (1.0 - opened[section]))
            d_convolved = d_active[section] * slope
            d_pre = d_convolved * taps[0]
            sums = [jnp.sum(d_convolved * pres[section], 0, keepdims=True)]
            for offset in range(1, KERNEL):
                d_pre = d_pre + tile.later(d_convolved, offset) * taps[offset]
                sums.append(
                    jnp.sum(d_convolved * tile.earlier(pres[section], offset), 0, keepdims=True)
                )
            d_param_ref[0:KERNEL, columns] += jnp.concatenate(sums, 0)
            d_pre_ref[:, columns] = d_pre.astype(bf)
    d_pre_ref[:, 4 * width :] = d_beta.astype(bf)


NO_COST = pl.CostEstimate(flops=0, bytes_accessed=0, transcendentals=0)


def call(kernel, operands, in_specs, out_specs, out_shape, grid=(), scratch=(), micros=0):
    results = pl.pallas_call(
        kernel,
        grid=grid,
        in_specs=in_specs,
        out_specs=out_specs,
        out_shape=out_shape,
        scratch_shapes=scratch,
        compiler_params=pltpu.CompilerParams(
            dimension_semantics=("arbitrary",) * len(grid), vmem_limit_bytes=48 * 2**20
        ),
        cost_estimate=pl.CostEstimate(
            flops=micros * 10**9, bytes_accessed=0, transcendentals=0
        ),
    )(*operands)
    return list(results)


def whole(array):
    return pl.BlockSpec(array.shape, lambda *step: (0,) * len(array.shape))


def mixer_specs(width):
    wide = 4 * width + SMALL
    heads = width // HEAD_DIM
    layout = pl.BlockSpec(memory_space=pltpu.SMEM)
    pre = pl.BlockSpec((GROUP_ROWS, wide), lambda group: (group, 0))
    param = pl.BlockSpec((2 * KERNEL, 3 * width), lambda group: (0, 0))
    narrow = pl.BlockSpec((GROUP_ROWS, width), lambda group: (group, 0))
    square = pl.BlockSpec((heads, GROUP_ROWS, HEAD_DIM), lambda group: (group, 0, 0))
    return layout, pre, param, narrow, square


def mixer_forward(layout, pre, params, width):
    groups = layout.shape[0]
    layout_spec, pre_spec, param_spec, narrow, square = mixer_specs(width)
    squares = pltpu.HBM((groups * width // HEAD_DIM, GROUP_ROWS, HEAD_DIM), f32)
    return call(
        mixer_forward_kernel,
        [layout, pre, params],
        [layout_spec, pre_spec, param_spec],
        [narrow] + [square] * 4,
        [jax.ShapeDtypeStruct((groups * GROUP_ROWS, width), bf)] + [squares] * 4,
        (groups,),
    )


def mixer_backward(layout, pre, params, weight, d_mixed, kept, width):
    groups = layout.shape[0]
    layout_spec, pre_spec, param_spec, _, square = mixer_specs(width)
    kept = [pltpu.with_memory_space_constraint(array, pltpu.HBM) for array in kept]
    return call(
        mixer_backward_kernel,
        [layout, pre, params, weight, *kept, *d_mixed],
        [layout_spec, pre_spec, param_spec, whole(weight)]
        + [square] * 4
        + [whole(block) for block in d_mixed],
        [pre_spec, param_spec],
        [jax.ShapeDtypeStruct(pre.shape, bf), jax.ShapeDtypeStruct(params.shape, f32)],
        (groups,),
        [pltpu.VMEM((GROUP_ROWS, width), f32)],
        micros=60,
    )


def first_kernel(gain_ref, weight_ref, *refs):
    *value_refs, normed_ref, out_ref, scale_ref, total_ref = refs
    step, depth = pl.program_id(0), weight_ref.shape[0]

    @pl.when(step == 0)
    def _():
        for group, ref in enumerate(value_refs):
            values = ref[...].astype(f32)
            scale = lax.rsqrt(jnp.mean(values * values, -1, keepdims=True) + 1e-06)
            rows = pl.ds(group * GROUP_ROWS, GROUP_ROWS)
            scale_ref[rows, :] = jnp.broadcast_to(scale, (GROUP_ROWS, 128))
        total_ref[...] = jnp.zeros_like(total_ref)

    columns = pl.ds(pl.multiple_of(step * depth, depth), depth)
    for group, ref in enumerate(value_refs):
        rows = pl.ds(group * GROUP_ROWS, GROUP_ROWS)
        values = ref[:, columns].astype(f32) * scale_ref[rows, :1] * gain_ref[...]
        normed_ref[rows, :] = values.astype(bf)
    total_ref[...] += plain_product(normed_ref[...], weight_ref[...])

    @pl.when(step == pl.num_programs(0) - 1)
    def _():
        out_ref[...] = total_ref[...]


def normed_product(blocks, gain, weight, depth=512):
    rows, (features, columns) = len(blocks) * GROUP_ROWS, weight.shape
    return call(
        first_kernel,
        [gain, weight, *blocks],
        [
            pl.BlockSpec((1, depth), lambda step: (0, step)),
            pl.BlockSpec((depth, columns), lambda step: (step, 0)),
        ]
        + [whole(block) for block in blocks],
        [
            pl.BlockSpec((rows, depth), lambda step: (0, step)),
            pl.BlockSpec((rows, columns), lambda step: (0, 0)),
        ],
        [
            jax.ShapeDtypeStruct((rows, features), bf),
            jax.ShapeDtypeStruct((rows, columns), f32),
        ],
        (features // depth,),
        [pltpu.VMEM((rows, 128), f32), pltpu.VMEM((rows, columns), f32)],
    )


def product_blocks(left, right, transposed=False, block=512, micros=0):
    product = transposed_product if transposed else plain_product
    columns = right.shape[0] if transposed else right.shape[1]
    groups = left.shape[0] // GROUP_ROWS

    def kernel(left_ref, right_ref, *out_refs):
        total = product(left_ref[...], right_ref[...])
        for group, ref in enumerate(out_refs):
            ref[...] = total[group * GROUP_ROWS : (group + 1) * GROUP_ROWS].astype(ref.dtype)

    if transposed:
        right_spec = pl.BlockSpec((block, right.shape[1]), lambda step: (step, 0))
    else:
        right_spec = pl.BlockSpec((right.shape[0], block), lambda step: (0, step))
    return call(
        kernel,
        [left, right],
        [whole(left), right_spec],
        [pl.BlockSpec((GROUP_ROWS, block), lambda step: (0, step))] * groups,
        [
            jax.ShapeDtypeStruct((GROUP_ROWS, columns), bf if group else f32)
            for group in range(groups)
        ],
        (columns // block,),
        micros=micros,
    )


def grad_product(left, right, block=256, micros=0):
    rows, features = left.shape
    if features % block:
        block = 128

    def kernel(left_ref, right_ref, out_ref):
        out_ref[...] = rows_product(left_ref[...], right_ref[...]).astype(bf)

    return call(
        kernel,
        [left, right],
        [pl.BlockSpec((rows, block), lambda step: (0, step)), whole(right)],
        [pl.BlockSpec((block, right.shape[1]), lambda step: (step, 0))],
        [pltpu.HBM((features, right.shape[1]), bf)],
        (features // block,),
        micros=micros,
    )[0]


def from_own(part, values):
    groups = values.shape[0] // GROUP_ROWS

    def kernel(part_ref, values_ref, out_ref):
        for step in range(groups):
            source = lax.rem(part_ref[0] + groups - step, groups) * GROUP_ROWS
            rows = pl.ds(pl.multiple_of(source, GROUP_ROWS), GROUP_ROWS)
            out_ref[step * GROUP_ROWS : (step + 1) * GROUP_ROWS] = values_ref[rows]

    return call(
        kernel,
        [part.reshape(1).astype(jnp.int32), values],
        [pl.BlockSpec(memory_space=pltpu.SMEM), whole(values)],
        [whole(values)],
        [jax.ShapeDtypeStruct(values.shape, values.dtype)],
        (1,),
    )[0]


def tie_all(values, *others):
    anywhere = pl.BlockSpec(memory_space=pl.ANY)
    others = [
        pltpu.with_memory_space_constraint(other, pltpu.HBM) if other.size > 2**21 else other
        for other in others
    ]
    tied = pl.pallas_call(
        lambda *refs: None,
        in_specs=[anywhere] * (len(values) + len(others)),
        out_specs=[anywhere] * len(values),
        out_shape=[
            (pltpu.HBM if value.size > 2**21 else jax.ShapeDtypeStruct)(value.shape, value.dtype)
            for value in values
        ],
        input_output_aliases={i: i for i in range(len(values))},
        cost_estimate=NO_COST,
    )(*values, *others)
    return list(tied)


def tie(value, *others):
    return tie_all([value], *others)[0]


def assemble(part, values, received, others):
    parts = values.shape[0]

    def kernel(part_ref, values_ref, *refs):
        own = part_ref[0]
        out_ref = refs[-1]
        out_ref[own] = values_ref[own]
        for step in range(1, parts):
            out_ref[lax.rem(own + parts - step, parts)] = refs[step - 1][...]

    vmem = pl.BlockSpec(memory_space=pltpu.VMEM)
    anywhere = pl.BlockSpec(memory_space=pl.ANY)
    return pl.pallas_call(
        kernel,
        in_specs=[pl.BlockSpec(memory_space=pltpu.SMEM)]
        + [vmem] * parts
        + [anywhere] * len(others),
        out_specs=vmem,
        out_shape=jax.ShapeDtypeStruct(values.shape, values.dtype),
        compiler_params=pltpu.CompilerParams(vmem_limit_bytes=32 * 2**20),
        cost_estimate=NO_COST,
    )(part.reshape(1).astype(jnp.int32), values, *received, *others)


def copy_columns(count, *refs):
    target = refs[-1]
    start = 0
    for source in refs[:count]:
        block = source[...].reshape(source.shape[-2:])
        columns = pl.ds(start, block.shape[1])
        if len(target.shape) == 3:
            target[0, :, columns] = block.astype(target.dtype)
        else:
            target[:, columns] = block.astype(target.dtype)
        start += block.shape[1]


def to_parts(sources, parts, dtype, others=()):
    rows = sources[0][0].shape[0]

    def spec(section, width):
        return pl.BlockSpec((rows, width), lambda p: (0, section * parts + p))

    total = sum(width for _, _, width in sources)
    return pl.pallas_call(
        functools.partial(copy_columns, len(sources)),
        grid=(parts,),
        in_specs=[spec(section, width) for _, section, width in sources]
        + [pl.BlockSpec(memory_space=pl.ANY)] * len(others),
        out_specs=pl.BlockSpec((1, rows, total), lambda p: (p, 0, 0)),
        out_shape=jax.ShapeDtypeStruct((parts, rows, total), dtype),
        cost_estimate=NO_COST,
    )(*[array for array, _, _ in sources], *others)


def updown_from_parts(slabs):
    parts, rows, width = slabs.shape
    units = width // 2

    def kernel(slabs_ref, out_ref):
        for p in range(parts):
            out_ref[:, p * units : (p + 1) * units] = slabs_ref[p].astype(f32)

    return pl.pallas_call(
        kernel,
        grid=(2,),
        in_specs=[pl.BlockSpec((parts, rows, units), lambda half: (0, 0, half))],
        out_specs=pl.BlockSpec((rows, parts * units), lambda half: (0, half)),
        out_shape=jax.ShapeDtypeStruct((rows, parts * width), f32),
        compiler_params=pltpu.CompilerParams(vmem_limit_bytes=32 * 2**20),
        cost_estimate=NO_COST,
    )(slabs)


def mixer_from_parts(slabs, width):
    parts, rows, _ = slabs.shape

    def kernel(slabs_ref, qkv_ref, gate_ref, strength_ref):
        for p in range(parts):
            for section in range(4):
                block = slabs_ref[p, :, section * width : (section + 1) * width].astype(f32)
                if section < 3:
                    start = (section * parts + p) * width
                    qkv_ref[:, start : start + width] = block
                else:
                    gate_ref[:, p * width : (p + 1) * width] = block
            last = slabs_ref[p, :, 4 * width :].astype(f32)
            strength_ref[:, p * SMALL : (p + 1) * SMALL] = last

    widths = [3 * parts * width, parts * width, parts * SMALL]
    return pl.pallas_call(
        kernel,
        out_shape=[jax.ShapeDtypeStruct((rows, size), f32) for size in widths],
        compiler_params=pltpu.CompilerParams(vmem_limit_bytes=32 * 2**20),
        cost_estimate=NO_COST,
    )(slabs)


def total_of(own_ref, received_refs):
    total = own_ref[...]
    for ref in received_refs:
        total = total + ref[...].astype(f32)
    return total


def row_scale(values):
    return lax.rsqrt(jnp.mean(values * values, -1, keepdims=True) + 1e-06)


def norm_slope(values, scale, gain, grad):
    mean = jnp.mean(gain * grad * values, -1, keepdims=True)
    return scale * gain * grad - values * (scale * scale * scale * mean)


def hidden_kernel(own_ref, *refs):
    *received, input_ref, gain_ref, hidden_ref, normed_ref = refs
    hidden = input_ref[...].astype(f32) + total_of(own_ref, received)
    hidden_ref[...] = hidden
    normed_ref[...] = (hidden * row_scale(hidden) * gain_ref[...]).astype(bf)


def hidden_back_kernel(own_ref, *refs):
    *received, hidden_ref, gain_ref, cot_ref, d_hidden_ref, d_mixed_ref, d_gain_ref = refs
    grad = total_of(own_ref, received)
    hidden = hidden_ref[...]
    scale = row_scale(hidden)

    @pl.when(pl.program_id(0) == 0)
    def _():
        d_gain_ref[...] = jnp.zeros_like(d_gain_ref)

    d_gain_ref[...] += jnp.sum(grad * hidden * scale, 0, keepdims=True)
    d_hidden = cot_ref[...].astype(f32) + norm_slope(hidden, scale, gain_ref[...], grad)
    d_hidden_ref[...] = d_hidden
    d_mixed_ref[...] = d_hidden.astype(bf)


def input_back_kernel(own_ref, *refs):
    *received, input_ref, gain_ref, d_hidden_ref, out_ref = refs
    grad = total_of(own_ref, received)
    values = input_ref[...].astype(f32)
    slope = norm_slope(values, row_scale(values), gain_ref[...], grad)
    out_ref[...] = (d_hidden_ref[...] + slope).astype(bf)


def block_out_kernel(own_ref, *refs):
    *received, hidden_ref, out_ref = refs
    out_ref[...] = (hidden_ref[...] + total_of(own_ref, received)).astype(bf)


def by_rows(kernel, arrays, outs, block=64):
    def spec(shape):
        if shape[0] == 1:
            return pl.BlockSpec(shape, lambda i: (0, 0))
        return pl.BlockSpec((block, shape[1]), lambda i: (i, 0))

    return pl.pallas_call(
        kernel,
        grid=(GROUP_ROWS // block,),
        in_specs=[spec(array.shape) for array in arrays],
        out_specs=[spec(shape) for shape, _ in outs],
        out_shape=[jax.ShapeDtypeStruct(shape, dtype) for shape, dtype in outs],
        compiler_params=pltpu.CompilerParams(dimension_semantics=("arbitrary",)),
        cost_estimate=NO_COST,
    )(*arrays)


def body(
    block_in,
    out_grad,
    norm1_gain,
    conv_weight,
    head_gain,
    qkv_weight,
    beta_weight,
    gate_weight,
    out_weight,
    norm2_gain,
    updown_weight,
    down_weight,
    seq_blocks,
    lead_blocks,
):
    devices = lax.axis_size("dp")
    parts = MODEL
    copies = devices // parts
    part = lax.axis_index("dp") // copies
    copy = lax.axis_index("dp") % copies
    rows_own = qkv_weight.shape[0]
    width = D // parts
    units = FF // parts
    heads_part = HEADS // parts
    wide = 4 * width + SMALL
    model_groups = [[m * copies + t for m in range(parts)] for t in range(copies)]
    copy_groups = [[m * copies + t for t in range(copies)] for m in range(parts)]

    def exchange(values):
        return lax.all_to_all(
            values, "dp", split_axis=0, concat_axis=0, axis_index_groups=model_groups, tiled=True
        )

    def shift(values, step):
        pairs = [
            (m * copies + t, (m + step) % parts * copies + t)
            for m in range(parts)
            for t in range(copies)
        ]
        return lax.ppermute(values, "dp", pairs)

    def send_apart(values, *others):
        cut = [
            lax.dynamic_index_in_dim(values, (part + step) % parts, 0, keepdims=False)
            for step in range(1, parts)
        ]
        cut = tie_all(cut, *others)
        return cut, [shift(piece, step) for step, piece in enumerate(cut, 1)]

    def gather_rows(values):
        return [values] + [shift(values, step) for step in range(1, parts)]

    def scatter_rows(terms):
        return [terms[0]] + [shift(block, -step) for step, block in enumerate(terms[1:], 1)]

    def gather_copies(values):
        return lax.all_gather(values, "dp", axis=0, axis_index_groups=copy_groups, tiled=True)

    def scatter_copies(values):
        return lax.psum_scatter(
            values.astype(bf),
            "dp",
            scatter_dimension=0,
            axis_index_groups=copy_groups,
            tiled=True,
        )

    def halves_across(values, bit, axis):
        pairs = [(i, i ^ (1 << bit)) for i in range(devices)]
        side = (copy >> bit) & 1
        own = lax.dynamic_index_in_dim(values, side, axis, keepdims=False)
        other = lax.dynamic_index_in_dim(values, 1 - side, axis, keepdims=False)
        return own, lax.ppermute(other, "dp", pairs)

    def halve(values, bit, axis, *others):
        own, received = halves_across(values, bit, axis)
        if others:
            received = tie(received, *others)
        return (own.astype(f32) + received.astype(f32)).astype(bf)

    by_halves = copies == 8

    def halve_cores(values, *others):
        if not by_halves:
            return values
        rows, columns = values.shape
        return halve(values.reshape(2, 2, 2, rows // 8, columns), 0, 2, *others)

    def halve_first(values):
        if not by_halves:
            return [values]
        middle = values.shape[-1] // 2
        return [halve(values[..., :middle], 1, 1), halve(values[..., middle:], 2, 0)]

    def halve_second(values):
        if not by_halves:
            return scatter_copies(values[0])
        return jnp.concatenate([halve(values[0], 2, 0), halve(values[1], 1, 0)], 1)

    def to_wire(values):
        return values.reshape(-1, parts, copies, rows_own).swapaxes(1, 2).reshape(-1, D)

    def from_wire(values):
        return values.reshape(-1, copies, parts, rows_own).swapaxes(1, 2).reshape(-1, D)

    w_down_own = to_wire(down_weight.astype(bf))
    w_down = gather_copies(w_down_own)
    strengths = beta_weight.reshape(rows_own, parts, heads_part)
    strengths = jnp.pad(strengths, ((0, 0), (0, 0), (0, SMALL - heads_part)))
    strengths = tie(strengths.reshape(rows_own, parts * SMALL), w_down_own)
    pieces = [(qkv_weight, section, width) for section in range(3)]
    pieces = to_parts(pieces + [(gate_weight, 0, width), (strengths, 0, SMALL)], parts, bf)
    mixer_pieces = tie(exchange(pieces), w_down)
    w_mixer = gather_copies(mixer_pieces.reshape(parts * rows_own, wide))
    inputs = tie(to_wire(block_in), mixer_pieces)
    input_rows = gather_rows(inputs)

    lanes = -(-3 * rows_own // 128) * 128
    numbers = jnp.concatenate([seq_blocks[0], lead_blocks]).astype(f32)
    small = [conv_weight.T, norm1_gain[None], head_gain[None], norm2_gain[None], numbers[None]]
    small = [jnp.pad(rows, ((0, 0), (0, lanes - rows.shape[1]))) for rows in small]
    small = jnp.pad(jnp.concatenate(small, 0).astype(bf), ((0, 2 * KERNEL), (0, 0)))
    small = jnp.broadcast_to(small[None], (devices,) + small.shape)
    small = lax.all_to_all(tie(small, *input_rows[1:]), "dp", 0, 0, tiled=True)
    taps = small[:, :KERNEL, : 3 * rows_own].swapaxes(0, 1).reshape(KERNEL, 3, parts, width)
    taps = lax.dynamic_index_in_dim(taps, part, 2, keepdims=False).reshape(KERNEL, 3 * width)
    gain_one, head_full, gain_two = (
        small[:, KERNEL + i, :rows_own].reshape(1, D).astype(f32) for i in range(3)
    )
    gain_one, gain_two = to_wire(gain_one), to_wire(gain_two)
    head_part = lax.dynamic_slice_in_dim(head_full, part * width, width, 1)
    params = jnp.concatenate([taps.astype(f32), jnp.pad(head_part, ((0, 0), (0, 2 * width)))], 0)
    params = jnp.pad(params, ((0, KERNEL - 1), (0, 0)))
    numbers = small[:, KERNEL + 3, :3].astype(f32).astype(jnp.int32)
    layouts = block_layouts(numbers[:, 0], numbers[:, 1], numbers[:, 2])
    layouts = layouts.reshape(parts, copies, 4)
    layouts = lax.dynamic_index_in_dim(layouts, copy, 1, keepdims=False)
    wanted = (part - jnp.arange(parts)) % parts
    wanted = (wanted[:, None] == jnp.arange(parts)).astype(f32)
    layouts = jnp.sum(wanted[:, :, None] * layouts, 1)

    pieces = [(updown_weight, half, units) for half in range(2)]
    updown_pieces = to_parts(pieces, parts, bf, [mixer_pieces])
    w_out_own = to_wire(out_weight.astype(bf))
    w_out = gather_copies(tie(w_out_own, *input_rows[1:]))
    cotangent_own = to_wire(out_grad)

    gain_first = tie(gain_one, w_out_own, cotangent_own, updown_pieces)
    normed, pre = normed_product(input_rows, gain_first, w_mixer)
    _, received = send_apart(updown_pieces, *input_rows[1:])
    updown_pieces = assemble(part, updown_pieces, received, [pre])
    late = tie(params, updown_pieces)
    mixed, *kept = mixer_forward(layouts, pre, late, width)
    out_terms = product_blocks(mixed, w_out)
    w_updown = gather_copies(updown_pieces.reshape(parts * rows_own, 2 * units))
    stream = ((GROUP_ROWS, D), f32)
    narrow = ((GROUP_ROWS, D), bf)
    hidden, normed_two = by_rows(
        hidden_kernel,
        scatter_rows(out_terms) + [inputs, gain_two],
        [stream, narrow],
    )
    normed_two = jnp.concatenate(gather_rows(normed_two), 0)

    def swiglu_units(updown):
        return jax.nn.silu(updown[:, :units]) * updown[:, units:]

    updown = plain_product(normed_two, w_updown)
    cotangent = lax.all_gather(
        tie(cotangent_own, updown_pieces),
        "dp",
        axis=0,
        axis_index_groups=model_groups,
        tiled=True,
    )
    cotangent = from_own(part, tie(cotangent, updown))
    active, swiglu_back = jax.vjp(swiglu_units, updown)
    active = active.astype(bf)
    d_active = transposed_product(cotangent, w_down)
    d_updown = swiglu_back(d_active)[0].astype(bf)
    d_normed_two = product_blocks(d_updown, w_updown, transposed=True)
    active = tie(active, *d_normed_two[1:])
    down_terms = grad_product(active, cotangent)
    updown_terms = grad_product(normed_two, tie(d_updown, down_terms))
    gain_late = tie(gain_two, updown_terms)
    d_normed_two = scatter_rows(d_normed_two)
    updown_grad = scatter_copies(tie(updown_terms, gain_late, *d_normed_two[1:]))
    d_hidden, d_mixed, gain_two_grad = by_rows(
        hidden_back_kernel,
        d_normed_two + [hidden, gain_late, cotangent_own],
        [stream, narrow, ((1, D), f32)],
    )


    out_terms = product_blocks(tie(active, d_mixed), w_down)
    down_terms = tie(down_terms, *out_terms[1:])
    d_mixed = gather_rows(d_mixed)
    late = tie(params, *out_terms)
    out_terms[1:] = tie_all(out_terms[1:], *d_mixed[1:])
    d_pre, d_params = mixer_backward(layouts, pre, late, w_out, d_mixed, kept, width)
    mixer_terms = tie(grad_product(normed, d_pre, micros=20), updown_grad)
    mixer_grad = scatter_copies(mixer_terms)

    d_normed_terms = product_blocks(
        tie(d_pre, mixer_terms), w_mixer, transposed=True, micros=150
    )
    hidden = tie(hidden, d_normed_terms[0])
    (block_out,) = by_rows(block_out_kernel, scatter_rows(out_terms) + [hidden], [narrow])
    d_normed_terms[1:] = tie_all(d_normed_terms[1:], block_out)
    d_normed = scatter_rows(d_normed_terms)
    down_grad = halve_first(halve_cores(down_terms, *d_normed_terms[1:]))
    gain_one_grad = 0.0
    for values, terms in zip(input_rows, d_normed_terms):
        values = values.astype(f32)
        terms = terms.astype(f32) * (values * row_scale(values))
        gain_one_grad = gain_one_grad + jnp.sum(terms, 0, keepdims=True)

    here = (jnp.arange(parts) == part).astype(f32)[:, None]
    taps_grad = d_params[:KERNEL].reshape(KERNEL, 3, 1, width) * here
    taps_grad = taps_grad.reshape(KERNEL, parts, copies, 3, rows_own).transpose(1, 2, 3, 0, 4)
    taps_grad = taps_grad.reshape(devices, 3 * KERNEL, rows_own)
    head_grad = (d_params[KERNEL, :width] * here).reshape(devices, 1, rows_own)
    gain_grads = [
        grad.reshape(copies, parts, 1, rows_own).swapaxes(0, 1).reshape(devices, 1, rows_own)
        for grad in (gain_one_grad, gain_two_grad)
    ]
    small_grad = jnp.concatenate([taps_grad, head_grad] + gain_grads, 1)
    small_grad = jnp.pad(small_grad, ((0, 0), (0, 1), (0, 128 - rows_own)))
    small_grad = jnp.sum(lax.all_to_all(small_grad, "dp", 0, 0, tiled=True), 0)[:, :rows_own]
    taps_shard = small_grad[: 3 * KERNEL].reshape(3, KERNEL, rows_own).swapaxes(1, 2)
    taps_shard = taps_shard.reshape(3 * rows_own, KERNEL)
    head_shard, gain_one_shard, gain_two_shard = small_grad[3 * KERNEL : 3 * KERNEL + 3]

    out_grads = grad_product(tie(mixed, d_normed_terms[0]), jnp.concatenate(d_mixed, 0))
    late = tie(gain_one, out_grads)
    (input_grad,) = by_rows(input_back_kernel, d_normed + [inputs, late, d_hidden], [narrow])
    updown_grad = updown_grad.reshape(parts, rows_own, 2 * units)
    cut, received = send_apart(updown_grad, input_grad)
    updown_grad = assemble(part, updown_grad, received, [])
    mixer_grad = tie(mixer_grad, updown_grad)
    updown_shard = updown_from_parts(updown_grad)
    down_shard = from_wire(halve_second(tie_all(down_grad, mixer_grad)).astype(f32))
    out_grads = halve_second(halve_first(halve_cores(tie(out_grads, mixer_grad))))
    out_shard = from_wire(out_grads.astype(f32))
    mixer_grad = exchange(mixer_grad.reshape(parts, rows_own, wide))
    qkv_shard, gate_shard, strengths = mixer_from_parts(mixer_grad, width)
    beta_shard = strengths.reshape(rows_own, parts, SMALL)[:, :, :heads_part]
    return (
        from_wire(block_out),
        from_wire(input_grad),
        gain_one_shard,
        taps_shard,
        head_shard,
        qkv_shard,
        beta_shard.reshape(rows_own, HEADS),
        gate_shard,
        out_shard,
        gain_two_shard,
        updown_shard,
        down_shard,
    )


def solution(mesh):
    placed = (
        P("dp", None),
        P("dp", None),
        P("dp"),
        P("dp", None),
        P("dp"),
        P("dp", None),
        P("dp", None),
        P("dp", None),
        P("dp", None),
        P("dp"),
        P("dp", None),
        P("dp", None),
        P("dp", None),
        P("dp"),
    )
    return jax.shard_map(
        body,
        mesh=mesh,
        in_specs=placed,
        out_specs=(
            P("dp", None),
            P("dp", None),
            P("dp"),
            P("dp", None),
            P("dp"),
            P("dp", None),
            P("dp", None),
            P("dp", None),
            P("dp", None),
            P("dp"),
            P("dp", None),
            P("dp", None),
        ),
        check_vma=False,
    )
```

```python
import functools

import jax
import jax.numpy as jnp
from jax import lax
from jax.experimental import pallas as pl
from jax.experimental.pallas import tpu as pltpu
from jax.sharding import PartitionSpec as P

D = 2048
HEADS = 16
HEAD_DIM = 128
FF = 5632
KERNEL = 4
BLOCK_ROWS = 64
BLOCKS_DEV = 2
GROUP_ROWS = BLOCK_ROWS * BLOCKS_DEV
SMALL = 128
MODEL = 4

f32 = jnp.float32
bf = jnp.bfloat16


def block_layouts(first, second, lead):
    def doc(block):
        in_first = (block >= lead) & (block < lead + first)
        in_second = (block >= lead + first) & (block < lead + first + second)
        return jnp.where(in_first, 1, jnp.where(in_second, 2, 0))

    starts = (lead == 1) | (lead + first == 1) & (second > 0)
    columns = [doc(0) > 0, doc(1) > 0, doc(0) == doc(1), ~starts]
    return jnp.stack(columns, 1).astype(f32)


def plain_product(left, right):
    return jnp.dot(left, right, preferred_element_type=f32)


def rows_product(left, right):
    return lax.dot_general(left, right, (((0,), (0,)), ((), ())), preferred_element_type=f32)


def transposed_product(left, right):
    return lax.dot_general(left, right, (((1,), (1,)), ((), ())), preferred_element_type=f32)


def halves(values):
    high = values.astype(bf)
    return high, (values - high.astype(f32)).astype(bf)


def exact(left, right, left_dim, right_dim):
    left_high, left_low = left if isinstance(left, tuple) else halves(left)
    right_high, right_low = right if isinstance(right, tuple) else halves(right)
    return lax.dot_general(
        jnp.concatenate([left_high, left_high, left_low], left_dim),
        jnp.concatenate([right_high, right_low, right_high], right_dim),
        (((left_dim,), (right_dim,)), ((), ())),
        preferred_element_type=f32,
    )


def stacked(first, second):
    return tuple(jnp.concatenate([a, b], 0) for a, b in zip(first, second))


class Tile:
    def __init__(self, layout_ref, group):
        live_first, live_second, same, persist = (layout_ref[group, i] for i in range(4))
        shape = (GROUP_ROWS, HEAD_DIM)
        row = lax.broadcasted_iota(jnp.int32, shape, 0)
        col = lax.broadcasted_iota(jnp.int32, shape, 1)
        late = row >= BLOCK_ROWS
        self.row, self.col = row, col
        self.live = jnp.where(late, live_second, live_first)
        self.taps = [None] + [
            jnp.where(
                row < offset,
                0.0,
                jnp.where(late & (row < BLOCK_ROWS + offset), same, 1.0),
            )
            for offset in range(1, KERNEL)
        ]
        cross = jnp.where(late & (col < BLOCK_ROWS), persist, 1.0)
        self.lower = jnp.where(row > col, cross, 0.0)
        self.lower_full = jnp.where(row >= col, cross, 0.0)

    def earlier(self, values, offset):
        return pltpu.roll(values, offset, 0) * self.taps[offset]

    def later(self, values, offset):
        return pltpu.roll(values * self.taps[offset], GROUP_ROWS - offset, 0)


def convolve(tile, values, taps):
    total = values * taps[0]
    for offset in range(1, KERNEL):
        total = total + tile.earlier(values, offset) * taps[offset]
    return total


def unit_scale(values):
    return lax.rsqrt(jnp.sum(values * values, -1, keepdims=True) + 1e-06)


def head_columns(part_width, section, head):
    return pl.ds(section * part_width + head * HEAD_DIM, HEAD_DIM)


def unit_inverses(tile, lowers):
    eye = jnp.where(tile.row == tile.col, 1.0, 0.0)
    inverses = None
    size = 1
    while size < GROUP_ROWS:
        pair = tile.row // (2 * size) == tile.col // (2 * size)
        split = pair & (tile.row // size != tile.col // size)
        parts = [jnp.where(split, lower, 0.0) for lower in lowers]
        if inverses is None:
            inverses = [eye - part for part in parts]
        else:
            kept = [halves(inverse) for inverse in inverses]
            inner = [exact(part, known, 1, 0) for part, known in zip(parts, kept)]
            outer = [exact(known, value, 1, 0) for known, value in zip(kept, inner)]
            inverses = [inverse - value for inverse, value in zip(inverses, outer)]
        size *= 2
    return inverses


def mixer_forward_kernel(
    layout_ref, pre_ref, param_ref, mixed_ref, inverse_ref, score_ref, solved_ref, out_ref
):
    width = mixed_ref.shape[1]
    heads = range(width // HEAD_DIM)
    tile = Tile(layout_ref, pl.program_id(0))
    queries, keys, values, strengths = [], [], [], []
    for head in heads:
        parts = []
        for section in range(3):
            columns = head_columns(width, section, head)
            taps = [param_ref[offset : offset + 1, columns] for offset in range(KERNEL)]
            convolved = convolve(tile, pre_ref[:, columns], taps)
            parts.append(convolved * jax.nn.sigmoid(convolved))
        queries.append(parts[0] * (unit_scale(parts[0]) * HEAD_DIM**-0.5))
        keys.append(parts[1] * unit_scale(parts[1]))
        values.append(parts[2])
        start = 4 * width + head
        strengths.append(jax.nn.sigmoid(pre_ref[:, start : start + 1]) * tile.live)
    lowers, scores = [], []
    for head in heads:
        key_halves = halves(keys[head])
        both = exact(stacked(key_halves, halves(queries[head])), key_halves, 1, 1)
        lowers.append(both[:GROUP_ROWS] * strengths[head] * tile.lower)
        scores.append(both[GROUP_ROWS:] * tile.lower_full)
    inverses = unit_inverses(tile, lowers)
    solved = [exact(inverses[head], values[head] * strengths[head], 1, 0) for head in heads]
    outs = [exact(scores[head], solved[head], 1, 0) for head in heads]
    for head in heads:
        out = outs[head]
        scaled = out * lax.rsqrt(jnp.mean(out * out, -1, keepdims=True) + 1e-05)
        gate = pre_ref[:, head_columns(width, 3, head)]
        gain = param_ref[KERNEL : KERNEL + 1, head_columns(width, 0, head)]
        mixed = scaled * gain * (gate * jax.nn.sigmoid(gate)) * tile.live
        mixed_ref[:, head_columns(width, 0, head)] = mixed.astype(bf)
        inverse_ref[head] = inverses[head]
        score_ref[head] = scores[head]
        solved_ref[head] = solved[head]
        out_ref[head] = out


def mixer_backward_kernel(
    layout_ref,
    pre_ref,
    param_ref,
    weight_ref,
    inverse_ref,
    score_ref,
    solved_ref,
    out_ref,
    *refs,
):
    *mixed_refs, d_pre_ref, d_param_ref, grad_ref = refs
    width = grad_ref.shape[1]
    heads = range(width // HEAD_DIM)
    tile = Tile(layout_ref, pl.program_id(0))
    for group, mixed_ref in enumerate(mixed_refs):

        @pl.when(pl.program_id(0) == group)
        def _():
            grad_ref[...] = transposed_product(mixed_ref[...], weight_ref[...])

    @pl.when(pl.program_id(0) == 0)
    def _():
        d_param_ref[...] = jnp.zeros_like(d_param_ref)

    def along(values):
        return jnp.sum(values, -1, keepdims=True)

    d_outs = []
    for head in heads:
        columns = head_columns(width, 0, head)
        d_mixed = grad_ref[:, columns] * tile.live
        out = out_ref[head]
        scale = lax.rsqrt(jnp.mean(out * out, -1, keepdims=True) + 1e-05)
        scaled = out * scale
        gate = pre_ref[:, head_columns(width, 3, head)]
        gate_open = jax.nn.sigmoid(gate)
        gain = param_ref[KERNEL : KERNEL + 1, columns]
        gated = d_mixed * (gate * gate_open)
        d_param_ref[KERNEL : KERNEL + 1, columns] += jnp.sum(gated * scaled, 0, keepdims=True)
        d_gate = d_mixed * scaled * gain * (gate_open * (1.0 + gate * (1.0 - gate_open)))
        d_pre_ref[:, head_columns(width, 3, head)] = d_gate.astype(bf)
        d_scaled = gated * gain
        mean = jnp.mean(d_scaled * out, -1, keepdims=True)
        d_outs.append(scale * d_scaled - out * (scale * scale * scale * mean))
    d_out_halves = [halves(value) for value in d_outs]
    solved_halves = [halves(solved_ref[head]) for head in heads]
    d_solved = [exact(score_ref[head], d_out_halves[head], 0, 0) for head in heads]
    d_scores = [
        exact(d_out_halves[head], solved_halves[head], 1, 1) * tile.lower_full for head in heads
    ]
    d_inner = [exact(inverse_ref[head], d_solved[head], 0, 0) for head in heads]
    d_lowers = [exact(d_inner[head], solved_halves[head], 1, 1) * -tile.lower for head in heads]
    d_beta = jnp.zeros((GROUP_ROWS, SMALL), f32)
    for head in heads:
        pres, convolved, opened, active = [], [], [], []
        for section in range(3):
            columns = head_columns(width, section, head)
            taps = [param_ref[offset : offset + 1, columns] for offset in range(KERNEL)]
            pres.append(pre_ref[:, columns])
            convolved.append(convolve(tile, pres[section], taps))
            opened.append(jax.nn.sigmoid(convolved[section]))
            active.append(convolved[section] * opened[section])
        query_scale = unit_scale(active[0])
        key_scale = unit_scale(active[1])
        query_unit = active[0] * query_scale
        key = active[1] * key_scale
        start = 4 * width + head
        opening = jax.nn.sigmoid(pre_ref[:, start : start + 1])
        strength = opening * tile.live
        d_both = stacked(halves(d_lowers[head]), halves(d_scores[head]))
        by_key = exact(d_both, key, 1, 0)
        d_query = by_key[GROUP_ROWS:] * HEAD_DIM**-0.5
        from_lower = by_key[:GROUP_ROWS]
        weighted = stacked(halves(key * strength), halves(query_unit * HEAD_DIM**-0.5))
        d_key = strength * from_lower + exact(d_both, weighted, 0, 0)
        d_strength = along(d_inner[head] * active[2] + from_lower * key)
        d_value = d_inner[head] * strength
        d_opening = d_strength * (opening * (1.0 - opening)) * tile.live
        d_beta = d_beta + jnp.where(tile.col == head, d_opening, 0.0)
        d_active = [
            (d_query - query_unit * along(query_unit * d_query)) * query_scale,
            (d_key - key * along(key * d_key)) * key_scale,
            d_value,
        ]
        for section in range(3):
            columns = head_columns(width, section, head)
            taps = [param_ref[offset : offset + 1, columns] for offset in range(KERNEL)]
            slope = opened[section] * (1.0 + convolved[section] * (1.0 - opened[section]))
            d_convolved = d_active[section] * slope
            d_pre = d_convolved * taps[0]
            sums = [jnp.sum(d_convolved * pres[section], 0, keepdims=True)]
            for offset in range(1, KERNEL):
                d_pre = d_pre + tile.later(d_convolved, offset) * taps[offset]
                sums.append(
                    jnp.sum(d_convolved * tile.earlier(pres[section], offset), 0, keepdims=True)
                )
            d_param_ref[0:KERNEL, columns] += jnp.concatenate(sums, 0)
            d_pre_ref[:, columns] = d_pre.astype(bf)
    d_pre_ref[:, 4 * width :] = d_beta.astype(bf)


NO_COST = pl.CostEstimate(flops=0, bytes_accessed=0, transcendentals=0)


def call(kernel, operands, in_specs, out_specs, out_shape, grid=(), scratch=(), micros=0):
    results = pl.pallas_call(
        kernel,
        grid=grid,
        in_specs=in_specs,
        out_specs=out_specs,
        out_shape=out_shape,
        scratch_shapes=scratch,
        compiler_params=pltpu.CompilerParams(
            dimension_semantics=("arbitrary",) * len(grid), vmem_limit_bytes=48 * 2**20
        ),
        cost_estimate=pl.CostEstimate(
            flops=micros * 10**9, bytes_accessed=0, transcendentals=0
        ),
    )(*operands)
    return list(results)


def whole(array):
    return pl.BlockSpec(array.shape, lambda *step: (0,) * len(array.shape))


def mixer_specs(width):
    wide = 4 * width + SMALL
    heads = width // HEAD_DIM
    layout = pl.BlockSpec(memory_space=pltpu.SMEM)
    pre = pl.BlockSpec((GROUP_ROWS, wide), lambda group: (group, 0))
    param = pl.BlockSpec((2 * KERNEL, 3 * width), lambda group: (0, 0))
    narrow = pl.BlockSpec((GROUP_ROWS, width), lambda group: (group, 0))
    square = pl.BlockSpec((heads, GROUP_ROWS, HEAD_DIM), lambda group: (group, 0, 0))
    return layout, pre, param, narrow, square


def mixer_forward(layout, pre, params, width):
    groups = layout.shape[0]
    layout_spec, pre_spec, param_spec, narrow, square = mixer_specs(width)
    squares = pltpu.HBM((groups * width // HEAD_DIM, GROUP_ROWS, HEAD_DIM), f32)
    return call(
        mixer_forward_kernel,
        [layout, pre, params],
        [layout_spec, pre_spec, param_spec],
        [narrow] + [square] * 4,
        [jax.ShapeDtypeStruct((groups * GROUP_ROWS, width), bf)] + [squares] * 4,
        (groups,),
    )


def mixer_backward(layout, pre, params, weight, d_mixed, kept, width):
    groups = layout.shape[0]
    layout_spec, pre_spec, param_spec, _, square = mixer_specs(width)
    kept = [pltpu.with_memory_space_constraint(array, pltpu.HBM) for array in kept]
    return call(
        mixer_backward_kernel,
        [layout, pre, params, weight, *kept, *d_mixed],
        [layout_spec, pre_spec, param_spec, whole(weight)]
        + [square] * 4
        + [whole(block) for block in d_mixed],
        [pre_spec, param_spec],
        [jax.ShapeDtypeStruct(pre.shape, bf), jax.ShapeDtypeStruct(params.shape, f32)],
        (groups,),
        [pltpu.VMEM((GROUP_ROWS, width), f32)],
        micros=60,
    )


def first_kernel(gain_ref, weight_ref, *refs):
    *value_refs, normed_ref, out_ref, scale_ref, total_ref = refs
    step, depth = pl.program_id(0), weight_ref.shape[0]

    @pl.when(step == 0)
    def _():
        for group, ref in enumerate(value_refs):
            values = ref[...].astype(f32)
            scale = lax.rsqrt(jnp.mean(values * values, -1, keepdims=True) + 1e-06)
            rows = pl.ds(group * GROUP_ROWS, GROUP_ROWS)
            scale_ref[rows, :] = jnp.broadcast_to(scale, (GROUP_ROWS, 128))
        total_ref[...] = jnp.zeros_like(total_ref)

    columns = pl.ds(pl.multiple_of(step * depth, depth), depth)
    for group, ref in enumerate(value_refs):
        rows = pl.ds(group * GROUP_ROWS, GROUP_ROWS)
        values = ref[:, columns].astype(f32) * scale_ref[rows, :1] * gain_ref[...]
        normed_ref[rows, :] = values.astype(bf)
    total_ref[...] += plain_product(normed_ref[...], weight_ref[...])

    @pl.when(step == pl.num_programs(0) - 1)
    def _():
        out_ref[...] = total_ref[...]


def normed_product(blocks, gain, weight, depth=512):
    rows, (features, columns) = len(blocks) * GROUP_ROWS, weight.shape
    return call(
        first_kernel,
        [gain, weight, *blocks],
        [
            pl.BlockSpec((1, depth), lambda step: (0, step)),
            pl.BlockSpec((depth, columns), lambda step: (step, 0)),
        ]
        + [whole(block) for block in blocks],
        [
            pl.BlockSpec((rows, depth), lambda step: (0, step)),
            pl.BlockSpec((rows, columns), lambda step: (0, 0)),
        ],
        [
            jax.ShapeDtypeStruct((rows, features), bf),
            jax.ShapeDtypeStruct((rows, columns), f32),
        ],
        (features // depth,),
        [pltpu.VMEM((rows, 128), f32), pltpu.VMEM((rows, columns), f32)],
    )


def product_blocks(left, right, transposed=False, block=512, micros=0):
    product = transposed_product if transposed else plain_product
    columns = right.shape[0] if transposed else right.shape[1]
    groups = left.shape[0] // GROUP_ROWS

    def kernel(left_ref, right_ref, *out_refs):
        total = product(left_ref[...], right_ref[...])
        for group, ref in enumerate(out_refs):
            ref[...] = total[group * GROUP_ROWS : (group + 1) * GROUP_ROWS].astype(ref.dtype)

    if transposed:
        right_spec = pl.BlockSpec((block, right.shape[1]), lambda step: (step, 0))
    else:
        right_spec = pl.BlockSpec((right.shape[0], block), lambda step: (0, step))
    return call(
        kernel,
        [left, right],
        [whole(left), right_spec],
        [pl.BlockSpec((GROUP_ROWS, block), lambda step: (0, step))] * groups,
        [
            jax.ShapeDtypeStruct((GROUP_ROWS, columns), bf if group else f32)
            for group in range(groups)
        ],
        (columns // block,),
        micros=micros,
    )


def grad_product(left, right, block=256, micros=0):
    rows, features = left.shape
    if features % block:
        block = 128

    def kernel(left_ref, right_ref, out_ref):
        out_ref[...] = rows_product(left_ref[...], right_ref[...]).astype(bf)

    return call(
        kernel,
        [left, right],
        [pl.BlockSpec((rows, block), lambda step: (0, step)), whole(right)],
        [pl.BlockSpec((block, right.shape[1]), lambda step: (step, 0))],
        [pltpu.HBM((features, right.shape[1]), bf)],
        (features // block,),
        micros=micros,
    )[0]


def from_own(part, values):
    groups = values.shape[0] // GROUP_ROWS

    def kernel(part_ref, values_ref, out_ref):
        for step in range(groups):
            source = lax.rem(part_ref[0] + groups - step, groups) * GROUP_ROWS
            rows = pl.ds(pl.multiple_of(source, GROUP_ROWS), GROUP_ROWS)
            out_ref[step * GROUP_ROWS : (step + 1) * GROUP_ROWS] = values_ref[rows]

    return call(
        kernel,
        [part.reshape(1).astype(jnp.int32), values],
        [pl.BlockSpec(memory_space=pltpu.SMEM), whole(values)],
        [whole(values)],
        [jax.ShapeDtypeStruct(values.shape, values.dtype)],
        (1,),
    )[0]


def tie_all(values, *others):
    anywhere = pl.BlockSpec(memory_space=pl.ANY)
    others = [
        pltpu.with_memory_space_constraint(other, pltpu.HBM) if other.size > 2**21 else other
        for other in others
    ]
    tied = pl.pallas_call(
        lambda *refs: None,
        in_specs=[anywhere] * (len(values) + len(others)),
        out_specs=[anywhere] * len(values),
        out_shape=[
            (pltpu.HBM if value.size > 2**21 else jax.ShapeDtypeStruct)(value.shape, value.dtype)
            for value in values
        ],
        input_output_aliases={i: i for i in range(len(values))},
        cost_estimate=NO_COST,
    )(*values, *others)
    return list(tied)


def tie(value, *others):
    return tie_all([value], *others)[0]


def assemble(part, values, received, others):
    parts = values.shape[0]

    def kernel(part_ref, values_ref, *refs):
        own = part_ref[0]
        out_ref = refs[-1]
        out_ref[own] = values_ref[own]
        for step in range(1, parts):
            out_ref[lax.rem(own + parts - step, parts)] = refs[step - 1][...]

    vmem = pl.BlockSpec(memory_space=pltpu.VMEM)
    anywhere = pl.BlockSpec(memory_space=pl.ANY)
    return pl.pallas_call(
        kernel,
        in_specs=[pl.BlockSpec(memory_space=pltpu.SMEM)]
        + [vmem] * parts
        + [anywhere] * len(others),
        out_specs=vmem,
        out_shape=jax.ShapeDtypeStruct(values.shape, values.dtype),
        compiler_params=pltpu.CompilerParams(vmem_limit_bytes=32 * 2**20),
        cost_estimate=NO_COST,
    )(part.reshape(1).astype(jnp.int32), values, *received, *others)


def copy_columns(count, *refs):
    target = refs[-1]
    start = 0
    for source in refs[:count]:
        block = source[...].reshape(source.shape[-2:])
        columns = pl.ds(start, block.shape[1])
        if len(target.shape) == 3:
            target[0, :, columns] = block.astype(target.dtype)
        else:
            target[:, columns] = block.astype(target.dtype)
        start += block.shape[1]


def to_parts(sources, parts, dtype, others=()):
    rows = sources[0][0].shape[0]

    def spec(section, width):
        return pl.BlockSpec((rows, width), lambda p: (0, section * parts + p))

    total = sum(width for _, _, width in sources)
    return pl.pallas_call(
        functools.partial(copy_columns, len(sources)),
        grid=(parts,),
        in_specs=[spec(section, width) for _, section, width in sources]
        + [pl.BlockSpec(memory_space=pl.ANY)] * len(others),
        out_specs=pl.BlockSpec((1, rows, total), lambda p: (p, 0, 0)),
        out_shape=jax.ShapeDtypeStruct((parts, rows, total), dtype),
        cost_estimate=NO_COST,
    )(*[array for array, _, _ in sources], *others)


def updown_from_parts(slabs):
    parts, rows, width = slabs.shape
    units = width // 2

    def kernel(slabs_ref, out_ref):
        for p in range(parts):
            out_ref[:, p * units : (p + 1) * units] = slabs_ref[p].astype(f32)

    return pl.pallas_call(
        kernel,
        grid=(2,),
        in_specs=[pl.BlockSpec((parts, rows, units), lambda half: (0, 0, half))],
        out_specs=pl.BlockSpec((rows, parts * units), lambda half: (0, half)),
        out_shape=jax.ShapeDtypeStruct((rows, parts * width), f32),
        compiler_params=pltpu.CompilerParams(vmem_limit_bytes=32 * 2**20),
        cost_estimate=NO_COST,
    )(slabs)


def mixer_from_parts(slabs, width):
    parts, rows, _ = slabs.shape

    def kernel(slabs_ref, qkv_ref, gate_ref, strength_ref):
        for p in range(parts):
            for section in range(4):
                block = slabs_ref[p, :, section * width : (section + 1) * width].astype(f32)
                if section < 3:
                    start = (section * parts + p) * width
                    qkv_ref[:, start : start + width] = block
                else:
                    gate_ref[:, p * width : (p + 1) * width] = block
            last = slabs_ref[p, :, 4 * width :].astype(f32)
            strength_ref[:, p * SMALL : (p + 1) * SMALL] = last

    widths = [3 * parts * width, parts * width, parts * SMALL]
    return pl.pallas_call(
        kernel,
        out_shape=[jax.ShapeDtypeStruct((rows, size), f32) for size in widths],
        compiler_params=pltpu.CompilerParams(vmem_limit_bytes=32 * 2**20),
        cost_estimate=NO_COST,
    )(slabs)


def total_of(own_ref, received_refs):
    total = own_ref[...]
    for ref in received_refs:
        total = total + ref[...].astype(f32)
    return total


def row_scale(values):
    return lax.rsqrt(jnp.mean(values * values, -1, keepdims=True) + 1e-06)


def norm_slope(values, scale, gain, grad):
    mean = jnp.mean(gain * grad * values, -1, keepdims=True)
    return scale * gain * grad - values * (scale * scale * scale * mean)


def hidden_kernel(own_ref, *refs):
    *received, input_ref, gain_ref, hidden_ref, normed_ref = refs
    hidden = input_ref[...].astype(f32) + total_of(own_ref, received)
    hidden_ref[...] = hidden
    normed_ref[...] = (hidden * row_scale(hidden) * gain_ref[...]).astype(bf)


def hidden_back_kernel(own_ref, *refs):
    *received, hidden_ref, gain_ref, cot_ref, d_hidden_ref, d_mixed_ref, d_gain_ref = refs
    grad = total_of(own_ref, received)
    hidden = hidden_ref[...]
    scale = row_scale(hidden)

    @pl.when(pl.program_id(0) == 0)
    def _():
        d_gain_ref[...] = jnp.zeros_like(d_gain_ref)

    d_gain_ref[...] += jnp.sum(grad * hidden * scale, 0, keepdims=True)
    d_hidden = cot_ref[...].astype(f32) + norm_slope(hidden, scale, gain_ref[...], grad)
    d_hidden_ref[...] = d_hidden
    d_mixed_ref[...] = d_hidden.astype(bf)


def input_back_kernel(own_ref, *refs):
    *received, input_ref, gain_ref, d_hidden_ref, out_ref = refs
    grad = total_of(own_ref, received)
    values = input_ref[...].astype(f32)
    slope = norm_slope(values, row_scale(values), gain_ref[...], grad)
    out_ref[...] = (d_hidden_ref[...] + slope).astype(bf)


def block_out_kernel(own_ref, *refs):
    *received, hidden_ref, out_ref = refs
    out_ref[...] = (hidden_ref[...] + total_of(own_ref, received)).astype(bf)


def by_rows(kernel, arrays, outs, block=64):
    def spec(shape):
        if shape[0] == 1:
            return pl.BlockSpec(shape, lambda i: (0, 0))
        return pl.BlockSpec((block, shape[1]), lambda i: (i, 0))

    return pl.pallas_call(
        kernel,
        grid=(GROUP_ROWS // block,),
        in_specs=[spec(array.shape) for array in arrays],
        out_specs=[spec(shape) for shape, _ in outs],
        out_shape=[jax.ShapeDtypeStruct(shape, dtype) for shape, dtype in outs],
        compiler_params=pltpu.CompilerParams(dimension_semantics=("arbitrary",)),
        cost_estimate=NO_COST,
    )(*arrays)


def body(
    block_in,
    out_grad,
    norm1_gain,
    conv_weight,
    head_gain,
    qkv_weight,
    beta_weight,
    gate_weight,
    out_weight,
    norm2_gain,
    updown_weight,
    down_weight,
    seq_blocks,
    lead_blocks,
):
    devices = lax.axis_size("dp")
    parts = MODEL
    copies = devices // parts
    part = lax.axis_index("dp") // copies
    copy = lax.axis_index("dp") % copies
    rows_own = qkv_weight.shape[0]
    width = D // parts
    units = FF // parts
    heads_part = HEADS // parts
    wide = 4 * width + SMALL
    model_groups = [[m * copies + t for m in range(parts)] for t in range(copies)]
    copy_groups = [[m * copies + t for t in range(copies)] for m in range(parts)]

    def exchange(values):
        return lax.all_to_all(
            values, "dp", split_axis=0, concat_axis=0, axis_index_groups=model_groups, tiled=True
        )

    def shift(values, step):
        pairs = [
            (m * copies + t, (m + step) % parts * copies + t)
            for m in range(parts)
            for t in range(copies)
        ]
        return lax.ppermute(values, "dp", pairs)

    def exchange_apart(values, before, after=()):
        cut = [
            lax.dynamic_index_in_dim(values, (part + step) % parts, 0, keepdims=False)
            for step in range(1, parts)
        ]
        received = [shift(piece, step) for step, piece in enumerate(tie_all(cut, *before), 1)]
        return assemble(part, values, received, after)

    def gather_rows(values):
        return [values] + [shift(values, step) for step in range(1, parts)]

    def scatter_rows(terms):
        return [terms[0]] + [shift(block, -step) for step, block in enumerate(terms[1:], 1)]

    def gather_copies(values):
        return lax.all_gather(values, "dp", axis=0, axis_index_groups=copy_groups, tiled=True)

    def scatter_copies(values):
        return lax.psum_scatter(
            values.astype(bf),
            "dp",
            scatter_dimension=0,
            axis_index_groups=copy_groups,
            tiled=True,
        )

    def halves_across(values, bit, axis):
        pairs = [(i, i ^ (1 << bit)) for i in range(devices)]
        side = (copy >> bit) & 1
        own = lax.dynamic_index_in_dim(values, side, axis, keepdims=False)
        other = lax.dynamic_index_in_dim(values, 1 - side, axis, keepdims=False)
        return own, lax.ppermute(other, "dp", pairs)

    def halve(values, bit, axis, *others):
        own, received = halves_across(values, bit, axis)
        if others:
            received = tie(received, *others)
        return (own.astype(f32) + received.astype(f32)).astype(bf)

    by_halves = copies == 8

    def halve_cores(values, *others):
        if not by_halves:
            return values
        rows, columns = values.shape
        return halve(values.reshape(2, 2, 2, rows // 8, columns), 0, 2, *others)

    def halve_first(values):
        if not by_halves:
            return [values]
        middle = values.shape[-1] // 2
        return [halve(values[..., :middle], 1, 1), halve(values[..., middle:], 2, 0)]

    def halve_second(values):
        if not by_halves:
            return scatter_copies(values[0])
        return jnp.concatenate([halve(values[0], 2, 0), halve(values[1], 1, 0)], 1)

    def to_wire(values):
        return values.reshape(-1, parts, copies, rows_own).swapaxes(1, 2).reshape(-1, D)

    def from_wire(values):
        return values.reshape(-1, copies, parts, rows_own).swapaxes(1, 2).reshape(-1, D)

    w_out_own = to_wire(out_weight.astype(bf))
    w_out = gather_copies(w_out_own)
    strengths = beta_weight.reshape(rows_own, parts, heads_part)
    strengths = jnp.pad(strengths, ((0, 0), (0, 0), (0, SMALL - heads_part)))
    strengths = tie(strengths.reshape(rows_own, parts * SMALL), w_out_own)
    pieces = [(qkv_weight, section, width) for section in range(3)]
    pieces = to_parts(pieces + [(gate_weight, 0, width), (strengths, 0, SMALL)], parts, bf)
    mixer_pieces = tie(exchange(pieces), w_out)
    w_mixer = gather_copies(mixer_pieces.reshape(parts * rows_own, wide))
    inputs = tie(to_wire(block_in), mixer_pieces)
    input_rows = gather_rows(inputs)

    lanes = -(-3 * rows_own // 128) * 128
    numbers = jnp.concatenate([seq_blocks[0], lead_blocks]).astype(f32)
    small = [conv_weight.T, norm1_gain[None], head_gain[None], norm2_gain[None], numbers[None]]
    small = [jnp.pad(rows, ((0, 0), (0, lanes - rows.shape[1]))) for rows in small]
    small = jnp.pad(jnp.concatenate(small, 0).astype(bf), ((0, 2 * KERNEL), (0, 0)))
    small = jnp.broadcast_to(small[None], (devices,) + small.shape)
    small = lax.all_to_all(tie(small, *input_rows[1:]), "dp", 0, 0, tiled=True)
    taps = small[:, :KERNEL, : 3 * rows_own].swapaxes(0, 1).reshape(KERNEL, 3, parts, width)
    taps = lax.dynamic_index_in_dim(taps, part, 2, keepdims=False).reshape(KERNEL, 3 * width)
    gain_one, head_full, gain_two = (
        small[:, KERNEL + i, :rows_own].reshape(1, D).astype(f32) for i in range(3)
    )
    gain_one, gain_two = to_wire(gain_one), to_wire(gain_two)
    head_part = lax.dynamic_slice_in_dim(head_full, part * width, width, 1)
    params = jnp.concatenate([taps.astype(f32), jnp.pad(head_part, ((0, 0), (0, 2 * width)))], 0)
    params = jnp.pad(params, ((0, KERNEL - 1), (0, 0)))
    numbers = small[:, KERNEL + 3, :3].astype(f32).astype(jnp.int32)
    layouts = block_layouts(numbers[:, 0], numbers[:, 1], numbers[:, 2])
    layouts = layouts.reshape(parts, copies, 4)
    layouts = lax.dynamic_index_in_dim(layouts, copy, 1, keepdims=False)
    wanted = (part - jnp.arange(parts)) % parts
    wanted = (wanted[:, None] == jnp.arange(parts)).astype(f32)
    layouts = jnp.sum(wanted[:, :, None] * layouts, 1)

    pieces = [(updown_weight, half, units) for half in range(2)]
    updown_pieces = to_parts(pieces, parts, bf, [mixer_pieces])
    w_down_own = to_wire(down_weight.astype(bf))
    w_down = gather_copies(tie(w_down_own, *input_rows[1:]))
    cotangent_own = to_wire(out_grad)

    cotangent = lax.all_gather(
        tie(cotangent_own, *input_rows[1:]), "dp", axis=0, axis_index_groups=model_groups, tiled=True
    )
    gain_first = tie(gain_one, w_down_own, cotangent_own, updown_pieces)
    normed, pre = normed_product(input_rows, gain_first, w_mixer)
    mixed, *kept = mixer_forward(layouts, pre, params, width)
    out_terms = product_blocks(mixed, w_out)
    updown_pieces = exchange_apart(updown_pieces, input_rows[1:], out_terms[1:])
    w_updown = gather_copies(updown_pieces.reshape(parts * rows_own, 2 * units))
    stream = ((GROUP_ROWS, D), f32)
    narrow = ((GROUP_ROWS, D), bf)
    hidden, normed_two = by_rows(
        hidden_kernel,
        scatter_rows(out_terms) + [inputs, gain_two],
        [stream, narrow],
    )
    cotangent = from_own(part, cotangent)
    normed_two = jnp.concatenate(gather_rows(normed_two), 0)

    def swiglu_units(updown):
        return jax.nn.silu(updown[:, :units]) * updown[:, units:]

    updown = plain_product(normed_two, w_updown)
    active, swiglu_back = jax.vjp(swiglu_units, updown)
    active = active.astype(bf)
    d_active = transposed_product(cotangent, w_down)
    d_updown = swiglu_back(d_active)[0].astype(bf)
    d_normed_two = product_blocks(d_updown, w_updown, transposed=True)
    active = tie(active, *d_normed_two[1:])
    down_terms = grad_product(active, cotangent)
    updown_terms = grad_product(normed_two, tie(d_updown, down_terms))
    gain_late = tie(gain_two, updown_terms)
    d_normed_two = scatter_rows(d_normed_two)
    updown_grad = scatter_copies(tie(updown_terms, gain_late, *d_normed_two[1:]))
    d_hidden, d_mixed, gain_two_grad = by_rows(
        hidden_back_kernel,
        d_normed_two + [hidden, gain_late, cotangent_own],
        [stream, narrow, ((1, D), f32)],
    )


    out_terms = product_blocks(tie(active, d_mixed), w_down)
    down_terms = tie(down_terms, *out_terms[1:])
    d_mixed = gather_rows(d_mixed)
    late = tie(params, *out_terms)
    out_terms[1:] = tie_all(out_terms[1:], *d_mixed[1:])
    d_pre, d_params = mixer_backward(layouts, pre, late, w_out, d_mixed, kept, width)
    mixer_terms = tie(grad_product(normed, d_pre, micros=20), updown_grad)
    mixer_grad = scatter_copies(mixer_terms)

    d_normed_terms = product_blocks(
        tie(d_pre, mixer_terms), w_mixer, transposed=True, micros=150
    )
    hidden = tie(hidden, d_normed_terms[0])
    (block_out,) = by_rows(block_out_kernel, scatter_rows(out_terms) + [hidden], [narrow])
    d_normed_terms[1:] = tie_all(d_normed_terms[1:], block_out)
    d_normed = scatter_rows(d_normed_terms)
    down_grad = halve_first(halve_cores(down_terms, *d_normed_terms[1:]))
    gain_one_grad = 0.0
    for values, terms in zip(input_rows, d_normed_terms):
        values = values.astype(f32)
        terms = terms.astype(f32) * (values * row_scale(values))
        gain_one_grad = gain_one_grad + jnp.sum(terms, 0, keepdims=True)

    here = (jnp.arange(parts) == part).astype(f32)[:, None]
    taps_grad = d_params[:KERNEL].reshape(KERNEL, 3, 1, width) * here
    taps_grad = taps_grad.reshape(KERNEL, parts, copies, 3, rows_own).transpose(1, 2, 3, 0, 4)
    taps_grad = taps_grad.reshape(devices, 3 * KERNEL, rows_own)
    head_grad = (d_params[KERNEL, :width] * here).reshape(devices, 1, rows_own)
    gain_grads = [
        grad.reshape(copies, parts, 1, rows_own).swapaxes(0, 1).reshape(devices, 1, rows_own)
        for grad in (gain_one_grad, gain_two_grad)
    ]
    small_grad = jnp.concatenate([taps_grad, head_grad] + gain_grads, 1)
    small_grad = jnp.pad(small_grad, ((0, 0), (0, 1), (0, 128 - rows_own)))
    small_grad = jnp.sum(lax.all_to_all(small_grad, "dp", 0, 0, tiled=True), 0)[:, :rows_own]
    taps_shard = small_grad[: 3 * KERNEL].reshape(3, KERNEL, rows_own).swapaxes(1, 2)
    taps_shard = taps_shard.reshape(3 * rows_own, KERNEL)
    head_shard, gain_one_shard, gain_two_shard = small_grad[3 * KERNEL : 3 * KERNEL + 3]

    out_grads = grad_product(tie(mixed, d_normed_terms[0]), jnp.concatenate(d_mixed, 0))
    late = tie(gain_one, out_grads)
    (input_grad,) = by_rows(input_back_kernel, d_normed + [inputs, late, d_hidden], [narrow])
    updown_grad = tie(updown_grad, mixer_terms).reshape(parts, rows_own, 2 * units)
    updown_grad = exchange(updown_grad)
    mixer_grad = tie(mixer_grad, updown_grad, input_grad)
    updown_shard = updown_from_parts(updown_grad)
    down_shard = from_wire(halve_second(tie_all(down_grad, input_grad)).astype(f32))
    out_grads = tie(halve_cores(tie(out_grads, input_grad)), mixer_grad)
    out_shard = from_wire(halve_second(halve_first(out_grads)).astype(f32))
    mixer_grad = exchange(mixer_grad.reshape(parts, rows_own, wide))
    qkv_shard, gate_shard, strengths = mixer_from_parts(mixer_grad, width)
    beta_shard = strengths.reshape(rows_own, parts, SMALL)[:, :, :heads_part]
    return (
        from_wire(block_out),
        from_wire(input_grad),
        gain_one_shard,
        taps_shard,
        head_shard,
        qkv_shard,
        beta_shard.reshape(rows_own, HEADS),
        gate_shard,
        out_shard,
        gain_two_shard,
        updown_shard,
        down_shard,
    )


def solution(mesh):
    placed = (
        P("dp", None),
        P("dp", None),
        P("dp"),
        P("dp", None),
        P("dp"),
        P("dp", None),
        P("dp", None),
        P("dp", None),
        P("dp", None),
        P("dp"),
        P("dp", None),
        P("dp", None),
        P("dp", None),
        P("dp"),
    )
    return jax.shard_map(
        body,
        mesh=mesh,
        in_specs=placed,
        out_specs=(
            P("dp", None),
            P("dp", None),
            P("dp"),
            P("dp", None),
            P("dp"),
            P("dp", None),
            P("dp", None),
            P("dp", None),
            P("dp", None),
            P("dp"),
            P("dp", None),
            P("dp", None),
        ),
        check_vma=False,
    )
```

```python
import functools

import jax
import jax.numpy as jnp
from jax import lax
from jax.experimental import pallas as pl
from jax.experimental.pallas import tpu as pltpu
from jax.sharding import PartitionSpec as P

D = 2048
HEADS = 16
HEAD_DIM = 128
FF = 5632
KERNEL = 4
BLOCK_ROWS = 64
BLOCKS_DEV = 2
GROUP_ROWS = BLOCK_ROWS * BLOCKS_DEV
SMALL = 128
MODEL = 4

f32 = jnp.float32
bf = jnp.bfloat16


def block_layouts(first, second, lead):
    def doc(block):
        in_first = (block >= lead) & (block < lead + first)
        in_second = (block >= lead + first) & (block < lead + first + second)
        return jnp.where(in_first, 1, jnp.where(in_second, 2, 0))

    starts = (lead == 1) | (lead + first == 1) & (second > 0)
    columns = [doc(0) > 0, doc(1) > 0, doc(0) == doc(1), ~starts]
    return jnp.stack(columns, 1).astype(f32)


def plain_product(left, right):
    return jnp.dot(left, right, preferred_element_type=f32)


def rows_product(left, right):
    return lax.dot_general(left, right, (((0,), (0,)), ((), ())), preferred_element_type=f32)


def transposed_product(left, right):
    return lax.dot_general(left, right, (((1,), (1,)), ((), ())), preferred_element_type=f32)


def halves(values):
    high = values.astype(bf)
    return high, (values - high.astype(f32)).astype(bf)


def exact(left, right, left_dim, right_dim):
    left_high, left_low = left if isinstance(left, tuple) else halves(left)
    right_high, right_low = right if isinstance(right, tuple) else halves(right)
    return lax.dot_general(
        jnp.concatenate([left_high, left_high, left_low], left_dim),
        jnp.concatenate([right_high, right_low, right_high], right_dim),
        (((left_dim,), (right_dim,)), ((), ())),
        preferred_element_type=f32,
    )


def stacked(first, second):
    return tuple(jnp.concatenate([a, b], 0) for a, b in zip(first, second))


class Tile:
    def __init__(self, layout_ref, group):
        live_first, live_second, same, persist = (layout_ref[group, i] for i in range(4))
        shape = (GROUP_ROWS, HEAD_DIM)
        row = lax.broadcasted_iota(jnp.int32, shape, 0)
        col = lax.broadcasted_iota(jnp.int32, shape, 1)
        late = row >= BLOCK_ROWS
        self.row, self.col = row, col
        self.live = jnp.where(late, live_second, live_first)
        self.taps = [None] + [
            jnp.where(
                row < offset,
                0.0,
                jnp.where(late & (row < BLOCK_ROWS + offset), same, 1.0),
            )
            for offset in range(1, KERNEL)
        ]
        cross = jnp.where(late & (col < BLOCK_ROWS), persist, 1.0)
        self.lower = jnp.where(row > col, cross, 0.0)
        self.lower_full = jnp.where(row >= col, cross, 0.0)

    def earlier(self, values, offset):
        return pltpu.roll(values, offset, 0) * self.taps[offset]

    def later(self, values, offset):
        return pltpu.roll(values * self.taps[offset], GROUP_ROWS - offset, 0)


def convolve(tile, values, taps):
    total = values * taps[0]
    for offset in range(1, KERNEL):
        total = total + tile.earlier(values, offset) * taps[offset]
    return total


def unit_scale(values):
    return lax.rsqrt(jnp.sum(values * values, -1, keepdims=True) + 1e-06)


def head_columns(part_width, section, head):
    return pl.ds(section * part_width + head * HEAD_DIM, HEAD_DIM)


def unit_inverses(tile, lowers):
    eye = jnp.where(tile.row == tile.col, 1.0, 0.0)
    inverses = None
    size = 1
    while size < GROUP_ROWS:
        pair = tile.row // (2 * size) == tile.col // (2 * size)
        split = pair & (tile.row // size != tile.col // size)
        parts = [jnp.where(split, lower, 0.0) for lower in lowers]
        if inverses is None:
            inverses = [eye - part for part in parts]
        else:
            kept = [halves(inverse) for inverse in inverses]
            inner = [exact(part, known, 1, 0) for part, known in zip(parts, kept)]
            outer = [exact(known, value, 1, 0) for known, value in zip(kept, inner)]
            inverses = [inverse - value for inverse, value in zip(inverses, outer)]
        size *= 2
    return inverses


def mixer_forward_kernel(
    layout_ref, pre_ref, param_ref, mixed_ref, inverse_ref, score_ref, solved_ref, out_ref
):
    width = mixed_ref.shape[1]
    heads = range(width // HEAD_DIM)
    tile = Tile(layout_ref, pl.program_id(0))
    queries, keys, values, strengths = [], [], [], []
    for head in heads:
        parts = []
        for section in range(3):
            columns = head_columns(width, section, head)
            taps = [param_ref[offset : offset + 1, columns] for offset in range(KERNEL)]
            convolved = convolve(tile, pre_ref[:, columns], taps)
            parts.append(convolved * jax.nn.sigmoid(convolved))
        queries.append(parts[0] * (unit_scale(parts[0]) * HEAD_DIM**-0.5))
        keys.append(parts[1] * unit_scale(parts[1]))
        values.append(parts[2])
        start = 4 * width + head
        strengths.append(jax.nn.sigmoid(pre_ref[:, start : start + 1]) * tile.live)
    lowers, scores = [], []
    for head in heads:
        key_halves = halves(keys[head])
        both = exact(stacked(key_halves, halves(queries[head])), key_halves, 1, 1)
        lowers.append(both[:GROUP_ROWS] * strengths[head] * tile.lower)
        scores.append(both[GROUP_ROWS:] * tile.lower_full)
    inverses = unit_inverses(tile, lowers)
    solved = [exact(inverses[head], values[head] * strengths[head], 1, 0) for head in heads]
    outs = [exact(scores[head], solved[head], 1, 0) for head in heads]
    for head in heads:
        out = outs[head]
        scaled = out * lax.rsqrt(jnp.mean(out * out, -1, keepdims=True) + 1e-05)
        gate = pre_ref[:, head_columns(width, 3, head)]
        gain = param_ref[KERNEL : KERNEL + 1, head_columns(width, 0, head)]
        mixed = scaled * gain * (gate * jax.nn.sigmoid(gate)) * tile.live
        mixed_ref[:, head_columns(width, 0, head)] = mixed.astype(bf)
        inverse_ref[head] = inverses[head]
        score_ref[head] = scores[head]
        solved_ref[head] = solved[head]
        out_ref[head] = out


def mixer_backward_kernel(
    layout_ref,
    pre_ref,
    param_ref,
    weight_ref,
    inverse_ref,
    score_ref,
    solved_ref,
    out_ref,
    *refs,
):
    *mixed_refs, d_pre_ref, d_param_ref, grad_ref = refs
    width = grad_ref.shape[1]
    heads = range(width // HEAD_DIM)
    tile = Tile(layout_ref, pl.program_id(0))
    for group, mixed_ref in enumerate(mixed_refs):

        @pl.when(pl.program_id(0) == group)
        def _():
            grad_ref[...] = transposed_product(mixed_ref[...], weight_ref[...])

    @pl.when(pl.program_id(0) == 0)
    def _():
        d_param_ref[...] = jnp.zeros_like(d_param_ref)

    def along(values):
        return jnp.sum(values, -1, keepdims=True)

    d_outs = []
    for head in heads:
        columns = head_columns(width, 0, head)
        d_mixed = grad_ref[:, columns] * tile.live
        out = out_ref[head]
        scale = lax.rsqrt(jnp.mean(out * out, -1, keepdims=True) + 1e-05)
        scaled = out * scale
        gate = pre_ref[:, head_columns(width, 3, head)]
        gate_open = jax.nn.sigmoid(gate)
        gain = param_ref[KERNEL : KERNEL + 1, columns]
        gated = d_mixed * (gate * gate_open)
        d_param_ref[KERNEL : KERNEL + 1, columns] += jnp.sum(gated * scaled, 0, keepdims=True)
        d_gate = d_mixed * scaled * gain * (gate_open * (1.0 + gate * (1.0 - gate_open)))
        d_pre_ref[:, head_columns(width, 3, head)] = d_gate.astype(bf)
        d_scaled = gated * gain
        mean = jnp.mean(d_scaled * out, -1, keepdims=True)
        d_outs.append(scale * d_scaled - out * (scale * scale * scale * mean))
    d_out_halves = [halves(value) for value in d_outs]
    solved_halves = [halves(solved_ref[head]) for head in heads]
    d_solved = [exact(score_ref[head], d_out_halves[head], 0, 0) for head in heads]
    d_scores = [
        exact(d_out_halves[head], solved_halves[head], 1, 1) * tile.lower_full for head in heads
    ]
    d_inner = [exact(inverse_ref[head], d_solved[head], 0, 0) for head in heads]
    d_lowers = [exact(d_inner[head], solved_halves[head], 1, 1) * -tile.lower for head in heads]
    d_beta = jnp.zeros((GROUP_ROWS, SMALL), f32)
    for head in heads:
        pres, convolved, opened, active = [], [], [], []
        for section in range(3):
            columns = head_columns(width, section, head)
            taps = [param_ref[offset : offset + 1, columns] for offset in range(KERNEL)]
            pres.append(pre_ref[:, columns])
            convolved.append(convolve(tile, pres[section], taps))
            opened.append(jax.nn.sigmoid(convolved[section]))
            active.append(convolved[section] * opened[section])
        query_scale = unit_scale(active[0])
        key_scale = unit_scale(active[1])
        query_unit = active[0] * query_scale
        key = active[1] * key_scale
        start = 4 * width + head
        opening = jax.nn.sigmoid(pre_ref[:, start : start + 1])
        strength = opening * tile.live
        d_both = stacked(halves(d_lowers[head]), halves(d_scores[head]))
        by_key = exact(d_both, key, 1, 0)
        d_query = by_key[GROUP_ROWS:] * HEAD_DIM**-0.5
        from_lower = by_key[:GROUP_ROWS]
        weighted = stacked(halves(key * strength), halves(query_unit * HEAD_DIM**-0.5))
        d_key = strength * from_lower + exact(d_both, weighted, 0, 0)
        d_strength = along(d_inner[head] * active[2] + from_lower * key)
        d_value = d_inner[head] * strength
        d_opening = d_strength * (opening * (1.0 - opening)) * tile.live
        d_beta = d_beta + jnp.where(tile.col == head, d_opening, 0.0)
        d_active = [
            (d_query - query_unit * along(query_unit * d_query)) * query_scale,
            (d_key - key * along(key * d_key)) * key_scale,
            d_value,
        ]
        for section in range(3):
            columns = head_columns(width, section, head)
            taps = [param_ref[offset : offset + 1, columns] for offset in range(KERNEL)]
            slope = opened[section] * (1.0 + convolved[section] * (1.0 - opened[section]))
            d_convolved = d_active[section] * slope
            d_pre = d_convolved * taps[0]
            sums = [jnp.sum(d_convolved * pres[section], 0, keepdims=True)]
            for offset in range(1, KERNEL):
                d_pre = d_pre + tile.later(d_convolved, offset) * taps[offset]
                sums.append(
                    jnp.sum(d_convolved * tile.earlier(pres[section], offset), 0, keepdims=True)
                )
            d_param_ref[0:KERNEL, columns] += jnp.concatenate(sums, 0)
            d_pre_ref[:, columns] = d_pre.astype(bf)
    d_pre_ref[:, 4 * width :] = d_beta.astype(bf)


NO_COST = pl.CostEstimate(flops=0, bytes_accessed=0, transcendentals=0)


def call(kernel, operands, in_specs, out_specs, out_shape, grid=(), scratch=(), micros=0):
    results = pl.pallas_call(
        kernel,
        grid=grid,
        in_specs=in_specs,
        out_specs=out_specs,
        out_shape=out_shape,
        scratch_shapes=scratch,
        compiler_params=pltpu.CompilerParams(
            dimension_semantics=("arbitrary",) * len(grid), vmem_limit_bytes=48 * 2**20
        ),
        cost_estimate=pl.CostEstimate(
            flops=micros * 10**9, bytes_accessed=0, transcendentals=0
        ),
    )(*operands)
    return list(results)


def whole(array):
    return pl.BlockSpec(array.shape, lambda *step: (0,) * len(array.shape))


def mixer_specs(width):
    wide = 4 * width + SMALL
    heads = width // HEAD_DIM
    layout = pl.BlockSpec(memory_space=pltpu.SMEM)
    pre = pl.BlockSpec((GROUP_ROWS, wide), lambda group: (group, 0))
    param = pl.BlockSpec((2 * KERNEL, 3 * width), lambda group: (0, 0))
    narrow = pl.BlockSpec((GROUP_ROWS, width), lambda group: (group, 0))
    square = pl.BlockSpec((heads, GROUP_ROWS, HEAD_DIM), lambda group: (group, 0, 0))
    return layout, pre, param, narrow, square


def mixer_forward(layout, pre, params, width):
    groups = layout.shape[0]
    layout_spec, pre_spec, param_spec, narrow, square = mixer_specs(width)
    squares = pltpu.HBM((groups * width // HEAD_DIM, GROUP_ROWS, HEAD_DIM), f32)
    return call(
        mixer_forward_kernel,
        [layout, pre, params],
        [layout_spec, pre_spec, param_spec],
        [narrow] + [square] * 4,
        [jax.ShapeDtypeStruct((groups * GROUP_ROWS, width), bf)] + [squares] * 4,
        (groups,),
    )


def mixer_backward(layout, pre, params, weight, d_mixed, kept, width):
    groups = layout.shape[0]
    layout_spec, pre_spec, param_spec, _, square = mixer_specs(width)
    kept = [pltpu.with_memory_space_constraint(array, pltpu.HBM) for array in kept]
    return call(
        mixer_backward_kernel,
        [layout, pre, params, weight, *kept, *d_mixed],
        [layout_spec, pre_spec, param_spec, whole(weight)]
        + [square] * 4
        + [whole(block) for block in d_mixed],
        [pre_spec, param_spec],
        [jax.ShapeDtypeStruct(pre.shape, bf), jax.ShapeDtypeStruct(params.shape, f32)],
        (groups,),
        [pltpu.VMEM((GROUP_ROWS, width), f32)],
        micros=60,
    )


def first_kernel(gain_ref, weight_ref, *refs):
    *value_refs, normed_ref, out_ref, scale_ref, total_ref = refs
    step, depth = pl.program_id(0), weight_ref.shape[0]

    @pl.when(step == 0)
    def _():
        for group, ref in enumerate(value_refs):
            values = ref[...].astype(f32)
            scale = lax.rsqrt(jnp.mean(values * values, -1, keepdims=True) + 1e-06)
            rows = pl.ds(group * GROUP_ROWS, GROUP_ROWS)
            scale_ref[rows, :] = jnp.broadcast_to(scale, (GROUP_ROWS, 128))
        total_ref[...] = jnp.zeros_like(total_ref)

    columns = pl.ds(pl.multiple_of(step * depth, depth), depth)
    for group, ref in enumerate(value_refs):
        rows = pl.ds(group * GROUP_ROWS, GROUP_ROWS)
        values = ref[:, columns].astype(f32) * scale_ref[rows, :1] * gain_ref[...]
        normed_ref[rows, :] = values.astype(bf)
    total_ref[...] += plain_product(normed_ref[...], weight_ref[...])

    @pl.when(step == pl.num_programs(0) - 1)
    def _():
        out_ref[...] = total_ref[...]


def normed_product(blocks, gain, weight, depth=512):
    rows, (features, columns) = len(blocks) * GROUP_ROWS, weight.shape
    return call(
        first_kernel,
        [gain, weight, *blocks],
        [
            pl.BlockSpec((1, depth), lambda step: (0, step)),
            pl.BlockSpec((depth, columns), lambda step: (step, 0)),
        ]
        + [whole(block) for block in blocks],
        [
            pl.BlockSpec((rows, depth), lambda step: (0, step)),
            pl.BlockSpec((rows, columns), lambda step: (0, 0)),
        ],
        [
            jax.ShapeDtypeStruct((rows, features), bf),
            jax.ShapeDtypeStruct((rows, columns), f32),
        ],
        (features // depth,),
        [pltpu.VMEM((rows, 128), f32), pltpu.VMEM((rows, columns), f32)],
    )


def product_blocks(left, right, transposed=False, block=512, micros=0):
    product = transposed_product if transposed else plain_product
    columns = right.shape[0] if transposed else right.shape[1]
    groups = left.shape[0] // GROUP_ROWS

    def kernel(left_ref, right_ref, *out_refs):
        total = product(left_ref[...], right_ref[...])
        for group, ref in enumerate(out_refs):
            ref[...] = total[group * GROUP_ROWS : (group + 1) * GROUP_ROWS].astype(ref.dtype)

    if transposed:
        right_spec = pl.BlockSpec((block, right.shape[1]), lambda step: (step, 0))
    else:
        right_spec = pl.BlockSpec((right.shape[0], block), lambda step: (0, step))
    return call(
        kernel,
        [left, right],
        [whole(left), right_spec],
        [pl.BlockSpec((GROUP_ROWS, block), lambda step: (0, step))] * groups,
        [
            jax.ShapeDtypeStruct((GROUP_ROWS, columns), bf if group else f32)
            for group in range(groups)
        ],
        (columns // block,),
        micros=micros,
    )


def grad_product(left, right, block=256, micros=0):
    rows, features = left.shape
    if features % block:
        block = 128

    def kernel(left_ref, right_ref, out_ref):
        out_ref[...] = rows_product(left_ref[...], right_ref[...]).astype(bf)

    return call(
        kernel,
        [left, right],
        [pl.BlockSpec((rows, block), lambda step: (0, step)), whole(right)],
        [pl.BlockSpec((block, right.shape[1]), lambda step: (step, 0))],
        [pltpu.HBM((features, right.shape[1]), bf)],
        (features // block,),
        micros=micros,
    )[0]


def from_own(part, values):
    groups = values.shape[0] // GROUP_ROWS

    def kernel(part_ref, values_ref, out_ref):
        for step in range(groups):
            source = lax.rem(part_ref[0] + groups - step, groups) * GROUP_ROWS
            rows = pl.ds(pl.multiple_of(source, GROUP_ROWS), GROUP_ROWS)
            out_ref[step * GROUP_ROWS : (step + 1) * GROUP_ROWS] = values_ref[rows]

    return call(
        kernel,
        [part.reshape(1).astype(jnp.int32), values],
        [pl.BlockSpec(memory_space=pltpu.SMEM), whole(values)],
        [whole(values)],
        [jax.ShapeDtypeStruct(values.shape, values.dtype)],
        (1,),
    )[0]


def tie_all(values, *others):
    anywhere = pl.BlockSpec(memory_space=pl.ANY)
    others = [
        pltpu.with_memory_space_constraint(other, pltpu.HBM) if other.size > 2**21 else other
        for other in others
    ]
    tied = pl.pallas_call(
        lambda *refs: None,
        in_specs=[anywhere] * (len(values) + len(others)),
        out_specs=[anywhere] * len(values),
        out_shape=[
            (pltpu.HBM if value.size > 2**21 else jax.ShapeDtypeStruct)(value.shape, value.dtype)
            for value in values
        ],
        input_output_aliases={i: i for i in range(len(values))},
        cost_estimate=NO_COST,
    )(*values, *others)
    return list(tied)


def tie(value, *others):
    return tie_all([value], *others)[0]


def assemble(part, values, received, others):
    parts = values.shape[0]

    def kernel(part_ref, values_ref, *refs):
        own = part_ref[0]
        out_ref = refs[-1]
        out_ref[own] = values_ref[own]
        for step in range(1, parts):
            out_ref[lax.rem(own + parts - step, parts)] = refs[step - 1][...]

    vmem = pl.BlockSpec(memory_space=pltpu.VMEM)
    anywhere = pl.BlockSpec(memory_space=pl.ANY)
    return pl.pallas_call(
        kernel,
        in_specs=[pl.BlockSpec(memory_space=pltpu.SMEM)]
        + [vmem] * parts
        + [anywhere] * len(others),
        out_specs=vmem,
        out_shape=jax.ShapeDtypeStruct(values.shape, values.dtype),
        compiler_params=pltpu.CompilerParams(vmem_limit_bytes=32 * 2**20),
        cost_estimate=NO_COST,
    )(part.reshape(1).astype(jnp.int32), values, *received, *others)


def copy_columns(count, *refs):
    target = refs[-1]
    start = 0
    for source in refs[:count]:
        block = source[...].reshape(source.shape[-2:])
        columns = pl.ds(start, block.shape[1])
        if len(target.shape) == 3:
            target[0, :, columns] = block.astype(target.dtype)
        else:
            target[:, columns] = block.astype(target.dtype)
        start += block.shape[1]


def to_parts(sources, parts, dtype, others=()):
    rows = sources[0][0].shape[0]

    def spec(section, width):
        return pl.BlockSpec((rows, width), lambda p: (0, section * parts + p))

    total = sum(width for _, _, width in sources)
    return pl.pallas_call(
        functools.partial(copy_columns, len(sources)),
        grid=(parts,),
        in_specs=[spec(section, width) for _, section, width in sources]
        + [pl.BlockSpec(memory_space=pl.ANY)] * len(others),
        out_specs=pl.BlockSpec((1, rows, total), lambda p: (p, 0, 0)),
        out_shape=jax.ShapeDtypeStruct((parts, rows, total), dtype),
        cost_estimate=NO_COST,
    )(*[array for array, _, _ in sources], *others)


def updown_from_parts(slabs):
    parts, rows, width = slabs.shape
    units = width // 2

    def kernel(slabs_ref, out_ref):
        for p in range(parts):
            out_ref[:, p * units : (p + 1) * units] = slabs_ref[p].astype(f32)

    return pl.pallas_call(
        kernel,
        grid=(2,),
        in_specs=[pl.BlockSpec((parts, rows, units), lambda half: (0, 0, half))],
        out_specs=pl.BlockSpec((rows, parts * units), lambda half: (0, half)),
        out_shape=jax.ShapeDtypeStruct((rows, parts * width), f32),
        compiler_params=pltpu.CompilerParams(vmem_limit_bytes=32 * 2**20),
        cost_estimate=NO_COST,
    )(slabs)


def mixer_from_parts(slabs, width):
    parts, rows, _ = slabs.shape

    def kernel(slabs_ref, qkv_ref, gate_ref, strength_ref):
        for p in range(parts):
            for section in range(4):
                block = slabs_ref[p, :, section * width : (section + 1) * width].astype(f32)
                if section < 3:
                    start = (section * parts + p) * width
                    qkv_ref[:, start : start + width] = block
                else:
                    gate_ref[:, p * width : (p + 1) * width] = block
            last = slabs_ref[p, :, 4 * width :].astype(f32)
            strength_ref[:, p * SMALL : (p + 1) * SMALL] = last

    widths = [3 * parts * width, parts * width, parts * SMALL]
    return pl.pallas_call(
        kernel,
        out_shape=[jax.ShapeDtypeStruct((rows, size), f32) for size in widths],
        compiler_params=pltpu.CompilerParams(vmem_limit_bytes=32 * 2**20),
        cost_estimate=NO_COST,
    )(slabs)


def own_order(values, parts, copies):
    size = values.shape[1] // (parts * copies)
    pieces = [
        values[:, (t * parts + m) * size : (t * parts + m + 1) * size]
        for m in range(parts)
        for t in range(copies)
    ]
    return jnp.concatenate(pieces, 1)


def total_of(own_ref, received_refs):
    total = own_ref[...]
    for ref in received_refs:
        total = total + ref[...].astype(f32)
    return total


def row_scale(values):
    return lax.rsqrt(jnp.mean(values * values, -1, keepdims=True) + 1e-06)


def norm_slope(values, scale, gain, grad):
    mean = jnp.mean(gain * grad * values, -1, keepdims=True)
    return scale * gain * grad - values * (scale * scale * scale * mean)


def hidden_kernel(own_ref, *refs):
    *received, input_ref, gain_ref, hidden_ref, normed_ref = refs
    hidden = input_ref[...].astype(f32) + total_of(own_ref, received)
    hidden_ref[...] = hidden
    normed_ref[...] = (hidden * row_scale(hidden) * gain_ref[...]).astype(bf)


def hidden_back_kernel(own_ref, *refs):
    *received, hidden_ref, gain_ref, cot_ref, d_hidden_ref, d_mixed_ref, d_gain_ref = refs
    grad = total_of(own_ref, received)
    hidden = hidden_ref[...]
    scale = row_scale(hidden)

    @pl.when(pl.program_id(0) == 0)
    def _():
        d_gain_ref[...] = jnp.zeros_like(d_gain_ref)

    d_gain_ref[...] += jnp.sum(grad * hidden * scale, 0, keepdims=True)
    d_hidden = cot_ref[...].astype(f32) + norm_slope(hidden, scale, gain_ref[...], grad)
    d_hidden_ref[...] = d_hidden
    d_mixed_ref[...] = d_hidden.astype(bf)


def input_back_kernel(parts, copies, own_ref, *refs):
    *received, input_ref, gain_ref, d_hidden_ref, out_ref = refs
    grad = total_of(own_ref, received)
    values = input_ref[...].astype(f32)
    slope = norm_slope(values, row_scale(values), gain_ref[...], grad)
    out_ref[...] = own_order(d_hidden_ref[...] + slope, parts, copies).astype(bf)


def block_out_kernel(parts, copies, own_ref, *refs):
    *received, hidden_ref, out_ref = refs
    total = hidden_ref[...] + total_of(own_ref, received)
    out_ref[...] = own_order(total, parts, copies).astype(bf)


def last_sum(sides, others, parts, copies):
    rows, columns = sides[0].shape

    def kernel(*refs):
        first, first_other, second, second_other = (ref[...].astype(f32) for ref in refs[:4])
        total = jnp.concatenate([first + first_other, second + second_other], 1)
        refs[-1][...] = own_order(total, parts, copies)

    vmem = pl.BlockSpec(memory_space=pltpu.VMEM)
    return pl.pallas_call(
        kernel,
        in_specs=[vmem] * 4 + [pl.BlockSpec(memory_space=pl.ANY)] * len(others),
        out_specs=vmem,
        out_shape=jax.ShapeDtypeStruct((rows, 2 * columns), f32),
        compiler_params=pltpu.CompilerParams(vmem_limit_bytes=32 * 2**20),
        cost_estimate=NO_COST,
    )(*sides, *others)


def by_rows(kernel, arrays, outs, block=64):
    def spec(shape):
        if shape[0] == 1:
            return pl.BlockSpec(shape, lambda i: (0, 0))
        return pl.BlockSpec((block, shape[1]), lambda i: (i, 0))

    return pl.pallas_call(
        kernel,
        grid=(GROUP_ROWS // block,),
        in_specs=[spec(array.shape) for array in arrays],
        out_specs=[spec(shape) for shape, _ in outs],
        out_shape=[jax.ShapeDtypeStruct(shape, dtype) for shape, dtype in outs],
        compiler_params=pltpu.CompilerParams(dimension_semantics=("arbitrary",)),
        cost_estimate=NO_COST,
    )(*arrays)


def body(
    block_in,
    out_grad,
    norm1_gain,
    conv_weight,
    head_gain,
    qkv_weight,
    beta_weight,
    gate_weight,
    out_weight,
    norm2_gain,
    updown_weight,
    down_weight,
    seq_blocks,
    lead_blocks,
):
    devices = lax.axis_size("dp")
    parts = MODEL
    copies = devices // parts
    part = lax.axis_index("dp") // copies
    copy = lax.axis_index("dp") % copies
    rows_own = qkv_weight.shape[0]
    width = D // parts
    units = FF // parts
    heads_part = HEADS // parts
    wide = 4 * width + SMALL
    model_groups = [[m * copies + t for m in range(parts)] for t in range(copies)]
    copy_groups = [[m * copies + t for t in range(copies)] for m in range(parts)]

    def exchange(values):
        return lax.all_to_all(
            values, "dp", split_axis=0, concat_axis=0, axis_index_groups=model_groups, tiled=True
        )

    def shift(values, step):
        pairs = [
            (m * copies + t, (m + step) % parts * copies + t)
            for m in range(parts)
            for t in range(copies)
        ]
        return lax.ppermute(values, "dp", pairs)

    def exchange_apart(values, before, after=()):
        cut = [
            lax.dynamic_index_in_dim(values, (part + step) % parts, 0, keepdims=False)
            for step in range(1, parts)
        ]
        received = [shift(piece, step) for step, piece in enumerate(tie_all(cut, *before), 1)]
        return assemble(part, values, received, after)

    def gather_rows(values):
        return [values] + [shift(values, step) for step in range(1, parts)]

    def scatter_rows(terms):
        return [terms[0]] + [shift(block, -step) for step, block in enumerate(terms[1:], 1)]

    def gather_copies(values):
        return lax.all_gather(values, "dp", axis=0, axis_index_groups=copy_groups, tiled=True)

    def scatter_copies(values):
        return lax.psum_scatter(
            values.astype(bf),
            "dp",
            scatter_dimension=0,
            axis_index_groups=copy_groups,
            tiled=True,
        )

    def halves_across(values, bit, axis):
        pairs = [(i, i ^ (1 << bit)) for i in range(devices)]
        side = (copy >> bit) & 1
        own = lax.dynamic_index_in_dim(values, side, axis, keepdims=False)
        other = lax.dynamic_index_in_dim(values, 1 - side, axis, keepdims=False)
        return own, lax.ppermute(other, "dp", pairs)

    def halve(values, bit, axis, *others):
        own, received = halves_across(values, bit, axis)
        if others:
            received = tie(received, *others)
        return (own.astype(f32) + received.astype(f32)).astype(bf)

    by_halves = copies == 8

    def halve_cores(values, *others):
        if not by_halves:
            return values
        rows, columns = values.shape
        return halve(values.reshape(2, 2, 2, rows // 8, columns), 0, 2, *others)

    def halve_first(values):
        if not by_halves:
            return [values]
        middle = values.shape[-1] // 2
        return [halve(values[..., :middle], 1, 1), halve(values[..., middle:], 2, 0)]

    def halve_second(values, *others):
        if not by_halves:
            return from_wire(scatter_copies(values[0]).astype(f32))
        sides = halves_across(values[0], 2, 0) + halves_across(values[1], 1, 0)
        return last_sum(sides, others, parts, copies)

    def to_wire(values):
        return values.reshape(-1, parts, copies, rows_own).swapaxes(1, 2).reshape(-1, D)

    def from_wire(values):
        return values.reshape(-1, copies, parts, rows_own).swapaxes(1, 2).reshape(-1, D)

    w_out_own = to_wire(out_weight.astype(bf))
    w_out = gather_copies(w_out_own)
    strengths = beta_weight.reshape(rows_own, parts, heads_part)
    strengths = jnp.pad(strengths, ((0, 0), (0, 0), (0, SMALL - heads_part)))
    strengths = tie(strengths.reshape(rows_own, parts * SMALL), w_out_own)
    pieces = [(qkv_weight, section, width) for section in range(3)]
    pieces = to_parts(pieces + [(gate_weight, 0, width), (strengths, 0, SMALL)], parts, bf)
    mixer_pieces = tie(exchange(pieces), w_out)
    w_mixer = gather_copies(mixer_pieces.reshape(parts * rows_own, wide))
    inputs = tie(to_wire(block_in), mixer_pieces)
    input_rows = gather_rows(inputs)

    lanes = -(-3 * rows_own // 128) * 128
    numbers = jnp.concatenate([seq_blocks[0], lead_blocks]).astype(f32)
    small = [conv_weight.T, norm1_gain[None], head_gain[None], norm2_gain[None], numbers[None]]
    small = [jnp.pad(rows, ((0, 0), (0, lanes - rows.shape[1]))) for rows in small]
    small = jnp.pad(jnp.concatenate(small, 0).astype(bf), ((0, 2 * KERNEL), (0, 0)))
    small = jnp.broadcast_to(small[None], (devices,) + small.shape)
    small = lax.all_to_all(tie(small, *input_rows[1:]), "dp", 0, 0, tiled=True)
    taps = small[:, :KERNEL, : 3 * rows_own].swapaxes(0, 1).reshape(KERNEL, 3, parts, width)
    taps = lax.dynamic_index_in_dim(taps, part, 2, keepdims=False).reshape(KERNEL, 3 * width)
    gain_one, head_full, gain_two = (
        small[:, KERNEL + i, :rows_own].reshape(1, D).astype(f32) for i in range(3)
    )
    gain_one, gain_two = to_wire(gain_one), to_wire(gain_two)
    head_part = lax.dynamic_slice_in_dim(head_full, part * width, width, 1)
    params = jnp.concatenate([taps.astype(f32), jnp.pad(head_part, ((0, 0), (0, 2 * width)))], 0)
    params = jnp.pad(params, ((0, KERNEL - 1), (0, 0)))
    numbers = small[:, KERNEL + 3, :3].astype(f32).astype(jnp.int32)
    layouts = block_layouts(numbers[:, 0], numbers[:, 1], numbers[:, 2])
    layouts = layouts.reshape(parts, copies, 4)
    layouts = lax.dynamic_index_in_dim(layouts, copy, 1, keepdims=False)
    wanted = (part - jnp.arange(parts)) % parts
    wanted = (wanted[:, None] == jnp.arange(parts)).astype(f32)
    layouts = jnp.sum(wanted[:, :, None] * layouts, 1)

    pieces = [(updown_weight, half, units) for half in range(2)]
    updown_pieces = to_parts(pieces, parts, bf, [mixer_pieces])
    w_down_own = to_wire(down_weight.astype(bf))
    w_down = gather_copies(tie(w_down_own, *input_rows[1:]))
    cotangent_own = to_wire(out_grad)

    cotangent = lax.all_gather(
        tie(cotangent_own, *input_rows[1:]), "dp", axis=0, axis_index_groups=model_groups, tiled=True
    )
    gain_first = tie(gain_one, w_down_own, cotangent_own, updown_pieces)
    normed, pre = normed_product(input_rows, gain_first, w_mixer)
    mixed, *kept = mixer_forward(layouts, pre, params, width)
    out_terms = product_blocks(mixed, w_out)
    updown_pieces = exchange_apart(updown_pieces, input_rows[1:], out_terms[1:])
    w_updown = gather_copies(updown_pieces.reshape(parts * rows_own, 2 * units))
    stream = ((GROUP_ROWS, D), f32)
    narrow = ((GROUP_ROWS, D), bf)
    hidden, normed_two = by_rows(
        hidden_kernel,
        scatter_rows(out_terms) + [inputs, gain_two],
        [stream, narrow],
    )
    cotangent = from_own(part, cotangent)
    normed_two = jnp.concatenate(gather_rows(normed_two), 0)

    def swiglu_units(updown):
        return jax.nn.silu(updown[:, :units]) * updown[:, units:]

    updown = plain_product(normed_two, w_updown)
    active, swiglu_back = jax.vjp(swiglu_units, updown)
    active = active.astype(bf)
    d_active = transposed_product(cotangent, w_down)
    d_updown = swiglu_back(d_active)[0].astype(bf)
    d_normed_two = product_blocks(d_updown, w_updown, transposed=True)
    active = tie(active, *d_normed_two[1:])
    down_terms = grad_product(active, cotangent)
    updown_terms = grad_product(normed_two, tie(d_updown, down_terms))
    gain_late = tie(gain_two, updown_terms)
    d_normed_two = scatter_rows(d_normed_two)
    updown_grad = scatter_copies(tie(updown_terms, gain_late, *d_normed_two[1:]))
    d_hidden, d_mixed, gain_two_grad = by_rows(
        hidden_back_kernel,
        d_normed_two + [hidden, gain_late, cotangent_own],
        [stream, narrow, ((1, D), f32)],
    )


    out_terms = product_blocks(tie(active, d_mixed), w_down)
    down_terms = tie(down_terms, *out_terms[1:])
    d_mixed = gather_rows(d_mixed)
    late = tie(params, *out_terms)
    out_terms[1:] = tie_all(out_terms[1:], *d_mixed[1:])
    d_pre, d_params = mixer_backward(layouts, pre, late, w_out, d_mixed, kept, width)
    mixer_terms = tie(grad_product(normed, d_pre, micros=20), updown_grad)
    mixer_grad = scatter_copies(mixer_terms)

    d_normed_terms = product_blocks(
        tie(d_pre, mixer_terms), w_mixer, transposed=True, micros=150
    )
    hidden = tie(hidden, d_normed_terms[0])
    (block_out,) = by_rows(
        functools.partial(block_out_kernel, parts, copies),
        scatter_rows(out_terms) + [hidden],
        [narrow],
    )
    d_normed_terms[1:] = tie_all(d_normed_terms[1:], block_out)
    d_normed = scatter_rows(d_normed_terms)
    down_grad = halve_first(halve_cores(down_terms, *d_normed_terms[1:]))
    gain_one_grad = 0.0
    for values, terms in zip(input_rows, d_normed_terms):
        values = values.astype(f32)
        terms = terms.astype(f32) * (values * row_scale(values))
        gain_one_grad = gain_one_grad + jnp.sum(terms, 0, keepdims=True)

    d_params = tie(d_params, mixer_terms)
    here = (jnp.arange(parts) == part).astype(f32)[:, None]
    taps_grad = d_params[:KERNEL].reshape(KERNEL, 3, 1, width) * here
    taps_grad = taps_grad.reshape(KERNEL, parts, copies, 3, rows_own).transpose(1, 2, 3, 0, 4)
    taps_grad = taps_grad.reshape(devices, 3 * KERNEL, rows_own)
    head_grad = (d_params[KERNEL, :width] * here).reshape(devices, 1, rows_own)
    gain_grads = [
        grad.reshape(copies, parts, 1, rows_own).swapaxes(0, 1).reshape(devices, 1, rows_own)
        for grad in (gain_one_grad, gain_two_grad)
    ]
    small_grad = jnp.concatenate([taps_grad, head_grad] + gain_grads, 1)
    small_grad = jnp.pad(small_grad, ((0, 0), (0, 1), (0, 128 - rows_own)))
    small_grad = jnp.sum(lax.all_to_all(small_grad, "dp", 0, 0, tiled=True), 0)[:, :rows_own]
    taps_shard = small_grad[: 3 * KERNEL].reshape(3, KERNEL, rows_own).swapaxes(1, 2)
    taps_shard = taps_shard.reshape(3 * rows_own, KERNEL)
    head_shard, gain_one_shard, gain_two_shard = small_grad[3 * KERNEL : 3 * KERNEL + 3]

    out_grads = grad_product(tie(mixed, d_normed_terms[0]), jnp.concatenate(d_mixed, 0))
    late = tie(gain_one, out_grads)
    (input_grad,) = by_rows(
        functools.partial(input_back_kernel, parts, copies),
        d_normed + [inputs, late, d_hidden],
        [narrow],
    )
    updown_grad = tie(updown_grad, mixer_terms).reshape(parts, rows_own, 2 * units)
    updown_grad = exchange(updown_grad)
    mixer_grad = tie(mixer_grad, updown_grad, input_grad)
    updown_shard = updown_from_parts(updown_grad)
    down_shard = halve_second(tie_all(down_grad, input_grad), mixer_grad)
    out_grads = tie(halve_cores(tie(out_grads, input_grad)), mixer_grad)
    out_shard = halve_second(halve_first(out_grads))
    mixer_grad = exchange(mixer_grad.reshape(parts, rows_own, wide))
    qkv_shard, gate_shard, strengths = mixer_from_parts(mixer_grad, width)
    beta_shard = strengths.reshape(rows_own, parts, SMALL)[:, :, :heads_part]
    return (
        block_out,
        input_grad,
        gain_one_shard,
        taps_shard,
        head_shard,
        qkv_shard,
        beta_shard.reshape(rows_own, HEADS),
        gate_shard,
        out_shard,
        gain_two_shard,
        updown_shard,
        down_shard,
    )


def solution(mesh):
    placed = (
        P("dp", None),
        P("dp", None),
        P("dp"),
        P("dp", None),
        P("dp"),
        P("dp", None),
        P("dp", None),
        P("dp", None),
        P("dp", None),
        P("dp"),
        P("dp", None),
        P("dp", None),
        P("dp", None),
        P("dp"),
    )
    return jax.shard_map(
        body,
        mesh=mesh,
        in_specs=placed,
        out_specs=(
            P("dp", None),
            P("dp", None),
            P("dp"),
            P("dp", None),
            P("dp"),
            P("dp", None),
            P("dp", None),
            P("dp", None),
            P("dp", None),
            P("dp"),
            P("dp", None),
            P("dp", None),
        ),
        check_vma=False,
    )
```

```python
import functools

import jax
import jax.numpy as jnp
from jax import lax
from jax.experimental import pallas as pl
from jax.experimental.pallas import tpu as pltpu
from jax.sharding import PartitionSpec as P

D = 2048
HEADS = 16
HEAD_DIM = 128
FF = 5632
KERNEL = 4
BLOCK_ROWS = 64
BLOCKS_DEV = 2
GROUP_ROWS = BLOCK_ROWS * BLOCKS_DEV
SMALL = 128
MODEL = 4

f32 = jnp.float32
bf = jnp.bfloat16


def block_layouts(first, second, lead):
    def doc(block):
        in_first = (block >= lead) & (block < lead + first)
        in_second = (block >= lead + first) & (block < lead + first + second)
        return jnp.where(in_first, 1, jnp.where(in_second, 2, 0))

    starts = (lead == 1) | (lead + first == 1) & (second > 0)
    columns = [doc(0) > 0, doc(1) > 0, doc(0) == doc(1), ~starts]
    return jnp.stack(columns, 1).astype(f32)


def plain_product(left, right):
    return jnp.dot(left, right, preferred_element_type=f32)


def rows_product(left, right):
    return lax.dot_general(left, right, (((0,), (0,)), ((), ())), preferred_element_type=f32)


def transposed_product(left, right):
    return lax.dot_general(left, right, (((1,), (1,)), ((), ())), preferred_element_type=f32)


def halves(values):
    high = values.astype(bf)
    return high, (values - high.astype(f32)).astype(bf)


def exact(left, right, left_dim, right_dim):
    left_high, left_low = left if isinstance(left, tuple) else halves(left)
    right_high, right_low = right if isinstance(right, tuple) else halves(right)
    return lax.dot_general(
        jnp.concatenate([left_high, left_high, left_low], left_dim),
        jnp.concatenate([right_high, right_low, right_high], right_dim),
        (((left_dim,), (right_dim,)), ((), ())),
        preferred_element_type=f32,
    )


def stacked(first, second):
    return tuple(jnp.concatenate([a, b], 0) for a, b in zip(first, second))


class Tile:
    def __init__(self, layout_ref, group):
        live_first, live_second, same, persist = (layout_ref[group, i] for i in range(4))
        shape = (GROUP_ROWS, HEAD_DIM)
        row = lax.broadcasted_iota(jnp.int32, shape, 0)
        col = lax.broadcasted_iota(jnp.int32, shape, 1)
        late = row >= BLOCK_ROWS
        self.row, self.col = row, col
        self.live = jnp.where(late, live_second, live_first)
        self.taps = [None] + [
            jnp.where(
                row < offset,
                0.0,
                jnp.where(late & (row < BLOCK_ROWS + offset), same, 1.0),
            )
            for offset in range(1, KERNEL)
        ]
        cross = jnp.where(late & (col < BLOCK_ROWS), persist, 1.0)
        self.lower = jnp.where(row > col, cross, 0.0)
        self.lower_full = jnp.where(row >= col, cross, 0.0)

    def earlier(self, values, offset):
        return pltpu.roll(values, offset, 0) * self.taps[offset]

    def later(self, values, offset):
        return pltpu.roll(values * self.taps[offset], GROUP_ROWS - offset, 0)


def convolve(tile, values, taps):
    total = values * taps[0]
    for offset in range(1, KERNEL):
        total = total + tile.earlier(values, offset) * taps[offset]
    return total


def unit_scale(values):
    return lax.rsqrt(jnp.sum(values * values, -1, keepdims=True) + 1e-06)


def head_columns(part_width, section, head):
    return pl.ds(section * part_width + head * HEAD_DIM, HEAD_DIM)


def unit_inverses(tile, lowers):
    eye = jnp.where(tile.row == tile.col, 1.0, 0.0)
    inverses = None
    size = 1
    while size < GROUP_ROWS:
        pair = tile.row // (2 * size) == tile.col // (2 * size)
        split = pair & (tile.row // size != tile.col // size)
        parts = [jnp.where(split, lower, 0.0) for lower in lowers]
        if inverses is None:
            inverses = [eye - part for part in parts]
        else:
            kept = [halves(inverse) for inverse in inverses]
            inner = [exact(part, known, 1, 0) for part, known in zip(parts, kept)]
            outer = [exact(known, value, 1, 0) for known, value in zip(kept, inner)]
            inverses = [inverse - value for inverse, value in zip(inverses, outer)]
        size *= 2
    return inverses


def mixer_forward_kernel(
    layout_ref, pre_ref, param_ref, mixed_ref, inverse_ref, score_ref, solved_ref, out_ref
):
    width = mixed_ref.shape[1]
    heads = range(width // HEAD_DIM)
    tile = Tile(layout_ref, pl.program_id(0))
    queries, keys, values, strengths = [], [], [], []
    for head in heads:
        parts = []
        for section in range(3):
            columns = head_columns(width, section, head)
            taps = [param_ref[offset : offset + 1, columns] for offset in range(KERNEL)]
            convolved = convolve(tile, pre_ref[:, columns], taps)
            parts.append(convolved * jax.nn.sigmoid(convolved))
        queries.append(parts[0] * (unit_scale(parts[0]) * HEAD_DIM**-0.5))
        keys.append(parts[1] * unit_scale(parts[1]))
        values.append(parts[2])
        start = 4 * width + head
        strengths.append(jax.nn.sigmoid(pre_ref[:, start : start + 1]) * tile.live)
    lowers, scores = [], []
    for head in heads:
        key_halves = halves(keys[head])
        both = exact(stacked(key_halves, halves(queries[head])), key_halves, 1, 1)
        lowers.append(both[:GROUP_ROWS] * strengths[head] * tile.lower)
        scores.append(both[GROUP_ROWS:] * tile.lower_full)
    inverses = unit_inverses(tile, lowers)
    solved = [exact(inverses[head], values[head] * strengths[head], 1, 0) for head in heads]
    outs = [exact(scores[head], solved[head], 1, 0) for head in heads]
    for head in heads:
        out = outs[head]
        scaled = out * lax.rsqrt(jnp.mean(out * out, -1, keepdims=True) + 1e-05)
        gate = pre_ref[:, head_columns(width, 3, head)]
        gain = param_ref[KERNEL : KERNEL + 1, head_columns(width, 0, head)]
        mixed = scaled * gain * (gate * jax.nn.sigmoid(gate)) * tile.live
        mixed_ref[:, head_columns(width, 0, head)] = mixed.astype(bf)
        inverse_ref[head] = inverses[head]
        score_ref[head] = scores[head]
        solved_ref[head] = solved[head]
        out_ref[head] = out


def mixer_backward_kernel(
    layout_ref,
    pre_ref,
    param_ref,
    weight_ref,
    inverse_ref,
    score_ref,
    solved_ref,
    out_ref,
    *refs,
):
    *mixed_refs, d_pre_ref, d_param_ref, grad_ref = refs
    width = grad_ref.shape[1]
    heads = range(width // HEAD_DIM)
    tile = Tile(layout_ref, pl.program_id(0))
    for group, mixed_ref in enumerate(mixed_refs):

        @pl.when(pl.program_id(0) == group)
        def _():
            grad_ref[...] = transposed_product(mixed_ref[...], weight_ref[...])

    @pl.when(pl.program_id(0) == 0)
    def _():
        d_param_ref[...] = jnp.zeros_like(d_param_ref)

    def along(values):
        return jnp.sum(values, -1, keepdims=True)

    d_outs = []
    for head in heads:
        columns = head_columns(width, 0, head)
        d_mixed = grad_ref[:, columns] * tile.live
        out = out_ref[head]
        scale = lax.rsqrt(jnp.mean(out * out, -1, keepdims=True) + 1e-05)
        scaled = out * scale
        gate = pre_ref[:, head_columns(width, 3, head)]
        gate_open = jax.nn.sigmoid(gate)
        gain = param_ref[KERNEL : KERNEL + 1, columns]
        gated = d_mixed * (gate * gate_open)
        d_param_ref[KERNEL : KERNEL + 1, columns] += jnp.sum(gated * scaled, 0, keepdims=True)
        d_gate = d_mixed * scaled * gain * (gate_open * (1.0 + gate * (1.0 - gate_open)))
        d_pre_ref[:, head_columns(width, 3, head)] = d_gate.astype(bf)
        d_scaled = gated * gain
        mean = jnp.mean(d_scaled * out, -1, keepdims=True)
        d_outs.append(scale * d_scaled - out * (scale * scale * scale * mean))
    d_out_halves = [halves(value) for value in d_outs]
    solved_halves = [halves(solved_ref[head]) for head in heads]
    d_solved = [exact(score_ref[head], d_out_halves[head], 0, 0) for head in heads]
    d_scores = [
        exact(d_out_halves[head], solved_halves[head], 1, 1) * tile.lower_full for head in heads
    ]
    d_inner = [exact(inverse_ref[head], d_solved[head], 0, 0) for head in heads]
    d_lowers = [exact(d_inner[head], solved_halves[head], 1, 1) * -tile.lower for head in heads]
    d_beta = jnp.zeros((GROUP_ROWS, SMALL), f32)
    for head in heads:
        pres, convolved, opened, active = [], [], [], []
        for section in range(3):
            columns = head_columns(width, section, head)
            taps = [param_ref[offset : offset + 1, columns] for offset in range(KERNEL)]
            pres.append(pre_ref[:, columns])
            convolved.append(convolve(tile, pres[section], taps))
            opened.append(jax.nn.sigmoid(convolved[section]))
            active.append(convolved[section] * opened[section])
        query_scale = unit_scale(active[0])
        key_scale = unit_scale(active[1])
        query_unit = active[0] * query_scale
        key = active[1] * key_scale
        start = 4 * width + head
        opening = jax.nn.sigmoid(pre_ref[:, start : start + 1])
        strength = opening * tile.live
        d_both = stacked(halves(d_lowers[head]), halves(d_scores[head]))
        by_key = exact(d_both, key, 1, 0)
        d_query = by_key[GROUP_ROWS:] * HEAD_DIM**-0.5
        from_lower = by_key[:GROUP_ROWS]
        weighted = stacked(halves(key * strength), halves(query_unit * HEAD_DIM**-0.5))
        d_key = strength * from_lower + exact(d_both, weighted, 0, 0)
        d_strength = along(d_inner[head] * active[2] + from_lower * key)
        d_value = d_inner[head] * strength
        d_opening = d_strength * (opening * (1.0 - opening)) * tile.live
        d_beta = d_beta + jnp.where(tile.col == head, d_opening, 0.0)
        d_active = [
            (d_query - query_unit * along(query_unit * d_query)) * query_scale,
            (d_key - key * along(key * d_key)) * key_scale,
            d_value,
        ]
        for section in range(3):
            columns = head_columns(width, section, head)
            taps = [param_ref[offset : offset + 1, columns] for offset in range(KERNEL)]
            slope = opened[section] * (1.0 + convolved[section] * (1.0 - opened[section]))
            d_convolved = d_active[section] * slope
            d_pre = d_convolved * taps[0]
            sums = [jnp.sum(d_convolved * pres[section], 0, keepdims=True)]
            for offset in range(1, KERNEL):
                d_pre = d_pre + tile.later(d_convolved, offset) * taps[offset]
                sums.append(
                    jnp.sum(d_convolved * tile.earlier(pres[section], offset), 0, keepdims=True)
                )
            d_param_ref[0:KERNEL, columns] += jnp.concatenate(sums, 0)
            d_pre_ref[:, columns] = d_pre.astype(bf)
    d_pre_ref[:, 4 * width :] = d_beta.astype(bf)


NO_COST = pl.CostEstimate(flops=0, bytes_accessed=0, transcendentals=0)


def call(kernel, operands, in_specs, out_specs, out_shape, grid=(), scratch=(), micros=0):
    results = pl.pallas_call(
        kernel,
        grid=grid,
        in_specs=in_specs,
        out_specs=out_specs,
        out_shape=out_shape,
        scratch_shapes=scratch,
        compiler_params=pltpu.CompilerParams(
            dimension_semantics=("arbitrary",) * len(grid), vmem_limit_bytes=48 * 2**20
        ),
        cost_estimate=pl.CostEstimate(
            flops=micros * 10**9, bytes_accessed=0, transcendentals=0
        ),
    )(*operands)
    return list(results)


def whole(array):
    return pl.BlockSpec(array.shape, lambda *step: (0,) * len(array.shape))


def mixer_specs(width):
    wide = 4 * width + SMALL
    heads = width // HEAD_DIM
    layout = pl.BlockSpec(memory_space=pltpu.SMEM)
    pre = pl.BlockSpec((GROUP_ROWS, wide), lambda group: (group, 0))
    param = pl.BlockSpec((2 * KERNEL, 3 * width), lambda group: (0, 0))
    narrow = pl.BlockSpec((GROUP_ROWS, width), lambda group: (group, 0))
    square = pl.BlockSpec((heads, GROUP_ROWS, HEAD_DIM), lambda group: (group, 0, 0))
    return layout, pre, param, narrow, square


def mixer_forward(layout, pre, params, width):
    groups = layout.shape[0]
    layout_spec, pre_spec, param_spec, narrow, square = mixer_specs(width)
    squares = pltpu.HBM((groups * width // HEAD_DIM, GROUP_ROWS, HEAD_DIM), f32)
    return call(
        mixer_forward_kernel,
        [layout, pre, params],
        [layout_spec, pre_spec, param_spec],
        [narrow] + [square] * 4,
        [jax.ShapeDtypeStruct((groups * GROUP_ROWS, width), bf)] + [squares] * 4,
        (groups,),
    )


def mixer_backward(layout, pre, params, weight, d_mixed, kept, width):
    groups = layout.shape[0]
    layout_spec, pre_spec, param_spec, _, square = mixer_specs(width)
    kept = [pltpu.with_memory_space_constraint(array, pltpu.HBM) for array in kept]
    return call(
        mixer_backward_kernel,
        [layout, pre, params, weight, *kept, *d_mixed],
        [layout_spec, pre_spec, param_spec, whole(weight)]
        + [square] * 4
        + [whole(block) for block in d_mixed],
        [pre_spec, param_spec],
        [jax.ShapeDtypeStruct(pre.shape, bf), jax.ShapeDtypeStruct(params.shape, f32)],
        (groups,),
        [pltpu.VMEM((GROUP_ROWS, width), f32)],
        micros=60,
    )


def first_kernel(gain_ref, weight_ref, *refs):
    *value_refs, normed_ref, out_ref, scale_ref, total_ref = refs
    step, depth = pl.program_id(0), weight_ref.shape[0]

    @pl.when(step == 0)
    def _():
        for group, ref in enumerate(value_refs):
            values = ref[...].astype(f32)
            scale = lax.rsqrt(jnp.mean(values * values, -1, keepdims=True) + 1e-06)
            rows = pl.ds(group * GROUP_ROWS, GROUP_ROWS)
            scale_ref[rows, :] = jnp.broadcast_to(scale, (GROUP_ROWS, 128))
        total_ref[...] = jnp.zeros_like(total_ref)

    columns = pl.ds(pl.multiple_of(step * depth, depth), depth)
    for group, ref in enumerate(value_refs):
        rows = pl.ds(group * GROUP_ROWS, GROUP_ROWS)
        values = ref[:, columns].astype(f32) * scale_ref[rows, :1] * gain_ref[...]
        normed_ref[rows, :] = values.astype(bf)
    total_ref[...] += plain_product(normed_ref[...], weight_ref[...])

    @pl.when(step == pl.num_programs(0) - 1)
    def _():
        out_ref[...] = total_ref[...]


def normed_product(blocks, gain, weight, depth=512):
    rows, (features, columns) = len(blocks) * GROUP_ROWS, weight.shape
    return call(
        first_kernel,
        [gain, weight, *blocks],
        [
            pl.BlockSpec((1, depth), lambda step: (0, step)),
            pl.BlockSpec((depth, columns), lambda step: (step, 0)),
        ]
        + [whole(block) for block in blocks],
        [
            pl.BlockSpec((rows, depth), lambda step: (0, step)),
            pl.BlockSpec((rows, columns), lambda step: (0, 0)),
        ],
        [
            jax.ShapeDtypeStruct((rows, features), bf),
            jax.ShapeDtypeStruct((rows, columns), f32),
        ],
        (features // depth,),
        [pltpu.VMEM((rows, 128), f32), pltpu.VMEM((rows, columns), f32)],
    )


def product_blocks(left, right, transposed=False, block=512, micros=0):
    product = transposed_product if transposed else plain_product
    columns = right.shape[0] if transposed else right.shape[1]
    groups = left.shape[0] // GROUP_ROWS

    def kernel(left_ref, right_ref, *out_refs):
        total = product(left_ref[...], right_ref[...])
        for group, ref in enumerate(out_refs):
            ref[...] = total[group * GROUP_ROWS : (group + 1) * GROUP_ROWS].astype(ref.dtype)

    if transposed:
        right_spec = pl.BlockSpec((block, right.shape[1]), lambda step: (step, 0))
    else:
        right_spec = pl.BlockSpec((right.shape[0], block), lambda step: (0, step))
    return call(
        kernel,
        [left, right],
        [whole(left), right_spec],
        [pl.BlockSpec((GROUP_ROWS, block), lambda step: (0, step))] * groups,
        [
            jax.ShapeDtypeStruct((GROUP_ROWS, columns), bf if group else f32)
            for group in range(groups)
        ],
        (columns // block,),
        micros=micros,
    )


def grad_product(left, right, block=256, micros=0):
    rows, features = left.shape
    if features % block:
        block = 128

    def kernel(left_ref, right_ref, out_ref):
        out_ref[...] = rows_product(left_ref[...], right_ref[...]).astype(bf)

    return call(
        kernel,
        [left, right],
        [pl.BlockSpec((rows, block), lambda step: (0, step)), whole(right)],
        [pl.BlockSpec((block, right.shape[1]), lambda step: (step, 0))],
        [pltpu.HBM((features, right.shape[1]), bf)],
        (features // block,),
        micros=micros,
    )[0]


def from_own(part, values):
    groups = values.shape[0] // GROUP_ROWS

    def kernel(part_ref, values_ref, out_ref):
        for step in range(groups):
            source = lax.rem(part_ref[0] + groups - step, groups) * GROUP_ROWS
            rows = pl.ds(pl.multiple_of(source, GROUP_ROWS), GROUP_ROWS)
            out_ref[step * GROUP_ROWS : (step + 1) * GROUP_ROWS] = values_ref[rows]

    return call(
        kernel,
        [part.reshape(1).astype(jnp.int32), values],
        [pl.BlockSpec(memory_space=pltpu.SMEM), whole(values)],
        [whole(values)],
        [jax.ShapeDtypeStruct(values.shape, values.dtype)],
        (1,),
    )[0]


def tie_all(values, *others):
    anywhere = pl.BlockSpec(memory_space=pl.ANY)
    others = [
        pltpu.with_memory_space_constraint(other, pltpu.HBM) if other.size > 2**21 else other
        for other in others
    ]
    tied = pl.pallas_call(
        lambda *refs: None,
        in_specs=[anywhere] * (len(values) + len(others)),
        out_specs=[anywhere] * len(values),
        out_shape=[
            (pltpu.HBM if value.size > 2**21 else jax.ShapeDtypeStruct)(value.shape, value.dtype)
            for value in values
        ],
        input_output_aliases={i: i for i in range(len(values))},
        cost_estimate=NO_COST,
    )(*values, *others)
    return list(tied)


def tie(value, *others):
    return tie_all([value], *others)[0]


def assemble(part, values, received, others):
    parts = values.shape[0]

    def kernel(part_ref, values_ref, *refs):
        own = part_ref[0]
        out_ref = refs[-1]
        out_ref[own] = values_ref[own]
        for step in range(1, parts):
            out_ref[lax.rem(own + parts - step, parts)] = refs[step - 1][...]

    vmem = pl.BlockSpec(memory_space=pltpu.VMEM)
    anywhere = pl.BlockSpec(memory_space=pl.ANY)
    return pl.pallas_call(
        kernel,
        in_specs=[pl.BlockSpec(memory_space=pltpu.SMEM)]
        + [vmem] * parts
        + [anywhere] * len(others),
        out_specs=vmem,
        out_shape=jax.ShapeDtypeStruct(values.shape, values.dtype),
        compiler_params=pltpu.CompilerParams(vmem_limit_bytes=32 * 2**20),
        cost_estimate=NO_COST,
    )(part.reshape(1).astype(jnp.int32), values, *received, *others)


def copy_columns(count, *refs):
    target = refs[-1]
    start = 0
    for source in refs[:count]:
        block = source[...].reshape(source.shape[-2:])
        columns = pl.ds(start, block.shape[1])
        if len(target.shape) == 3:
            target[0, :, columns] = block.astype(target.dtype)
        else:
            target[:, columns] = block.astype(target.dtype)
        start += block.shape[1]


def to_parts(sources, parts, dtype, others=()):
    rows = sources[0][0].shape[0]

    def spec(section, width):
        return pl.BlockSpec((rows, width), lambda p: (0, section * parts + p))

    total = sum(width for _, _, width in sources)
    return pl.pallas_call(
        functools.partial(copy_columns, len(sources)),
        grid=(parts,),
        in_specs=[spec(section, width) for _, section, width in sources]
        + [pl.BlockSpec(memory_space=pl.ANY)] * len(others),
        out_specs=pl.BlockSpec((1, rows, total), lambda p: (p, 0, 0)),
        out_shape=jax.ShapeDtypeStruct((parts, rows, total), dtype),
        cost_estimate=NO_COST,
    )(*[array for array, _, _ in sources], *others)


def updown_from_parts(slabs):
    parts, rows, width = slabs.shape
    units = width // 2

    def kernel(slabs_ref, out_ref):
        for p in range(parts):
            out_ref[:, p * units : (p + 1) * units] = slabs_ref[p].astype(f32)

    return pl.pallas_call(
        kernel,
        grid=(2,),
        in_specs=[pl.BlockSpec((parts, rows, units), lambda half: (0, 0, half))],
        out_specs=pl.BlockSpec((rows, parts * units), lambda half: (0, half)),
        out_shape=jax.ShapeDtypeStruct((rows, parts * width), f32),
        compiler_params=pltpu.CompilerParams(vmem_limit_bytes=32 * 2**20),
        cost_estimate=NO_COST,
    )(slabs)


def mixer_from_parts(slabs, width):
    parts, rows, _ = slabs.shape

    def kernel(slabs_ref, qkv_ref, gate_ref, strength_ref):
        for p in range(parts):
            for section in range(4):
                block = slabs_ref[p, :, section * width : (section + 1) * width].astype(f32)
                if section < 3:
                    start = (section * parts + p) * width
                    qkv_ref[:, start : start + width] = block
                else:
                    gate_ref[:, p * width : (p + 1) * width] = block
            last = slabs_ref[p, :, 4 * width :].astype(f32)
            strength_ref[:, p * SMALL : (p + 1) * SMALL] = last

    widths = [3 * parts * width, parts * width, parts * SMALL]
    return pl.pallas_call(
        kernel,
        out_shape=[jax.ShapeDtypeStruct((rows, size), f32) for size in widths],
        compiler_params=pltpu.CompilerParams(vmem_limit_bytes=32 * 2**20),
        cost_estimate=NO_COST,
    )(slabs)


def own_order(values, parts, copies):
    size = values.shape[1] // (parts * copies)
    pieces = [
        values[:, (t * parts + m) * size : (t * parts + m + 1) * size]
        for m in range(parts)
        for t in range(copies)
    ]
    return jnp.concatenate(pieces, 1)


def total_of(own_ref, received_refs):
    total = own_ref[...]
    for ref in received_refs:
        total = total + ref[...].astype(f32)
    return total


def row_scale(values):
    return lax.rsqrt(jnp.mean(values * values, -1, keepdims=True) + 1e-06)


def norm_slope(values, scale, gain, grad):
    mean = jnp.mean(gain * grad * values, -1, keepdims=True)
    return scale * gain * grad - values * (scale * scale * scale * mean)


def hidden_kernel(own_ref, *refs):
    *received, input_ref, gain_ref, hidden_ref, normed_ref = refs
    hidden = input_ref[...].astype(f32) + total_of(own_ref, received)
    hidden_ref[...] = hidden
    normed_ref[...] = (hidden * row_scale(hidden) * gain_ref[...]).astype(bf)


def hidden_back_kernel(own_ref, *refs):
    *received, hidden_ref, gain_ref, cot_ref, d_hidden_ref, d_mixed_ref, d_gain_ref = refs
    grad = total_of(own_ref, received)
    hidden = hidden_ref[...]
    scale = row_scale(hidden)

    @pl.when(pl.program_id(0) == 0)
    def _():
        d_gain_ref[...] = jnp.zeros_like(d_gain_ref)

    d_gain_ref[...] += jnp.sum(grad * hidden * scale, 0, keepdims=True)
    d_hidden = cot_ref[...].astype(f32) + norm_slope(hidden, scale, gain_ref[...], grad)
    d_hidden_ref[...] = d_hidden
    d_mixed_ref[...] = d_hidden.astype(bf)


def input_back_kernel(parts, copies, own_ref, *refs):
    *received, input_ref, gain_ref, d_hidden_ref, out_ref = refs
    grad = total_of(own_ref, received)
    values = input_ref[...].astype(f32)
    slope = norm_slope(values, row_scale(values), gain_ref[...], grad)
    out_ref[...] = own_order(d_hidden_ref[...] + slope, parts, copies).astype(bf)


def block_out_kernel(parts, copies, own_ref, *refs):
    *received, hidden_ref, out_ref = refs
    total = hidden_ref[...] + total_of(own_ref, received)
    out_ref[...] = own_order(total, parts, copies).astype(bf)


def last_sum(sides, others, parts, copies):
    rows, columns = sides[0].shape

    def kernel(*refs):
        first, first_other, second, second_other = (ref[...].astype(f32) for ref in refs[:4])
        total = jnp.concatenate([first + first_other, second + second_other], 1)
        refs[-1][...] = own_order(total, parts, copies)

    vmem = pl.BlockSpec(memory_space=pltpu.VMEM)
    return pl.pallas_call(
        kernel,
        in_specs=[vmem] * 4 + [pl.BlockSpec(memory_space=pl.ANY)] * len(others),
        out_specs=vmem,
        out_shape=jax.ShapeDtypeStruct((rows, 2 * columns), f32),
        compiler_params=pltpu.CompilerParams(vmem_limit_bytes=32 * 2**20),
        cost_estimate=NO_COST,
    )(*sides, *others)


def by_rows(kernel, arrays, outs, block=64):
    def spec(shape):
        if shape[0] == 1:
            return pl.BlockSpec(shape, lambda i: (0, 0))
        return pl.BlockSpec((block, shape[1]), lambda i: (i, 0))

    return pl.pallas_call(
        kernel,
        grid=(GROUP_ROWS // block,),
        in_specs=[spec(array.shape) for array in arrays],
        out_specs=[spec(shape) for shape, _ in outs],
        out_shape=[jax.ShapeDtypeStruct(shape, dtype) for shape, dtype in outs],
        compiler_params=pltpu.CompilerParams(dimension_semantics=("arbitrary",)),
        cost_estimate=NO_COST,
    )(*arrays)


def body(
    block_in,
    out_grad,
    norm1_gain,
    conv_weight,
    head_gain,
    qkv_weight,
    beta_weight,
    gate_weight,
    out_weight,
    norm2_gain,
    updown_weight,
    down_weight,
    seq_blocks,
    lead_blocks,
):
    devices = lax.axis_size("dp")
    parts = MODEL
    copies = devices // parts
    part = lax.axis_index("dp") // copies
    copy = lax.axis_index("dp") % copies
    rows_own = qkv_weight.shape[0]
    width = D // parts
    units = FF // parts
    heads_part = HEADS // parts
    wide = 4 * width + SMALL
    model_groups = [[m * copies + t for m in range(parts)] for t in range(copies)]
    copy_groups = [[m * copies + t for t in range(copies)] for m in range(parts)]

    def exchange(values):
        return lax.all_to_all(
            values, "dp", split_axis=0, concat_axis=0, axis_index_groups=model_groups, tiled=True
        )

    def shift(values, step):
        pairs = [
            (m * copies + t, (m + step) % parts * copies + t)
            for m in range(parts)
            for t in range(copies)
        ]
        return lax.ppermute(values, "dp", pairs)

    def exchange_apart(values, before, after=()):
        cut = [
            lax.dynamic_index_in_dim(values, (part + step) % parts, 0, keepdims=False)
            for step in range(1, parts)
        ]
        received = [shift(piece, step) for step, piece in enumerate(tie_all(cut, *before), 1)]
        return assemble(part, values, received, after)

    def gather_rows(values):
        return [values] + [shift(values, step) for step in range(1, parts)]

    def scatter_rows(terms):
        return [terms[0]] + [shift(block, -step) for step, block in enumerate(terms[1:], 1)]

    def gather_copies(values):
        return lax.all_gather(values, "dp", axis=0, axis_index_groups=copy_groups, tiled=True)

    def scatter_copies(values):
        return lax.psum_scatter(
            values.astype(bf),
            "dp",
            scatter_dimension=0,
            axis_index_groups=copy_groups,
            tiled=True,
        )

    def halves_across(values, bit, axis):
        pairs = [(i, i ^ (1 << bit)) for i in range(devices)]
        side = (copy >> bit) & 1
        own = lax.dynamic_index_in_dim(values, side, axis, keepdims=False)
        other = lax.dynamic_index_in_dim(values, 1 - side, axis, keepdims=False)
        return own, lax.ppermute(other, "dp", pairs)

    def halve(values, bit, axis, *others):
        own, received = halves_across(values, bit, axis)
        if others:
            received = tie(received, *others)
        return (own.astype(f32) + received.astype(f32)).astype(bf)

    by_halves = copies == 8

    def halve_cores(values, *others):
        if not by_halves:
            return values
        rows, columns = values.shape
        return halve(values.reshape(2, 2, 2, rows // 8, columns), 0, 2, *others)

    def halve_first(values):
        if not by_halves:
            return [values]
        middle = values.shape[-1] // 2
        return [halve(values[..., :middle], 1, 1), halve(values[..., middle:], 2, 0)]

    def halve_second(values, *others):
        if not by_halves:
            return from_wire(scatter_copies(values[0]).astype(f32))
        sides = halves_across(values[0], 2, 0) + halves_across(values[1], 1, 0)
        return last_sum(sides, others, parts, copies)

    def to_wire(values):
        return values.reshape(-1, parts, copies, rows_own).swapaxes(1, 2).reshape(-1, D)

    def from_wire(values):
        return values.reshape(-1, copies, parts, rows_own).swapaxes(1, 2).reshape(-1, D)

    w_out_own = to_wire(out_weight.astype(bf))
    w_out = gather_copies(w_out_own)
    strengths = beta_weight.reshape(rows_own, parts, heads_part)
    strengths = jnp.pad(strengths, ((0, 0), (0, 0), (0, SMALL - heads_part)))
    strengths = tie(strengths.reshape(rows_own, parts * SMALL), w_out_own)
    pieces = [(qkv_weight, section, width) for section in range(3)]
    pieces = to_parts(pieces + [(gate_weight, 0, width), (strengths, 0, SMALL)], parts, bf)
    mixer_pieces = tie(exchange(pieces), w_out)
    w_mixer = gather_copies(mixer_pieces.reshape(parts * rows_own, wide))
    inputs = tie(to_wire(block_in), mixer_pieces)
    input_rows = gather_rows(inputs)

    lanes = -(-3 * rows_own // 128) * 128
    numbers = jnp.concatenate([seq_blocks[0], lead_blocks]).astype(f32)
    small = [conv_weight.T, norm1_gain[None], head_gain[None], norm2_gain[None], numbers[None]]
    small = [jnp.pad(rows, ((0, 0), (0, lanes - rows.shape[1]))) for rows in small]
    small = jnp.pad(jnp.concatenate(small, 0).astype(bf), ((0, 2 * KERNEL), (0, 0)))
    small = jnp.broadcast_to(small[None], (devices,) + small.shape)
    small = lax.all_to_all(tie(small, *input_rows[1:]), "dp", 0, 0, tiled=True)
    taps = small[:, :KERNEL, : 3 * rows_own].swapaxes(0, 1).reshape(KERNEL, 3, parts, width)
    taps = lax.dynamic_index_in_dim(taps, part, 2, keepdims=False).reshape(KERNEL, 3 * width)
    gain_one, head_full, gain_two = (
        small[:, KERNEL + i, :rows_own].reshape(1, D).astype(f32) for i in range(3)
    )
    gain_one, gain_two = to_wire(gain_one), to_wire(gain_two)
    head_part = lax.dynamic_slice_in_dim(head_full, part * width, width, 1)
    params = jnp.concatenate([taps.astype(f32), jnp.pad(head_part, ((0, 0), (0, 2 * width)))], 0)
    params = jnp.pad(params, ((0, KERNEL - 1), (0, 0)))
    numbers = small[:, KERNEL + 3, :3].astype(f32).astype(jnp.int32)
    layouts = block_layouts(numbers[:, 0], numbers[:, 1], numbers[:, 2])
    layouts = layouts.reshape(parts, copies, 4)
    layouts = lax.dynamic_index_in_dim(layouts, copy, 1, keepdims=False)
    wanted = (part - jnp.arange(parts)) % parts
    wanted = (wanted[:, None] == jnp.arange(parts)).astype(f32)
    layouts = jnp.sum(wanted[:, :, None] * layouts, 1)

    pieces = [(updown_weight, half, units) for half in range(2)]
    updown_pieces = to_parts(pieces, parts, bf, [mixer_pieces])
    w_down_own = to_wire(down_weight.astype(bf))
    w_down = gather_copies(tie(w_down_own, *input_rows[1:]))
    cotangent_own = to_wire(out_grad)

    cotangent = lax.all_gather(
        tie(cotangent_own, *input_rows[1:]), "dp", axis=0, axis_index_groups=model_groups, tiled=True
    )
    gain_first = tie(gain_one, w_down_own, cotangent_own, updown_pieces)
    normed, pre = normed_product(input_rows, gain_first, w_mixer)
    mixed, *kept = mixer_forward(layouts, pre, params, width)
    out_terms = product_blocks(mixed, w_out)
    updown_pieces = exchange_apart(updown_pieces, input_rows[1:], out_terms[1:])
    w_updown = gather_copies(updown_pieces.reshape(parts * rows_own, 2 * units))
    stream = ((GROUP_ROWS, D), f32)
    narrow = ((GROUP_ROWS, D), bf)
    hidden, normed_two = by_rows(
        hidden_kernel,
        scatter_rows(out_terms) + [inputs, gain_two],
        [stream, narrow],
    )
    cotangent = from_own(part, cotangent)
    normed_two = jnp.concatenate(gather_rows(normed_two), 0)

    def swiglu_units(updown):
        return jax.nn.silu(updown[:, :units]) * updown[:, units:]

    updown = plain_product(normed_two, w_updown)
    active, swiglu_back = jax.vjp(swiglu_units, updown)
    active = active.astype(bf)
    d_active = transposed_product(cotangent, w_down)
    d_updown = swiglu_back(d_active)[0].astype(bf)
    d_normed_two = product_blocks(d_updown, w_updown, transposed=True)
    active = tie(active, *d_normed_two[1:])
    down_terms = grad_product(active, cotangent)
    updown_terms = grad_product(normed_two, tie(d_updown, down_terms))
    gain_late = tie(gain_two, updown_terms)
    d_normed_two = scatter_rows(d_normed_two)
    updown_grad = scatter_copies(tie(updown_terms, gain_late, *d_normed_two[1:]))
    d_hidden, d_mixed, gain_two_grad = by_rows(
        hidden_back_kernel,
        d_normed_two + [hidden, gain_late, cotangent_own],
        [stream, narrow, ((1, D), f32)],
    )


    out_terms = product_blocks(tie(active, d_mixed), w_down)
    down_terms = tie(down_terms, *out_terms[1:])
    d_mixed = gather_rows(d_mixed)
    late = tie(params, *out_terms)
    out_terms[1:] = tie_all(out_terms[1:], *d_mixed[1:])
    d_pre, d_params = mixer_backward(layouts, pre, late, w_out, d_mixed, kept, width)
    mixer_terms = tie(grad_product(normed, d_pre, micros=20), updown_grad)
    mixer_grad = scatter_copies(mixer_terms)

    d_normed_terms = product_blocks(
        tie(d_pre, mixer_terms), w_mixer, transposed=True, micros=150
    )
    hidden = tie(hidden, d_normed_terms[0])
    (block_out,) = by_rows(
        functools.partial(block_out_kernel, parts, copies),
        scatter_rows(out_terms) + [hidden],
        [narrow],
    )
    d_normed_terms[1:] = tie_all(d_normed_terms[1:], block_out)
    d_normed = scatter_rows(d_normed_terms)
    down_grad = halve_first(halve_cores(down_terms, *d_normed_terms[1:]))
    gain_one_grad = 0.0
    for values, terms in zip(input_rows, d_normed_terms):
        values = values.astype(f32)
        terms = terms.astype(f32) * (values * row_scale(values))
        gain_one_grad = gain_one_grad + jnp.sum(terms, 0, keepdims=True)

    d_params = tie(d_params, mixer_terms)
    here = (jnp.arange(parts) == part).astype(f32)[:, None]
    taps_grad = d_params[:KERNEL].reshape(KERNEL, 3, 1, width) * here
    taps_grad = taps_grad.reshape(KERNEL, parts, copies, 3, rows_own).transpose(1, 2, 3, 0, 4)
    taps_grad = taps_grad.reshape(devices, 3 * KERNEL, rows_own)
    head_grad = (d_params[KERNEL, :width] * here).reshape(devices, 1, rows_own)
    gain_grads = [
        grad.reshape(copies, parts, 1, rows_own).swapaxes(0, 1).reshape(devices, 1, rows_own)
        for grad in (gain_one_grad, gain_two_grad)
    ]
    small_grad = jnp.concatenate([taps_grad, head_grad] + gain_grads, 1)
    d_mixed = jnp.concatenate([tie(d_mixed[0], d_normed_terms[0])] + d_mixed[1:], 0)
    out_grads = grad_product(mixed, d_mixed)
    late = tie(gain_one, out_grads, *down_grad)
    (input_grad,) = by_rows(
        functools.partial(input_back_kernel, parts, copies),
        d_normed + [inputs, late, d_hidden],
        [narrow],
    )
    small_grad = jnp.pad(tie(small_grad, input_grad), ((0, 0), (0, 1), (0, 128 - rows_own)))
    small_grad = jnp.sum(lax.all_to_all(small_grad, "dp", 0, 0, tiled=True), 0)[:, :rows_own]
    taps_shard = small_grad[: 3 * KERNEL].reshape(3, KERNEL, rows_own).swapaxes(1, 2)
    taps_shard = taps_shard.reshape(3 * rows_own, KERNEL)
    head_shard, gain_one_shard, gain_two_shard = small_grad[3 * KERNEL : 3 * KERNEL + 3]

    updown_grad = tie(updown_grad, mixer_terms).reshape(parts, rows_own, 2 * units)
    updown_grad = exchange(updown_grad)
    mixer_grad = tie(mixer_grad, updown_grad, input_grad)
    updown_shard = updown_from_parts(tie(updown_grad, mixer_grad))
    down_shard = halve_second(tie_all(down_grad, input_grad), mixer_grad)
    out_grads = tie(halve_cores(tie(out_grads, input_grad)), mixer_grad)
    out_shard = halve_second(halve_first(out_grads))
    mixer_grad = exchange(mixer_grad.reshape(parts, rows_own, wide))
    qkv_shard, gate_shard, strengths = mixer_from_parts(mixer_grad, width)
    beta_shard = strengths.reshape(rows_own, parts, SMALL)[:, :, :heads_part]
    return (
        block_out,
        input_grad,
        gain_one_shard,
        taps_shard,
        head_shard,
        qkv_shard,
        beta_shard.reshape(rows_own, HEADS),
        gate_shard,
        out_shard,
        gain_two_shard,
        updown_shard,
        down_shard,
    )


def solution(mesh):
    placed = (
        P("dp", None),
        P("dp", None),
        P("dp"),
        P("dp", None),
        P("dp"),
        P("dp", None),
        P("dp", None),
        P("dp", None),
        P("dp", None),
        P("dp"),
        P("dp", None),
        P("dp", None),
        P("dp", None),
        P("dp"),
    )
    return jax.shard_map(
        body,
        mesh=mesh,
        in_specs=placed,
        out_specs=(
            P("dp", None),
            P("dp", None),
            P("dp"),
            P("dp", None),
            P("dp"),
            P("dp", None),
            P("dp", None),
            P("dp", None),
            P("dp", None),
            P("dp"),
            P("dp", None),
            P("dp", None),
        ),
        check_vma=False,
    )
```

```python
import functools

import jax
import jax.numpy as jnp
from jax import lax
from jax.experimental import pallas as pl
from jax.experimental.pallas import tpu as pltpu
from jax.sharding import PartitionSpec as P

D = 2048
HEADS = 16
HEAD_DIM = 128
FF = 5632
KERNEL = 4
BLOCK_ROWS = 64
BLOCKS_DEV = 2
GROUP_ROWS = BLOCK_ROWS * BLOCKS_DEV
SMALL = 128
MODEL = 4

f32 = jnp.float32
bf = jnp.bfloat16


def block_layouts(first, second, lead):
    def doc(block):
        in_first = (block >= lead) & (block < lead + first)
        in_second = (block >= lead + first) & (block < lead + first + second)
        return jnp.where(in_first, 1, jnp.where(in_second, 2, 0))

    starts = (lead == 1) | (lead + first == 1) & (second > 0)
    columns = [doc(0) > 0, doc(1) > 0, doc(0) == doc(1), ~starts]
    return jnp.stack(columns, 1).astype(f32)


def plain_product(left, right):
    return jnp.dot(left, right, preferred_element_type=f32)


def rows_product(left, right):
    return lax.dot_general(left, right, (((0,), (0,)), ((), ())), preferred_element_type=f32)


def transposed_product(left, right):
    return lax.dot_general(left, right, (((1,), (1,)), ((), ())), preferred_element_type=f32)


def halves(values):
    high = values.astype(bf)
    return high, (values - high.astype(f32)).astype(bf)


def exact(left, right, left_dim, right_dim):
    left_high, left_low = left if isinstance(left, tuple) else halves(left)
    right_high, right_low = right if isinstance(right, tuple) else halves(right)
    return lax.dot_general(
        jnp.concatenate([left_high, left_high, left_low], left_dim),
        jnp.concatenate([right_high, right_low, right_high], right_dim),
        (((left_dim,), (right_dim,)), ((), ())),
        preferred_element_type=f32,
    )


def stacked(first, second):
    return tuple(jnp.concatenate([a, b], 0) for a, b in zip(first, second))


class Tile:
    def __init__(self, layout_ref, group):
        live_first, live_second, same, persist = (layout_ref[group, i] for i in range(4))
        shape = (GROUP_ROWS, HEAD_DIM)
        row = lax.broadcasted_iota(jnp.int32, shape, 0)
        col = lax.broadcasted_iota(jnp.int32, shape, 1)
        late = row >= BLOCK_ROWS
        self.row, self.col = row, col
        self.live = jnp.where(late, live_second, live_first)
        self.taps = [None] + [
            jnp.where(
                row < offset,
                0.0,
                jnp.where(late & (row < BLOCK_ROWS + offset), same, 1.0),
            )
            for offset in range(1, KERNEL)
        ]
        cross = jnp.where(late & (col < BLOCK_ROWS), persist, 1.0)
        self.lower = jnp.where(row > col, cross, 0.0)
        self.lower_full = jnp.where(row >= col, cross, 0.0)

    def earlier(self, values, offset):
        return pltpu.roll(values, offset, 0) * self.taps[offset]

    def later(self, values, offset):
        return pltpu.roll(values * self.taps[offset], GROUP_ROWS - offset, 0)


def convolve(tile, values, taps):
    total = values * taps[0]
    for offset in range(1, KERNEL):
        total = total + tile.earlier(values, offset) * taps[offset]
    return total


def unit_scale(values):
    return lax.rsqrt(jnp.sum(values * values, -1, keepdims=True) + 1e-06)


def head_columns(part_width, section, head):
    return pl.ds(section * part_width + head * HEAD_DIM, HEAD_DIM)


def unit_inverses(tile, lowers):
    eye = jnp.where(tile.row == tile.col, 1.0, 0.0)
    inverses = None
    size = 1
    while size < GROUP_ROWS:
        pair = tile.row // (2 * size) == tile.col // (2 * size)
        split = pair & (tile.row // size != tile.col // size)
        parts = [jnp.where(split, lower, 0.0) for lower in lowers]
        if inverses is None:
            inverses = [eye - part for part in parts]
        else:
            kept = [halves(inverse) for inverse in inverses]
            inner = [exact(part, known, 1, 0) for part, known in zip(parts, kept)]
            outer = [exact(known, value, 1, 0) for known, value in zip(kept, inner)]
            inverses = [inverse - value for inverse, value in zip(inverses, outer)]
        size *= 2
    return inverses


def mixer_forward_kernel(
    layout_ref, pre_ref, param_ref, mixed_ref, inverse_ref, score_ref, solved_ref, out_ref
):
    width = mixed_ref.shape[1]
    heads = range(width // HEAD_DIM)
    tile = Tile(layout_ref, pl.program_id(0))
    queries, keys, values, strengths = [], [], [], []
    for head in heads:
        parts = []
        for section in range(3):
            columns = head_columns(width, section, head)
            taps = [param_ref[offset : offset + 1, columns] for offset in range(KERNEL)]
            convolved = convolve(tile, pre_ref[:, columns], taps)
            parts.append(convolved * jax.nn.sigmoid(convolved))
        queries.append(parts[0] * (unit_scale(parts[0]) * HEAD_DIM**-0.5))
        keys.append(parts[1] * unit_scale(parts[1]))
        values.append(parts[2])
        start = 4 * width + head
        strengths.append(jax.nn.sigmoid(pre_ref[:, start : start + 1]) * tile.live)
    lowers, scores = [], []
    for head in heads:
        key_halves = halves(keys[head])
        both = exact(stacked(key_halves, halves(queries[head])), key_halves, 1, 1)
        lowers.append(both[:GROUP_ROWS] * strengths[head] * tile.lower)
        scores.append(both[GROUP_ROWS:] * tile.lower_full)
    inverses = unit_inverses(tile, lowers)
    solved = [exact(inverses[head], values[head] * strengths[head], 1, 0) for head in heads]
    outs = [exact(scores[head], solved[head], 1, 0) for head in heads]
    for head in heads:
        out = outs[head]
        scaled = out * lax.rsqrt(jnp.mean(out * out, -1, keepdims=True) + 1e-05)
        gate = pre_ref[:, head_columns(width, 3, head)]
        gain = param_ref[KERNEL : KERNEL + 1, head_columns(width, 0, head)]
        mixed = scaled * gain * (gate * jax.nn.sigmoid(gate)) * tile.live
        mixed_ref[:, head_columns(width, 0, head)] = mixed.astype(bf)
        inverse_ref[head] = inverses[head]
        score_ref[head] = scores[head]
        solved_ref[head] = solved[head]
        out_ref[head] = out


def mixer_backward_kernel(
    layout_ref,
    pre_ref,
    param_ref,
    weight_ref,
    inverse_ref,
    score_ref,
    solved_ref,
    out_ref,
    *refs,
):
    *mixed_refs, d_pre_ref, d_param_ref, grad_ref = refs
    width = grad_ref.shape[1]
    heads = range(width // HEAD_DIM)
    tile = Tile(layout_ref, pl.program_id(0))
    for group, mixed_ref in enumerate(mixed_refs):

        @pl.when(pl.program_id(0) == group)
        def _():
            grad_ref[...] = transposed_product(mixed_ref[...], weight_ref[...])

    @pl.when(pl.program_id(0) == 0)
    def _():
        d_param_ref[...] = jnp.zeros_like(d_param_ref)

    def along(values):
        return jnp.sum(values, -1, keepdims=True)

    d_outs = []
    for head in heads:
        columns = head_columns(width, 0, head)
        d_mixed = grad_ref[:, columns] * tile.live
        out = out_ref[head]
        scale = lax.rsqrt(jnp.mean(out * out, -1, keepdims=True) + 1e-05)
        scaled = out * scale
        gate = pre_ref[:, head_columns(width, 3, head)]
        gate_open = jax.nn.sigmoid(gate)
        gain = param_ref[KERNEL : KERNEL + 1, columns]
        gated = d_mixed * (gate * gate_open)
        d_param_ref[KERNEL : KERNEL + 1, columns] += jnp.sum(gated * scaled, 0, keepdims=True)
        d_gate = d_mixed * scaled * gain * (gate_open * (1.0 + gate * (1.0 - gate_open)))
        d_pre_ref[:, head_columns(width, 3, head)] = d_gate.astype(bf)
        d_scaled = gated * gain
        mean = jnp.mean(d_scaled * out, -1, keepdims=True)
        d_outs.append(scale * d_scaled - out * (scale * scale * scale * mean))
    d_out_halves = [halves(value) for value in d_outs]
    solved_halves = [halves(solved_ref[head]) for head in heads]
    d_solved = [exact(score_ref[head], d_out_halves[head], 0, 0) for head in heads]
    d_scores = [
        exact(d_out_halves[head], solved_halves[head], 1, 1) * tile.lower_full for head in heads
    ]
    d_inner = [exact(inverse_ref[head], d_solved[head], 0, 0) for head in heads]
    d_lowers = [exact(d_inner[head], solved_halves[head], 1, 1) * -tile.lower for head in heads]
    d_beta = jnp.zeros((GROUP_ROWS, SMALL), f32)
    for head in heads:
        pres, convolved, opened, active = [], [], [], []
        for section in range(3):
            columns = head_columns(width, section, head)
            taps = [param_ref[offset : offset + 1, columns] for offset in range(KERNEL)]
            pres.append(pre_ref[:, columns])
            convolved.append(convolve(tile, pres[section], taps))
            opened.append(jax.nn.sigmoid(convolved[section]))
            active.append(convolved[section] * opened[section])
        query_scale = unit_scale(active[0])
        key_scale = unit_scale(active[1])
        query_unit = active[0] * query_scale
        key = active[1] * key_scale
        start = 4 * width + head
        opening = jax.nn.sigmoid(pre_ref[:, start : start + 1])
        strength = opening * tile.live
        d_both = stacked(halves(d_lowers[head]), halves(d_scores[head]))
        by_key = exact(d_both, key, 1, 0)
        d_query = by_key[GROUP_ROWS:] * HEAD_DIM**-0.5
        from_lower = by_key[:GROUP_ROWS]
        weighted = stacked(halves(key * strength), halves(query_unit * HEAD_DIM**-0.5))
        d_key = strength * from_lower + exact(d_both, weighted, 0, 0)
        d_strength = along(d_inner[head] * active[2] + from_lower * key)
        d_value = d_inner[head] * strength
        d_opening = d_strength * (opening * (1.0 - opening)) * tile.live
        d_beta = d_beta + jnp.where(tile.col == head, d_opening, 0.0)
        d_active = [
            (d_query - query_unit * along(query_unit * d_query)) * query_scale,
            (d_key - key * along(key * d_key)) * key_scale,
            d_value,
        ]
        for section in range(3):
            columns = head_columns(width, section, head)
            taps = [param_ref[offset : offset + 1, columns] for offset in range(KERNEL)]
            slope = opened[section] * (1.0 + convolved[section] * (1.0 - opened[section]))
            d_convolved = d_active[section] * slope
            d_pre = d_convolved * taps[0]
            sums = [jnp.sum(d_convolved * pres[section], 0, keepdims=True)]
            for offset in range(1, KERNEL):
                d_pre = d_pre + tile.later(d_convolved, offset) * taps[offset]
                sums.append(
                    jnp.sum(d_convolved * tile.earlier(pres[section], offset), 0, keepdims=True)
                )
            d_param_ref[0:KERNEL, columns] += jnp.concatenate(sums, 0)
            d_pre_ref[:, columns] = d_pre.astype(bf)
    d_pre_ref[:, 4 * width :] = d_beta.astype(bf)


NO_COST = pl.CostEstimate(flops=0, bytes_accessed=0, transcendentals=0)


def call(kernel, operands, in_specs, out_specs, out_shape, grid=(), scratch=(), micros=0):
    results = pl.pallas_call(
        kernel,
        grid=grid,
        in_specs=in_specs,
        out_specs=out_specs,
        out_shape=out_shape,
        scratch_shapes=scratch,
        compiler_params=pltpu.CompilerParams(
            dimension_semantics=("arbitrary",) * len(grid), vmem_limit_bytes=48 * 2**20
        ),
        cost_estimate=pl.CostEstimate(
            flops=micros * 10**9, bytes_accessed=0, transcendentals=0
        ),
    )(*operands)
    return list(results)


def whole(array):
    return pl.BlockSpec(array.shape, lambda *step: (0,) * len(array.shape))


def mixer_specs(width):
    wide = 4 * width + SMALL
    heads = width // HEAD_DIM
    layout = pl.BlockSpec(memory_space=pltpu.SMEM)
    pre = pl.BlockSpec((GROUP_ROWS, wide), lambda group: (group, 0))
    param = pl.BlockSpec((2 * KERNEL, 3 * width), lambda group: (0, 0))
    narrow = pl.BlockSpec((GROUP_ROWS, width), lambda group: (group, 0))
    square = pl.BlockSpec((heads, GROUP_ROWS, HEAD_DIM), lambda group: (group, 0, 0))
    return layout, pre, param, narrow, square


def mixer_forward(layout, pre, params, width):
    groups = layout.shape[0]
    layout_spec, pre_spec, param_spec, narrow, square = mixer_specs(width)
    squares = pltpu.HBM((groups * width // HEAD_DIM, GROUP_ROWS, HEAD_DIM), f32)
    return call(
        mixer_forward_kernel,
        [layout, pre, params],
        [layout_spec, pre_spec, param_spec],
        [narrow] + [square] * 4,
        [jax.ShapeDtypeStruct((groups * GROUP_ROWS, width), bf)] + [squares] * 4,
        (groups,),
    )


def mixer_backward(layout, pre, params, weight, d_mixed, kept, width):
    groups = layout.shape[0]
    layout_spec, pre_spec, param_spec, _, square = mixer_specs(width)
    kept = [pltpu.with_memory_space_constraint(array, pltpu.HBM) for array in kept]
    return call(
        mixer_backward_kernel,
        [layout, pre, params, weight, *kept, *d_mixed],
        [layout_spec, pre_spec, param_spec, whole(weight)]
        + [square] * 4
        + [whole(block) for block in d_mixed],
        [pre_spec, param_spec],
        [jax.ShapeDtypeStruct(pre.shape, bf), jax.ShapeDtypeStruct(params.shape, f32)],
        (groups,),
        [pltpu.VMEM((GROUP_ROWS, width), f32)],
        micros=60,
    )


def first_kernel(gain_ref, weight_ref, *refs):
    *value_refs, normed_ref, out_ref, scale_ref, total_ref = refs
    step, depth = pl.program_id(0), weight_ref.shape[0]

    @pl.when(step == 0)
    def _():
        for group, ref in enumerate(value_refs):
            values = ref[...].astype(f32)
            scale = lax.rsqrt(jnp.mean(values * values, -1, keepdims=True) + 1e-06)
            rows = pl.ds(group * GROUP_ROWS, GROUP_ROWS)
            scale_ref[rows, :] = jnp.broadcast_to(scale, (GROUP_ROWS, 128))
        total_ref[...] = jnp.zeros_like(total_ref)

    columns = pl.ds(pl.multiple_of(step * depth, depth), depth)
    for group, ref in enumerate(value_refs):
        rows = pl.ds(group * GROUP_ROWS, GROUP_ROWS)
        values = ref[:, columns].astype(f32) * scale_ref[rows, :1] * gain_ref[...]
        normed_ref[rows, :] = values.astype(bf)
    total_ref[...] += plain_product(normed_ref[...], weight_ref[...])

    @pl.when(step == pl.num_programs(0) - 1)
    def _():
        out_ref[...] = total_ref[...]


def normed_product(blocks, gain, weight, depth=512):
    rows, (features, columns) = len(blocks) * GROUP_ROWS, weight.shape
    return call(
        first_kernel,
        [gain, weight, *blocks],
        [
            pl.BlockSpec((1, depth), lambda step: (0, step)),
            pl.BlockSpec((depth, columns), lambda step: (step, 0)),
        ]
        + [whole(block) for block in blocks],
        [
            pl.BlockSpec((rows, depth), lambda step: (0, step)),
            pl.BlockSpec((rows, columns), lambda step: (0, 0)),
        ],
        [
            jax.ShapeDtypeStruct((rows, features), bf),
            jax.ShapeDtypeStruct((rows, columns), f32),
        ],
        (features // depth,),
        [pltpu.VMEM((rows, 128), f32), pltpu.VMEM((rows, columns), f32)],
    )


def product_blocks(left, right, transposed=False, block=512, micros=0):
    product = transposed_product if transposed else plain_product
    columns = right.shape[0] if transposed else right.shape[1]
    groups = left.shape[0] // GROUP_ROWS

    def kernel(left_ref, right_ref, *out_refs):
        total = product(left_ref[...], right_ref[...])
        for group, ref in enumerate(out_refs):
            ref[...] = total[group * GROUP_ROWS : (group + 1) * GROUP_ROWS].astype(ref.dtype)

    if transposed:
        right_spec = pl.BlockSpec((block, right.shape[1]), lambda step: (step, 0))
    else:
        right_spec = pl.BlockSpec((right.shape[0], block), lambda step: (0, step))
    return call(
        kernel,
        [left, right],
        [whole(left), right_spec],
        [pl.BlockSpec((GROUP_ROWS, block), lambda step: (0, step))] * groups,
        [
            jax.ShapeDtypeStruct((GROUP_ROWS, columns), bf if group else f32)
            for group in range(groups)
        ],
        (columns // block,),
        micros=micros,
    )


def grad_product(left, right, block=256, micros=0):
    rows, features = left.shape
    if features % block:
        block = 128

    def kernel(left_ref, right_ref, out_ref):
        out_ref[...] = rows_product(left_ref[...], right_ref[...]).astype(bf)

    return call(
        kernel,
        [left, right],
        [pl.BlockSpec((rows, block), lambda step: (0, step)), whole(right)],
        [pl.BlockSpec((block, right.shape[1]), lambda step: (step, 0))],
        [pltpu.HBM((features, right.shape[1]), bf)],
        (features // block,),
        micros=micros,
    )[0]


def from_own(part, values):
    groups = values.shape[0] // GROUP_ROWS

    def kernel(part_ref, values_ref, out_ref):
        for step in range(groups):
            source = lax.rem(part_ref[0] + groups - step, groups) * GROUP_ROWS
            rows = pl.ds(pl.multiple_of(source, GROUP_ROWS), GROUP_ROWS)
            out_ref[step * GROUP_ROWS : (step + 1) * GROUP_ROWS] = values_ref[rows]

    return call(
        kernel,
        [part.reshape(1).astype(jnp.int32), values],
        [pl.BlockSpec(memory_space=pltpu.SMEM), whole(values)],
        [whole(values)],
        [jax.ShapeDtypeStruct(values.shape, values.dtype)],
        (1,),
    )[0]


def tie_all(values, *others):
    anywhere = pl.BlockSpec(memory_space=pl.ANY)
    others = [
        pltpu.with_memory_space_constraint(other, pltpu.HBM) if other.size > 2**21 else other
        for other in others
    ]
    tied = pl.pallas_call(
        lambda *refs: None,
        in_specs=[anywhere] * (len(values) + len(others)),
        out_specs=[anywhere] * len(values),
        out_shape=[
            (pltpu.HBM if value.size > 2**21 else jax.ShapeDtypeStruct)(value.shape, value.dtype)
            for value in values
        ],
        input_output_aliases={i: i for i in range(len(values))},
        cost_estimate=NO_COST,
    )(*values, *others)
    return list(tied)


def tie(value, *others):
    return tie_all([value], *others)[0]


def assemble(part, values, received, others):
    parts = values.shape[0]

    def kernel(part_ref, values_ref, *refs):
        own = part_ref[0]
        out_ref = refs[-1]
        out_ref[own] = values_ref[own]
        for step in range(1, parts):
            out_ref[lax.rem(own + parts - step, parts)] = refs[step - 1][...]

    vmem = pl.BlockSpec(memory_space=pltpu.VMEM)
    anywhere = pl.BlockSpec(memory_space=pl.ANY)
    return pl.pallas_call(
        kernel,
        in_specs=[pl.BlockSpec(memory_space=pltpu.SMEM)]
        + [vmem] * parts
        + [anywhere] * len(others),
        out_specs=vmem,
        out_shape=jax.ShapeDtypeStruct(values.shape, values.dtype),
        compiler_params=pltpu.CompilerParams(vmem_limit_bytes=32 * 2**20),
        cost_estimate=NO_COST,
    )(part.reshape(1).astype(jnp.int32), values, *received, *others)


def copy_columns(count, *refs):
    target = refs[-1]
    start = 0
    for source in refs[:count]:
        block = source[...].reshape(source.shape[-2:])
        columns = pl.ds(start, block.shape[1])
        if len(target.shape) == 3:
            target[0, :, columns] = block.astype(target.dtype)
        else:
            target[:, columns] = block.astype(target.dtype)
        start += block.shape[1]


def to_parts(sources, parts, dtype, others=()):
    rows = sources[0][0].shape[0]

    def spec(section, width):
        return pl.BlockSpec((rows, width), lambda p: (0, section * parts + p))

    total = sum(width for _, _, width in sources)
    return pl.pallas_call(
        functools.partial(copy_columns, len(sources)),
        grid=(parts,),
        in_specs=[spec(section, width) for _, section, width in sources]
        + [pl.BlockSpec(memory_space=pl.ANY)] * len(others),
        out_specs=pl.BlockSpec((1, rows, total), lambda p: (p, 0, 0)),
        out_shape=jax.ShapeDtypeStruct((parts, rows, total), dtype),
        cost_estimate=NO_COST,
    )(*[array for array, _, _ in sources], *others)


def updown_from_parts(slabs):
    parts, rows, width = slabs.shape
    units = width // 2

    def kernel(slabs_ref, out_ref):
        for p in range(parts):
            out_ref[:, p * units : (p + 1) * units] = slabs_ref[p].astype(f32)

    return pl.pallas_call(
        kernel,
        grid=(2,),
        in_specs=[pl.BlockSpec((parts, rows, units), lambda half: (0, 0, half))],
        out_specs=pl.BlockSpec((rows, parts * units), lambda half: (0, half)),
        out_shape=jax.ShapeDtypeStruct((rows, parts * width), f32),
        compiler_params=pltpu.CompilerParams(vmem_limit_bytes=32 * 2**20),
        cost_estimate=NO_COST,
    )(slabs)


def mixer_from_parts(slabs, width):
    parts, rows, _ = slabs.shape

    def kernel(slabs_ref, qkv_ref, gate_ref, strength_ref):
        for p in range(parts):
            for section in range(4):
                block = slabs_ref[p, :, section * width : (section + 1) * width].astype(f32)
                if section < 3:
                    start = (section * parts + p) * width
                    qkv_ref[:, start : start + width] = block
                else:
                    gate_ref[:, p * width : (p + 1) * width] = block
            last = slabs_ref[p, :, 4 * width :].astype(f32)
            strength_ref[:, p * SMALL : (p + 1) * SMALL] = last

    widths = [3 * parts * width, parts * width, parts * SMALL]
    return pl.pallas_call(
        kernel,
        out_shape=[jax.ShapeDtypeStruct((rows, size), f32) for size in widths],
        compiler_params=pltpu.CompilerParams(vmem_limit_bytes=32 * 2**20),
        cost_estimate=NO_COST,
    )(slabs)


def own_order(values, parts, copies):
    size = values.shape[1] // (parts * copies)
    pieces = [
        values[:, (t * parts + m) * size : (t * parts + m + 1) * size]
        for m in range(parts)
        for t in range(copies)
    ]
    return jnp.concatenate(pieces, 1)


def total_of(own_ref, received_refs):
    total = own_ref[...]
    for ref in received_refs:
        total = total + ref[...].astype(f32)
    return total


def row_scale(values):
    return lax.rsqrt(jnp.mean(values * values, -1, keepdims=True) + 1e-06)


def norm_slope(values, scale, gain, grad):
    mean = jnp.mean(gain * grad * values, -1, keepdims=True)
    return scale * gain * grad - values * (scale * scale * scale * mean)


def hidden_kernel(own_ref, *refs):
    *received, input_ref, gain_ref, hidden_ref, normed_ref = refs
    hidden = input_ref[...].astype(f32) + total_of(own_ref, received)
    hidden_ref[...] = hidden
    normed_ref[...] = (hidden * row_scale(hidden) * gain_ref[...]).astype(bf)


def hidden_back_kernel(own_ref, *refs):
    *received, hidden_ref, gain_ref, cot_ref, d_hidden_ref, d_mixed_ref, d_gain_ref = refs
    grad = total_of(own_ref, received)
    hidden = hidden_ref[...]
    scale = row_scale(hidden)

    @pl.when(pl.program_id(0) == 0)
    def _():
        d_gain_ref[...] = jnp.zeros_like(d_gain_ref)

    d_gain_ref[...] += jnp.sum(grad * hidden * scale, 0, keepdims=True)
    d_hidden = cot_ref[...].astype(f32) + norm_slope(hidden, scale, gain_ref[...], grad)
    d_hidden_ref[...] = d_hidden
    d_mixed_ref[...] = d_hidden.astype(bf)


def input_back_kernel(parts, copies, own_ref, *refs):
    *received, input_ref, gain_ref, d_hidden_ref, out_ref = refs
    grad = total_of(own_ref, received)
    values = input_ref[...].astype(f32)
    slope = norm_slope(values, row_scale(values), gain_ref[...], grad)
    out_ref[...] = own_order(d_hidden_ref[...] + slope, parts, copies).astype(bf)


def block_out_kernel(parts, copies, own_ref, *refs):
    *received, hidden_ref, out_ref = refs
    total = hidden_ref[...] + total_of(own_ref, received)
    out_ref[...] = own_order(total, parts, copies).astype(bf)


def last_sum(sides, others, parts, copies):
    rows, columns = sides[0].shape

    def kernel(*refs):
        first, first_other, second, second_other = (ref[...].astype(f32) for ref in refs[:4])
        total = jnp.concatenate([first + first_other, second + second_other], 1)
        refs[-1][...] = own_order(total, parts, copies)

    vmem = pl.BlockSpec(memory_space=pltpu.VMEM)
    return pl.pallas_call(
        kernel,
        in_specs=[vmem] * 4 + [pl.BlockSpec(memory_space=pl.ANY)] * len(others),
        out_specs=vmem,
        out_shape=jax.ShapeDtypeStruct((rows, 2 * columns), f32),
        compiler_params=pltpu.CompilerParams(vmem_limit_bytes=32 * 2**20),
        cost_estimate=NO_COST,
    )(*sides, *others)


def by_rows(kernel, arrays, outs, block=64):
    def spec(shape):
        if shape[0] == 1:
            return pl.BlockSpec(shape, lambda i: (0, 0))
        return pl.BlockSpec((block, shape[1]), lambda i: (i, 0))

    return pl.pallas_call(
        kernel,
        grid=(GROUP_ROWS // block,),
        in_specs=[spec(array.shape) for array in arrays],
        out_specs=[spec(shape) for shape, _ in outs],
        out_shape=[jax.ShapeDtypeStruct(shape, dtype) for shape, dtype in outs],
        compiler_params=pltpu.CompilerParams(dimension_semantics=("arbitrary",)),
        cost_estimate=NO_COST,
    )(*arrays)


def body(
    block_in,
    out_grad,
    norm1_gain,
    conv_weight,
    head_gain,
    qkv_weight,
    beta_weight,
    gate_weight,
    out_weight,
    norm2_gain,
    updown_weight,
    down_weight,
    seq_blocks,
    lead_blocks,
):
    devices = lax.axis_size("dp")
    parts = MODEL
    copies = devices // parts
    part = lax.axis_index("dp") // copies
    copy = lax.axis_index("dp") % copies
    rows_own = qkv_weight.shape[0]
    width = D // parts
    units = FF // parts
    heads_part = HEADS // parts
    wide = 4 * width + SMALL
    model_groups = [[m * copies + t for m in range(parts)] for t in range(copies)]
    copy_groups = [[m * copies + t for t in range(copies)] for m in range(parts)]

    def exchange(values):
        return lax.all_to_all(
            values, "dp", split_axis=0, concat_axis=0, axis_index_groups=model_groups, tiled=True
        )

    def shift(values, step):
        pairs = [
            (m * copies + t, (m + step) % parts * copies + t)
            for m in range(parts)
            for t in range(copies)
        ]
        return lax.ppermute(values, "dp", pairs)

    def exchange_apart(values, before, after=()):
        cut = [
            lax.dynamic_index_in_dim(values, (part + step) % parts, 0, keepdims=False)
            for step in range(1, parts)
        ]
        received = [shift(piece, step) for step, piece in enumerate(tie_all(cut, *before), 1)]
        return assemble(part, values, received, after)

    def gather_rows(values):
        return [values] + [shift(values, step) for step in range(1, parts)]

    def scatter_rows(terms):
        return [terms[0]] + [shift(block, -step) for step, block in enumerate(terms[1:], 1)]

    def gather_copies(values):
        return lax.all_gather(values, "dp", axis=0, axis_index_groups=copy_groups, tiled=True)

    def scatter_copies(values):
        return lax.psum_scatter(
            values.astype(bf),
            "dp",
            scatter_dimension=0,
            axis_index_groups=copy_groups,
            tiled=True,
        )

    def halves_across(values, bit, axis):
        pairs = [(i, i ^ (1 << bit)) for i in range(devices)]
        side = (copy >> bit) & 1
        own = lax.dynamic_index_in_dim(values, side, axis, keepdims=False)
        other = lax.dynamic_index_in_dim(values, 1 - side, axis, keepdims=False)
        return own, lax.ppermute(other, "dp", pairs)

    def halve(values, bit, axis, *others):
        own, received = halves_across(values, bit, axis)
        if others:
            received = tie(received, *others)
        return (own.astype(f32) + received.astype(f32)).astype(bf)

    by_halves = copies == 8

    def halve_cores(values, *others):
        if not by_halves:
            return values
        rows, columns = values.shape
        return halve(values.reshape(2, 2, 2, rows // 8, columns), 0, 2, *others)

    def halve_first(values):
        if not by_halves:
            return [values]
        middle = values.shape[-1] // 2
        return [halve(values[..., :middle], 1, 1), halve(values[..., middle:], 2, 0)]

    def halve_second(values, *others):
        if not by_halves:
            return from_wire(scatter_copies(values[0]).astype(f32))
        sides = halves_across(values[0], 2, 0) + halves_across(values[1], 1, 0)
        return last_sum(sides, others, parts, copies)

    def to_wire(values):
        return values.reshape(-1, parts, copies, rows_own).swapaxes(1, 2).reshape(-1, D)

    def from_wire(values):
        return values.reshape(-1, copies, parts, rows_own).swapaxes(1, 2).reshape(-1, D)

    w_out_own = to_wire(out_weight.astype(bf))
    w_out = gather_copies(w_out_own)
    strengths = beta_weight.reshape(rows_own, parts, heads_part)
    strengths = jnp.pad(strengths, ((0, 0), (0, 0), (0, SMALL - heads_part)))
    strengths = tie(strengths.reshape(rows_own, parts * SMALL), w_out_own)
    pieces = [(qkv_weight, section, width) for section in range(3)]
    pieces = to_parts(pieces + [(gate_weight, 0, width), (strengths, 0, SMALL)], parts, bf)
    mixer_pieces = tie(exchange(pieces), w_out)
    w_mixer = gather_copies(mixer_pieces.reshape(parts * rows_own, wide))
    inputs = tie(to_wire(block_in), mixer_pieces)
    input_rows = gather_rows(inputs)

    lanes = -(-3 * rows_own // 128) * 128
    numbers = jnp.concatenate([seq_blocks[0], lead_blocks]).astype(f32)
    small = [conv_weight.T, norm1_gain[None], head_gain[None], norm2_gain[None], numbers[None]]
    small = [jnp.pad(rows, ((0, 0), (0, lanes - rows.shape[1]))) for rows in small]
    small = jnp.pad(jnp.concatenate(small, 0).astype(bf), ((0, 2 * KERNEL), (0, 0)))
    small = jnp.broadcast_to(small[None], (devices,) + small.shape)
    small = lax.all_to_all(tie(small, *input_rows[1:]), "dp", 0, 0, tiled=True)
    taps = small[:, :KERNEL, : 3 * rows_own].swapaxes(0, 1).reshape(KERNEL, 3, parts, width)
    taps = lax.dynamic_index_in_dim(taps, part, 2, keepdims=False).reshape(KERNEL, 3 * width)
    gain_one, head_full, gain_two = (
        small[:, KERNEL + i, :rows_own].reshape(1, D).astype(f32) for i in range(3)
    )
    gain_one, gain_two = to_wire(gain_one), to_wire(gain_two)
    head_part = lax.dynamic_slice_in_dim(head_full, part * width, width, 1)
    params = jnp.concatenate([taps.astype(f32), jnp.pad(head_part, ((0, 0), (0, 2 * width)))], 0)
    params = jnp.pad(params, ((0, KERNEL - 1), (0, 0)))
    numbers = small[:, KERNEL + 3, :3].astype(f32).astype(jnp.int32)
    layouts = block_layouts(numbers[:, 0], numbers[:, 1], numbers[:, 2])
    layouts = layouts.reshape(parts, copies, 4)
    layouts = lax.dynamic_index_in_dim(layouts, copy, 1, keepdims=False)
    wanted = (part - jnp.arange(parts)) % parts
    wanted = (wanted[:, None] == jnp.arange(parts)).astype(f32)
    layouts = jnp.sum(wanted[:, :, None] * layouts, 1)

    pieces = [(updown_weight, half, units) for half in range(2)]
    updown_pieces = to_parts(pieces, parts, bf, [mixer_pieces])
    w_down_own = to_wire(down_weight.astype(bf))
    w_down = gather_copies(tie(w_down_own, *input_rows[1:]))
    cotangent_own = to_wire(out_grad)

    cotangent = lax.all_gather(
        tie(cotangent_own, *input_rows[1:]), "dp", axis=0, axis_index_groups=model_groups, tiled=True
    )
    gain_first = tie(gain_one, w_down_own, cotangent_own, updown_pieces)
    normed, pre = normed_product(input_rows, gain_first, w_mixer)
    mixed, *kept = mixer_forward(layouts, pre, params, width)
    out_terms = product_blocks(mixed, w_out)
    updown_pieces = exchange_apart(updown_pieces, input_rows[1:], out_terms[1:])
    w_updown = gather_copies(updown_pieces.reshape(parts * rows_own, 2 * units))
    stream = ((GROUP_ROWS, D), f32)
    narrow = ((GROUP_ROWS, D), bf)
    hidden, normed_two = by_rows(
        hidden_kernel,
        scatter_rows(out_terms) + [inputs, gain_two],
        [stream, narrow],
    )
    cotangent = from_own(part, cotangent)
    normed_two = jnp.concatenate(gather_rows(normed_two), 0)

    def swiglu_units(updown):
        return jax.nn.silu(updown[:, :units]) * updown[:, units:]

    updown = plain_product(normed_two, w_updown)
    active, swiglu_back = jax.vjp(swiglu_units, updown)
    active = active.astype(bf)
    d_active = transposed_product(cotangent, w_down)
    d_updown = swiglu_back(d_active)[0].astype(bf)
    d_normed_two = product_blocks(d_updown, w_updown, transposed=True)
    active = tie(active, *d_normed_two[1:])
    down_terms = grad_product(active, cotangent)
    updown_terms = grad_product(normed_two, tie(d_updown, down_terms))
    gain_late = tie(gain_two, updown_terms)
    d_normed_two = scatter_rows(d_normed_two)
    updown_grad = scatter_copies(tie(updown_terms, gain_late, *d_normed_two[1:]))
    d_hidden, d_mixed, gain_two_grad = by_rows(
        hidden_back_kernel,
        d_normed_two + [hidden, gain_late, cotangent_own],
        [stream, narrow, ((1, D), f32)],
    )


    out_terms = product_blocks(tie(active, d_mixed), w_down)
    down_terms = tie(down_terms, *out_terms[1:])
    d_mixed = gather_rows(d_mixed)
    late = tie(params, *out_terms)
    out_terms[1:] = tie_all(out_terms[1:], *d_mixed[1:])
    d_pre, d_params = mixer_backward(layouts, pre, late, w_out, d_mixed, kept, width)
    mixer_terms = tie(grad_product(normed, d_pre, micros=20), updown_grad)
    mixer_grad = scatter_copies(mixer_terms)

    d_normed_terms = product_blocks(
        tie(d_pre, mixer_terms), w_mixer, transposed=True, micros=150
    )
    hidden = tie(hidden, d_normed_terms[0])
    (block_out,) = by_rows(
        functools.partial(block_out_kernel, parts, copies),
        scatter_rows(out_terms) + [hidden],
        [narrow],
    )
    d_normed_terms[1:] = tie_all(d_normed_terms[1:], block_out)
    d_normed = scatter_rows(d_normed_terms)
    down_grad = halve_first(halve_cores(down_terms, *d_normed_terms[1:]))
    gain_one_grad = 0.0
    for values, terms in zip(input_rows, d_normed_terms):
        values = values.astype(f32)
        terms = terms.astype(f32) * (values * row_scale(values))
        gain_one_grad = gain_one_grad + jnp.sum(terms, 0, keepdims=True)

    d_params = tie(d_params, mixer_terms)
    here = (jnp.arange(parts) == part).astype(f32)[:, None]
    taps_grad = d_params[:KERNEL].reshape(KERNEL, 3, 1, width) * here
    taps_grad = taps_grad.reshape(KERNEL, parts, copies, 3, rows_own).transpose(1, 2, 3, 0, 4)
    taps_grad = taps_grad.reshape(devices, 3 * KERNEL, rows_own)
    head_grad = (d_params[KERNEL, :width] * here).reshape(devices, 1, rows_own)
    gain_grads = [
        grad.reshape(copies, parts, 1, rows_own).swapaxes(0, 1).reshape(devices, 1, rows_own)
        for grad in (gain_one_grad, gain_two_grad)
    ]
    small_grad = jnp.concatenate([taps_grad, head_grad] + gain_grads, 1)
    small_grad = jnp.pad(small_grad, ((0, 0), (0, 1), (0, 128 - rows_own)))
    small_grad = lax.all_to_all(small_grad, "dp", 0, 0, tiled=True)
    updown_grad = tie(updown_grad, mixer_terms, small_grad)
    small_grad = jnp.sum(small_grad, 0)[:, :rows_own]
    taps_shard = small_grad[: 3 * KERNEL].reshape(3, KERNEL, rows_own).swapaxes(1, 2)
    taps_shard = taps_shard.reshape(3 * rows_own, KERNEL)
    head_shard, gain_one_shard, gain_two_shard = small_grad[3 * KERNEL : 3 * KERNEL + 3]

    d_mixed = jnp.concatenate([tie(d_mixed[0], d_normed_terms[0])] + d_mixed[1:], 0)
    out_grads = grad_product(mixed, d_mixed)
    updown_grad = exchange(updown_grad.reshape(parts, rows_own, 2 * units))
    late = tie(gain_one, out_grads, updown_grad, *down_grad)
    (input_grad,) = by_rows(
        functools.partial(input_back_kernel, parts, copies),
        d_normed + [inputs, late, d_hidden],
        [narrow],
    )
    mixer_grad = tie(mixer_grad, updown_grad, input_grad)
    updown_shard = updown_from_parts(tie(updown_grad, mixer_grad))
    down_shard = halve_second(tie_all(down_grad, input_grad), mixer_grad)
    out_grads = halve_cores(tie(out_grads, input_grad), mixer_grad)
    out_shard = halve_second(halve_first(out_grads))
    mixer_grad = exchange(mixer_grad.reshape(parts, rows_own, wide))
    qkv_shard, gate_shard, strengths = mixer_from_parts(mixer_grad, width)
    beta_shard = strengths.reshape(rows_own, parts, SMALL)[:, :, :heads_part]
    return (
        block_out,
        input_grad,
        gain_one_shard,
        taps_shard,
        head_shard,
        qkv_shard,
        beta_shard.reshape(rows_own, HEADS),
        gate_shard,
        out_shard,
        gain_two_shard,
        updown_shard,
        down_shard,
    )


def solution(mesh):
    placed = (
        P("dp", None),
        P("dp", None),
        P("dp"),
        P("dp", None),
        P("dp"),
        P("dp", None),
        P("dp", None),
        P("dp", None),
        P("dp", None),
        P("dp"),
        P("dp", None),
        P("dp", None),
        P("dp", None),
        P("dp"),
    )
    return jax.shard_map(
        body,
        mesh=mesh,
        in_specs=placed,
        out_specs=(
            P("dp", None),
            P("dp", None),
            P("dp"),
            P("dp", None),
            P("dp"),
            P("dp", None),
            P("dp", None),
            P("dp", None),
            P("dp", None),
            P("dp"),
            P("dp", None),
            P("dp", None),
        ),
        check_vma=False,
    )
```

```python
import functools

import jax
import jax.numpy as jnp
from jax import lax
from jax.experimental import pallas as pl
from jax.experimental.pallas import tpu as pltpu
from jax.sharding import PartitionSpec as P

D = 2048
HEADS = 16
HEAD_DIM = 128
FF = 5632
KERNEL = 4
BLOCK_ROWS = 64
BLOCKS_DEV = 2
GROUP_ROWS = BLOCK_ROWS * BLOCKS_DEV
SMALL = 128
MODEL = 4

f32 = jnp.float32
bf = jnp.bfloat16


def block_layouts(first, second, lead):
    def doc(block):
        in_first = (block >= lead) & (block < lead + first)
        in_second = (block >= lead + first) & (block < lead + first + second)
        return jnp.where(in_first, 1, jnp.where(in_second, 2, 0))

    starts = (lead == 1) | (lead + first == 1) & (second > 0)
    columns = [doc(0) > 0, doc(1) > 0, doc(0) == doc(1), ~starts]
    return jnp.stack(columns, 1).astype(f32)


def plain_product(left, right):
    return jnp.dot(left, right, preferred_element_type=f32)


def rows_product(left, right):
    return lax.dot_general(left, right, (((0,), (0,)), ((), ())), preferred_element_type=f32)


def transposed_product(left, right):
    return lax.dot_general(left, right, (((1,), (1,)), ((), ())), preferred_element_type=f32)


def halves(values):
    high = values.astype(bf)
    return high, (values - high.astype(f32)).astype(bf)


def exact(left, right, left_dim, right_dim):
    left_high, left_low = left if isinstance(left, tuple) else halves(left)
    right_high, right_low = right if isinstance(right, tuple) else halves(right)
    return lax.dot_general(
        jnp.concatenate([left_high, left_high, left_low], left_dim),
        jnp.concatenate([right_high, right_low, right_high], right_dim),
        (((left_dim,), (right_dim,)), ((), ())),
        preferred_element_type=f32,
    )


def stacked(first, second):
    return tuple(jnp.concatenate([a, b], 0) for a, b in zip(first, second))


class Tile:
    def __init__(self, layout_ref, group):
        live_first, live_second, same, persist = (layout_ref[group, i] for i in range(4))
        shape = (GROUP_ROWS, HEAD_DIM)
        row = lax.broadcasted_iota(jnp.int32, shape, 0)
        col = lax.broadcasted_iota(jnp.int32, shape, 1)
        late = row >= BLOCK_ROWS
        self.row, self.col = row, col
        self.live = jnp.where(late, live_second, live_first)
        self.taps = [None] + [
            jnp.where(
                row < offset,
                0.0,
                jnp.where(late & (row < BLOCK_ROWS + offset), same, 1.0),
            )
            for offset in range(1, KERNEL)
        ]
        cross = jnp.where(late & (col < BLOCK_ROWS), persist, 1.0)
        self.lower = jnp.where(row > col, cross, 0.0)
        self.lower_full = jnp.where(row >= col, cross, 0.0)

    def earlier(self, values, offset):
        return pltpu.roll(values, offset, 0) * self.taps[offset]

    def later(self, values, offset):
        return pltpu.roll(values * self.taps[offset], GROUP_ROWS - offset, 0)


def convolve(tile, values, taps):
    total = values * taps[0]
    for offset in range(1, KERNEL):
        total = total + tile.earlier(values, offset) * taps[offset]
    return total


def unit_scale(values):
    return lax.rsqrt(jnp.sum(values * values, -1, keepdims=True) + 1e-06)


def head_columns(part_width, section, head):
    return pl.ds(section * part_width + head * HEAD_DIM, HEAD_DIM)


def unit_inverses(tile, lowers):
    eye = jnp.where(tile.row == tile.col, 1.0, 0.0)
    inverses = None
    size = 1
    while size < GROUP_ROWS:
        pair = tile.row // (2 * size) == tile.col // (2 * size)
        split = pair & (tile.row // size != tile.col // size)
        parts = [jnp.where(split, lower, 0.0) for lower in lowers]
        if inverses is None:
            inverses = [eye - part for part in parts]
        else:
            kept = [halves(inverse) for inverse in inverses]
            inner = [exact(part, known, 1, 0) for part, known in zip(parts, kept)]
            outer = [exact(known, value, 1, 0) for known, value in zip(kept, inner)]
            inverses = [inverse - value for inverse, value in zip(inverses, outer)]
        size *= 2
    return inverses


def mixer_forward_kernel(
    layout_ref, pre_ref, param_ref, mixed_ref, inverse_ref, score_ref, solved_ref, out_ref
):
    width = mixed_ref.shape[1]
    heads = range(width // HEAD_DIM)
    tile = Tile(layout_ref, pl.program_id(0))
    queries, keys, values, strengths = [], [], [], []
    for head in heads:
        parts = []
        for section in range(3):
            columns = head_columns(width, section, head)
            taps = [param_ref[offset : offset + 1, columns] for offset in range(KERNEL)]
            convolved = convolve(tile, pre_ref[:, columns], taps)
            parts.append(convolved * jax.nn.sigmoid(convolved))
        queries.append(parts[0] * (unit_scale(parts[0]) * HEAD_DIM**-0.5))
        keys.append(parts[1] * unit_scale(parts[1]))
        values.append(parts[2])
        start = 4 * width + head
        strengths.append(jax.nn.sigmoid(pre_ref[:, start : start + 1]) * tile.live)
    lowers, scores = [], []
    for head in heads:
        key_halves = halves(keys[head])
        both = exact(stacked(key_halves, halves(queries[head])), key_halves, 1, 1)
        lowers.append(both[:GROUP_ROWS] * strengths[head] * tile.lower)
        scores.append(both[GROUP_ROWS:] * tile.lower_full)
    inverses = unit_inverses(tile, lowers)
    solved = [exact(inverses[head], values[head] * strengths[head], 1, 0) for head in heads]
    outs = [exact(scores[head], solved[head], 1, 0) for head in heads]
    for head in heads:
        out = outs[head]
        scaled = out * lax.rsqrt(jnp.mean(out * out, -1, keepdims=True) + 1e-05)
        gate = pre_ref[:, head_columns(width, 3, head)]
        gain = param_ref[KERNEL : KERNEL + 1, head_columns(width, 0, head)]
        mixed = scaled * gain * (gate * jax.nn.sigmoid(gate)) * tile.live
        mixed_ref[:, head_columns(width, 0, head)] = mixed.astype(bf)
        inverse_ref[head] = inverses[head]
        score_ref[head] = scores[head]
        solved_ref[head] = solved[head]
        out_ref[head] = out


def mixer_backward_kernel(
    layout_ref,
    pre_ref,
    param_ref,
    weight_ref,
    inverse_ref,
    score_ref,
    solved_ref,
    out_ref,
    *refs,
):
    *mixed_refs, d_pre_ref, d_param_ref, grad_ref = refs
    width = grad_ref.shape[1]
    heads = range(width // HEAD_DIM)
    tile = Tile(layout_ref, pl.program_id(0))
    for group, mixed_ref in enumerate(mixed_refs):

        @pl.when(pl.program_id(0) == group)
        def _():
            grad_ref[...] = transposed_product(mixed_ref[...], weight_ref[...])

    @pl.when(pl.program_id(0) == 0)
    def _():
        d_param_ref[...] = jnp.zeros_like(d_param_ref)

    def along(values):
        return jnp.sum(values, -1, keepdims=True)

    d_outs = []
    for head in heads:
        columns = head_columns(width, 0, head)
        d_mixed = grad_ref[:, columns] * tile.live
        out = out_ref[head]
        scale = lax.rsqrt(jnp.mean(out * out, -1, keepdims=True) + 1e-05)
        scaled = out * scale
        gate = pre_ref[:, head_columns(width, 3, head)]
        gate_open = jax.nn.sigmoid(gate)
        gain = param_ref[KERNEL : KERNEL + 1, columns]
        gated = d_mixed * (gate * gate_open)
        d_param_ref[KERNEL : KERNEL + 1, columns] += jnp.sum(gated * scaled, 0, keepdims=True)
        d_gate = d_mixed * scaled * gain * (gate_open * (1.0 + gate * (1.0 - gate_open)))
        d_pre_ref[:, head_columns(width, 3, head)] = d_gate.astype(bf)
        d_scaled = gated * gain
        mean = jnp.mean(d_scaled * out, -1, keepdims=True)
        d_outs.append(scale * d_scaled - out * (scale * scale * scale * mean))
    d_out_halves = [halves(value) for value in d_outs]
    solved_halves = [halves(solved_ref[head]) for head in heads]
    d_solved = [exact(score_ref[head], d_out_halves[head], 0, 0) for head in heads]
    d_scores = [
        exact(d_out_halves[head], solved_halves[head], 1, 1) * tile.lower_full for head in heads
    ]
    d_inner = [exact(inverse_ref[head], d_solved[head], 0, 0) for head in heads]
    d_lowers = [exact(d_inner[head], solved_halves[head], 1, 1) * -tile.lower for head in heads]
    d_beta = jnp.zeros((GROUP_ROWS, SMALL), f32)
    for head in heads:
        pres, convolved, opened, active = [], [], [], []
        for section in range(3):
            columns = head_columns(width, section, head)
            taps = [param_ref[offset : offset + 1, columns] for offset in range(KERNEL)]
            pres.append(pre_ref[:, columns])
            convolved.append(convolve(tile, pres[section], taps))
            opened.append(jax.nn.sigmoid(convolved[section]))
            active.append(convolved[section] * opened[section])
        query_scale = unit_scale(active[0])
        key_scale = unit_scale(active[1])
        query_unit = active[0] * query_scale
        key = active[1] * key_scale
        start = 4 * width + head
        opening = jax.nn.sigmoid(pre_ref[:, start : start + 1])
        strength = opening * tile.live
        d_both = stacked(halves(d_lowers[head]), halves(d_scores[head]))
        by_key = exact(d_both, key, 1, 0)
        d_query = by_key[GROUP_ROWS:] * HEAD_DIM**-0.5
        from_lower = by_key[:GROUP_ROWS]
        weighted = stacked(halves(key * strength), halves(query_unit * HEAD_DIM**-0.5))
        d_key = strength * from_lower + exact(d_both, weighted, 0, 0)
        d_strength = along(d_inner[head] * active[2] + from_lower * key)
        d_value = d_inner[head] * strength
        d_opening = d_strength * (opening * (1.0 - opening)) * tile.live
        d_beta = d_beta + jnp.where(tile.col == head, d_opening, 0.0)
        d_active = [
            (d_query - query_unit * along(query_unit * d_query)) * query_scale,
            (d_key - key * along(key * d_key)) * key_scale,
            d_value,
        ]
        for section in range(3):
            columns = head_columns(width, section, head)
            taps = [param_ref[offset : offset + 1, columns] for offset in range(KERNEL)]
            slope = opened[section] * (1.0 + convolved[section] * (1.0 - opened[section]))
            d_convolved = d_active[section] * slope
            d_pre = d_convolved * taps[0]
            sums = [jnp.sum(d_convolved * pres[section], 0, keepdims=True)]
            for offset in range(1, KERNEL):
                d_pre = d_pre + tile.later(d_convolved, offset) * taps[offset]
                sums.append(
                    jnp.sum(d_convolved * tile.earlier(pres[section], offset), 0, keepdims=True)
                )
            d_param_ref[0:KERNEL, columns] += jnp.concatenate(sums, 0)
            d_pre_ref[:, columns] = d_pre.astype(bf)
    d_pre_ref[:, 4 * width :] = d_beta.astype(bf)


NO_COST = pl.CostEstimate(flops=0, bytes_accessed=0, transcendentals=0)


def call(kernel, operands, in_specs, out_specs, out_shape, grid=(), scratch=(), micros=0):
    results = pl.pallas_call(
        kernel,
        grid=grid,
        in_specs=in_specs,
        out_specs=out_specs,
        out_shape=out_shape,
        scratch_shapes=scratch,
        compiler_params=pltpu.CompilerParams(
            dimension_semantics=("arbitrary",) * len(grid), vmem_limit_bytes=48 * 2**20
        ),
        cost_estimate=pl.CostEstimate(
            flops=micros * 10**9, bytes_accessed=0, transcendentals=0
        ),
    )(*operands)
    return list(results)


def whole(array):
    return pl.BlockSpec(array.shape, lambda *step: (0,) * len(array.shape))


def mixer_specs(width):
    wide = 4 * width + SMALL
    heads = width // HEAD_DIM
    layout = pl.BlockSpec(memory_space=pltpu.SMEM)
    pre = pl.BlockSpec((GROUP_ROWS, wide), lambda group: (group, 0))
    param = pl.BlockSpec((2 * KERNEL, 3 * width), lambda group: (0, 0))
    narrow = pl.BlockSpec((GROUP_ROWS, width), lambda group: (group, 0))
    square = pl.BlockSpec((heads, GROUP_ROWS, HEAD_DIM), lambda group: (group, 0, 0))
    return layout, pre, param, narrow, square


def mixer_forward(layout, pre, params, width):
    groups = layout.shape[0]
    layout_spec, pre_spec, param_spec, narrow, square = mixer_specs(width)
    squares = pltpu.HBM((groups * width // HEAD_DIM, GROUP_ROWS, HEAD_DIM), f32)
    return call(
        mixer_forward_kernel,
        [layout, pre, params],
        [layout_spec, pre_spec, param_spec],
        [narrow] + [square] * 4,
        [jax.ShapeDtypeStruct((groups * GROUP_ROWS, width), bf)] + [squares] * 4,
        (groups,),
    )


def mixer_backward(layout, pre, params, weight, d_mixed, kept, width):
    groups = layout.shape[0]
    layout_spec, pre_spec, param_spec, _, square = mixer_specs(width)
    kept = [pltpu.with_memory_space_constraint(array, pltpu.HBM) for array in kept]
    return call(
        mixer_backward_kernel,
        [layout, pre, params, weight, *kept, *d_mixed],
        [layout_spec, pre_spec, param_spec, whole(weight)]
        + [square] * 4
        + [whole(block) for block in d_mixed],
        [pre_spec, param_spec],
        [jax.ShapeDtypeStruct(pre.shape, bf), jax.ShapeDtypeStruct(params.shape, f32)],
        (groups,),
        [pltpu.VMEM((GROUP_ROWS, width), f32)],
        micros=60,
    )


def first_kernel(gain_ref, weight_ref, *refs):
    *value_refs, normed_ref, out_ref, scale_ref, total_ref = refs
    step, depth = pl.program_id(0), weight_ref.shape[0]

    @pl.when(step == 0)
    def _():
        for group, ref in enumerate(value_refs):
            values = ref[...].astype(f32)
            scale = lax.rsqrt(jnp.mean(values * values, -1, keepdims=True) + 1e-06)
            rows = pl.ds(group * GROUP_ROWS, GROUP_ROWS)
            scale_ref[rows, :] = jnp.broadcast_to(scale, (GROUP_ROWS, 128))
        total_ref[...] = jnp.zeros_like(total_ref)

    columns = pl.ds(pl.multiple_of(step * depth, depth), depth)
    for group, ref in enumerate(value_refs):
        rows = pl.ds(group * GROUP_ROWS, GROUP_ROWS)
        values = ref[:, columns].astype(f32) * scale_ref[rows, :1] * gain_ref[...]
        normed_ref[rows, :] = values.astype(bf)
    total_ref[...] += plain_product(normed_ref[...], weight_ref[...])

    @pl.when(step == pl.num_programs(0) - 1)
    def _():
        out_ref[...] = total_ref[...]


def normed_product(blocks, gain, weight, depth=512):
    rows, (features, columns) = len(blocks) * GROUP_ROWS, weight.shape
    return call(
        first_kernel,
        [gain, weight, *blocks],
        [
            pl.BlockSpec((1, depth), lambda step: (0, step)),
            pl.BlockSpec((depth, columns), lambda step: (step, 0)),
        ]
        + [whole(block) for block in blocks],
        [
            pl.BlockSpec((rows, depth), lambda step: (0, step)),
            pl.BlockSpec((rows, columns), lambda step: (0, 0)),
        ],
        [
            jax.ShapeDtypeStruct((rows, features), bf),
            jax.ShapeDtypeStruct((rows, columns), f32),
        ],
        (features // depth,),
        [pltpu.VMEM((rows, 128), f32), pltpu.VMEM((rows, columns), f32)],
    )


def product_blocks(left, right, transposed=False, block=512, micros=0):
    product = transposed_product if transposed else plain_product
    columns = right.shape[0] if transposed else right.shape[1]
    groups = left.shape[0] // GROUP_ROWS

    def kernel(left_ref, right_ref, *out_refs):
        total = product(left_ref[...], right_ref[...])
        for group, ref in enumerate(out_refs):
            ref[...] = total[group * GROUP_ROWS : (group + 1) * GROUP_ROWS].astype(ref.dtype)

    if transposed:
        right_spec = pl.BlockSpec((block, right.shape[1]), lambda step: (step, 0))
    else:
        right_spec = pl.BlockSpec((right.shape[0], block), lambda step: (0, step))
    return call(
        kernel,
        [left, right],
        [whole(left), right_spec],
        [pl.BlockSpec((GROUP_ROWS, block), lambda step: (0, step))] * groups,
        [
            jax.ShapeDtypeStruct((GROUP_ROWS, columns), bf if group else f32)
            for group in range(groups)
        ],
        (columns // block,),
        micros=micros,
    )


def grad_product(left, right, block=256, micros=0):
    rows, features = left.shape
    if features % block:
        block = 128

    def kernel(left_ref, right_ref, out_ref):
        out_ref[...] = rows_product(left_ref[...], right_ref[...]).astype(bf)

    return call(
        kernel,
        [left, right],
        [pl.BlockSpec((rows, block), lambda step: (0, step)), whole(right)],
        [pl.BlockSpec((block, right.shape[1]), lambda step: (step, 0))],
        [pltpu.HBM((features, right.shape[1]), bf)],
        (features // block,),
        micros=micros,
    )[0]


def from_own(part, values):
    groups = values.shape[0] // GROUP_ROWS

    def kernel(part_ref, values_ref, out_ref):
        for step in range(groups):
            source = lax.rem(part_ref[0] + groups - step, groups) * GROUP_ROWS
            rows = pl.ds(pl.multiple_of(source, GROUP_ROWS), GROUP_ROWS)
            out_ref[step * GROUP_ROWS : (step + 1) * GROUP_ROWS] = values_ref[rows]

    return call(
        kernel,
        [part.reshape(1).astype(jnp.int32), values],
        [pl.BlockSpec(memory_space=pltpu.SMEM), whole(values)],
        [whole(values)],
        [jax.ShapeDtypeStruct(values.shape, values.dtype)],
        (1,),
    )[0]


def tie_all(values, *others):
    anywhere = pl.BlockSpec(memory_space=pl.ANY)
    others = [
        pltpu.with_memory_space_constraint(other, pltpu.HBM) if other.size > 2**21 else other
        for other in others
    ]
    tied = pl.pallas_call(
        lambda *refs: None,
        in_specs=[anywhere] * (len(values) + len(others)),
        out_specs=[anywhere] * len(values),
        out_shape=[
            (pltpu.HBM if value.size > 2**21 else jax.ShapeDtypeStruct)(value.shape, value.dtype)
            for value in values
        ],
        input_output_aliases={i: i for i in range(len(values))},
        cost_estimate=NO_COST,
    )(*values, *others)
    return list(tied)


def tie(value, *others):
    return tie_all([value], *others)[0]


def assemble(part, values, received, others):
    parts = values.shape[0]

    def kernel(part_ref, values_ref, *refs):
        own = part_ref[0]
        out_ref = refs[-1]
        out_ref[own] = values_ref[own]
        for step in range(1, parts):
            out_ref[lax.rem(own + parts - step, parts)] = refs[step - 1][...]

    vmem = pl.BlockSpec(memory_space=pltpu.VMEM)
    anywhere = pl.BlockSpec(memory_space=pl.ANY)
    return pl.pallas_call(
        kernel,
        in_specs=[pl.BlockSpec(memory_space=pltpu.SMEM)]
        + [vmem] * parts
        + [anywhere] * len(others),
        out_specs=vmem,
        out_shape=jax.ShapeDtypeStruct(values.shape, values.dtype),
        compiler_params=pltpu.CompilerParams(vmem_limit_bytes=32 * 2**20),
        cost_estimate=NO_COST,
    )(part.reshape(1).astype(jnp.int32), values, *received, *others)


def copy_columns(count, *refs):
    target = refs[-1]
    start = 0
    for source in refs[:count]:
        block = source[...].reshape(source.shape[-2:])
        columns = pl.ds(start, block.shape[1])
        if len(target.shape) == 3:
            target[0, :, columns] = block.astype(target.dtype)
        else:
            target[:, columns] = block.astype(target.dtype)
        start += block.shape[1]


def to_parts(sources, parts, dtype, others=()):
    rows = sources[0][0].shape[0]

    def spec(section, width):
        return pl.BlockSpec((rows, width), lambda p: (0, section * parts + p))

    total = sum(width for _, _, width in sources)
    return pl.pallas_call(
        functools.partial(copy_columns, len(sources)),
        grid=(parts,),
        in_specs=[spec(section, width) for _, section, width in sources]
        + [pl.BlockSpec(memory_space=pl.ANY)] * len(others),
        out_specs=pl.BlockSpec((1, rows, total), lambda p: (p, 0, 0)),
        out_shape=jax.ShapeDtypeStruct((parts, rows, total), dtype),
        cost_estimate=NO_COST,
    )(*[array for array, _, _ in sources], *others)


def updown_from_parts(slabs):
    parts, rows, width = slabs.shape
    units = width // 2

    def kernel(slabs_ref, out_ref):
        for p in range(parts):
            out_ref[:, p * units : (p + 1) * units] = slabs_ref[p].astype(f32)

    return pl.pallas_call(
        kernel,
        grid=(2,),
        in_specs=[pl.BlockSpec((parts, rows, units), lambda half: (0, 0, half))],
        out_specs=pl.BlockSpec((rows, parts * units), lambda half: (0, half)),
        out_shape=jax.ShapeDtypeStruct((rows, parts * width), f32),
        compiler_params=pltpu.CompilerParams(vmem_limit_bytes=32 * 2**20),
        cost_estimate=NO_COST,
    )(slabs)


def mixer_from_parts(slabs, width):
    parts, rows, _ = slabs.shape

    def kernel(slabs_ref, qkv_ref, gate_ref, strength_ref):
        for p in range(parts):
            for section in range(4):
                block = slabs_ref[p, :, section * width : (section + 1) * width].astype(f32)
                if section < 3:
                    start = (section * parts + p) * width
                    qkv_ref[:, start : start + width] = block
                else:
                    gate_ref[:, p * width : (p + 1) * width] = block
            last = slabs_ref[p, :, 4 * width :].astype(f32)
            strength_ref[:, p * SMALL : (p + 1) * SMALL] = last

    widths = [3 * parts * width, parts * width, parts * SMALL]
    return pl.pallas_call(
        kernel,
        out_shape=[jax.ShapeDtypeStruct((rows, size), f32) for size in widths],
        compiler_params=pltpu.CompilerParams(vmem_limit_bytes=32 * 2**20),
        cost_estimate=NO_COST,
    )(slabs)


def own_order(values, parts, copies):
    size = values.shape[1] // (parts * copies)
    pieces = [
        values[:, (t * parts + m) * size : (t * parts + m + 1) * size]
        for m in range(parts)
        for t in range(copies)
    ]
    return jnp.concatenate(pieces, 1)


def total_of(own_ref, received_refs):
    total = own_ref[...]
    for ref in received_refs:
        total = total + ref[...].astype(f32)
    return total


def row_scale(values):
    return lax.rsqrt(jnp.mean(values * values, -1, keepdims=True) + 1e-06)


def norm_slope(values, scale, gain, grad):
    mean = jnp.mean(gain * grad * values, -1, keepdims=True)
    return scale * gain * grad - values * (scale * scale * scale * mean)


def hidden_kernel(own_ref, *refs):
    *received, input_ref, gain_ref, hidden_ref, normed_ref = refs
    hidden = input_ref[...].astype(f32) + total_of(own_ref, received)
    hidden_ref[...] = hidden
    normed_ref[...] = (hidden * row_scale(hidden) * gain_ref[...]).astype(bf)


def hidden_back_kernel(own_ref, *refs):
    *received, hidden_ref, gain_ref, cot_ref, d_hidden_ref, d_mixed_ref, d_gain_ref = refs
    grad = total_of(own_ref, received)
    hidden = hidden_ref[...]
    scale = row_scale(hidden)

    @pl.when(pl.program_id(0) == 0)
    def _():
        d_gain_ref[...] = jnp.zeros_like(d_gain_ref)

    d_gain_ref[...] += jnp.sum(grad * hidden * scale, 0, keepdims=True)
    d_hidden = cot_ref[...].astype(f32) + norm_slope(hidden, scale, gain_ref[...], grad)
    d_hidden_ref[...] = d_hidden
    d_mixed_ref[...] = d_hidden.astype(bf)


def input_back_kernel(parts, copies, own_ref, *refs):
    *received, input_ref, gain_ref, d_hidden_ref, out_ref = refs
    grad = total_of(own_ref, received)
    values = input_ref[...].astype(f32)
    slope = norm_slope(values, row_scale(values), gain_ref[...], grad)
    out_ref[...] = own_order(d_hidden_ref[...] + slope, parts, copies).astype(bf)


def block_out_kernel(parts, copies, own_ref, *refs):
    *received, hidden_ref, out_ref = refs
    total = hidden_ref[...] + total_of(own_ref, received)
    out_ref[...] = own_order(total, parts, copies).astype(bf)


def last_sum(sides, others, parts, copies):
    rows, columns = sides[0].shape

    def kernel(*refs):
        first, first_other, second, second_other = (ref[...].astype(f32) for ref in refs[:4])
        total = jnp.concatenate([first + first_other, second + second_other], 1)
        refs[-1][...] = own_order(total, parts, copies)

    vmem = pl.BlockSpec(memory_space=pltpu.VMEM)
    return pl.pallas_call(
        kernel,
        in_specs=[vmem] * 4 + [pl.BlockSpec(memory_space=pl.ANY)] * len(others),
        out_specs=vmem,
        out_shape=jax.ShapeDtypeStruct((rows, 2 * columns), f32),
        compiler_params=pltpu.CompilerParams(vmem_limit_bytes=32 * 2**20),
        cost_estimate=NO_COST,
    )(*sides, *others)


def by_rows(kernel, arrays, outs, block=64):
    def spec(shape):
        if shape[0] == 1:
            return pl.BlockSpec(shape, lambda i: (0, 0))
        return pl.BlockSpec((block, shape[1]), lambda i: (i, 0))

    return pl.pallas_call(
        kernel,
        grid=(GROUP_ROWS // block,),
        in_specs=[spec(array.shape) for array in arrays],
        out_specs=[spec(shape) for shape, _ in outs],
        out_shape=[jax.ShapeDtypeStruct(shape, dtype) for shape, dtype in outs],
        compiler_params=pltpu.CompilerParams(dimension_semantics=("arbitrary",)),
        cost_estimate=NO_COST,
    )(*arrays)


def body(
    block_in,
    out_grad,
    norm1_gain,
    conv_weight,
    head_gain,
    qkv_weight,
    beta_weight,
    gate_weight,
    out_weight,
    norm2_gain,
    updown_weight,
    down_weight,
    seq_blocks,
    lead_blocks,
):
    devices = lax.axis_size("dp")
    parts = MODEL
    copies = devices // parts
    part = lax.axis_index("dp") // copies
    copy = lax.axis_index("dp") % copies
    rows_own = qkv_weight.shape[0]
    width = D // parts
    units = FF // parts
    heads_part = HEADS // parts
    wide = 4 * width + SMALL
    model_groups = [[m * copies + t for m in range(parts)] for t in range(copies)]
    copy_groups = [[m * copies + t for t in range(copies)] for m in range(parts)]

    def exchange(values):
        return lax.all_to_all(
            values, "dp", split_axis=0, concat_axis=0, axis_index_groups=model_groups, tiled=True
        )

    def shift(values, step):
        pairs = [
            (m * copies + t, (m + step) % parts * copies + t)
            for m in range(parts)
            for t in range(copies)
        ]
        return lax.ppermute(values, "dp", pairs)

    def cut_pieces(values):
        return [
            lax.dynamic_index_in_dim(values, (part + step) % parts, 0, keepdims=False)
            for step in range(1, parts)
        ]

    def gather_rows(values):
        return [values] + [shift(values, step) for step in range(1, parts)]

    def scatter_rows(terms):
        return [terms[0]] + [shift(block, -step) for step, block in enumerate(terms[1:], 1)]

    def gather_copies(values):
        return lax.all_gather(values, "dp", axis=0, axis_index_groups=copy_groups, tiled=True)

    def scatter_copies(values):
        return lax.psum_scatter(
            values.astype(bf),
            "dp",
            scatter_dimension=0,
            axis_index_groups=copy_groups,
            tiled=True,
        )

    def halves_across(values, bit, axis):
        pairs = [(i, i ^ (1 << bit)) for i in range(devices)]
        side = (copy >> bit) & 1
        own = lax.dynamic_index_in_dim(values, side, axis, keepdims=False)
        other = lax.dynamic_index_in_dim(values, 1 - side, axis, keepdims=False)
        return own, lax.ppermute(other, "dp", pairs)

    def halve(values, bit, axis, *others):
        own, received = halves_across(values, bit, axis)
        if others:
            received = tie(received, *others)
        return (own.astype(f32) + received.astype(f32)).astype(bf)

    by_halves = copies == 8

    def halve_cores(values, *others):
        if not by_halves:
            return values
        rows, columns = values.shape
        return halve(values.reshape(2, 2, 2, rows // 8, columns), 0, 2, *others)

    def halve_first(values):
        if not by_halves:
            return [values]
        middle = values.shape[-1] // 2
        return [halve(values[..., :middle], 1, 1), halve(values[..., middle:], 2, 0)]

    def halve_second(values, *others):
        if not by_halves:
            return from_wire(scatter_copies(values[0]).astype(f32))
        sides = halves_across(values[0], 2, 0) + halves_across(values[1], 1, 0)
        return last_sum(sides, others, parts, copies)

    def to_wire(values):
        return values.reshape(-1, parts, copies, rows_own).swapaxes(1, 2).reshape(-1, D)

    def from_wire(values):
        return values.reshape(-1, copies, parts, rows_own).swapaxes(1, 2).reshape(-1, D)

    w_out_own = to_wire(out_weight.astype(bf))
    w_out = gather_copies(w_out_own)
    strengths = beta_weight.reshape(rows_own, parts, heads_part)
    strengths = jnp.pad(strengths, ((0, 0), (0, 0), (0, SMALL - heads_part)))
    strengths = tie(strengths.reshape(rows_own, parts * SMALL), w_out_own)
    pieces = [(qkv_weight, section, width) for section in range(3)]
    pieces = to_parts(pieces + [(gate_weight, 0, width), (strengths, 0, SMALL)], parts, bf)
    mixer_pieces = tie(exchange(pieces), w_out)
    w_mixer = gather_copies(mixer_pieces.reshape(parts * rows_own, wide))
    inputs = tie(to_wire(block_in), mixer_pieces)
    input_rows = gather_rows(inputs)

    pieces = [(updown_weight, half, units) for half in range(2)]
    updown_pieces = to_parts(pieces, parts, bf, [mixer_pieces])
    cut = cut_pieces(updown_pieces)

    lanes = -(-3 * rows_own // 128) * 128
    numbers = jnp.concatenate([seq_blocks[0], lead_blocks]).astype(f32)
    small = [conv_weight.T, norm1_gain[None], head_gain[None], norm2_gain[None], numbers[None]]
    small = [jnp.pad(rows, ((0, 0), (0, lanes - rows.shape[1]))) for rows in small]
    small = jnp.pad(jnp.concatenate(small, 0).astype(bf), ((0, 2 * KERNEL), (0, 0)))
    small = jnp.broadcast_to(small[None], (devices,) + small.shape)
    small = lax.all_to_all(tie(small, *cut, *input_rows[1:]), "dp", 0, 0, tiled=True)
    taps = small[:, :KERNEL, : 3 * rows_own].swapaxes(0, 1).reshape(KERNEL, 3, parts, width)
    taps = lax.dynamic_index_in_dim(taps, part, 2, keepdims=False).reshape(KERNEL, 3 * width)
    gain_one, head_full, gain_two = (
        small[:, KERNEL + i, :rows_own].reshape(1, D).astype(f32) for i in range(3)
    )
    gain_one, gain_two = to_wire(gain_one), to_wire(gain_two)
    head_part = lax.dynamic_slice_in_dim(head_full, part * width, width, 1)
    params = jnp.concatenate([taps.astype(f32), jnp.pad(head_part, ((0, 0), (0, 2 * width)))], 0)
    params = jnp.pad(params, ((0, KERNEL - 1), (0, 0)))
    numbers = small[:, KERNEL + 3, :3].astype(f32).astype(jnp.int32)
    layouts = block_layouts(numbers[:, 0], numbers[:, 1], numbers[:, 2])
    layouts = layouts.reshape(parts, copies, 4)
    layouts = lax.dynamic_index_in_dim(layouts, copy, 1, keepdims=False)
    wanted = (part - jnp.arange(parts)) % parts
    wanted = (wanted[:, None] == jnp.arange(parts)).astype(f32)
    layouts = jnp.sum(wanted[:, :, None] * layouts, 1)

    w_down_own = to_wire(down_weight.astype(bf))
    w_down = gather_copies(tie(w_down_own, *input_rows[1:]))
    cotangent_own = to_wire(out_grad)

    cotangent = lax.all_gather(
        tie(cotangent_own, *input_rows[1:]), "dp", axis=0, axis_index_groups=model_groups, tiled=True
    )
    gain_first = tie(gain_one, w_down_own, cotangent_own, updown_pieces)
    normed, pre = normed_product(input_rows, gain_first, w_mixer)
    mixed, *kept = mixer_forward(layouts, pre, params, width)
    out_terms = product_blocks(mixed, w_out)
    cut = tie_all(cut, *input_rows[1:])
    received = [shift(piece, step) for step, piece in enumerate(cut, 1)]
    updown_pieces = assemble(part, updown_pieces, received, out_terms[1:])
    w_updown = gather_copies(updown_pieces.reshape(parts * rows_own, 2 * units))
    stream = ((GROUP_ROWS, D), f32)
    narrow = ((GROUP_ROWS, D), bf)
    hidden, normed_two = by_rows(
        hidden_kernel,
        scatter_rows(out_terms) + [inputs, gain_two],
        [stream, narrow],
    )
    cotangent = from_own(part, cotangent)
    normed_two = jnp.concatenate(gather_rows(normed_two), 0)

    def swiglu_units(updown):
        return jax.nn.silu(updown[:, :units]) * updown[:, units:]

    updown = plain_product(normed_two, w_updown)
    active, swiglu_back = jax.vjp(swiglu_units, updown)
    active = active.astype(bf)
    d_active = transposed_product(cotangent, w_down)
    d_updown = swiglu_back(d_active)[0].astype(bf)
    d_normed_two = product_blocks(d_updown, w_updown, transposed=True)
    active = tie(active, *d_normed_two[1:])
    down_terms = grad_product(active, cotangent)
    updown_terms = grad_product(normed_two, tie(d_updown, down_terms))
    gain_late = tie(gain_two, updown_terms)
    d_normed_two = scatter_rows(d_normed_two)
    updown_grad = scatter_copies(tie(updown_terms, gain_late, *d_normed_two[1:]))
    d_hidden, d_mixed, gain_two_grad = by_rows(
        hidden_back_kernel,
        d_normed_two + [hidden, gain_late, cotangent_own],
        [stream, narrow, ((1, D), f32)],
    )


    out_terms = product_blocks(tie(active, d_mixed), w_down)
    down_terms = tie(down_terms, *out_terms[1:])
    d_mixed = gather_rows(d_mixed)
    late = tie(params, *out_terms)
    out_terms[1:] = tie_all(out_terms[1:], *d_mixed[1:])
    d_pre, d_params = mixer_backward(layouts, pre, late, w_out, d_mixed, kept, width)
    mixer_terms = tie(grad_product(normed, d_pre, micros=20), updown_grad)
    mixer_grad = scatter_copies(mixer_terms)

    d_normed_terms = product_blocks(
        tie(d_pre, mixer_terms), w_mixer, transposed=True, micros=150
    )
    hidden = tie(hidden, d_normed_terms[0])
    (block_out,) = by_rows(
        functools.partial(block_out_kernel, parts, copies),
        scatter_rows(out_terms) + [hidden],
        [narrow],
    )
    d_normed_terms[1:] = tie_all(d_normed_terms[1:], block_out)
    d_normed = scatter_rows(d_normed_terms)
    down_grad = halve_first(halve_cores(down_terms, *d_normed_terms[1:]))
    gain_one_grad = 0.0
    for values, terms in zip(input_rows, d_normed_terms):
        values = values.astype(f32)
        terms = terms.astype(f32) * (values * row_scale(values))
        gain_one_grad = gain_one_grad + jnp.sum(terms, 0, keepdims=True)

    d_params = tie(d_params, mixer_terms)
    here = (jnp.arange(parts) == part).astype(f32)[:, None]
    taps_grad = d_params[:KERNEL].reshape(KERNEL, 3, 1, width) * here
    taps_grad = taps_grad.reshape(KERNEL, parts, copies, 3, rows_own).transpose(1, 2, 3, 0, 4)
    taps_grad = taps_grad.reshape(devices, 3 * KERNEL, rows_own)
    head_grad = (d_params[KERNEL, :width] * here).reshape(devices, 1, rows_own)
    gain_grads = [
        grad.reshape(copies, parts, 1, rows_own).swapaxes(0, 1).reshape(devices, 1, rows_own)
        for grad in (gain_one_grad, gain_two_grad)
    ]
    small_grad = jnp.concatenate([taps_grad, head_grad] + gain_grads, 1)
    d_mixed = jnp.concatenate([tie(d_mixed[0], d_normed_terms[0])] + d_mixed[1:], 0)
    out_grads = grad_product(mixed, d_mixed)
    late = tie(gain_one, out_grads, *down_grad)
    (input_grad,) = by_rows(
        functools.partial(input_back_kernel, parts, copies),
        d_normed + [inputs, late, d_hidden],
        [narrow],
    )
    small_grad = jnp.pad(tie(small_grad, input_grad), ((0, 0), (0, 1), (0, 128 - rows_own)))
    small_grad = jnp.sum(lax.all_to_all(small_grad, "dp", 0, 0, tiled=True), 0)[:, :rows_own]
    taps_shard = small_grad[: 3 * KERNEL].reshape(3, KERNEL, rows_own).swapaxes(1, 2)
    taps_shard = taps_shard.reshape(3 * rows_own, KERNEL)
    head_shard, gain_one_shard, gain_two_shard = small_grad[3 * KERNEL : 3 * KERNEL + 3]

    updown_grad = tie(updown_grad, mixer_terms).reshape(parts, rows_own, 2 * units)
    updown_grad = exchange(updown_grad)
    mixer_grad = tie(mixer_grad, updown_grad, input_grad)
    updown_shard = updown_from_parts(tie(updown_grad, mixer_grad))
    down_shard = halve_second(tie_all(down_grad, input_grad), mixer_grad)
    out_grads = tie(halve_cores(tie(out_grads, input_grad)), mixer_grad)
    out_shard = halve_second(halve_first(out_grads))
    mixer_grad = exchange(mixer_grad.reshape(parts, rows_own, wide))
    qkv_shard, gate_shard, strengths = mixer_from_parts(mixer_grad, width)
    beta_shard = strengths.reshape(rows_own, parts, SMALL)[:, :, :heads_part]
    return (
        block_out,
        input_grad,
        gain_one_shard,
        taps_shard,
        head_shard,
        qkv_shard,
        beta_shard.reshape(rows_own, HEADS),
        gate_shard,
        out_shard,
        gain_two_shard,
        updown_shard,
        down_shard,
    )


def solution(mesh):
    placed = (
        P("dp", None),
        P("dp", None),
        P("dp"),
        P("dp", None),
        P("dp"),
        P("dp", None),
        P("dp", None),
        P("dp", None),
        P("dp", None),
        P("dp"),
        P("dp", None),
        P("dp", None),
        P("dp", None),
        P("dp"),
    )
    return jax.shard_map(
        body,
        mesh=mesh,
        in_specs=placed,
        out_specs=(
            P("dp", None),
            P("dp", None),
            P("dp"),
            P("dp", None),
            P("dp"),
            P("dp", None),
            P("dp", None),
            P("dp", None),
            P("dp", None),
            P("dp"),
            P("dp", None),
            P("dp", None),
        ),
        check_vma=False,
    )
```

```python
import functools

import jax
import jax.numpy as jnp
from jax import lax
from jax.experimental import pallas as pl
from jax.experimental.pallas import tpu as pltpu
from jax.sharding import PartitionSpec as P

D = 2048
HEADS = 16
HEAD_DIM = 128
FF = 5632
KERNEL = 4
BLOCK_ROWS = 64
BLOCKS_DEV = 2
GROUP_ROWS = BLOCK_ROWS * BLOCKS_DEV
SMALL = 128
MODEL = 4

f32 = jnp.float32
bf = jnp.bfloat16


def block_layouts(first, second, lead):
    def doc(block):
        in_first = (block >= lead) & (block < lead + first)
        in_second = (block >= lead + first) & (block < lead + first + second)
        return jnp.where(in_first, 1, jnp.where(in_second, 2, 0))

    starts = (lead == 1) | (lead + first == 1) & (second > 0)
    columns = [doc(0) > 0, doc(1) > 0, doc(0) == doc(1), ~starts]
    return jnp.stack(columns, 1).astype(f32)


def plain_product(left, right):
    return jnp.dot(left, right, preferred_element_type=f32)


def rows_product(left, right):
    return lax.dot_general(left, right, (((0,), (0,)), ((), ())), preferred_element_type=f32)


def transposed_product(left, right):
    return lax.dot_general(left, right, (((1,), (1,)), ((), ())), preferred_element_type=f32)


def halves(values):
    high = values.astype(bf)
    return high, (values - high.astype(f32)).astype(bf)


def exact(left, right, left_dim, right_dim):
    left_high, left_low = left if isinstance(left, tuple) else halves(left)
    right_high, right_low = right if isinstance(right, tuple) else halves(right)
    return lax.dot_general(
        jnp.concatenate([left_high, left_high, left_low], left_dim),
        jnp.concatenate([right_high, right_low, right_high], right_dim),
        (((left_dim,), (right_dim,)), ((), ())),
        preferred_element_type=f32,
    )


def stacked(first, second):
    return tuple(jnp.concatenate([a, b], 0) for a, b in zip(first, second))


class Tile:
    def __init__(self, layout_ref, group):
        live_first, live_second, same, persist = (layout_ref[group, i] for i in range(4))
        shape = (GROUP_ROWS, HEAD_DIM)
        row = lax.broadcasted_iota(jnp.int32, shape, 0)
        col = lax.broadcasted_iota(jnp.int32, shape, 1)
        late = row >= BLOCK_ROWS
        self.row, self.col = row, col
        self.live = jnp.where(late, live_second, live_first)
        self.taps = [None] + [
            jnp.where(
                row < offset,
                0.0,
                jnp.where(late & (row < BLOCK_ROWS + offset), same, 1.0),
            )
            for offset in range(1, KERNEL)
        ]
        cross = jnp.where(late & (col < BLOCK_ROWS), persist, 1.0)
        self.lower = jnp.where(row > col, cross, 0.0)
        self.lower_full = jnp.where(row >= col, cross, 0.0)

    def earlier(self, values, offset):
        return pltpu.roll(values, offset, 0) * self.taps[offset]

    def later(self, values, offset):
        return pltpu.roll(values * self.taps[offset], GROUP_ROWS - offset, 0)


def convolve(tile, values, taps):
    total = values * taps[0]
    for offset in range(1, KERNEL):
        total = total + tile.earlier(values, offset) * taps[offset]
    return total


def unit_scale(values):
    return lax.rsqrt(jnp.sum(values * values, -1, keepdims=True) + 1e-06)


def head_columns(part_width, section, head):
    return pl.ds(section * part_width + head * HEAD_DIM, HEAD_DIM)


def unit_inverses(tile, lowers):
    eye = jnp.where(tile.row == tile.col, 1.0, 0.0)
    inverses = None
    size = 1
    while size < GROUP_ROWS:
        pair = tile.row // (2 * size) == tile.col // (2 * size)
        split = pair & (tile.row // size != tile.col // size)
        parts = [jnp.where(split, lower, 0.0) for lower in lowers]
        if inverses is None:
            inverses = [eye - part for part in parts]
        else:
            kept = [halves(inverse) for inverse in inverses]
            inner = [exact(part, known, 1, 0) for part, known in zip(parts, kept)]
            outer = [exact(known, value, 1, 0) for known, value in zip(kept, inner)]
            inverses = [inverse - value for inverse, value in zip(inverses, outer)]
        size *= 2
    return inverses


def mixer_forward_kernel(
    layout_ref, pre_ref, param_ref, mixed_ref, inverse_ref, score_ref, solved_ref, out_ref
):
    width = mixed_ref.shape[1]
    heads = range(width // HEAD_DIM)
    tile = Tile(layout_ref, pl.program_id(0))
    queries, keys, values, strengths = [], [], [], []
    for head in heads:
        parts = []
        for section in range(3):
            columns = head_columns(width, section, head)
            taps = [param_ref[offset : offset + 1, columns] for offset in range(KERNEL)]
            convolved = convolve(tile, pre_ref[:, columns], taps)
            parts.append(convolved * jax.nn.sigmoid(convolved))
        queries.append(parts[0] * (unit_scale(parts[0]) * HEAD_DIM**-0.5))
        keys.append(parts[1] * unit_scale(parts[1]))
        values.append(parts[2])
        start = 4 * width + head
        strengths.append(jax.nn.sigmoid(pre_ref[:, start : start + 1]) * tile.live)
    lowers, scores = [], []
    for head in heads:
        key_halves = halves(keys[head])
        both = exact(stacked(key_halves, halves(queries[head])), key_halves, 1, 1)
        lowers.append(both[:GROUP_ROWS] * strengths[head] * tile.lower)
        scores.append(both[GROUP_ROWS:] * tile.lower_full)
    inverses = unit_inverses(tile, lowers)
    solved = [exact(inverses[head], values[head] * strengths[head], 1, 0) for head in heads]
    outs = [exact(scores[head], solved[head], 1, 0) for head in heads]
    for head in heads:
        out = outs[head]
        scaled = out * lax.rsqrt(jnp.mean(out * out, -1, keepdims=True) + 1e-05)
        gate = pre_ref[:, head_columns(width, 3, head)]
        gain = param_ref[KERNEL : KERNEL + 1, head_columns(width, 0, head)]
        mixed = scaled * gain * (gate * jax.nn.sigmoid(gate)) * tile.live
        mixed_ref[:, head_columns(width, 0, head)] = mixed.astype(bf)
        inverse_ref[head] = inverses[head]
        score_ref[head] = scores[head]
        solved_ref[head] = solved[head]
        out_ref[head] = out


def mixer_backward_kernel(
    layout_ref,
    pre_ref,
    param_ref,
    weight_ref,
    inverse_ref,
    score_ref,
    solved_ref,
    out_ref,
    *refs,
):
    *mixed_refs, d_pre_ref, d_param_ref, grad_ref = refs
    width = grad_ref.shape[1]
    heads = range(width // HEAD_DIM)
    tile = Tile(layout_ref, pl.program_id(0))
    for group, mixed_ref in enumerate(mixed_refs):

        @pl.when(pl.program_id(0) == group)
        def _():
            grad_ref[...] = transposed_product(mixed_ref[...], weight_ref[...])

    @pl.when(pl.program_id(0) == 0)
    def _():
        d_param_ref[...] = jnp.zeros_like(d_param_ref)

    def along(values):
        return jnp.sum(values, -1, keepdims=True)

    d_outs = []
    for head in heads:
        columns = head_columns(width, 0, head)
        d_mixed = grad_ref[:, columns] * tile.live
        out = out_ref[head]
        scale = lax.rsqrt(jnp.mean(out * out, -1, keepdims=True) + 1e-05)
        scaled = out * scale
        gate = pre_ref[:, head_columns(width, 3, head)]
        gate_open = jax.nn.sigmoid(gate)
        gain = param_ref[KERNEL : KERNEL + 1, columns]
        gated = d_mixed * (gate * gate_open)
        d_param_ref[KERNEL : KERNEL + 1, columns] += jnp.sum(gated * scaled, 0, keepdims=True)
        d_gate = d_mixed * scaled * gain * (gate_open * (1.0 + gate * (1.0 - gate_open)))
        d_pre_ref[:, head_columns(width, 3, head)] = d_gate.astype(bf)
        d_scaled = gated * gain
        mean = jnp.mean(d_scaled * out, -1, keepdims=True)
        d_outs.append(scale * d_scaled - out * (scale * scale * scale * mean))
    d_out_halves = [halves(value) for value in d_outs]
    solved_halves = [halves(solved_ref[head]) for head in heads]
    d_solved = [exact(score_ref[head], d_out_halves[head], 0, 0) for head in heads]
    d_scores = [
        exact(d_out_halves[head], solved_halves[head], 1, 1) * tile.lower_full for head in heads
    ]
    d_inner = [exact(inverse_ref[head], d_solved[head], 0, 0) for head in heads]
    d_lowers = [exact(d_inner[head], solved_halves[head], 1, 1) * -tile.lower for head in heads]
    d_beta = jnp.zeros((GROUP_ROWS, SMALL), f32)
    for head in heads:
        pres, convolved, opened, active = [], [], [], []
        for section in range(3):
            columns = head_columns(width, section, head)
            taps = [param_ref[offset : offset + 1, columns] for offset in range(KERNEL)]
            pres.append(pre_ref[:, columns])
            convolved.append(convolve(tile, pres[section], taps))
            opened.append(jax.nn.sigmoid(convolved[section]))
            active.append(convolved[section] * opened[section])
        query_scale = unit_scale(active[0])
        key_scale = unit_scale(active[1])
        query_unit = active[0] * query_scale
        key = active[1] * key_scale
        start = 4 * width + head
        opening = jax.nn.sigmoid(pre_ref[:, start : start + 1])
        strength = opening * tile.live
        d_both = stacked(halves(d_lowers[head]), halves(d_scores[head]))
        by_key = exact(d_both, key, 1, 0)
        d_query = by_key[GROUP_ROWS:] * HEAD_DIM**-0.5
        from_lower = by_key[:GROUP_ROWS]
        weighted = stacked(halves(key * strength), halves(query_unit * HEAD_DIM**-0.5))
        d_key = strength * from_lower + exact(d_both, weighted, 0, 0)
        d_strength = along(d_inner[head] * active[2] + from_lower * key)
        d_value = d_inner[head] * strength
        d_opening = d_strength * (opening * (1.0 - opening)) * tile.live
        d_beta = d_beta + jnp.where(tile.col == head, d_opening, 0.0)
        d_active = [
            (d_query - query_unit * along(query_unit * d_query)) * query_scale,
            (d_key - key * along(key * d_key)) * key_scale,
            d_value,
        ]
        for section in range(3):
            columns = head_columns(width, section, head)
            taps = [param_ref[offset : offset + 1, columns] for offset in range(KERNEL)]
            slope = opened[section] * (1.0 + convolved[section] * (1.0 - opened[section]))
            d_convolved = d_active[section] * slope
            d_pre = d_convolved * taps[0]
            sums = [jnp.sum(d_convolved * pres[section], 0, keepdims=True)]
            for offset in range(1, KERNEL):
                d_pre = d_pre + tile.later(d_convolved, offset) * taps[offset]
                sums.append(
                    jnp.sum(d_convolved * tile.earlier(pres[section], offset), 0, keepdims=True)
                )
            d_param_ref[0:KERNEL, columns] += jnp.concatenate(sums, 0)
            d_pre_ref[:, columns] = d_pre.astype(bf)
    d_pre_ref[:, 4 * width :] = d_beta.astype(bf)


NO_COST = pl.CostEstimate(flops=0, bytes_accessed=0, transcendentals=0)


def call(kernel, operands, in_specs, out_specs, out_shape, grid=(), scratch=(), micros=0):
    results = pl.pallas_call(
        kernel,
        grid=grid,
        in_specs=in_specs,
        out_specs=out_specs,
        out_shape=out_shape,
        scratch_shapes=scratch,
        compiler_params=pltpu.CompilerParams(
            dimension_semantics=("arbitrary",) * len(grid), vmem_limit_bytes=48 * 2**20
        ),
        cost_estimate=pl.CostEstimate(
            flops=micros * 10**9, bytes_accessed=0, transcendentals=0
        ),
    )(*operands)
    return list(results)


def whole(array):
    return pl.BlockSpec(array.shape, lambda *step: (0,) * len(array.shape))


def mixer_specs(width):
    wide = 4 * width + SMALL
    heads = width // HEAD_DIM
    layout = pl.BlockSpec(memory_space=pltpu.SMEM)
    pre = pl.BlockSpec((GROUP_ROWS, wide), lambda group: (group, 0))
    param = pl.BlockSpec((2 * KERNEL, 3 * width), lambda group: (0, 0))
    narrow = pl.BlockSpec((GROUP_ROWS, width), lambda group: (group, 0))
    square = pl.BlockSpec((heads, GROUP_ROWS, HEAD_DIM), lambda group: (group, 0, 0))
    return layout, pre, param, narrow, square


def mixer_forward(layout, pre, params, width):
    groups = layout.shape[0]
    layout_spec, pre_spec, param_spec, narrow, square = mixer_specs(width)
    squares = pltpu.HBM((groups * width // HEAD_DIM, GROUP_ROWS, HEAD_DIM), f32)
    return call(
        mixer_forward_kernel,
        [layout, pre, params],
        [layout_spec, pre_spec, param_spec],
        [narrow] + [square] * 4,
        [jax.ShapeDtypeStruct((groups * GROUP_ROWS, width), bf)] + [squares] * 4,
        (groups,),
    )


def mixer_backward(layout, pre, params, weight, d_mixed, kept, width):
    groups = layout.shape[0]
    layout_spec, pre_spec, param_spec, _, square = mixer_specs(width)
    kept = [pltpu.with_memory_space_constraint(array, pltpu.HBM) for array in kept]
    return call(
        mixer_backward_kernel,
        [layout, pre, params, weight, *kept, *d_mixed],
        [layout_spec, pre_spec, param_spec, whole(weight)]
        + [square] * 4
        + [whole(block) for block in d_mixed],
        [pre_spec, param_spec],
        [jax.ShapeDtypeStruct(pre.shape, bf), jax.ShapeDtypeStruct(params.shape, f32)],
        (groups,),
        [pltpu.VMEM((GROUP_ROWS, width), f32)],
        micros=60,
    )


def first_kernel(gain_ref, weight_ref, *refs):
    *value_refs, normed_ref, out_ref, scale_ref, total_ref = refs
    step, depth = pl.program_id(0), weight_ref.shape[0]

    @pl.when(step == 0)
    def _():
        for group, ref in enumerate(value_refs):
            values = ref[...].astype(f32)
            scale = lax.rsqrt(jnp.mean(values * values, -1, keepdims=True) + 1e-06)
            rows = pl.ds(group * GROUP_ROWS, GROUP_ROWS)
            scale_ref[rows, :] = jnp.broadcast_to(scale, (GROUP_ROWS, 128))
        total_ref[...] = jnp.zeros_like(total_ref)

    columns = pl.ds(pl.multiple_of(step * depth, depth), depth)
    for group, ref in enumerate(value_refs):
        rows = pl.ds(group * GROUP_ROWS, GROUP_ROWS)
        values = ref[:, columns].astype(f32) * scale_ref[rows, :1] * gain_ref[...]
        normed_ref[rows, :] = values.astype(bf)
    total_ref[...] += plain_product(normed_ref[...], weight_ref[...])

    @pl.when(step == pl.num_programs(0) - 1)
    def _():
        out_ref[...] = total_ref[...]


def normed_product(blocks, gain, weight, depth=512):
    rows, (features, columns) = len(blocks) * GROUP_ROWS, weight.shape
    return call(
        first_kernel,
        [gain, weight, *blocks],
        [
            pl.BlockSpec((1, depth), lambda step: (0, step)),
            pl.BlockSpec((depth, columns), lambda step: (step, 0)),
        ]
        + [whole(block) for block in blocks],
        [
            pl.BlockSpec((rows, depth), lambda step: (0, step)),
            pl.BlockSpec((rows, columns), lambda step: (0, 0)),
        ],
        [
            jax.ShapeDtypeStruct((rows, features), bf),
            jax.ShapeDtypeStruct((rows, columns), f32),
        ],
        (features // depth,),
        [pltpu.VMEM((rows, 128), f32), pltpu.VMEM((rows, columns), f32)],
    )


def product_blocks(left, right, transposed=False, block=512, micros=0):
    product = transposed_product if transposed else plain_product
    columns = right.shape[0] if transposed else right.shape[1]
    groups = left.shape[0] // GROUP_ROWS

    def kernel(left_ref, right_ref, *out_refs):
        total = product(left_ref[...], right_ref[...])
        for group, ref in enumerate(out_refs):
            ref[...] = total[group * GROUP_ROWS : (group + 1) * GROUP_ROWS].astype(ref.dtype)

    if transposed:
        right_spec = pl.BlockSpec((block, right.shape[1]), lambda step: (step, 0))
    else:
        right_spec = pl.BlockSpec((right.shape[0], block), lambda step: (0, step))
    return call(
        kernel,
        [left, right],
        [whole(left), right_spec],
        [pl.BlockSpec((GROUP_ROWS, block), lambda step: (0, step))] * groups,
        [
            jax.ShapeDtypeStruct((GROUP_ROWS, columns), bf if group else f32)
            for group in range(groups)
        ],
        (columns // block,),
        micros=micros,
    )


def grad_product(left, right, block=256, micros=0):
    rows, features = left.shape
    if features % block:
        block = 128

    def kernel(left_ref, right_ref, out_ref):
        out_ref[...] = rows_product(left_ref[...], right_ref[...]).astype(bf)

    return call(
        kernel,
        [left, right],
        [pl.BlockSpec((rows, block), lambda step: (0, step)), whole(right)],
        [pl.BlockSpec((block, right.shape[1]), lambda step: (step, 0))],
        [pltpu.HBM((features, right.shape[1]), bf)],
        (features // block,),
        micros=micros,
    )[0]


def from_own(part, values):
    groups = values.shape[0] // GROUP_ROWS

    def kernel(part_ref, values_ref, out_ref):
        for step in range(groups):
            source = lax.rem(part_ref[0] + groups - step, groups) * GROUP_ROWS
            rows = pl.ds(pl.multiple_of(source, GROUP_ROWS), GROUP_ROWS)
            out_ref[step * GROUP_ROWS : (step + 1) * GROUP_ROWS] = values_ref[rows]

    return call(
        kernel,
        [part.reshape(1).astype(jnp.int32), values],
        [pl.BlockSpec(memory_space=pltpu.SMEM), whole(values)],
        [whole(values)],
        [jax.ShapeDtypeStruct(values.shape, values.dtype)],
        (1,),
    )[0]


def tie_all(values, *others):
    anywhere = pl.BlockSpec(memory_space=pl.ANY)
    others = [
        pltpu.with_memory_space_constraint(other, pltpu.HBM) if other.size > 2**21 else other
        for other in others
    ]
    tied = pl.pallas_call(
        lambda *refs: None,
        in_specs=[anywhere] * (len(values) + len(others)),
        out_specs=[anywhere] * len(values),
        out_shape=[
            (pltpu.HBM if value.size > 2**21 else jax.ShapeDtypeStruct)(value.shape, value.dtype)
            for value in values
        ],
        input_output_aliases={i: i for i in range(len(values))},
        cost_estimate=NO_COST,
    )(*values, *others)
    return list(tied)


def tie(value, *others):
    return tie_all([value], *others)[0]


def assemble(part, values, received, others):
    parts = values.shape[0]

    def kernel(part_ref, values_ref, *refs):
        own = part_ref[0]
        out_ref = refs[-1]
        out_ref[own] = values_ref[own]
        for step in range(1, parts):
            out_ref[lax.rem(own + parts - step, parts)] = refs[step - 1][...]

    vmem = pl.BlockSpec(memory_space=pltpu.VMEM)
    anywhere = pl.BlockSpec(memory_space=pl.ANY)
    return pl.pallas_call(
        kernel,
        in_specs=[pl.BlockSpec(memory_space=pltpu.SMEM)]
        + [vmem] * parts
        + [anywhere] * len(others),
        out_specs=vmem,
        out_shape=jax.ShapeDtypeStruct(values.shape, values.dtype),
        compiler_params=pltpu.CompilerParams(vmem_limit_bytes=32 * 2**20),
        cost_estimate=NO_COST,
    )(part.reshape(1).astype(jnp.int32), values, *received, *others)


def copy_columns(count, *refs):
    target = refs[-1]
    start = 0
    for source in refs[:count]:
        block = source[...].reshape(source.shape[-2:])
        columns = pl.ds(start, block.shape[1])
        if len(target.shape) == 3:
            target[0, :, columns] = block.astype(target.dtype)
        else:
            target[:, columns] = block.astype(target.dtype)
        start += block.shape[1]


def to_parts(sources, parts, dtype, others=()):
    rows = sources[0][0].shape[0]

    def spec(section, width):
        return pl.BlockSpec((rows, width), lambda p: (0, section * parts + p))

    total = sum(width for _, _, width in sources)
    return pl.pallas_call(
        functools.partial(copy_columns, len(sources)),
        grid=(parts,),
        in_specs=[spec(section, width) for _, section, width in sources]
        + [pl.BlockSpec(memory_space=pl.ANY)] * len(others),
        out_specs=pl.BlockSpec((1, rows, total), lambda p: (p, 0, 0)),
        out_shape=jax.ShapeDtypeStruct((parts, rows, total), dtype),
        cost_estimate=NO_COST,
    )(*[array for array, _, _ in sources], *others)


def updown_from_parts(slabs):
    parts, rows, width = slabs.shape
    units = width // 2

    def kernel(slabs_ref, out_ref):
        for p in range(parts):
            out_ref[:, p * units : (p + 1) * units] = slabs_ref[p].astype(f32)

    return pl.pallas_call(
        kernel,
        grid=(2,),
        in_specs=[pl.BlockSpec((parts, rows, units), lambda half: (0, 0, half))],
        out_specs=pl.BlockSpec((rows, parts * units), lambda half: (0, half)),
        out_shape=jax.ShapeDtypeStruct((rows, parts * width), f32),
        compiler_params=pltpu.CompilerParams(vmem_limit_bytes=32 * 2**20),
        cost_estimate=NO_COST,
    )(slabs)


def mixer_from_parts(slabs, width):
    parts, rows, _ = slabs.shape

    def kernel(slabs_ref, qkv_ref, gate_ref, strength_ref):
        for p in range(parts):
            for section in range(4):
                block = slabs_ref[p, :, section * width : (section + 1) * width].astype(f32)
                if section < 3:
                    start = (section * parts + p) * width
                    qkv_ref[:, start : start + width] = block
                else:
                    gate_ref[:, p * width : (p + 1) * width] = block
            last = slabs_ref[p, :, 4 * width :].astype(f32)
            strength_ref[:, p * SMALL : (p + 1) * SMALL] = last

    widths = [3 * parts * width, parts * width, parts * SMALL]
    return pl.pallas_call(
        kernel,
        out_shape=[jax.ShapeDtypeStruct((rows, size), f32) for size in widths],
        compiler_params=pltpu.CompilerParams(vmem_limit_bytes=32 * 2**20),
        cost_estimate=NO_COST,
    )(slabs)


def own_order(values, parts, copies):
    size = values.shape[1] // (parts * copies)
    pieces = [
        values[:, (t * parts + m) * size : (t * parts + m + 1) * size]
        for m in range(parts)
        for t in range(copies)
    ]
    return jnp.concatenate(pieces, 1)


def total_of(own_ref, received_refs):
    total = own_ref[...]
    for ref in received_refs:
        total = total + ref[...].astype(f32)
    return total


def row_scale(values):
    return lax.rsqrt(jnp.mean(values * values, -1, keepdims=True) + 1e-06)


def norm_slope(values, scale, gain, grad):
    mean = jnp.mean(gain * grad * values, -1, keepdims=True)
    return scale * gain * grad - values * (scale * scale * scale * mean)


def hidden_kernel(own_ref, *refs):
    *received, input_ref, gain_ref, hidden_ref, normed_ref = refs
    hidden = input_ref[...].astype(f32) + total_of(own_ref, received)
    hidden_ref[...] = hidden
    normed_ref[...] = (hidden * row_scale(hidden) * gain_ref[...]).astype(bf)


def hidden_back_kernel(own_ref, *refs):
    *received, hidden_ref, gain_ref, cot_ref, d_hidden_ref, d_mixed_ref, d_gain_ref = refs
    grad = total_of(own_ref, received)
    hidden = hidden_ref[...]
    scale = row_scale(hidden)

    @pl.when(pl.program_id(0) == 0)
    def _():
        d_gain_ref[...] = jnp.zeros_like(d_gain_ref)

    d_gain_ref[...] += jnp.sum(grad * hidden * scale, 0, keepdims=True)
    d_hidden = cot_ref[...].astype(f32) + norm_slope(hidden, scale, gain_ref[...], grad)
    d_hidden_ref[...] = d_hidden
    d_mixed_ref[...] = d_hidden.astype(bf)


def input_back_kernel(parts, copies, own_ref, *refs):
    *received, input_ref, gain_ref, d_hidden_ref, out_ref = refs
    grad = total_of(own_ref, received)
    values = input_ref[...].astype(f32)
    slope = norm_slope(values, row_scale(values), gain_ref[...], grad)
    out_ref[...] = own_order(d_hidden_ref[...] + slope, parts, copies).astype(bf)


def block_out_kernel(parts, copies, own_ref, *refs):
    *received, hidden_ref, out_ref = refs
    total = hidden_ref[...] + total_of(own_ref, received)
    out_ref[...] = own_order(total, parts, copies).astype(bf)


def last_sum(sides, others, parts, copies):
    rows, columns = sides[0].shape

    def kernel(*refs):
        first, first_other, second, second_other = (ref[...].astype(f32) for ref in refs[:4])
        total = jnp.concatenate([first + first_other, second + second_other], 1)
        refs[-1][...] = own_order(total, parts, copies)

    vmem = pl.BlockSpec(memory_space=pltpu.VMEM)
    return pl.pallas_call(
        kernel,
        in_specs=[vmem] * 4 + [pl.BlockSpec(memory_space=pl.ANY)] * len(others),
        out_specs=vmem,
        out_shape=jax.ShapeDtypeStruct((rows, 2 * columns), f32),
        compiler_params=pltpu.CompilerParams(vmem_limit_bytes=32 * 2**20),
        cost_estimate=NO_COST,
    )(*sides, *others)


def by_rows(kernel, arrays, outs, block=64):
    def spec(shape):
        if shape[0] == 1:
            return pl.BlockSpec(shape, lambda i: (0, 0))
        return pl.BlockSpec((block, shape[1]), lambda i: (i, 0))

    return pl.pallas_call(
        kernel,
        grid=(GROUP_ROWS // block,),
        in_specs=[spec(array.shape) for array in arrays],
        out_specs=[spec(shape) for shape, _ in outs],
        out_shape=[jax.ShapeDtypeStruct(shape, dtype) for shape, dtype in outs],
        compiler_params=pltpu.CompilerParams(dimension_semantics=("arbitrary",)),
        cost_estimate=NO_COST,
    )(*arrays)


def body(
    block_in,
    out_grad,
    norm1_gain,
    conv_weight,
    head_gain,
    qkv_weight,
    beta_weight,
    gate_weight,
    out_weight,
    norm2_gain,
    updown_weight,
    down_weight,
    seq_blocks,
    lead_blocks,
):
    devices = lax.axis_size("dp")
    parts = MODEL
    copies = devices // parts
    part = lax.axis_index("dp") // copies
    copy = lax.axis_index("dp") % copies
    rows_own = qkv_weight.shape[0]
    width = D // parts
    units = FF // parts
    heads_part = HEADS // parts
    wide = 4 * width + SMALL
    model_groups = [[m * copies + t for m in range(parts)] for t in range(copies)]
    copy_groups = [[m * copies + t for t in range(copies)] for m in range(parts)]

    def exchange(values):
        return lax.all_to_all(
            values, "dp", split_axis=0, concat_axis=0, axis_index_groups=model_groups, tiled=True
        )

    def shift(values, step):
        pairs = [
            (m * copies + t, (m + step) % parts * copies + t)
            for m in range(parts)
            for t in range(copies)
        ]
        return lax.ppermute(values, "dp", pairs)

    def exchange_apart(values, before, after=()):
        cut = [
            lax.dynamic_index_in_dim(values, (part + step) % parts, 0, keepdims=False)
            for step in range(1, parts)
        ]
        received = [shift(piece, step) for step, piece in enumerate(tie_all(cut, *before), 1)]
        return assemble(part, values, received, after)

    def gather_rows(values):
        return [values] + [shift(values, step) for step in range(1, parts)]

    def scatter_rows(terms):
        return [terms[0]] + [shift(block, -step) for step, block in enumerate(terms[1:], 1)]

    def gather_copies(values):
        return lax.all_gather(values, "dp", axis=0, axis_index_groups=copy_groups, tiled=True)

    def scatter_copies(values):
        return lax.psum_scatter(
            values.astype(bf),
            "dp",
            scatter_dimension=0,
            axis_index_groups=copy_groups,
            tiled=True,
        )

    def halves_across(values, bit, axis):
        pairs = [(i, i ^ (1 << bit)) for i in range(devices)]
        side = (copy >> bit) & 1
        own = lax.dynamic_index_in_dim(values, side, axis, keepdims=False)
        other = lax.dynamic_index_in_dim(values, 1 - side, axis, keepdims=False)
        return own, lax.ppermute(other, "dp", pairs)

    def halve(values, bit, axis, *others):
        own, received = halves_across(values, bit, axis)
        if others:
            received = tie(received, *others)
        return (own.astype(f32) + received.astype(f32)).astype(bf)

    by_halves = copies == 8

    def halve_cores(values, *others):
        if not by_halves:
            return values
        rows, columns = values.shape
        return halve(values.reshape(2, 2, 2, rows // 8, columns), 0, 2, *others)

    def halve_first(values):
        if not by_halves:
            return [values]
        middle = values.shape[-1] // 2
        return [halve(values[..., :middle], 1, 1), halve(values[..., middle:], 2, 0)]

    def halve_second(values, *others):
        if not by_halves:
            return from_wire(scatter_copies(values[0]).astype(f32))
        sides = halves_across(values[0], 2, 0) + halves_across(values[1], 1, 0)
        return last_sum(sides, others, parts, copies)

    def to_wire(values):
        return values.reshape(-1, parts, copies, rows_own).swapaxes(1, 2).reshape(-1, D)

    def from_wire(values):
        return values.reshape(-1, copies, parts, rows_own).swapaxes(1, 2).reshape(-1, D)

    w_out_own = to_wire(out_weight.astype(bf))
    w_out = gather_copies(w_out_own)
    strengths = beta_weight.reshape(rows_own, parts, heads_part)
    strengths = jnp.pad(strengths, ((0, 0), (0, 0), (0, SMALL - heads_part)))
    strengths = tie(strengths.reshape(rows_own, parts * SMALL), w_out_own)
    pieces = [(qkv_weight, section, width) for section in range(3)]
    pieces = to_parts(pieces + [(gate_weight, 0, width), (strengths, 0, SMALL)], parts, bf)
    mixer_pieces = tie(exchange(pieces), w_out)
    w_mixer = gather_copies(mixer_pieces.reshape(parts * rows_own, wide))
    inputs = tie(to_wire(block_in), mixer_pieces)
    input_rows = gather_rows(inputs)

    lanes = -(-3 * rows_own // 128) * 128
    numbers = jnp.concatenate([seq_blocks[0], lead_blocks]).astype(f32)
    small = [conv_weight.T, norm1_gain[None], head_gain[None], norm2_gain[None], numbers[None]]
    small = [jnp.pad(rows, ((0, 0), (0, lanes - rows.shape[1]))) for rows in small]
    small = jnp.pad(jnp.concatenate(small, 0).astype(bf), ((0, 2 * KERNEL), (0, 0)))
    small = jnp.broadcast_to(small[None], (devices,) + small.shape)
    small = lax.all_to_all(tie(small, *input_rows[1:]), "dp", 0, 0, tiled=True)
    taps = small[:, :KERNEL, : 3 * rows_own].swapaxes(0, 1).reshape(KERNEL, 3, parts, width)
    taps = lax.dynamic_index_in_dim(taps, part, 2, keepdims=False).reshape(KERNEL, 3 * width)
    gain_one, head_full, gain_two = (
        small[:, KERNEL + i, :rows_own].reshape(1, D).astype(f32) for i in range(3)
    )
    gain_one, gain_two = to_wire(gain_one), to_wire(gain_two)
    head_part = lax.dynamic_slice_in_dim(head_full, part * width, width, 1)
    params = jnp.concatenate([taps.astype(f32), jnp.pad(head_part, ((0, 0), (0, 2 * width)))], 0)
    params = jnp.pad(params, ((0, KERNEL - 1), (0, 0)))
    numbers = small[:, KERNEL + 3, :3].astype(f32).astype(jnp.int32)
    layouts = block_layouts(numbers[:, 0], numbers[:, 1], numbers[:, 2])
    layouts = layouts.reshape(parts, copies, 4)
    layouts = lax.dynamic_index_in_dim(layouts, copy, 1, keepdims=False)
    wanted = (part - jnp.arange(parts)) % parts
    wanted = (wanted[:, None] == jnp.arange(parts)).astype(f32)
    layouts = jnp.sum(wanted[:, :, None] * layouts, 1)

    pieces = [(updown_weight, half, units) for half in range(2)]
    updown_pieces = to_parts(pieces, parts, bf, [mixer_pieces])
    w_down_own = to_wire(down_weight.astype(bf))
    w_down = gather_copies(tie(w_down_own, *input_rows[1:]))
    cotangent_own = to_wire(out_grad)

    gain_first = tie(gain_one, w_down_own, cotangent_own, updown_pieces)
    normed, pre = normed_product(input_rows, gain_first, w_mixer)
    updown_pieces = exchange_apart(updown_pieces, input_rows[1:], [pre])
    mixed, *kept = mixer_forward(layouts, pre, params, width)
    out_terms = product_blocks(mixed, w_out)
    updown_pieces = tie(updown_pieces, w_down, mixed)
    w_updown = gather_copies(updown_pieces.reshape(parts * rows_own, 2 * units))
    stream = ((GROUP_ROWS, D), f32)
    narrow = ((GROUP_ROWS, D), bf)
    hidden, normed_two = by_rows(
        hidden_kernel,
        scatter_rows(out_terms) + [inputs, gain_two],
        [stream, narrow],
    )
    normed_two = jnp.concatenate(gather_rows(normed_two), 0)

    def swiglu_units(updown):
        return jax.nn.silu(updown[:, :units]) * updown[:, units:]

    updown = plain_product(normed_two, w_updown)
    cotangent = lax.all_gather(
        tie(cotangent_own, updown_pieces),
        "dp",
        axis=0,
        axis_index_groups=model_groups,
        tiled=True,
    )
    cotangent = from_own(part, tie(cotangent, updown))
    active, swiglu_back = jax.vjp(swiglu_units, updown)
    active = active.astype(bf)
    d_active = transposed_product(cotangent, w_down)
    d_updown = swiglu_back(d_active)[0].astype(bf)
    d_normed_two = product_blocks(d_updown, w_updown, transposed=True)
    active = tie(active, *d_normed_two[1:])
    down_terms = grad_product(active, cotangent)
    updown_terms = grad_product(normed_two, tie(d_updown, down_terms))
    gain_late = tie(gain_two, updown_terms)
    d_normed_two = scatter_rows(d_normed_two)
    updown_grad = scatter_copies(tie(updown_terms, gain_late, *d_normed_two[1:]))
    d_hidden, d_mixed, gain_two_grad = by_rows(
        hidden_back_kernel,
        d_normed_two + [hidden, gain_late, cotangent_own],
        [stream, narrow, ((1, D), f32)],
    )


    out_terms = product_blocks(tie(active, d_mixed), w_down)
    down_terms = tie(down_terms, *out_terms[1:])
    d_mixed = gather_rows(d_mixed)
    late = tie(params, *out_terms)
    out_terms[1:] = tie_all(out_terms[1:], *d_mixed[1:])
    d_pre, d_params = mixer_backward(layouts, pre, late, w_out, d_mixed, kept, width)
    mixer_terms = tie(grad_product(normed, d_pre, micros=20), updown_grad)
    mixer_grad = scatter_copies(mixer_terms)

    d_normed_terms = product_blocks(
        tie(d_pre, mixer_terms), w_mixer, transposed=True, micros=150
    )
    hidden = tie(hidden, d_normed_terms[0])
    (block_out,) = by_rows(
        functools.partial(block_out_kernel, parts, copies),
        scatter_rows(out_terms) + [hidden],
        [narrow],
    )
    d_normed_terms[1:] = tie_all(d_normed_terms[1:], block_out)
    d_normed = scatter_rows(d_normed_terms)
    down_grad = halve_first(halve_cores(down_terms, *d_normed_terms[1:]))
    gain_one_grad = 0.0
    for values, terms in zip(input_rows, d_normed_terms):
        values = values.astype(f32)
        terms = terms.astype(f32) * (values * row_scale(values))
        gain_one_grad = gain_one_grad + jnp.sum(terms, 0, keepdims=True)

    d_params = tie(d_params, mixer_terms)
    here = (jnp.arange(parts) == part).astype(f32)[:, None]
    taps_grad = d_params[:KERNEL].reshape(KERNEL, 3, 1, width) * here
    taps_grad = taps_grad.reshape(KERNEL, parts, copies, 3, rows_own).transpose(1, 2, 3, 0, 4)
    taps_grad = taps_grad.reshape(devices, 3 * KERNEL, rows_own)
    head_grad = (d_params[KERNEL, :width] * here).reshape(devices, 1, rows_own)
    gain_grads = [
        grad.reshape(copies, parts, 1, rows_own).swapaxes(0, 1).reshape(devices, 1, rows_own)
        for grad in (gain_one_grad, gain_two_grad)
    ]
    small_grad = jnp.concatenate([taps_grad, head_grad] + gain_grads, 1)
    d_mixed = jnp.concatenate([tie(d_mixed[0], d_normed_terms[0])] + d_mixed[1:], 0)
    out_grads = grad_product(mixed, d_mixed)
    late = tie(gain_one, out_grads, *down_grad)
    (input_grad,) = by_rows(
        functools.partial(input_back_kernel, parts, copies),
        d_normed + [inputs, late, d_hidden],
        [narrow],
    )
    small_grad = jnp.pad(tie(small_grad, input_grad), ((0, 0), (0, 1), (0, 128 - rows_own)))
    small_grad = jnp.sum(lax.all_to_all(small_grad, "dp", 0, 0, tiled=True), 0)[:, :rows_own]
    taps_shard = small_grad[: 3 * KERNEL].reshape(3, KERNEL, rows_own).swapaxes(1, 2)
    taps_shard = taps_shard.reshape(3 * rows_own, KERNEL)
    head_shard, gain_one_shard, gain_two_shard = small_grad[3 * KERNEL : 3 * KERNEL + 3]

    updown_grad = tie(updown_grad, mixer_terms).reshape(parts, rows_own, 2 * units)
    updown_grad = exchange(updown_grad)
    mixer_grad = tie(mixer_grad, updown_grad, input_grad)
    updown_shard = updown_from_parts(tie(updown_grad, mixer_grad))
    down_shard = halve_second(tie_all(down_grad, input_grad), mixer_grad)
    out_grads = tie(halve_cores(tie(out_grads, input_grad)), mixer_grad)
    out_shard = halve_second(halve_first(out_grads))
    mixer_grad = exchange(mixer_grad.reshape(parts, rows_own, wide))
    qkv_shard, gate_shard, strengths = mixer_from_parts(mixer_grad, width)
    beta_shard = strengths.reshape(rows_own, parts, SMALL)[:, :, :heads_part]
    return (
        block_out,
        input_grad,
        gain_one_shard,
        taps_shard,
        head_shard,
        qkv_shard,
        beta_shard.reshape(rows_own, HEADS),
        gate_shard,
        out_shard,
        gain_two_shard,
        updown_shard,
        down_shard,
    )


def solution(mesh):
    placed = (
        P("dp", None),
        P("dp", None),
        P("dp"),
        P("dp", None),
        P("dp"),
        P("dp", None),
        P("dp", None),
        P("dp", None),
        P("dp", None),
        P("dp"),
        P("dp", None),
        P("dp", None),
        P("dp", None),
        P("dp"),
    )
    return jax.shard_map(
        body,
        mesh=mesh,
        in_specs=placed,
        out_specs=(
            P("dp", None),
            P("dp", None),
            P("dp"),
            P("dp", None),
            P("dp"),
            P("dp", None),
            P("dp", None),
            P("dp", None),
            P("dp", None),
            P("dp"),
            P("dp", None),
            P("dp", None),
        ),
        check_vma=False,
    )
```

```python
import functools

import jax
import jax.numpy as jnp
from jax import lax
from jax.experimental import pallas as pl
from jax.experimental.pallas import tpu as pltpu
from jax.sharding import PartitionSpec as P

D = 2048
HEADS = 16
HEAD_DIM = 128
FF = 5632
KERNEL = 4
BLOCK_ROWS = 64
BLOCKS_DEV = 2
GROUP_ROWS = BLOCK_ROWS * BLOCKS_DEV
SMALL = 128
MODEL = 4

f32 = jnp.float32
bf = jnp.bfloat16


def block_layouts(first, second, lead):
    def doc(block):
        in_first = (block >= lead) & (block < lead + first)
        in_second = (block >= lead + first) & (block < lead + first + second)
        return jnp.where(in_first, 1, jnp.where(in_second, 2, 0))

    starts = (lead == 1) | (lead + first == 1) & (second > 0)
    columns = [doc(0) > 0, doc(1) > 0, doc(0) == doc(1), ~starts]
    return jnp.stack(columns, 1).astype(f32)


def plain_product(left, right):
    return jnp.dot(left, right, preferred_element_type=f32)


def rows_product(left, right):
    return lax.dot_general(left, right, (((0,), (0,)), ((), ())), preferred_element_type=f32)


def transposed_product(left, right):
    return lax.dot_general(left, right, (((1,), (1,)), ((), ())), preferred_element_type=f32)


def halves(values):
    high = values.astype(bf)
    return high, (values - high.astype(f32)).astype(bf)


def exact(left, right, left_dim, right_dim):
    left_high, left_low = left if isinstance(left, tuple) else halves(left)
    right_high, right_low = right if isinstance(right, tuple) else halves(right)
    return lax.dot_general(
        jnp.concatenate([left_high, left_high, left_low], left_dim),
        jnp.concatenate([right_high, right_low, right_high], right_dim),
        (((left_dim,), (right_dim,)), ((), ())),
        preferred_element_type=f32,
    )


def stacked(first, second):
    return tuple(jnp.concatenate([a, b], 0) for a, b in zip(first, second))


class Tile:
    def __init__(self, layout_ref, group):
        live_first, live_second, same, persist = (layout_ref[group, i] for i in range(4))
        shape = (GROUP_ROWS, HEAD_DIM)
        row = lax.broadcasted_iota(jnp.int32, shape, 0)
        col = lax.broadcasted_iota(jnp.int32, shape, 1)
        late = row >= BLOCK_ROWS
        self.row, self.col = row, col
        self.live = jnp.where(late, live_second, live_first)
        self.taps = [None] + [
            jnp.where(
                row < offset,
                0.0,
                jnp.where(late & (row < BLOCK_ROWS + offset), same, 1.0),
            )
            for offset in range(1, KERNEL)
        ]
        cross = jnp.where(late & (col < BLOCK_ROWS), persist, 1.0)
        self.lower = jnp.where(row > col, cross, 0.0)
        self.lower_full = jnp.where(row >= col, cross, 0.0)

    def earlier(self, values, offset):
        return pltpu.roll(values, offset, 0) * self.taps[offset]

    def later(self, values, offset):
        return pltpu.roll(values * self.taps[offset], GROUP_ROWS - offset, 0)


def convolve(tile, values, taps):
    total = values * taps[0]
    for offset in range(1, KERNEL):
        total = total + tile.earlier(values, offset) * taps[offset]
    return total


def unit_scale(values):
    return lax.rsqrt(jnp.sum(values * values, -1, keepdims=True) + 1e-06)


def head_columns(part_width, section, head):
    return pl.ds(section * part_width + head * HEAD_DIM, HEAD_DIM)


def unit_inverses(tile, lowers):
    eye = jnp.where(tile.row == tile.col, 1.0, 0.0)
    inverses = None
    size = 1
    while size < GROUP_ROWS:
        pair = tile.row // (2 * size) == tile.col // (2 * size)
        split = pair & (tile.row // size != tile.col // size)
        parts = [jnp.where(split, lower, 0.0) for lower in lowers]
        if inverses is None:
            inverses = [eye - part for part in parts]
        else:
            kept = [halves(inverse) for inverse in inverses]
            inner = [exact(part, known, 1, 0) for part, known in zip(parts, kept)]
            outer = [exact(known, value, 1, 0) for known, value in zip(kept, inner)]
            inverses = [inverse - value for inverse, value in zip(inverses, outer)]
        size *= 2
    return inverses


def mixer_forward_kernel(
    layout_ref, pre_ref, param_ref, mixed_ref, inverse_ref, score_ref, solved_ref, out_ref
):
    width = mixed_ref.shape[1]
    heads = range(width // HEAD_DIM)
    tile = Tile(layout_ref, pl.program_id(0))
    queries, keys, values, strengths = [], [], [], []
    for head in heads:
        parts = []
        for section in range(3):
            columns = head_columns(width, section, head)
            taps = [param_ref[offset : offset + 1, columns] for offset in range(KERNEL)]
            convolved = convolve(tile, pre_ref[:, columns], taps)
            parts.append(convolved * jax.nn.sigmoid(convolved))
        queries.append(parts[0] * (unit_scale(parts[0]) * HEAD_DIM**-0.5))
        keys.append(parts[1] * unit_scale(parts[1]))
        values.append(parts[2])
        start = 4 * width + head
        strengths.append(jax.nn.sigmoid(pre_ref[:, start : start + 1]) * tile.live)
    lowers, scores = [], []
    for head in heads:
        key_halves = halves(keys[head])
        both = exact(stacked(key_halves, halves(queries[head])), key_halves, 1, 1)
        lowers.append(both[:GROUP_ROWS] * strengths[head] * tile.lower)
        scores.append(both[GROUP_ROWS:] * tile.lower_full)
    inverses = unit_inverses(tile, lowers)
    solved = [exact(inverses[head], values[head] * strengths[head], 1, 0) for head in heads]
    outs = [exact(scores[head], solved[head], 1, 0) for head in heads]
    for head in heads:
        out = outs[head]
        scaled = out * lax.rsqrt(jnp.mean(out * out, -1, keepdims=True) + 1e-05)
        gate = pre_ref[:, head_columns(width, 3, head)]
        gain = param_ref[KERNEL : KERNEL + 1, head_columns(width, 0, head)]
        mixed = scaled * gain * (gate * jax.nn.sigmoid(gate)) * tile.live
        mixed_ref[:, head_columns(width, 0, head)] = mixed.astype(bf)
        inverse_ref[head] = inverses[head]
        score_ref[head] = scores[head]
        solved_ref[head] = solved[head]
        out_ref[head] = out


def mixer_backward_kernel(
    layout_ref,
    pre_ref,
    param_ref,
    weight_ref,
    inverse_ref,
    score_ref,
    solved_ref,
    out_ref,
    *refs,
):
    *mixed_refs, d_pre_ref, d_param_ref, grad_ref = refs
    width = grad_ref.shape[1]
    heads = range(width // HEAD_DIM)
    tile = Tile(layout_ref, pl.program_id(0))
    for group, mixed_ref in enumerate(mixed_refs):

        @pl.when(pl.program_id(0) == group)
        def _():
            grad_ref[...] = transposed_product(mixed_ref[...], weight_ref[...])

    @pl.when(pl.program_id(0) == 0)
    def _():
        d_param_ref[...] = jnp.zeros_like(d_param_ref)

    def along(values):
        return jnp.sum(values, -1, keepdims=True)

    d_outs = []
    for head in heads:
        columns = head_columns(width, 0, head)
        d_mixed = grad_ref[:, columns] * tile.live
        out = out_ref[head]
        scale = lax.rsqrt(jnp.mean(out * out, -1, keepdims=True) + 1e-05)
        scaled = out * scale
        gate = pre_ref[:, head_columns(width, 3, head)]
        gate_open = jax.nn.sigmoid(gate)
        gain = param_ref[KERNEL : KERNEL + 1, columns]
        gated = d_mixed * (gate * gate_open)
        d_param_ref[KERNEL : KERNEL + 1, columns] += jnp.sum(gated * scaled, 0, keepdims=True)
        d_gate = d_mixed * scaled * gain * (gate_open * (1.0 + gate * (1.0 - gate_open)))
        d_pre_ref[:, head_columns(width, 3, head)] = d_gate.astype(bf)
        d_scaled = gated * gain
        mean = jnp.mean(d_scaled * out, -1, keepdims=True)
        d_outs.append(scale * d_scaled - out * (scale * scale * scale * mean))
    d_out_halves = [halves(value) for value in d_outs]
    solved_halves = [halves(solved_ref[head]) for head in heads]
    d_solved = [exact(score_ref[head], d_out_halves[head], 0, 0) for head in heads]
    d_scores = [
        exact(d_out_halves[head], solved_halves[head], 1, 1) * tile.lower_full for head in heads
    ]
    d_inner = [exact(inverse_ref[head], d_solved[head], 0, 0) for head in heads]
    d_lowers = [exact(d_inner[head], solved_halves[head], 1, 1) * -tile.lower for head in heads]
    d_beta = jnp.zeros((GROUP_ROWS, SMALL), f32)
    for head in heads:
        pres, convolved, opened, active = [], [], [], []
        for section in range(3):
            columns = head_columns(width, section, head)
            taps = [param_ref[offset : offset + 1, columns] for offset in range(KERNEL)]
            pres.append(pre_ref[:, columns])
            convolved.append(convolve(tile, pres[section], taps))
            opened.append(jax.nn.sigmoid(convolved[section]))
            active.append(convolved[section] * opened[section])
        query_scale = unit_scale(active[0])
        key_scale = unit_scale(active[1])
        query_unit = active[0] * query_scale
        key = active[1] * key_scale
        start = 4 * width + head
        opening = jax.nn.sigmoid(pre_ref[:, start : start + 1])
        strength = opening * tile.live
        d_both = stacked(halves(d_lowers[head]), halves(d_scores[head]))
        by_key = exact(d_both, key, 1, 0)
        d_query = by_key[GROUP_ROWS:] * HEAD_DIM**-0.5
        from_lower = by_key[:GROUP_ROWS]
        weighted = stacked(halves(key * strength), halves(query_unit * HEAD_DIM**-0.5))
        d_key = strength * from_lower + exact(d_both, weighted, 0, 0)
        d_strength = along(d_inner[head] * active[2] + from_lower * key)
        d_value = d_inner[head] * strength
        d_opening = d_strength * (opening * (1.0 - opening)) * tile.live
        d_beta = d_beta + jnp.where(tile.col == head, d_opening, 0.0)
        d_active = [
            (d_query - query_unit * along(query_unit * d_query)) * query_scale,
            (d_key - key * along(key * d_key)) * key_scale,
            d_value,
        ]
        for section in range(3):
            columns = head_columns(width, section, head)
            taps = [param_ref[offset : offset + 1, columns] for offset in range(KERNEL)]
            slope = opened[section] * (1.0 + convolved[section] * (1.0 - opened[section]))
            d_convolved = d_active[section] * slope
            d_pre = d_convolved * taps[0]
            sums = [jnp.sum(d_convolved * pres[section], 0, keepdims=True)]
            for offset in range(1, KERNEL):
                d_pre = d_pre + tile.later(d_convolved, offset) * taps[offset]
                sums.append(
                    jnp.sum(d_convolved * tile.earlier(pres[section], offset), 0, keepdims=True)
                )
            d_param_ref[0:KERNEL, columns] += jnp.concatenate(sums, 0)
            d_pre_ref[:, columns] = d_pre.astype(bf)
    d_pre_ref[:, 4 * width :] = d_beta.astype(bf)


NO_COST = pl.CostEstimate(flops=0, bytes_accessed=0, transcendentals=0)


def call(kernel, operands, in_specs, out_specs, out_shape, grid=(), scratch=(), micros=0):
    results = pl.pallas_call(
        kernel,
        grid=grid,
        in_specs=in_specs,
        out_specs=out_specs,
        out_shape=out_shape,
        scratch_shapes=scratch,
        compiler_params=pltpu.CompilerParams(
            dimension_semantics=("arbitrary",) * len(grid), vmem_limit_bytes=48 * 2**20
        ),
        cost_estimate=pl.CostEstimate(
            flops=micros * 10**9, bytes_accessed=0, transcendentals=0
        ),
    )(*operands)
    return list(results)


def whole(array):
    return pl.BlockSpec(array.shape, lambda *step: (0,) * len(array.shape))


def mixer_specs(width):
    wide = 4 * width + SMALL
    heads = width // HEAD_DIM
    layout = pl.BlockSpec(memory_space=pltpu.SMEM)
    pre = pl.BlockSpec((GROUP_ROWS, wide), lambda group: (group, 0))
    param = pl.BlockSpec((2 * KERNEL, 3 * width), lambda group: (0, 0))
    narrow = pl.BlockSpec((GROUP_ROWS, width), lambda group: (group, 0))
    square = pl.BlockSpec((heads, GROUP_ROWS, HEAD_DIM), lambda group: (group, 0, 0))
    return layout, pre, param, narrow, square


def mixer_forward(layout, pre, params, width):
    groups = layout.shape[0]
    layout_spec, pre_spec, param_spec, narrow, square = mixer_specs(width)
    squares = pltpu.HBM((groups * width // HEAD_DIM, GROUP_ROWS, HEAD_DIM), f32)
    return call(
        mixer_forward_kernel,
        [layout, pre, params],
        [layout_spec, pre_spec, param_spec],
        [narrow] + [square] * 4,
        [jax.ShapeDtypeStruct((groups * GROUP_ROWS, width), bf)] + [squares] * 4,
        (groups,),
    )


def mixer_backward(layout, pre, params, weight, d_mixed, kept, width):
    groups = layout.shape[0]
    layout_spec, pre_spec, param_spec, _, square = mixer_specs(width)
    kept = [pltpu.with_memory_space_constraint(array, pltpu.HBM) for array in kept]
    return call(
        mixer_backward_kernel,
        [layout, pre, params, weight, *kept, *d_mixed],
        [layout_spec, pre_spec, param_spec, whole(weight)]
        + [square] * 4
        + [whole(block) for block in d_mixed],
        [pre_spec, param_spec],
        [jax.ShapeDtypeStruct(pre.shape, bf), jax.ShapeDtypeStruct(params.shape, f32)],
        (groups,),
        [pltpu.VMEM((GROUP_ROWS, width), f32)],
        micros=60,
    )


def first_kernel(gain_ref, weight_ref, *refs):
    *value_refs, normed_ref, out_ref, scale_ref, total_ref = refs
    step, depth = pl.program_id(0), weight_ref.shape[0]

    @pl.when(step == 0)
    def _():
        for group, ref in enumerate(value_refs):
            values = ref[...].astype(f32)
            scale = lax.rsqrt(jnp.mean(values * values, -1, keepdims=True) + 1e-06)
            rows = pl.ds(group * GROUP_ROWS, GROUP_ROWS)
            scale_ref[rows, :] = jnp.broadcast_to(scale, (GROUP_ROWS, 128))
        total_ref[...] = jnp.zeros_like(total_ref)

    columns = pl.ds(pl.multiple_of(step * depth, depth), depth)
    for group, ref in enumerate(value_refs):
        rows = pl.ds(group * GROUP_ROWS, GROUP_ROWS)
        values = ref[:, columns].astype(f32) * scale_ref[rows, :1] * gain_ref[...]
        normed_ref[rows, :] = values.astype(bf)
    total_ref[...] += plain_product(normed_ref[...], weight_ref[...])

    @pl.when(step == pl.num_programs(0) - 1)
    def _():
        out_ref[...] = total_ref[...]


def normed_product(blocks, gain, weight, depth=512):
    rows, (features, columns) = len(blocks) * GROUP_ROWS, weight.shape
    return call(
        first_kernel,
        [gain, weight, *blocks],
        [
            pl.BlockSpec((1, depth), lambda step: (0, step)),
            pl.BlockSpec((depth, columns), lambda step: (step, 0)),
        ]
        + [whole(block) for block in blocks],
        [
            pl.BlockSpec((rows, depth), lambda step: (0, step)),
            pl.BlockSpec((rows, columns), lambda step: (0, 0)),
        ],
        [
            jax.ShapeDtypeStruct((rows, features), bf),
            jax.ShapeDtypeStruct((rows, columns), f32),
        ],
        (features // depth,),
        [pltpu.VMEM((rows, 128), f32), pltpu.VMEM((rows, columns), f32)],
    )


def product_blocks(left, right, transposed=False, block=512, micros=0):
    product = transposed_product if transposed else plain_product
    columns = right.shape[0] if transposed else right.shape[1]
    groups = left.shape[0] // GROUP_ROWS

    def kernel(left_ref, right_ref, *out_refs):
        total = product(left_ref[...], right_ref[...])
        for group, ref in enumerate(out_refs):
            ref[...] = total[group * GROUP_ROWS : (group + 1) * GROUP_ROWS].astype(ref.dtype)

    if transposed:
        right_spec = pl.BlockSpec((block, right.shape[1]), lambda step: (step, 0))
    else:
        right_spec = pl.BlockSpec((right.shape[0], block), lambda step: (0, step))
    return call(
        kernel,
        [left, right],
        [whole(left), right_spec],
        [pl.BlockSpec((GROUP_ROWS, block), lambda step: (0, step))] * groups,
        [
            jax.ShapeDtypeStruct((GROUP_ROWS, columns), bf if group else f32)
            for group in range(groups)
        ],
        (columns // block,),
        micros=micros,
    )


def grad_product(left, right, block=256, micros=0):
    rows, features = left.shape
    if features % block:
        block = 128

    def kernel(left_ref, right_ref, out_ref):
        out_ref[...] = rows_product(left_ref[...], right_ref[...]).astype(bf)

    return call(
        kernel,
        [left, right],
        [pl.BlockSpec((rows, block), lambda step: (0, step)), whole(right)],
        [pl.BlockSpec((block, right.shape[1]), lambda step: (step, 0))],
        [pltpu.HBM((features, right.shape[1]), bf)],
        (features // block,),
        micros=micros,
    )[0]


def from_own(part, values):
    groups = values.shape[0] // GROUP_ROWS

    def kernel(part_ref, values_ref, out_ref):
        for step in range(groups):
            source = lax.rem(part_ref[0] + groups - step, groups) * GROUP_ROWS
            rows = pl.ds(pl.multiple_of(source, GROUP_ROWS), GROUP_ROWS)
            out_ref[step * GROUP_ROWS : (step + 1) * GROUP_ROWS] = values_ref[rows]

    return call(
        kernel,
        [part.reshape(1).astype(jnp.int32), values],
        [pl.BlockSpec(memory_space=pltpu.SMEM), whole(values)],
        [whole(values)],
        [jax.ShapeDtypeStruct(values.shape, values.dtype)],
        (1,),
    )[0]


def tie_all(values, *others):
    anywhere = pl.BlockSpec(memory_space=pl.ANY)
    others = [
        pltpu.with_memory_space_constraint(other, pltpu.HBM) if other.size > 2**21 else other
        for other in others
    ]
    tied = pl.pallas_call(
        lambda *refs: None,
        in_specs=[anywhere] * (len(values) + len(others)),
        out_specs=[anywhere] * len(values),
        out_shape=[
            (pltpu.HBM if value.size > 2**21 else jax.ShapeDtypeStruct)(value.shape, value.dtype)
            for value in values
        ],
        input_output_aliases={i: i for i in range(len(values))},
        cost_estimate=NO_COST,
    )(*values, *others)
    return list(tied)


def tie(value, *others):
    return tie_all([value], *others)[0]


def assemble(part, values, received, others):
    parts = values.shape[0]

    def kernel(part_ref, values_ref, *refs):
        own = part_ref[0]
        out_ref = refs[-1]
        out_ref[own] = values_ref[own]
        for step in range(1, parts):
            out_ref[lax.rem(own + parts - step, parts)] = refs[step - 1][...]

    vmem = pl.BlockSpec(memory_space=pltpu.VMEM)
    anywhere = pl.BlockSpec(memory_space=pl.ANY)
    return pl.pallas_call(
        kernel,
        in_specs=[pl.BlockSpec(memory_space=pltpu.SMEM)]
        + [vmem] * parts
        + [anywhere] * len(others),
        out_specs=vmem,
        out_shape=jax.ShapeDtypeStruct(values.shape, values.dtype),
        compiler_params=pltpu.CompilerParams(vmem_limit_bytes=32 * 2**20),
        cost_estimate=NO_COST,
    )(part.reshape(1).astype(jnp.int32), values, *received, *others)


def copy_columns(count, *refs):
    target = refs[-1]
    start = 0
    for source in refs[:count]:
        block = source[...].reshape(source.shape[-2:])
        columns = pl.ds(start, block.shape[1])
        if len(target.shape) == 3:
            target[0, :, columns] = block.astype(target.dtype)
        else:
            target[:, columns] = block.astype(target.dtype)
        start += block.shape[1]


def to_parts(sources, parts, dtype, others=()):
    rows = sources[0][0].shape[0]

    def spec(section, width):
        return pl.BlockSpec((rows, width), lambda p: (0, section * parts + p))

    total = sum(width for _, _, width in sources)
    return pl.pallas_call(
        functools.partial(copy_columns, len(sources)),
        grid=(parts,),
        in_specs=[spec(section, width) for _, section, width in sources]
        + [pl.BlockSpec(memory_space=pl.ANY)] * len(others),
        out_specs=pl.BlockSpec((1, rows, total), lambda p: (p, 0, 0)),
        out_shape=jax.ShapeDtypeStruct((parts, rows, total), dtype),
        cost_estimate=NO_COST,
    )(*[array for array, _, _ in sources], *others)


def updown_from_parts(slabs):
    parts, rows, width = slabs.shape
    units = width // 2

    def kernel(slabs_ref, out_ref):
        for p in range(parts):
            out_ref[:, p * units : (p + 1) * units] = slabs_ref[p].astype(f32)

    return pl.pallas_call(
        kernel,
        grid=(2,),
        in_specs=[pl.BlockSpec((parts, rows, units), lambda half: (0, 0, half))],
        out_specs=pl.BlockSpec((rows, parts * units), lambda half: (0, half)),
        out_shape=jax.ShapeDtypeStruct((rows, parts * width), f32),
        compiler_params=pltpu.CompilerParams(vmem_limit_bytes=32 * 2**20),
        cost_estimate=NO_COST,
    )(slabs)


def mixer_from_parts(slabs, width):
    parts, rows, _ = slabs.shape

    def kernel(slabs_ref, qkv_ref, gate_ref, strength_ref):
        for p in range(parts):
            for section in range(4):
                block = slabs_ref[p, :, section * width : (section + 1) * width].astype(f32)
                if section < 3:
                    start = (section * parts + p) * width
                    qkv_ref[:, start : start + width] = block
                else:
                    gate_ref[:, p * width : (p + 1) * width] = block
            last = slabs_ref[p, :, 4 * width :].astype(f32)
            strength_ref[:, p * SMALL : (p + 1) * SMALL] = last

    widths = [3 * parts * width, parts * width, parts * SMALL]
    return pl.pallas_call(
        kernel,
        out_shape=[jax.ShapeDtypeStruct((rows, size), f32) for size in widths],
        compiler_params=pltpu.CompilerParams(vmem_limit_bytes=32 * 2**20),
        cost_estimate=NO_COST,
    )(slabs)


def own_order(values, parts, copies):
    size = values.shape[1] // (parts * copies)
    pieces = [
        values[:, (t * parts + m) * size : (t * parts + m + 1) * size]
        for m in range(parts)
        for t in range(copies)
    ]
    return jnp.concatenate(pieces, 1)


def total_of(own_ref, received_refs):
    total = own_ref[...]
    for ref in received_refs:
        total = total + ref[...].astype(f32)
    return total


def row_scale(values):
    return lax.rsqrt(jnp.mean(values * values, -1, keepdims=True) + 1e-06)


def norm_slope(values, scale, gain, grad):
    mean = jnp.mean(gain * grad * values, -1, keepdims=True)
    return scale * gain * grad - values * (scale * scale * scale * mean)


def hidden_kernel(own_ref, *refs):
    *received, input_ref, gain_ref, hidden_ref, normed_ref = refs
    hidden = input_ref[...].astype(f32) + total_of(own_ref, received)
    hidden_ref[...] = hidden
    normed_ref[...] = (hidden * row_scale(hidden) * gain_ref[...]).astype(bf)


def hidden_back_kernel(own_ref, *refs):
    *received, hidden_ref, gain_ref, cot_ref, d_hidden_ref, d_mixed_ref, d_gain_ref = refs
    grad = total_of(own_ref, received)
    hidden = hidden_ref[...]
    scale = row_scale(hidden)

    @pl.when(pl.program_id(0) == 0)
    def _():
        d_gain_ref[...] = jnp.zeros_like(d_gain_ref)

    d_gain_ref[...] += jnp.sum(grad * hidden * scale, 0, keepdims=True)
    d_hidden = cot_ref[...].astype(f32) + norm_slope(hidden, scale, gain_ref[...], grad)
    d_hidden_ref[...] = d_hidden
    d_mixed_ref[...] = d_hidden.astype(bf)


def input_back_kernel(parts, copies, own_ref, *refs):
    *received, input_ref, gain_ref, d_hidden_ref, out_ref = refs
    grad = total_of(own_ref, received)
    values = input_ref[...].astype(f32)
    slope = norm_slope(values, row_scale(values), gain_ref[...], grad)
    out_ref[...] = own_order(d_hidden_ref[...] + slope, parts, copies).astype(bf)


def block_out_kernel(parts, copies, own_ref, *refs):
    *received, hidden_ref, out_ref = refs
    total = hidden_ref[...] + total_of(own_ref, received)
    out_ref[...] = own_order(total, parts, copies).astype(bf)


def last_sum(sides, others, parts, copies):
    rows, columns = sides[0].shape

    def kernel(*refs):
        first, first_other, second, second_other = (ref[...].astype(f32) for ref in refs[:4])
        total = jnp.concatenate([first + first_other, second + second_other], 1)
        refs[-1][...] = own_order(total, parts, copies)

    vmem = pl.BlockSpec(memory_space=pltpu.VMEM)
    return pl.pallas_call(
        kernel,
        in_specs=[vmem] * 4 + [pl.BlockSpec(memory_space=pl.ANY)] * len(others),
        out_specs=vmem,
        out_shape=jax.ShapeDtypeStruct((rows, 2 * columns), f32),
        compiler_params=pltpu.CompilerParams(vmem_limit_bytes=32 * 2**20),
        cost_estimate=NO_COST,
    )(*sides, *others)


def by_rows(kernel, arrays, outs, block=64):
    def spec(shape):
        if shape[0] == 1:
            return pl.BlockSpec(shape, lambda i: (0, 0))
        return pl.BlockSpec((block, shape[1]), lambda i: (i, 0))

    return pl.pallas_call(
        kernel,
        grid=(GROUP_ROWS // block,),
        in_specs=[spec(array.shape) for array in arrays],
        out_specs=[spec(shape) for shape, _ in outs],
        out_shape=[jax.ShapeDtypeStruct(shape, dtype) for shape, dtype in outs],
        compiler_params=pltpu.CompilerParams(dimension_semantics=("arbitrary",)),
        cost_estimate=NO_COST,
    )(*arrays)


def body(
    block_in,
    out_grad,
    norm1_gain,
    conv_weight,
    head_gain,
    qkv_weight,
    beta_weight,
    gate_weight,
    out_weight,
    norm2_gain,
    updown_weight,
    down_weight,
    seq_blocks,
    lead_blocks,
):
    devices = lax.axis_size("dp")
    parts = MODEL
    copies = devices // parts
    part = lax.axis_index("dp") // copies
    copy = lax.axis_index("dp") % copies
    rows_own = qkv_weight.shape[0]
    width = D // parts
    units = FF // parts
    heads_part = HEADS // parts
    wide = 4 * width + SMALL
    model_groups = [[m * copies + t for m in range(parts)] for t in range(copies)]
    copy_groups = [[m * copies + t for t in range(copies)] for m in range(parts)]

    def exchange(values):
        return lax.all_to_all(
            values, "dp", split_axis=0, concat_axis=0, axis_index_groups=model_groups, tiled=True
        )

    def shift(values, step):
        pairs = [
            (m * copies + t, (m + step) % parts * copies + t)
            for m in range(parts)
            for t in range(copies)
        ]
        return lax.ppermute(values, "dp", pairs)

    def exchange_apart(values, before, after=()):
        cut = [
            lax.dynamic_index_in_dim(values, (part + step) % parts, 0, keepdims=False)
            for step in range(1, parts)
        ]
        received = [shift(piece, step) for step, piece in enumerate(tie_all(cut, *before), 1)]
        return assemble(part, values, received, after)

    def gather_rows(values):
        return [values] + [shift(values, step) for step in range(1, parts)]

    def scatter_rows(terms):
        return [terms[0]] + [shift(block, -step) for step, block in enumerate(terms[1:], 1)]

    def gather_copies(values):
        return lax.all_gather(values, "dp", axis=0, axis_index_groups=copy_groups, tiled=True)

    def scatter_copies(values):
        return lax.psum_scatter(
            values.astype(bf),
            "dp",
            scatter_dimension=0,
            axis_index_groups=copy_groups,
            tiled=True,
        )

    def halves_across(values, bit, axis):
        pairs = [(i, i ^ (1 << bit)) for i in range(devices)]
        side = (copy >> bit) & 1
        own = lax.dynamic_index_in_dim(values, side, axis, keepdims=False)
        other = lax.dynamic_index_in_dim(values, 1 - side, axis, keepdims=False)
        return own, lax.ppermute(other, "dp", pairs)

    def halve(values, bit, axis, *others):
        own, received = halves_across(values, bit, axis)
        if others:
            received = tie(received, *others)
        return (own.astype(f32) + received.astype(f32)).astype(bf)

    by_halves = copies == 8

    def halve_cores(values, *others):
        if not by_halves:
            return values
        rows, columns = values.shape
        return halve(values.reshape(2, 2, 2, rows // 8, columns), 0, 2, *others)

    def halve_first(values):
        if not by_halves:
            return [values]
        middle = values.shape[-1] // 2
        return [halve(values[..., :middle], 1, 1), halve(values[..., middle:], 2, 0)]

    def halve_second(values, *others):
        if not by_halves:
            return from_wire(scatter_copies(values[0]).astype(f32))
        sides = halves_across(values[0], 2, 0) + halves_across(values[1], 1, 0)
        return last_sum(sides, others, parts, copies)

    def to_wire(values):
        return values.reshape(-1, parts, copies, rows_own).swapaxes(1, 2).reshape(-1, D)

    def from_wire(values):
        return values.reshape(-1, copies, parts, rows_own).swapaxes(1, 2).reshape(-1, D)

    w_out_own = to_wire(out_weight.astype(bf))
    w_out = gather_copies(w_out_own)
    strengths = beta_weight.reshape(rows_own, parts, heads_part)
    strengths = jnp.pad(strengths, ((0, 0), (0, 0), (0, SMALL - heads_part)))
    strengths = tie(strengths.reshape(rows_own, parts * SMALL), w_out_own)
    pieces = [(qkv_weight, section, width) for section in range(3)]
    pieces = to_parts(pieces + [(gate_weight, 0, width), (strengths, 0, SMALL)], parts, bf)
    mixer_pieces = tie(exchange(pieces), w_out)
    w_mixer = gather_copies(mixer_pieces.reshape(parts * rows_own, wide))
    inputs = tie(to_wire(block_in), mixer_pieces)
    input_rows = gather_rows(inputs)

    lanes = -(-3 * rows_own // 128) * 128
    numbers = jnp.concatenate([seq_blocks[0], lead_blocks]).astype(f32)
    small = [conv_weight.T, norm1_gain[None], head_gain[None], norm2_gain[None], numbers[None]]
    small = [jnp.pad(rows, ((0, 0), (0, lanes - rows.shape[1]))) for rows in small]
    small = jnp.pad(jnp.concatenate(small, 0).astype(bf), ((0, 2 * KERNEL), (0, 0)))
    small = jnp.broadcast_to(small[None], (devices,) + small.shape)
    small = lax.all_to_all(tie(small, *input_rows[1:]), "dp", 0, 0, tiled=True)
    taps = small[:, :KERNEL, : 3 * rows_own].swapaxes(0, 1).reshape(KERNEL, 3, parts, width)
    taps = lax.dynamic_index_in_dim(taps, part, 2, keepdims=False).reshape(KERNEL, 3 * width)
    gain_one, head_full, gain_two = (
        small[:, KERNEL + i, :rows_own].reshape(1, D).astype(f32) for i in range(3)
    )
    gain_one, gain_two = to_wire(gain_one), to_wire(gain_two)
    head_part = lax.dynamic_slice_in_dim(head_full, part * width, width, 1)
    params = jnp.concatenate([taps.astype(f32), jnp.pad(head_part, ((0, 0), (0, 2 * width)))], 0)
    params = jnp.pad(params, ((0, KERNEL - 1), (0, 0)))
    numbers = small[:, KERNEL + 3, :3].astype(f32).astype(jnp.int32)
    layouts = block_layouts(numbers[:, 0], numbers[:, 1], numbers[:, 2])
    layouts = layouts.reshape(parts, copies, 4)
    layouts = lax.dynamic_index_in_dim(layouts, copy, 1, keepdims=False)
    wanted = (part - jnp.arange(parts)) % parts
    wanted = (wanted[:, None] == jnp.arange(parts)).astype(f32)
    layouts = jnp.sum(wanted[:, :, None] * layouts, 1)

    pieces = [(updown_weight, half, units) for half in range(2)]
    updown_pieces = to_parts(pieces, parts, bf, [mixer_pieces])
    w_down_own = to_wire(down_weight.astype(bf))
    w_down = gather_copies(tie(w_down_own, *input_rows[1:]))
    cotangent_own = to_wire(out_grad)

    cotangent = lax.all_gather(
        tie(cotangent_own, *input_rows[1:]), "dp", axis=0, axis_index_groups=model_groups, tiled=True
    )
    gain_first = tie(gain_one, w_down_own, cotangent_own, updown_pieces)
    normed, pre = normed_product(input_rows, gain_first, w_mixer)
    mixed, *kept = mixer_forward(layouts, pre, params, width)
    out_terms = product_blocks(mixed, w_out)
    updown_pieces = exchange_apart(updown_pieces, input_rows[1:], out_terms[1:])
    w_updown = gather_copies(updown_pieces.reshape(parts * rows_own, 2 * units))
    stream = ((GROUP_ROWS, D), f32)
    narrow = ((GROUP_ROWS, D), bf)
    hidden, normed_two = by_rows(
        hidden_kernel,
        scatter_rows(out_terms) + [inputs, gain_two],
        [stream, narrow],
    )
    cotangent = from_own(part, cotangent)
    normed_two = jnp.concatenate(gather_rows(normed_two), 0)

    def swiglu_units(updown):
        return jax.nn.silu(updown[:, :units]) * updown[:, units:]

    updown = plain_product(normed_two, w_updown)
    active, swiglu_back = jax.vjp(swiglu_units, updown)
    active = active.astype(bf)
    d_active = transposed_product(cotangent, w_down)
    d_updown = swiglu_back(d_active)[0].astype(bf)
    d_normed_two = product_blocks(d_updown, w_updown, transposed=True)
    active = tie(active, *d_normed_two[1:])
    down_terms = grad_product(active, cotangent)
    updown_terms = grad_product(normed_two, tie(d_updown, down_terms))
    gain_late = tie(gain_two, updown_terms)
    d_normed_two = scatter_rows(d_normed_two)
    updown_grad = scatter_copies(tie(updown_terms, gain_late, *d_normed_two[1:]))
    d_hidden, d_mixed, gain_two_grad = by_rows(
        hidden_back_kernel,
        d_normed_two + [hidden, gain_late, cotangent_own],
        [stream, narrow, ((1, D), f32)],
    )


    out_terms = product_blocks(tie(active, d_mixed), w_down)
    down_terms = tie(down_terms, *out_terms[1:])
    d_mixed = gather_rows(d_mixed)
    late = tie(params, *out_terms)
    out_terms[1:] = tie_all(out_terms[1:], *d_mixed[1:])
    d_pre, d_params = mixer_backward(layouts, pre, late, w_out, d_mixed, kept, width)
    mixer_terms = tie(grad_product(normed, d_pre, micros=20), updown_grad)
    mixer_grad = scatter_copies(mixer_terms)

    d_normed_terms = product_blocks(
        tie(d_pre, mixer_terms), w_mixer, transposed=True, micros=150
    )
    hidden = tie(hidden, d_normed_terms[0])
    (block_out,) = by_rows(
        functools.partial(block_out_kernel, parts, copies),
        scatter_rows(out_terms) + [hidden],
        [narrow],
    )
    d_normed_terms[1:] = tie_all(d_normed_terms[1:], block_out)
    d_normed = scatter_rows(d_normed_terms)
    down_grad = halve_first(halve_cores(down_terms, *d_normed_terms[1:]))
    gain_one_grad = 0.0
    for values, terms in zip(input_rows, d_normed_terms):
        values = values.astype(f32)
        terms = terms.astype(f32) * (values * row_scale(values))
        gain_one_grad = gain_one_grad + jnp.sum(terms, 0, keepdims=True)

    d_params = tie(d_params, mixer_terms)
    here = (jnp.arange(parts) == part).astype(f32)[:, None]
    taps_grad = d_params[:KERNEL].reshape(KERNEL, 3, 1, width) * here
    taps_grad = taps_grad.reshape(KERNEL, parts, copies, 3, rows_own).transpose(1, 2, 3, 0, 4)
    taps_grad = taps_grad.reshape(devices, 3 * KERNEL, rows_own)
    head_grad = (d_params[KERNEL, :width] * here).reshape(devices, 1, rows_own)
    gain_grads = [
        grad.reshape(copies, parts, 1, rows_own).swapaxes(0, 1).reshape(devices, 1, rows_own)
        for grad in (gain_one_grad, gain_two_grad)
    ]
    small_grad = jnp.concatenate([taps_grad, head_grad] + gain_grads, 1)
    d_mixed = jnp.concatenate([tie(d_mixed[0], d_normed_terms[0])] + d_mixed[1:], 0)
    out_grads = grad_product(mixed, d_mixed)
    late = tie(gain_one, out_grads, *down_grad)
    (input_grad,) = by_rows(
        functools.partial(input_back_kernel, parts, copies),
        d_normed + [inputs, late, d_hidden],
        [narrow],
    )
    small_grad = jnp.pad(tie(small_grad, input_grad), ((0, 0), (0, 1), (0, 128 - rows_own)))
    small_grad = jnp.sum(lax.all_to_all(small_grad, "dp", 0, 0, tiled=True), 0)[:, :rows_own]
    taps_shard = small_grad[: 3 * KERNEL].reshape(3, KERNEL, rows_own).swapaxes(1, 2)
    taps_shard = taps_shard.reshape(3 * rows_own, KERNEL)
    head_shard, gain_one_shard, gain_two_shard = small_grad[3 * KERNEL : 3 * KERNEL + 3]

    updown_grad = tie(updown_grad, mixer_terms).reshape(parts, rows_own, 2 * units)
    updown_grad = exchange(updown_grad)
    mixer_grad = tie(mixer_grad, input_grad)
    updown_shard = updown_from_parts(tie(updown_grad, mixer_grad))
    down_shard = halve_second(tie_all(down_grad, input_grad), mixer_grad)
    out_grads = tie(halve_cores(tie(out_grads, input_grad)), mixer_grad, down_shard)
    out_shard = halve_second(halve_first(out_grads))
    mixer_grad = exchange_apart(mixer_grad.reshape(parts, rows_own, wide), [input_grad])
    qkv_shard, gate_shard, strengths = mixer_from_parts(mixer_grad, width)
    beta_shard = strengths.reshape(rows_own, parts, SMALL)[:, :, :heads_part]
    return (
        block_out,
        input_grad,
        gain_one_shard,
        taps_shard,
        head_shard,
        qkv_shard,
        beta_shard.reshape(rows_own, HEADS),
        gate_shard,
        out_shard,
        gain_two_shard,
        updown_shard,
        down_shard,
    )


def solution(mesh):
    placed = (
        P("dp", None),
        P("dp", None),
        P("dp"),
        P("dp", None),
        P("dp"),
        P("dp", None),
        P("dp", None),
        P("dp", None),
        P("dp", None),
        P("dp"),
        P("dp", None),
        P("dp", None),
        P("dp", None),
        P("dp"),
    )
    return jax.shard_map(
        body,
        mesh=mesh,
        in_specs=placed,
        out_specs=(
            P("dp", None),
            P("dp", None),
            P("dp"),
            P("dp", None),
            P("dp"),
            P("dp", None),
            P("dp", None),
            P("dp", None),
            P("dp", None),
            P("dp"),
            P("dp", None),
            P("dp", None),
        ),
        check_vma=False,
    )
```

```python
import functools

import jax
import jax.numpy as jnp
from jax import lax
from jax.experimental import pallas as pl
from jax.experimental.pallas import tpu as pltpu
from jax.sharding import PartitionSpec as P

D = 2048
HEADS = 16
HEAD_DIM = 128
FF = 5632
KERNEL = 4
BLOCK_ROWS = 64
BLOCKS_DEV = 2
GROUP_ROWS = BLOCK_ROWS * BLOCKS_DEV
SMALL = 128
MODEL = 4

f32 = jnp.float32
bf = jnp.bfloat16


def block_layouts(first, second, lead):
    def doc(block):
        in_first = (block >= lead) & (block < lead + first)
        in_second = (block >= lead + first) & (block < lead + first + second)
        return jnp.where(in_first, 1, jnp.where(in_second, 2, 0))

    starts = (lead == 1) | (lead + first == 1) & (second > 0)
    columns = [doc(0) > 0, doc(1) > 0, doc(0) == doc(1), ~starts]
    return jnp.stack(columns, 1).astype(f32)


def plain_product(left, right):
    return jnp.dot(left, right, preferred_element_type=f32)


def rows_product(left, right):
    return lax.dot_general(left, right, (((0,), (0,)), ((), ())), preferred_element_type=f32)


def transposed_product(left, right):
    return lax.dot_general(left, right, (((1,), (1,)), ((), ())), preferred_element_type=f32)


def halves(values):
    high = values.astype(bf)
    return high, (values - high.astype(f32)).astype(bf)


def exact(left, right, left_dim, right_dim):
    left_high, left_low = left if isinstance(left, tuple) else halves(left)
    right_high, right_low = right if isinstance(right, tuple) else halves(right)
    return lax.dot_general(
        jnp.concatenate([left_high, left_high, left_low], left_dim),
        jnp.concatenate([right_high, right_low, right_high], right_dim),
        (((left_dim,), (right_dim,)), ((), ())),
        preferred_element_type=f32,
    )


def stacked(first, second):
    return tuple(jnp.concatenate([a, b], 0) for a, b in zip(first, second))


class Tile:
    def __init__(self, layout_ref, group):
        live_first, live_second, same, persist = (layout_ref[group, i] for i in range(4))
        shape = (GROUP_ROWS, HEAD_DIM)
        row = lax.broadcasted_iota(jnp.int32, shape, 0)
        col = lax.broadcasted_iota(jnp.int32, shape, 1)
        late = row >= BLOCK_ROWS
        self.row, self.col = row, col
        self.live = jnp.where(late, live_second, live_first)
        self.taps = [None] + [
            jnp.where(
                row < offset,
                0.0,
                jnp.where(late & (row < BLOCK_ROWS + offset), same, 1.0),
            )
            for offset in range(1, KERNEL)
        ]
        cross = jnp.where(late & (col < BLOCK_ROWS), persist, 1.0)
        self.lower = jnp.where(row > col, cross, 0.0)
        self.lower_full = jnp.where(row >= col, cross, 0.0)

    def earlier(self, values, offset):
        return pltpu.roll(values, offset, 0) * self.taps[offset]

    def later(self, values, offset):
        return pltpu.roll(values * self.taps[offset], GROUP_ROWS - offset, 0)


def convolve(tile, values, taps):
    total = values * taps[0]
    for offset in range(1, KERNEL):
        total = total + tile.earlier(values, offset) * taps[offset]
    return total


def unit_scale(values):
    return lax.rsqrt(jnp.sum(values * values, -1, keepdims=True) + 1e-06)


def head_columns(part_width, section, head):
    return pl.ds(section * part_width + head * HEAD_DIM, HEAD_DIM)


def unit_inverses(tile, lowers):
    eye = jnp.where(tile.row == tile.col, 1.0, 0.0)
    inverses = None
    size = 1
    while size < GROUP_ROWS:
        pair = tile.row // (2 * size) == tile.col // (2 * size)
        split = pair & (tile.row // size != tile.col // size)
        parts = [jnp.where(split, lower, 0.0) for lower in lowers]
        if inverses is None:
            inverses = [eye - part for part in parts]
        else:
            kept = [halves(inverse) for inverse in inverses]
            inner = [exact(part, known, 1, 0) for part, known in zip(parts, kept)]
            outer = [exact(known, value, 1, 0) for known, value in zip(kept, inner)]
            inverses = [inverse - value for inverse, value in zip(inverses, outer)]
        size *= 2
    return inverses


def mixer_forward_kernel(
    layout_ref, pre_ref, param_ref, mixed_ref, inverse_ref, score_ref, solved_ref, out_ref
):
    width = mixed_ref.shape[1]
    heads = range(width // HEAD_DIM)
    tile = Tile(layout_ref, pl.program_id(0))
    queries, keys, values, strengths = [], [], [], []
    for head in heads:
        parts = []
        for section in range(3):
            columns = head_columns(width, section, head)
            taps = [param_ref[offset : offset + 1, columns] for offset in range(KERNEL)]
            convolved = convolve(tile, pre_ref[:, columns], taps)
            parts.append(convolved * jax.nn.sigmoid(convolved))
        queries.append(parts[0] * (unit_scale(parts[0]) * HEAD_DIM**-0.5))
        keys.append(parts[1] * unit_scale(parts[1]))
        values.append(parts[2])
        start = 4 * width + head
        strengths.append(jax.nn.sigmoid(pre_ref[:, start : start + 1]) * tile.live)
    lowers, scores = [], []
    for head in heads:
        key_halves = halves(keys[head])
        both = exact(stacked(key_halves, halves(queries[head])), key_halves, 1, 1)
        lowers.append(both[:GROUP_ROWS] * strengths[head] * tile.lower)
        scores.append(both[GROUP_ROWS:] * tile.lower_full)
    inverses = unit_inverses(tile, lowers)
    solved = [exact(inverses[head], values[head] * strengths[head], 1, 0) for head in heads]
    outs = [exact(scores[head], solved[head], 1, 0) for head in heads]
    for head in heads:
        out = outs[head]
        scaled = out * lax.rsqrt(jnp.mean(out * out, -1, keepdims=True) + 1e-05)
        gate = pre_ref[:, head_columns(width, 3, head)]
        gain = param_ref[KERNEL : KERNEL + 1, head_columns(width, 0, head)]
        mixed = scaled * gain * (gate * jax.nn.sigmoid(gate)) * tile.live
        mixed_ref[:, head_columns(width, 0, head)] = mixed.astype(bf)
        inverse_ref[head] = inverses[head]
        score_ref[head] = scores[head]
        solved_ref[head] = solved[head]
        out_ref[head] = out


def mixer_backward_kernel(
    layout_ref,
    pre_ref,
    param_ref,
    weight_ref,
    inverse_ref,
    score_ref,
    solved_ref,
    out_ref,
    *refs,
):
    *mixed_refs, d_pre_ref, d_param_ref, grad_ref = refs
    width = grad_ref.shape[1]
    heads = range(width // HEAD_DIM)
    tile = Tile(layout_ref, pl.program_id(0))
    for group, mixed_ref in enumerate(mixed_refs):

        @pl.when(pl.program_id(0) == group)
        def _():
            grad_ref[...] = transposed_product(mixed_ref[...], weight_ref[...])

    @pl.when(pl.program_id(0) == 0)
    def _():
        d_param_ref[...] = jnp.zeros_like(d_param_ref)

    def along(values):
        return jnp.sum(values, -1, keepdims=True)

    d_outs = []
    for head in heads:
        columns = head_columns(width, 0, head)
        d_mixed = grad_ref[:, columns] * tile.live
        out = out_ref[head]
        scale = lax.rsqrt(jnp.mean(out * out, -1, keepdims=True) + 1e-05)
        scaled = out * scale
        gate = pre_ref[:, head_columns(width, 3, head)]
        gate_open = jax.nn.sigmoid(gate)
        gain = param_ref[KERNEL : KERNEL + 1, columns]
        gated = d_mixed * (gate * gate_open)
        d_param_ref[KERNEL : KERNEL + 1, columns] += jnp.sum(gated * scaled, 0, keepdims=True)
        d_gate = d_mixed * scaled * gain * (gate_open * (1.0 + gate * (1.0 - gate_open)))
        d_pre_ref[:, head_columns(width, 3, head)] = d_gate.astype(bf)
        d_scaled = gated * gain
        mean = jnp.mean(d_scaled * out, -1, keepdims=True)
        d_outs.append(scale * d_scaled - out * (scale * scale * scale * mean))
    d_out_halves = [halves(value) for value in d_outs]
    solved_halves = [halves(solved_ref[head]) for head in heads]
    d_solved = [exact(score_ref[head], d_out_halves[head], 0, 0) for head in heads]
    d_scores = [
        exact(d_out_halves[head], solved_halves[head], 1, 1) * tile.lower_full for head in heads
    ]
    d_inner = [exact(inverse_ref[head], d_solved[head], 0, 0) for head in heads]
    d_lowers = [exact(d_inner[head], solved_halves[head], 1, 1) * -tile.lower for head in heads]
    d_beta = jnp.zeros((GROUP_ROWS, SMALL), f32)
    for head in heads:
        pres, convolved, opened, active = [], [], [], []
        for section in range(3):
            columns = head_columns(width, section, head)
            taps = [param_ref[offset : offset + 1, columns] for offset in range(KERNEL)]
            pres.append(pre_ref[:, columns])
            convolved.append(convolve(tile, pres[section], taps))
            opened.append(jax.nn.sigmoid(convolved[section]))
            active.append(convolved[section] * opened[section])
        query_scale = unit_scale(active[0])
        key_scale = unit_scale(active[1])
        query_unit = active[0] * query_scale
        key = active[1] * key_scale
        start = 4 * width + head
        opening = jax.nn.sigmoid(pre_ref[:, start : start + 1])
        strength = opening * tile.live
        d_both = stacked(halves(d_lowers[head]), halves(d_scores[head]))
        by_key = exact(d_both, key, 1, 0)
        d_query = by_key[GROUP_ROWS:] * HEAD_DIM**-0.5
        from_lower = by_key[:GROUP_ROWS]
        weighted = stacked(halves(key * strength), halves(query_unit * HEAD_DIM**-0.5))
        d_key = strength * from_lower + exact(d_both, weighted, 0, 0)
        d_strength = along(d_inner[head] * active[2] + from_lower * key)
        d_value = d_inner[head] * strength
        d_opening = d_strength * (opening * (1.0 - opening)) * tile.live
        d_beta = d_beta + jnp.where(tile.col == head, d_opening, 0.0)
        d_active = [
            (d_query - query_unit * along(query_unit * d_query)) * query_scale,
            (d_key - key * along(key * d_key)) * key_scale,
            d_value,
        ]
        for section in range(3):
            columns = head_columns(width, section, head)
            taps = [param_ref[offset : offset + 1, columns] for offset in range(KERNEL)]
            slope = opened[section] * (1.0 + convolved[section] * (1.0 - opened[section]))
            d_convolved = d_active[section] * slope
            d_pre = d_convolved * taps[0]
            sums = [jnp.sum(d_convolved * pres[section], 0, keepdims=True)]
            for offset in range(1, KERNEL):
                d_pre = d_pre + tile.later(d_convolved, offset) * taps[offset]
                sums.append(
                    jnp.sum(d_convolved * tile.earlier(pres[section], offset), 0, keepdims=True)
                )
            d_param_ref[0:KERNEL, columns] += jnp.concatenate(sums, 0)
            d_pre_ref[:, columns] = d_pre.astype(bf)
    d_pre_ref[:, 4 * width :] = d_beta.astype(bf)


NO_COST = pl.CostEstimate(flops=0, bytes_accessed=0, transcendentals=0)


def call(kernel, operands, in_specs, out_specs, out_shape, grid=(), scratch=(), micros=0):
    results = pl.pallas_call(
        kernel,
        grid=grid,
        in_specs=in_specs,
        out_specs=out_specs,
        out_shape=out_shape,
        scratch_shapes=scratch,
        compiler_params=pltpu.CompilerParams(
            dimension_semantics=("arbitrary",) * len(grid), vmem_limit_bytes=48 * 2**20
        ),
        cost_estimate=pl.CostEstimate(
            flops=micros * 10**9, bytes_accessed=0, transcendentals=0
        ),
    )(*operands)
    return list(results)


def whole(array):
    return pl.BlockSpec(array.shape, lambda *step: (0,) * len(array.shape))


def mixer_specs(width):
    wide = 4 * width + SMALL
    heads = width // HEAD_DIM
    layout = pl.BlockSpec(memory_space=pltpu.SMEM)
    pre = pl.BlockSpec((GROUP_ROWS, wide), lambda group: (group, 0))
    param = pl.BlockSpec((2 * KERNEL, 3 * width), lambda group: (0, 0))
    narrow = pl.BlockSpec((GROUP_ROWS, width), lambda group: (group, 0))
    square = pl.BlockSpec((heads, GROUP_ROWS, HEAD_DIM), lambda group: (group, 0, 0))
    return layout, pre, param, narrow, square


def mixer_forward(layout, pre, params, width):
    groups = layout.shape[0]
    layout_spec, pre_spec, param_spec, narrow, square = mixer_specs(width)
    squares = pltpu.HBM((groups * width // HEAD_DIM, GROUP_ROWS, HEAD_DIM), f32)
    return call(
        mixer_forward_kernel,
        [layout, pre, params],
        [layout_spec, pre_spec, param_spec],
        [narrow] + [square] * 4,
        [jax.ShapeDtypeStruct((groups * GROUP_ROWS, width), bf)] + [squares] * 4,
        (groups,),
    )


def mixer_backward(layout, pre, params, weight, d_mixed, kept, width):
    groups = layout.shape[0]
    layout_spec, pre_spec, param_spec, _, square = mixer_specs(width)
    kept = [pltpu.with_memory_space_constraint(array, pltpu.HBM) for array in kept]
    return call(
        mixer_backward_kernel,
        [layout, pre, params, weight, *kept, *d_mixed],
        [layout_spec, pre_spec, param_spec, whole(weight)]
        + [square] * 4
        + [whole(block) for block in d_mixed],
        [pre_spec, param_spec],
        [jax.ShapeDtypeStruct(pre.shape, bf), jax.ShapeDtypeStruct(params.shape, f32)],
        (groups,),
        [pltpu.VMEM((GROUP_ROWS, width), f32)],
        micros=60,
    )


def first_kernel(gain_ref, weight_ref, *refs):
    *value_refs, normed_ref, out_ref, scale_ref, total_ref = refs
    step, depth = pl.program_id(0), weight_ref.shape[0]

    @pl.when(step == 0)
    def _():
        for group, ref in enumerate(value_refs):
            values = ref[...].astype(f32)
            scale = lax.rsqrt(jnp.mean(values * values, -1, keepdims=True) + 1e-06)
            rows = pl.ds(group * GROUP_ROWS, GROUP_ROWS)
            scale_ref[rows, :] = jnp.broadcast_to(scale, (GROUP_ROWS, 128))
        total_ref[...] = jnp.zeros_like(total_ref)

    columns = pl.ds(pl.multiple_of(step * depth, depth), depth)
    for group, ref in enumerate(value_refs):
        rows = pl.ds(group * GROUP_ROWS, GROUP_ROWS)
        values = ref[:, columns].astype(f32) * scale_ref[rows, :1] * gain_ref[...]
        normed_ref[rows, :] = values.astype(bf)
    total_ref[...] += plain_product(normed_ref[...], weight_ref[...])

    @pl.when(step == pl.num_programs(0) - 1)
    def _():
        out_ref[...] = total_ref[...]


def normed_product(blocks, gain, weight, depth=512):
    rows, (features, columns) = len(blocks) * GROUP_ROWS, weight.shape
    return call(
        first_kernel,
        [gain, weight, *blocks],
        [
            pl.BlockSpec((1, depth), lambda step: (0, step)),
            pl.BlockSpec((depth, columns), lambda step: (step, 0)),
        ]
        + [whole(block) for block in blocks],
        [
            pl.BlockSpec((rows, depth), lambda step: (0, step)),
            pl.BlockSpec((rows, columns), lambda step: (0, 0)),
        ],
        [
            jax.ShapeDtypeStruct((rows, features), bf),
            jax.ShapeDtypeStruct((rows, columns), f32),
        ],
        (features // depth,),
        [pltpu.VMEM((rows, 128), f32), pltpu.VMEM((rows, columns), f32)],
    )


def product_blocks(left, right, transposed=False, block=512, micros=0):
    product = transposed_product if transposed else plain_product
    columns = right.shape[0] if transposed else right.shape[1]
    groups = left.shape[0] // GROUP_ROWS

    def kernel(left_ref, right_ref, *out_refs):
        total = product(left_ref[...], right_ref[...])
        for group, ref in enumerate(out_refs):
            ref[...] = total[group * GROUP_ROWS : (group + 1) * GROUP_ROWS].astype(ref.dtype)

    if transposed:
        right_spec = pl.BlockSpec((block, right.shape[1]), lambda step: (step, 0))
    else:
        right_spec = pl.BlockSpec((right.shape[0], block), lambda step: (0, step))
    return call(
        kernel,
        [left, right],
        [whole(left), right_spec],
        [pl.BlockSpec((GROUP_ROWS, block), lambda step: (0, step))] * groups,
        [
            jax.ShapeDtypeStruct((GROUP_ROWS, columns), bf if group else f32)
            for group in range(groups)
        ],
        (columns // block,),
        micros=micros,
    )


def grad_product(left, right, block=512, micros=0):
    rows, features = left.shape
    if features <= block:
        block = 256
    if features % block:
        block = 128

    def kernel(left_ref, right_ref, out_ref):
        out_ref[...] = rows_product(left_ref[...], right_ref[...]).astype(bf)

    return call(
        kernel,
        [left, right],
        [pl.BlockSpec((rows, block), lambda step: (0, step)), whole(right)],
        [pl.BlockSpec((block, right.shape[1]), lambda step: (step, 0))],
        [pltpu.HBM((features, right.shape[1]), bf)],
        (features // block,),
        micros=micros,
    )[0]


def from_own(part, values):
    groups = values.shape[0] // GROUP_ROWS

    def kernel(part_ref, values_ref, out_ref):
        for step in range(groups):
            source = lax.rem(part_ref[0] + groups - step, groups) * GROUP_ROWS
            rows = pl.ds(pl.multiple_of(source, GROUP_ROWS), GROUP_ROWS)
            out_ref[step * GROUP_ROWS : (step + 1) * GROUP_ROWS] = values_ref[rows]

    return call(
        kernel,
        [part.reshape(1).astype(jnp.int32), values],
        [pl.BlockSpec(memory_space=pltpu.SMEM), whole(values)],
        [whole(values)],
        [jax.ShapeDtypeStruct(values.shape, values.dtype)],
        (1,),
    )[0]


def tie_all(values, *others):
    anywhere = pl.BlockSpec(memory_space=pl.ANY)
    others = [
        pltpu.with_memory_space_constraint(other, pltpu.HBM) if other.size > 2**21 else other
        for other in others
    ]
    tied = pl.pallas_call(
        lambda *refs: None,
        in_specs=[anywhere] * (len(values) + len(others)),
        out_specs=[anywhere] * len(values),
        out_shape=[
            (pltpu.HBM if value.size > 2**21 else jax.ShapeDtypeStruct)(value.shape, value.dtype)
            for value in values
        ],
        input_output_aliases={i: i for i in range(len(values))},
        cost_estimate=NO_COST,
    )(*values, *others)
    return list(tied)


def tie(value, *others):
    return tie_all([value], *others)[0]


def assemble(part, values, received, others):
    parts = values.shape[0]

    def kernel(part_ref, values_ref, *refs):
        own = part_ref[0]
        out_ref = refs[-1]
        out_ref[own] = values_ref[own]
        for step in range(1, parts):
            out_ref[lax.rem(own + parts - step, parts)] = refs[step - 1][...]

    vmem = pl.BlockSpec(memory_space=pltpu.VMEM)
    anywhere = pl.BlockSpec(memory_space=pl.ANY)
    return pl.pallas_call(
        kernel,
        in_specs=[pl.BlockSpec(memory_space=pltpu.SMEM)]
        + [vmem] * parts
        + [anywhere] * len(others),
        out_specs=vmem,
        out_shape=jax.ShapeDtypeStruct(values.shape, values.dtype),
        compiler_params=pltpu.CompilerParams(vmem_limit_bytes=32 * 2**20),
        cost_estimate=NO_COST,
    )(part.reshape(1).astype(jnp.int32), values, *received, *others)


def copy_columns(count, *refs):
    target = refs[-1]
    start = 0
    for source in refs[:count]:
        block = source[...].reshape(source.shape[-2:])
        columns = pl.ds(start, block.shape[1])
        if len(target.shape) == 3:
            target[0, :, columns] = block.astype(target.dtype)
        else:
            target[:, columns] = block.astype(target.dtype)
        start += block.shape[1]


def to_parts(sources, parts, dtype, others=()):
    rows = sources[0][0].shape[0]

    def spec(section, width):
        return pl.BlockSpec((rows, width), lambda p: (0, section * parts + p))

    total = sum(width for _, _, width in sources)
    return pl.pallas_call(
        functools.partial(copy_columns, len(sources)),
        grid=(parts,),
        in_specs=[spec(section, width) for _, section, width in sources]
        + [pl.BlockSpec(memory_space=pl.ANY)] * len(others),
        out_specs=pl.BlockSpec((1, rows, total), lambda p: (p, 0, 0)),
        out_shape=jax.ShapeDtypeStruct((parts, rows, total), dtype),
        cost_estimate=NO_COST,
    )(*[array for array, _, _ in sources], *others)


def updown_from_parts(slabs):
    parts, rows, width = slabs.shape
    units = width // 2

    def kernel(slabs_ref, out_ref):
        for p in range(parts):
            out_ref[:, p * units : (p + 1) * units] = slabs_ref[p].astype(f32)

    return pl.pallas_call(
        kernel,
        grid=(2,),
        in_specs=[pl.BlockSpec((parts, rows, units), lambda half: (0, 0, half))],
        out_specs=pl.BlockSpec((rows, parts * units), lambda half: (0, half)),
        out_shape=jax.ShapeDtypeStruct((rows, parts * width), f32),
        compiler_params=pltpu.CompilerParams(vmem_limit_bytes=32 * 2**20),
        cost_estimate=NO_COST,
    )(slabs)


def mixer_from_parts(slabs, width):
    parts, rows, _ = slabs.shape

    def kernel(slabs_ref, qkv_ref, gate_ref, strength_ref):
        for p in range(parts):
            for section in range(4):
                block = slabs_ref[p, :, section * width : (section + 1) * width].astype(f32)
                if section < 3:
                    start = (section * parts + p) * width
                    qkv_ref[:, start : start + width] = block
                else:
                    gate_ref[:, p * width : (p + 1) * width] = block
            last = slabs_ref[p, :, 4 * width :].astype(f32)
            strength_ref[:, p * SMALL : (p + 1) * SMALL] = last

    widths = [3 * parts * width, parts * width, parts * SMALL]
    return pl.pallas_call(
        kernel,
        out_shape=[jax.ShapeDtypeStruct((rows, size), f32) for size in widths],
        compiler_params=pltpu.CompilerParams(vmem_limit_bytes=32 * 2**20),
        cost_estimate=NO_COST,
    )(slabs)


def own_order(values, parts, copies):
    size = values.shape[1] // (parts * copies)
    pieces = [
        values[:, (t * parts + m) * size : (t * parts + m + 1) * size]
        for m in range(parts)
        for t in range(copies)
    ]
    return jnp.concatenate(pieces, 1)


def total_of(own_ref, received_refs):
    total = own_ref[...]
    for ref in received_refs:
        total = total + ref[...].astype(f32)
    return total


def row_scale(values):
    return lax.rsqrt(jnp.mean(values * values, -1, keepdims=True) + 1e-06)


def norm_slope(values, scale, gain, grad):
    mean = jnp.mean(gain * grad * values, -1, keepdims=True)
    return scale * gain * grad - values * (scale * scale * scale * mean)


def hidden_kernel(own_ref, *refs):
    *received, input_ref, gain_ref, hidden_ref, normed_ref = refs
    hidden = input_ref[...].astype(f32) + total_of(own_ref, received)
    hidden_ref[...] = hidden
    normed_ref[...] = (hidden * row_scale(hidden) * gain_ref[...]).astype(bf)


def hidden_back_kernel(own_ref, *refs):
    *received, hidden_ref, gain_ref, cot_ref, d_hidden_ref, d_mixed_ref, d_gain_ref = refs
    grad = total_of(own_ref, received)
    hidden = hidden_ref[...]
    scale = row_scale(hidden)

    @pl.when(pl.program_id(0) == 0)
    def _():
        d_gain_ref[...] = jnp.zeros_like(d_gain_ref)

    d_gain_ref[...] += jnp.sum(grad * hidden * scale, 0, keepdims=True)
    d_hidden = cot_ref[...].astype(f32) + norm_slope(hidden, scale, gain_ref[...], grad)
    d_hidden_ref[...] = d_hidden
    d_mixed_ref[...] = d_hidden.astype(bf)


def input_back_kernel(parts, copies, own_ref, *refs):
    *received, input_ref, gain_ref, d_hidden_ref, out_ref = refs
    grad = total_of(own_ref, received)
    values = input_ref[...].astype(f32)
    slope = norm_slope(values, row_scale(values), gain_ref[...], grad)
    out_ref[...] = own_order(d_hidden_ref[...] + slope, parts, copies).astype(bf)


def block_out_kernel(parts, copies, own_ref, *refs):
    *received, hidden_ref, out_ref = refs
    total = hidden_ref[...] + total_of(own_ref, received)
    out_ref[...] = own_order(total, parts, copies).astype(bf)


def last_sum(sides, others, parts, copies):
    rows, columns = sides[0].shape

    def kernel(*refs):
        first, first_other, second, second_other = (ref[...].astype(f32) for ref in refs[:4])
        total = jnp.concatenate([first + first_other, second + second_other], 1)
        refs[-1][...] = own_order(total, parts, copies)

    vmem = pl.BlockSpec(memory_space=pltpu.VMEM)
    return pl.pallas_call(
        kernel,
        in_specs=[vmem] * 4 + [pl.BlockSpec(memory_space=pl.ANY)] * len(others),
        out_specs=vmem,
        out_shape=jax.ShapeDtypeStruct((rows, 2 * columns), f32),
        compiler_params=pltpu.CompilerParams(vmem_limit_bytes=32 * 2**20),
        cost_estimate=NO_COST,
    )(*sides, *others)


def by_rows(kernel, arrays, outs, block=64):
    def spec(shape):
        if shape[0] == 1:
            return pl.BlockSpec(shape, lambda i: (0, 0))
        return pl.BlockSpec((block, shape[1]), lambda i: (i, 0))

    return pl.pallas_call(
        kernel,
        grid=(GROUP_ROWS // block,),
        in_specs=[spec(array.shape) for array in arrays],
        out_specs=[spec(shape) for shape, _ in outs],
        out_shape=[jax.ShapeDtypeStruct(shape, dtype) for shape, dtype in outs],
        compiler_params=pltpu.CompilerParams(dimension_semantics=("arbitrary",)),
        cost_estimate=NO_COST,
    )(*arrays)


def body(
    block_in,
    out_grad,
    norm1_gain,
    conv_weight,
    head_gain,
    qkv_weight,
    beta_weight,
    gate_weight,
    out_weight,
    norm2_gain,
    updown_weight,
    down_weight,
    seq_blocks,
    lead_blocks,
):
    devices = lax.axis_size("dp")
    parts = MODEL
    copies = devices // parts
    part = lax.axis_index("dp") // copies
    copy = lax.axis_index("dp") % copies
    rows_own = qkv_weight.shape[0]
    width = D // parts
    units = FF // parts
    heads_part = HEADS // parts
    wide = 4 * width + SMALL
    model_groups = [[m * copies + t for m in range(parts)] for t in range(copies)]
    copy_groups = [[m * copies + t for t in range(copies)] for m in range(parts)]

    def exchange(values):
        return lax.all_to_all(
            values, "dp", split_axis=0, concat_axis=0, axis_index_groups=model_groups, tiled=True
        )

    def shift(values, step):
        pairs = [
            (m * copies + t, (m + step) % parts * copies + t)
            for m in range(parts)
            for t in range(copies)
        ]
        return lax.ppermute(values, "dp", pairs)

    def exchange_apart(values, before, after=()):
        cut = [
            lax.dynamic_index_in_dim(values, (part + step) % parts, 0, keepdims=False)
            for step in range(1, parts)
        ]
        received = [shift(piece, step) for step, piece in enumerate(tie_all(cut, *before), 1)]
        return assemble(part, values, received, after)

    def gather_rows(values):
        return [values] + [shift(values, step) for step in range(1, parts)]

    def scatter_rows(terms):
        return [terms[0]] + [shift(block, -step) for step, block in enumerate(terms[1:], 1)]

    def gather_copies(values):
        return lax.all_gather(values, "dp", axis=0, axis_index_groups=copy_groups, tiled=True)

    def scatter_copies(values):
        return lax.psum_scatter(
            values.astype(bf),
            "dp",
            scatter_dimension=0,
            axis_index_groups=copy_groups,
            tiled=True,
        )

    def halves_across(values, bit, axis):
        pairs = [(i, i ^ (1 << bit)) for i in range(devices)]
        side = (copy >> bit) & 1
        own = lax.dynamic_index_in_dim(values, side, axis, keepdims=False)
        other = lax.dynamic_index_in_dim(values, 1 - side, axis, keepdims=False)
        return own, lax.ppermute(other, "dp", pairs)

    def halve(values, bit, axis, *others):
        own, received = halves_across(values, bit, axis)
        if others:
            received = tie(received, *others)
        return (own.astype(f32) + received.astype(f32)).astype(bf)

    by_halves = copies == 8

    def halve_cores(values, *others):
        if not by_halves:
            return values
        rows, columns = values.shape
        return halve(values.reshape(2, 2, 2, rows // 8, columns), 0, 2, *others)

    def halve_first(values):
        if not by_halves:
            return [values]
        middle = values.shape[-1] // 2
        return [halve(values[..., :middle], 1, 1), halve(values[..., middle:], 2, 0)]

    def halve_second(values, *others):
        if not by_halves:
            return from_wire(scatter_copies(values[0]).astype(f32))
        sides = halves_across(values[0], 2, 0) + halves_across(values[1], 1, 0)
        return last_sum(sides, others, parts, copies)

    def to_wire(values):
        return values.reshape(-1, parts, copies, rows_own).swapaxes(1, 2).reshape(-1, D)

    def from_wire(values):
        return values.reshape(-1, copies, parts, rows_own).swapaxes(1, 2).reshape(-1, D)

    w_out_own = to_wire(out_weight.astype(bf))
    w_out = gather_copies(w_out_own)
    strengths = beta_weight.reshape(rows_own, parts, heads_part)
    strengths = jnp.pad(strengths, ((0, 0), (0, 0), (0, SMALL - heads_part)))
    strengths = tie(strengths.reshape(rows_own, parts * SMALL), w_out_own)
    pieces = [(qkv_weight, section, width) for section in range(3)]
    pieces = to_parts(pieces + [(gate_weight, 0, width), (strengths, 0, SMALL)], parts, bf)
    mixer_pieces = tie(exchange(pieces), w_out)
    w_mixer = gather_copies(mixer_pieces.reshape(parts * rows_own, wide))
    inputs = tie(to_wire(block_in), mixer_pieces)
    input_rows = gather_rows(inputs)

    lanes = -(-3 * rows_own // 128) * 128
    numbers = jnp.concatenate([seq_blocks[0], lead_blocks]).astype(f32)
    small = [conv_weight.T, norm1_gain[None], head_gain[None], norm2_gain[None], numbers[None]]
    small = [jnp.pad(rows, ((0, 0), (0, lanes - rows.shape[1]))) for rows in small]
    small = jnp.pad(jnp.concatenate(small, 0).astype(bf), ((0, 2 * KERNEL), (0, 0)))
    small = jnp.broadcast_to(small[None], (devices,) + small.shape)
    small = lax.all_to_all(tie(small, *input_rows[1:]), "dp", 0, 0, tiled=True)
    taps = small[:, :KERNEL, : 3 * rows_own].swapaxes(0, 1).reshape(KERNEL, 3, parts, width)
    taps = lax.dynamic_index_in_dim(taps, part, 2, keepdims=False).reshape(KERNEL, 3 * width)
    gain_one, head_full, gain_two = (
        small[:, KERNEL + i, :rows_own].reshape(1, D).astype(f32) for i in range(3)
    )
    gain_one, gain_two = to_wire(gain_one), to_wire(gain_two)
    head_part = lax.dynamic_slice_in_dim(head_full, part * width, width, 1)
    params = jnp.concatenate([taps.astype(f32), jnp.pad(head_part, ((0, 0), (0, 2 * width)))], 0)
    params = jnp.pad(params, ((0, KERNEL - 1), (0, 0)))
    numbers = small[:, KERNEL + 3, :3].astype(f32).astype(jnp.int32)
    layouts = block_layouts(numbers[:, 0], numbers[:, 1], numbers[:, 2])
    layouts = layouts.reshape(parts, copies, 4)
    layouts = lax.dynamic_index_in_dim(layouts, copy, 1, keepdims=False)
    wanted = (part - jnp.arange(parts)) % parts
    wanted = (wanted[:, None] == jnp.arange(parts)).astype(f32)
    layouts = jnp.sum(wanted[:, :, None] * layouts, 1)

    pieces = [(updown_weight, half, units) for half in range(2)]
    updown_pieces = to_parts(pieces, parts, bf, [mixer_pieces])
    w_down_own = to_wire(down_weight.astype(bf))
    w_down = gather_copies(tie(w_down_own, *input_rows[1:]))
    cotangent_own = to_wire(out_grad)

    cotangent = lax.all_gather(
        tie(cotangent_own, *input_rows[1:]), "dp", axis=0, axis_index_groups=model_groups, tiled=True
    )
    gain_first = tie(gain_one, w_down_own, cotangent_own, updown_pieces)
    normed, pre = normed_product(input_rows, gain_first, w_mixer)
    mixed, *kept = mixer_forward(layouts, pre, params, width)
    out_terms = product_blocks(mixed, w_out)
    updown_pieces = exchange_apart(updown_pieces, input_rows[1:], out_terms[1:])
    w_updown = gather_copies(updown_pieces.reshape(parts * rows_own, 2 * units))
    stream = ((GROUP_ROWS, D), f32)
    narrow = ((GROUP_ROWS, D), bf)
    hidden, normed_two = by_rows(
        hidden_kernel,
        scatter_rows(out_terms) + [inputs, gain_two],
        [stream, narrow],
    )
    cotangent = from_own(part, cotangent)
    normed_two = jnp.concatenate(gather_rows(normed_two), 0)

    def swiglu_units(updown):
        return jax.nn.silu(updown[:, :units]) * updown[:, units:]

    updown = plain_product(normed_two, w_updown)
    active, swiglu_back = jax.vjp(swiglu_units, updown)
    active = active.astype(bf)
    d_active = transposed_product(cotangent, w_down)
    d_updown = swiglu_back(d_active)[0].astype(bf)
    d_normed_two = product_blocks(d_updown, w_updown, transposed=True)
    active = tie(active, *d_normed_two[1:])
    down_terms = grad_product(active, cotangent)
    updown_terms = grad_product(normed_two, tie(d_updown, down_terms))
    gain_late = tie(gain_two, updown_terms)
    d_normed_two = scatter_rows(d_normed_two)
    updown_grad = scatter_copies(tie(updown_terms, gain_late, *d_normed_two[1:]))
    d_hidden, d_mixed, gain_two_grad = by_rows(
        hidden_back_kernel,
        d_normed_two + [hidden, gain_late, cotangent_own],
        [stream, narrow, ((1, D), f32)],
    )


    out_terms = product_blocks(tie(active, d_mixed), w_down)
    down_terms = tie(down_terms, *out_terms[1:])
    d_mixed = gather_rows(d_mixed)
    late = tie(params, *out_terms)
    out_terms[1:] = tie_all(out_terms[1:], *d_mixed[1:])
    d_pre, d_params = mixer_backward(layouts, pre, late, w_out, d_mixed, kept, width)
    mixer_terms = tie(grad_product(normed, d_pre, micros=20), updown_grad)
    mixer_grad = scatter_copies(mixer_terms)

    d_normed_terms = product_blocks(
        tie(d_pre, mixer_terms), w_mixer, transposed=True, micros=150
    )
    hidden = tie(hidden, d_normed_terms[0])
    (block_out,) = by_rows(
        functools.partial(block_out_kernel, parts, copies),
        scatter_rows(out_terms) + [hidden],
        [narrow],
    )
    d_normed_terms[1:] = tie_all(d_normed_terms[1:], block_out)
    d_normed = scatter_rows(d_normed_terms)
    down_grad = halve_first(halve_cores(down_terms, *d_normed_terms[1:]))
    gain_one_grad = 0.0
    for values, terms in zip(input_rows, d_normed_terms):
        values = values.astype(f32)
        terms = terms.astype(f32) * (values * row_scale(values))
        gain_one_grad = gain_one_grad + jnp.sum(terms, 0, keepdims=True)

    d_params = tie(d_params, mixer_terms)
    here = (jnp.arange(parts) == part).astype(f32)[:, None]
    taps_grad = d_params[:KERNEL].reshape(KERNEL, 3, 1, width) * here
    taps_grad = taps_grad.reshape(KERNEL, parts, copies, 3, rows_own).transpose(1, 2, 3, 0, 4)
    taps_grad = taps_grad.reshape(devices, 3 * KERNEL, rows_own)
    head_grad = (d_params[KERNEL, :width] * here).reshape(devices, 1, rows_own)
    gain_grads = [
        grad.reshape(copies, parts, 1, rows_own).swapaxes(0, 1).reshape(devices, 1, rows_own)
        for grad in (gain_one_grad, gain_two_grad)
    ]
    small_grad = jnp.concatenate([taps_grad, head_grad] + gain_grads, 1)
    d_mixed = jnp.concatenate([tie(d_mixed[0], d_normed_terms[0])] + d_mixed[1:], 0)
    out_grads = grad_product(mixed, d_mixed)
    late = tie(gain_one, out_grads, *down_grad)
    (input_grad,) = by_rows(
        functools.partial(input_back_kernel, parts, copies),
        d_normed + [inputs, late, d_hidden],
        [narrow],
    )
    small_grad = jnp.pad(tie(small_grad, input_grad), ((0, 0), (0, 1), (0, 128 - rows_own)))
    small_grad = jnp.sum(lax.all_to_all(small_grad, "dp", 0, 0, tiled=True), 0)[:, :rows_own]
    taps_shard = small_grad[: 3 * KERNEL].reshape(3, KERNEL, rows_own).swapaxes(1, 2)
    taps_shard = taps_shard.reshape(3 * rows_own, KERNEL)
    head_shard, gain_one_shard, gain_two_shard = small_grad[3 * KERNEL : 3 * KERNEL + 3]

    updown_grad = tie(updown_grad, mixer_terms).reshape(parts, rows_own, 2 * units)
    updown_grad = exchange(updown_grad)
    mixer_grad = tie(mixer_grad, updown_grad, input_grad)
    updown_shard = updown_from_parts(tie(updown_grad, mixer_grad))
    down_shard = halve_second(tie_all(down_grad, input_grad), mixer_grad)
    out_grads = tie(halve_cores(tie(out_grads, input_grad)), mixer_grad)
    out_shard = halve_second(halve_first(out_grads))
    mixer_grad = exchange(mixer_grad.reshape(parts, rows_own, wide))
    qkv_shard, gate_shard, strengths = mixer_from_parts(mixer_grad, width)
    beta_shard = strengths.reshape(rows_own, parts, SMALL)[:, :, :heads_part]
    return (
        block_out,
        input_grad,
        gain_one_shard,
        taps_shard,
        head_shard,
        qkv_shard,
        beta_shard.reshape(rows_own, HEADS),
        gate_shard,
        out_shard,
        gain_two_shard,
        updown_shard,
        down_shard,
    )


def solution(mesh):
    placed = (
        P("dp", None),
        P("dp", None),
        P("dp"),
        P("dp", None),
        P("dp"),
        P("dp", None),
        P("dp", None),
        P("dp", None),
        P("dp", None),
        P("dp"),
        P("dp", None),
        P("dp", None),
        P("dp", None),
        P("dp"),
    )
    return jax.shard_map(
        body,
        mesh=mesh,
        in_specs=placed,
        out_specs=(
            P("dp", None),
            P("dp", None),
            P("dp"),
            P("dp", None),
            P("dp"),
            P("dp", None),
            P("dp", None),
            P("dp", None),
            P("dp", None),
            P("dp"),
            P("dp", None),
            P("dp", None),
        ),
        check_vma=False,
    )
```
